32 devices in a mesh: leaf: 8 (over z, core), blk: 4 (over y, x).
Axes of the slice: x: 2, y: 2, z: 4, core: 2. Of those that a mesh axis runs over, the one named last changes fastest.
Arguments:
- tokens: bfloat16 [16384, 512], P(('leaf', 'blk')), may hold values from -6 to 6
- cotangent: bfloat16 [16384, 512], P(('leaf', 'blk')), may hold values from -6 to 6
- encoded: bfloat16 [512, 512], P(('leaf', 'blk')), may hold values from -6 to 6
- parents: int32 [8, 16], P('leaf'), may hold values from 0 to 14, as said below
- timestep: int32 [8], P('leaf'), may hold values from 0 to 49
- w_qkv: bfloat16 [512, 1536], P(('leaf', 'blk')), may hold values from -0.375 to 0.375
- w_o: bfloat16 [512, 512], P(('leaf', 'blk')), may hold values from -1.5 to 1.5
- w_cq: bfloat16 [512, 512], P(('leaf', 'blk')), may hold values from -0.375 to 0.375
- w_ckv: bfloat16 [512, 1024], P(('leaf', 'blk')), may hold values from -0.375 to 0.375
- w_co: bfloat16 [512, 512], P(('leaf', 'blk')), may hold values from -0.5 to 0.5
- w_in: bfloat16 [512, 2048], P(('leaf', 'blk')), may hold values from -0.25 to 0.25
- w_out: bfloat16 [2048, 512], P(('leaf', 'blk')), may hold values from -0.25 to 0.25
- mod_table: bfloat16 [50, 3072], P(None, ('leaf', 'blk')), may hold values from -2 to 2
Outputs:
- mixed: bfloat16 [16384, 512], P(('leaf', 'blk'))
- grad_tokens: float32 [16384, 512], P(('leaf', 'blk'))
- grad_encoded: float32 [512, 512], P(('leaf', 'blk'))
- grad_qkv: float32 [512, 1536], P(('leaf', 'blk'))
- grad_o: float32 [512, 512], P(('leaf', 'blk'))
- grad_cq: float32 [512, 512], P(('leaf', 'blk'))
- grad_ckv: float32 [512, 1024], P(('leaf', 'blk'))
- grad_co: float32 [512, 512], P(('leaf', 'blk'))
- grad_in: float32 [512, 2048], P(('leaf', 'blk'))
- grad_out: float32 [2048, 512], P(('leaf', 'blk'))
- grad_table: float32 [50, 3072], P(None, ('leaf', 'blk'))
The draws below stay inside these ranges and needn't reach their ends.
Inputs may be any that keep to these rules, and one draw needn't show every extreme that they name: `parents`: block 0 of each tree is its own parent; every other block's parent is an earlier block of the same tree, and the last block's parent is the block before it.
All inputs are finite; a program needn't handle non-finite values.
Results may differ from the reference program's by a relative error of at most 0.02.
The reference program's roundings to bfloat16 on the way count: a program that leaves them out, or rounds other values in their place, can miss the bound.
Values may be sent and summed in bfloat16 or wider, within the bound.
A program may use at most 192 MiB of HBM per device.

```python
import jax
import jax.numpy as jnp
from jax import lax

D = 512
HEADS = 8
FF = 2048
HEAD = 64
BLOCK = 128
STEPS = 50
NB = 16
TREE_TOK = 2048
TREES = 8
TOKENS = 16384
ENC = 64


def draw_parents(key, part):
    keys = jax.random.split(jax.random.fold_in(key, 11), 2)
    indices = jnp.arange(NB, dtype=jnp.int32)
    coins = jax.random.randint(keys[0], (TREES, NB), 0, 10)
    earlier = jax.random.randint(keys[1], (TREES, NB), 0, jnp.maximum(indices, 1)[None, :])
    parent = jnp.where(coins < 7, jnp.maximum(indices - 1, 0)[None, :], earlier)
    parent = jnp.where(indices[None, :] == NB - 1, NB - 2, parent)
    parent = jnp.where(indices[None, :] == 0, 0, parent)
    return parent.astype(jnp.int32)


def with_ends(entries, rng, least, top_value):
    longest = entries.shape.index(max(entries.shape))
    spots = []
    for shift in (0, 1):
        where = [jax.random.randint(jax.random.fold_in(rng, axis), (), 0, length) for axis, length in enumerate(entries.shape)]
        where[longest] = (where[longest] + shift) % entries.shape[longest]
        spots.append(tuple(where))
    return entries.at[spots[0]].set(least).at[spots[1]].set(top_value)


def strengthened(values, rng, source, target, parts, factor):
    owner, partner = [(jnp.arange(values.shape[position]) // (values.shape[position] // parts)).reshape([-1 if axis == position else 1 for axis in range(values.ndim)]) for position in (source, target)]
    chosen = jax.random.permutation(rng, parts)[partner]
    strong = (owner == chosen) | (owner == (partner + parts // 2) % parts)
    return jnp.where(strong, factor * values, values)


def shard_levels(stream_key, shape, cuts, smallest, top_value):
    def one(axis_at, blocks):
        steps = jax.random.uniform(jax.random.fold_in(jax.random.fold_in(stream_key, 6), axis_at), (blocks,), jnp.float32, smallest / len(cuts), top_value / len(cuts))
        return jnp.repeat(jnp.exp(steps), shape[axis_at] // blocks).reshape((-1,) + (1,) * (len(shape) - axis_at - 1))

    level = one(*cuts[0])
    for cut in cuts[1:]:
        level = level * one(*cut)
    return level


def bell_draw(own_key, extent, scale, reach, shards=(), kind=jnp.bfloat16):
    drawn = scale * jax.random.normal(own_key, extent, jnp.float32)
    if shards:
        drawn = drawn * shard_levels(own_key, extent, shards, -0.22, 0.18)
    return jnp.clip(drawn, -reach, reach).astype(kind)


def bell_draw_with(rng, extent, deviation, limit, shards, heavy, kind=jnp.bfloat16):
    array = deviation * jax.random.normal(rng, extent, jnp.float32)
    if shards:
        array = array * shard_levels(rng, extent, shards, -0.22, 0.18)
    return jnp.clip(strengthened(array, jax.random.fold_in(rng, 3), *heavy), -limit, limit).astype(kind)


def setup_inputs(seed: int = 0) -> dict:
    streams_of = jax.random.split(jax.random.key(seed), 14)
    return {
        "tokens": bell_draw_with(streams_of[0], (TOKENS, D), 1.0, 6.0, ((0, 32),), (0, 1, 32, 2.75)),
        "cotangent": bell_draw(streams_of[1], (TOKENS, D), 1.0, 6.0, ((0, 32),)),
        "encoded": bell_draw(streams_of[2], (TREES * ENC, D), 1.0, 6.0, ((0, 32),)),
        "parents": draw_parents(jax.random.fold_in(streams_of[13], 71), 0),
        "timestep": with_ends(jax.random.randint(streams_of[4], (TREES,), 0, STEPS), jax.random.fold_in(streams_of[4], 1), 0, STEPS - 1).astype(jnp.int32),
        "w_qkv": bell_draw(streams_of[5], (D, 3 * D), (D // 2) ** -0.5, 0.375, ((0, 32),)),
        "w_o": bell_draw(streams_of[6], (D, D), (D // 32) ** -0.5, 1.5, ((0, 32),)),
        "w_cq": bell_draw(streams_of[7], (D, D), (D // 2) ** -0.5, 0.375, ((0, 32),)),
        "w_ckv": bell_draw(streams_of[8], (D, 2 * D), (D // 2) ** -0.5, 0.375, ((0, 32),)),
        "w_co": bell_draw(streams_of[9], (D, D), (D // 4) ** -0.5, 0.5, ((0, 32),)),
        "w_in": bell_draw(streams_of[10], (D, FF), D ** -0.5, 0.25, ((0, 32),)),
        "w_out": bell_draw(streams_of[11], (FF, D), (FF // 4) ** -0.5, 0.25, ((0, 32),)),
        "mod_table": bell_draw(streams_of[12], (STEPS, 6 * D), 0.3, 2.0, ((1, 32),)),
    }


@jax.custom_vjp
def low(v):
    return lax.optimization_barrier(v.astype(jnp.bfloat16)).astype(jnp.float32)

@jax.custom_vjp
def low_back(v):
    return v

def low_keep(v):
    return (low(v), None)

def low_pass(kept, grad):
    return (grad,)

def back_keep(v):
    return (v, None)

def back_low(kept, grad):
    return (low(grad),)
low.defvjp(low_keep, low_pass)
low_back.defvjp(back_keep, back_low)
PRECISE = lax.Precision.HIGHEST
MASKED = -1e+30

def matmul_high(left, right):
    return jnp.dot(left, right, precision=PRECISE)

def ancestors(parent_row):
    count = parent_row.shape[0]
    indices = jnp.arange(count, dtype=jnp.int32)

    def climb(step, state):
        reach_map, current = state
        current = parent_row[current].astype(jnp.int32)
        reach_map = jnp.maximum(reach_map, (current[:, None] == indices[None, :]).astype(jnp.float32))
        return (reach_map, current)
    start = ((indices[:, None] == indices[None, :]).astype(jnp.float32), indices)
    reach_map, current = lax.fori_loop(0, count, climb, start)
    return reach_map

def normalize(values, shift, scaling):
    centred = values - lax.optimization_barrier(jnp.mean(values, axis=-1, keepdims=True))
    spread = lax.optimization_barrier(jnp.mean(centred * centred, axis=-1, keepdims=True))
    return centred * lax.rsqrt(spread + 1e-05) * (1.0 + scaling) + shift

def self_attention(queries, keys, values, reach_map):
    length = queries.shape[0]
    width = 4 * BLOCK
    indices = jnp.arange(length, dtype=jnp.int32)
    block_of = indices // BLOCK
    place = indices % BLOCK

    def one_span(span):
        start = span * width
        part_q = lax.dynamic_slice_in_dim(queries, start, width, 0)
        rows_block = lax.dynamic_slice_in_dim(block_of, start, width, 0)
        rows_place = lax.dynamic_slice_in_dim(place, start, width, 0)
        link = reach_map[rows_block][:, block_of]
        allowed = (link > 0.5) & ((rows_block[:, None] != block_of[None, :]) | (place[None, :] <= rows_place[:, None]))
        raw = jnp.einsum('qhd,khd->hqk', part_q, keys, precision=PRECISE) * HEAD ** (-0.5)
        scores = jnp.where(allowed[None], low_back(raw), MASKED)
        probs = low(jax.nn.softmax(scores, axis=-1))
        return jnp.einsum('hqk,khd->qhd', probs, values, precision=PRECISE)
    spans = jnp.arange(length // width, dtype=jnp.int32)
    results = lax.map(jax.checkpoint(one_span), spans)
    return results.reshape(length, D)

def tree_forward(inputs, source, reach_map, modulate, weights):
    w_qkv, w_o, w_cq, w_ckv, w_co, w_in, w_out = weights
    length = inputs.shape[0]
    pieces = [modulate[i * D:(i + 1) * D] for i in range(6)]
    h_first = low(normalize(inputs, pieces[0], pieces[1]))
    projected = low(low_back(matmul_high(h_first, w_qkv)))
    queries = projected[:, :D].reshape(length, HEADS, HEAD)
    keys = projected[:, D:2 * D].reshape(length, HEADS, HEAD)
    values = projected[:, 2 * D:].reshape(length, HEADS, HEAD)
    attended = low(low_back(self_attention(queries, keys, values, reach_map)))
    middle_one = inputs + low_back(matmul_high(attended, w_o))
    h_second = low(normalize(middle_one, pieces[2], pieces[3]))
    cross_q = low(low_back(matmul_high(h_second, w_cq))).reshape(length, HEADS, HEAD)
    cross_kv = low(low_back(matmul_high(source, w_ckv)))
    cross_k = cross_kv[:, :D].reshape(-1, HEADS, HEAD)
    cross_v = cross_kv[:, D:].reshape(-1, HEADS, HEAD)
    cross_raw = low_back(jnp.einsum('qhd,khd->hqk', cross_q, cross_k, precision=PRECISE) * HEAD ** (-0.5))
    cross_prob = low(jax.nn.softmax(cross_raw, axis=-1))
    cross_out = low(low_back(jnp.einsum('hqk,khd->qhd', cross_prob, cross_v, precision=PRECISE).reshape(length, D)))
    middle_two = middle_one + low_back(matmul_high(cross_out, w_co))
    h_third = low(normalize(middle_two, pieces[4], pieces[5]))
    hidden_pre = low_back(matmul_high(h_third, w_in))
    activated = low(jax.nn.gelu(hidden_pre, approximate=True))
    return middle_two + low_back(matmul_high(activated, w_out))

def reference(tokens, cotangent, encoded, parents, timestep, w_qkv, w_o, w_cq, w_ckv, w_co, w_in, w_out, mod_table):
    weights = tuple((w.astype(jnp.float32) for w in (w_qkv, w_o, w_cq, w_ckv, w_co, w_in, w_out)))
    table = mod_table.astype(jnp.float32)
    tree_inputs = tokens.astype(jnp.float32).reshape(TREES, TREE_TOK, D)
    tree_cots = cotangent.astype(jnp.float32).reshape(TREES, TREE_TOK, D)
    tree_sources = encoded.astype(jnp.float32).reshape(TREES, ENC, D)

    def per_tree(totals, item):
        inputs, cots, source, parent_row, step_id = item
        reach_map = ancestors(parent_row)
        select = (jnp.arange(STEPS, dtype=jnp.int32) == step_id).astype(jnp.float32)

        def forward(inputs, source, table, weights):
            modulate = matmul_high(select[None, :], table)[0]
            return tree_forward(inputs, source, reach_map, modulate, weights)
        result, pull = jax.vjp(forward, inputs, source, table, weights)
        d_inputs, d_source, d_table, d_weights = pull(cots)
        totals = jax.tree.map(lambda first, second: first + second, totals, (d_table, d_weights))
        return (totals, (result, d_inputs, d_source))
    start = (jnp.zeros_like(table), tuple((jnp.zeros_like(w) for w in weights)))
    totals, (results, d_inputs, d_sources) = lax.scan(per_tree, start, (tree_inputs, tree_cots, tree_sources, parents, timestep))
    grad_table, grad_weights = totals
    return (results.reshape(TOKENS, D).astype(jnp.bfloat16), d_inputs.reshape(TOKENS, D), d_sources.reshape(TREES * ENC, D), grad_weights[0], grad_weights[1], grad_weights[2], grad_weights[3], grad_weights[4], grad_weights[5], grad_weights[6], grad_table)
```

```python
import functools

import jax
import jax.numpy as jnp
from jax import lax
from jax.experimental import pallas as pl
from jax.experimental.pallas import tpu as pltpu
from jax.sharding import PartitionSpec as P


D = 512
HEADS = 8
HEAD = 64
BLOCK = 128
STEPS = 50


PRECISE = lax.Precision.HIGHEST
MASKED = -1e30


def ancestors(parent_row):
    count = parent_row.shape[0]
    indices = jnp.arange(count, dtype=jnp.int32)
    reach_map = (indices[:, None] == indices[None, :]).astype(jnp.float32)
    reach_map = jnp.minimum(
        reach_map + (parent_row[:, None] == indices[None, :]).astype(jnp.float32), 1.0
    )
    for rounds in range(max(1, (count - 1).bit_length())):
        reach_map = jnp.minimum(jnp.dot(reach_map, reach_map, precision=PRECISE), 1.0)
    return reach_map


def normalize(values, shift, scaling):
    centred = values - jnp.mean(values, axis=-1, keepdims=True)
    spread = jnp.mean(centred * centred, axis=-1, keepdims=True)
    return centred * lax.rsqrt(spread + 1e-05) * (1.0 + scaling) + shift


def span_link(reach_rows, span):
    return lax.dynamic_slice_in_dim(reach_rows, span * 4, 4, 1)


def span_reached(reach_rows, span):
    return jnp.max(span_link(reach_rows, span)) > 0.5


def span_mask(reach_rows, first_block, span, row_count, width):
    query_index = jnp.arange(row_count, dtype=jnp.int32)
    key_index = jnp.arange(width, dtype=jnp.int32)
    query_block = first_block + query_index // BLOCK
    key_block = span * 4 + key_index // BLOCK
    link = span_link(reach_rows, span)
    link = jnp.repeat(jnp.repeat(link, BLOCK, axis=0), BLOCK, axis=1)
    same = query_block[:, None] == key_block[None, :]
    return (link > 0.5) & (
        jnp.logical_not(same) | (key_index[None, :] % BLOCK <= query_index[:, None] % BLOCK)
    )


def scores_of(queries, key_rows, allowed):
    raw = jnp.einsum(
        "qhd,khd->hqk", queries, key_rows, preferred_element_type=jnp.float32
    ) * HEAD ** (-0.5)
    return jnp.where(allowed[None], raw, MASKED)


def split_spans(keys, values):
    width = 4 * BLOCK
    count = keys.shape[0] // width
    return (
        jnp.arange(count, dtype=jnp.int32),
        keys.reshape(count, width, HEADS, HEAD),
        values.reshape(count, width, HEADS, HEAD),
    )


def tree_forward_attention(queries, keys, values, reach_rows, first_block):
    row_count = queries.shape[0]
    width = 4 * BLOCK
    spans, key_spans, value_spans = split_spans(keys, values)

    def stats(carry, item):
        span, key_rows = item

        def stats_visit(state):
            top, total = state
            allowed = span_mask(reach_rows, first_block, span, row_count, width)
            score = scores_of(queries, key_rows, allowed)
            new_top = jnp.maximum(top, jnp.max(score, axis=-1))
            weight = jnp.where(allowed[None], jnp.exp(score - new_top[..., None]), 0.0)
            return (new_top, total * jnp.exp(top - new_top) + jnp.sum(weight, axis=-1))

        return (
            lax.cond(span_reached(reach_rows, span), stats_visit, lambda state: state, carry),
            None,
        )

    start = (
        jnp.full((HEADS, row_count), MASKED, jnp.float32),
        jnp.zeros((HEADS, row_count), jnp.float32),
    )
    (top, total), unused = lax.scan(stats, start, (spans, key_spans))
    log_total = top + jnp.log(total)

    def collect(accum, item):
        span, key_rows, value_rows = item

        def collect_visit(current):
            allowed = span_mask(reach_rows, first_block, span, row_count, width)
            weight = jnp.where(
                allowed[None],
                jnp.exp(scores_of(queries, key_rows, allowed) - log_total[..., None]),
                0.0,
            )
            return current + jnp.einsum(
                "hqk,khd->qhd",
                weight.astype(jnp.bfloat16),
                value_rows,
                preferred_element_type=jnp.float32,
            )

        return (
            lax.cond(span_reached(reach_rows, span), collect_visit, lambda current: current, accum),
            None,
        )

    attended, unused = lax.scan(
        collect, jnp.zeros((row_count, HEADS, HEAD), jnp.float32), (spans, key_spans, value_spans)
    )
    return (attended, log_total)


def tree_backward_attention(queries, keys, values, reach_rows, first_block, log_total, grad_attn):
    row_count = queries.shape[0]
    width = 4 * BLOCK
    spans, key_spans, value_spans = split_spans(keys, values)

    def probs_of(span, key_rows):
        allowed = span_mask(reach_rows, first_block, span, row_count, width)
        return jnp.where(
            allowed[None],
            jnp.exp(scores_of(queries, key_rows, allowed) - log_total[..., None]),
            0.0,
        )

    def inner_pass(total, item):
        span, key_rows, value_rows = item

        def inner_visit(current):
            weight = probs_of(span, key_rows)
            d_weight = jnp.einsum(
                "qhd,khd->hqk", grad_attn, value_rows, preferred_element_type=jnp.float32
            )
            return current + jnp.sum(weight * d_weight, axis=-1)

        return (
            lax.cond(span_reached(reach_rows, span), inner_visit, lambda current: current, total),
            None,
        )

    delta, unused = lax.scan(
        inner_pass, jnp.zeros((HEADS, row_count), jnp.float32), (spans, key_spans, value_spans)
    )

    def grad_pass(d_queries, item):
        span, key_rows, value_rows = item

        def grad_visit(current):
            weight = probs_of(span, key_rows)
            d_weight = jnp.einsum(
                "qhd,khd->hqk", grad_attn, value_rows, preferred_element_type=jnp.float32
            )
            d_score = (weight * (d_weight - delta[..., None])).astype(jnp.bfloat16)
            current = current + jnp.einsum(
                "hqk,khd->qhd", d_score, key_rows, preferred_element_type=jnp.float32
            )
            d_keys = jnp.einsum(
                "hqk,qhd->khd", d_score, queries, preferred_element_type=jnp.float32
            ) * HEAD ** (-0.5)
            d_values = jnp.einsum(
                "hqk,qhd->khd",
                weight.astype(jnp.bfloat16),
                grad_attn,
                preferred_element_type=jnp.float32,
            )
            return (
                current,
                jnp.concatenate((d_keys.reshape(width, D), d_values.reshape(width, D)), axis=1),
            )

        def skip(current):
            return (current, jnp.zeros((width, 2 * D), jnp.float32))

        return lax.cond(span_reached(reach_rows, span), grad_visit, skip, d_queries)

    d_queries, terms = lax.scan(
        grad_pass, jnp.zeros((row_count, HEADS, HEAD), jnp.float32), (spans, key_spans, value_spans)
    )
    return (d_queries * HEAD ** (-0.5), terms.reshape(-1, 2 * D))


def generic_device(
    tokens,
    cotangent,
    encoded,
    parents,
    timestep,
    w_qkv,
    w_o,
    w_cq,
    w_ckv,
    w_co,
    w_in,
    w_out,
    mod_table,
):
    gathered = (
        lax.all_gather(w_qkv, ("leaf", "blk"), axis=0, tiled=True),
        lax.all_gather(w_o, ("leaf", "blk"), axis=0, tiled=True),
        lax.all_gather(w_cq, ("leaf", "blk"), axis=0, tiled=True),
        lax.all_gather(w_ckv, ("leaf", "blk"), axis=0, tiled=True),
        lax.all_gather(w_co, ("leaf", "blk"), axis=0, tiled=True),
        lax.all_gather(w_in, ("leaf", "blk"), axis=0, tiled=True),
        lax.all_gather(w_out, ("leaf", "blk"), axis=0, tiled=True),
        lax.all_gather(mod_table, ("leaf", "blk"), axis=1, tiled=True),
    )
    g_qkv, g_o, g_cq, g_ckv, g_co, g_in, g_out, g_table = gathered
    select = (jnp.arange(STEPS, dtype=jnp.int32) == timestep[0]).astype(jnp.float32)
    modulate = jnp.dot(
        select.astype(jnp.bfloat16)[None, :], g_table, preferred_element_type=jnp.float32
    )[0]
    pieces = [modulate[i * D : (i + 1) * D] for i in range(6)]
    inputs = tokens.astype(jnp.float32)
    row_count = tokens.shape[0]
    local_blocks = row_count // BLOCK
    first_block = lax.axis_index("blk") * local_blocks
    reach_map = ancestors(parents[0])
    reach_rows = lax.dynamic_slice_in_dim(reach_map, first_block, local_blocks, 0)
    scaling = HEAD ** (-0.5)
    normed_one, pull_one = jax.vjp(normalize, inputs, pieces[0], pieces[1])
    h_first = normed_one.astype(jnp.bfloat16)
    projected = jnp.dot(h_first, g_qkv, preferred_element_type=jnp.float32).astype(jnp.bfloat16)
    queries = projected[:, :D].reshape(row_count, HEADS, HEAD)
    keys, values = (
        lax.all_gather(projected[:, D : 2 * D], "blk", axis=0, tiled=True),
        lax.all_gather(projected[:, 2 * D :], "blk", axis=0, tiled=True),
    )
    attended, log_total = tree_forward_attention(queries, keys, values, reach_rows, first_block)
    attn_low = attended.reshape(row_count, D).astype(jnp.bfloat16)
    middle_one = inputs + jnp.dot(attn_low, g_o, preferred_element_type=jnp.float32)
    normed_two, pull_two = jax.vjp(normalize, middle_one, pieces[2], pieces[3])
    h_second = normed_two.astype(jnp.bfloat16)
    cross_q = (
        jnp.dot(h_second, g_cq, preferred_element_type=jnp.float32)
        .astype(jnp.bfloat16)
        .reshape(row_count, HEADS, HEAD)
    )
    source_local = jnp.dot(encoded, g_ckv, preferred_element_type=jnp.float32).astype(jnp.bfloat16)
    source_all = lax.all_gather(source_local, "blk", axis=0, tiled=True)
    cross_k = source_all[:, :D].reshape(-1, HEADS, HEAD)
    cross_v = source_all[:, D:].reshape(-1, HEADS, HEAD)
    cross_raw = (
        jnp.einsum("qhd,khd->hqk", cross_q, cross_k, preferred_element_type=jnp.float32) * scaling
    )
    cross_prob = jax.nn.softmax(cross_raw, axis=-1)
    cross_low = cross_prob.astype(jnp.bfloat16)
    cross_out = (
        jnp.einsum("hqk,khd->qhd", cross_low, cross_v, preferred_element_type=jnp.float32)
        .reshape(row_count, D)
        .astype(jnp.bfloat16)
    )
    middle_two = middle_one + jnp.dot(cross_out, g_co, preferred_element_type=jnp.float32)
    normed_three, pull_three = jax.vjp(normalize, middle_two, pieces[4], pieces[5])
    h_third = normed_three.astype(jnp.bfloat16)
    hidden_pre = jnp.dot(h_third, g_in, preferred_element_type=jnp.float32)
    activated, pull_gelu = jax.vjp(
        lambda values_in: jax.nn.gelu(values_in, approximate=True), hidden_pre
    )
    act_low = activated.astype(jnp.bfloat16)
    result = middle_two + jnp.dot(act_low, g_out, preferred_element_type=jnp.float32)
    mixed_out = result.astype(jnp.bfloat16)
    back_weights = (
        lax.all_gather(w_qkv, ("leaf", "blk"), axis=0, tiled=True),
        lax.all_gather(w_o, ("leaf", "blk"), axis=0, tiled=True),
        lax.all_gather(w_cq, ("leaf", "blk"), axis=0, tiled=True),
        lax.all_gather(w_ckv, ("leaf", "blk"), axis=0, tiled=True),
        lax.all_gather(w_co, ("leaf", "blk"), axis=0, tiled=True),
        lax.all_gather(w_in, ("leaf", "blk"), axis=0, tiled=True),
        lax.all_gather(w_out, ("leaf", "blk"), axis=0, tiled=True),
        lax.all_gather(mod_table, ("leaf", "blk"), axis=1, tiled=True),
    )
    b_qkv, b_o, b_cq, b_ckv, b_co, b_in, b_out = back_weights[:7]
    d_act = jnp.dot(cotangent, b_out.T, preferred_element_type=jnp.float32)
    d_hidden = pull_gelu(d_act)[0].astype(jnp.bfloat16)
    grad_out_w = jnp.dot(act_low.T, cotangent, preferred_element_type=jnp.float32)
    grad_in_w = jnp.dot(h_third.T, d_hidden, preferred_element_type=jnp.float32)
    d_h_third = jnp.dot(d_hidden, b_in.T, preferred_element_type=jnp.float32)
    d_middle_part, d_shift_three, d_scale_three = pull_three(d_h_third)
    d_middle_two = cotangent.astype(jnp.float32) + d_middle_part
    d_branch_two = d_middle_two.astype(jnp.bfloat16)
    grad_co_w = jnp.dot(cross_out.T, d_branch_two, preferred_element_type=jnp.float32)
    d_cross_out = (
        jnp.dot(d_branch_two, b_co.T, preferred_element_type=jnp.float32)
        .astype(jnp.bfloat16)
        .reshape(row_count, HEADS, HEAD)
    )
    d_cross_prob = jnp.einsum(
        "qhd,khd->hqk", d_cross_out, cross_v, preferred_element_type=jnp.float32
    )
    d_cross_raw = (
        cross_prob * (d_cross_prob - jnp.sum(cross_prob * d_cross_prob, axis=-1, keepdims=True))
    ).astype(jnp.bfloat16)
    d_cross_q = (
        (
            jnp.einsum("hqk,khd->qhd", d_cross_raw, cross_k, preferred_element_type=jnp.float32)
            * scaling
        )
        .reshape(row_count, D)
        .astype(jnp.bfloat16)
    )
    d_cross_k = (
        jnp.einsum("hqk,qhd->khd", d_cross_raw, cross_q, preferred_element_type=jnp.float32)
        * scaling
    )
    d_cross_v = jnp.einsum(
        "hqk,qhd->khd", cross_low, d_cross_out, preferred_element_type=jnp.float32
    )
    source_terms = jnp.concatenate((d_cross_k.reshape(-1, D), d_cross_v.reshape(-1, D)), axis=1)
    d_source = lax.psum_scatter(
        source_terms.astype(jnp.bfloat16), "blk", scatter_dimension=0, tiled=True
    )
    grad_ckv_w = jnp.dot(encoded.T, d_source, preferred_element_type=jnp.float32)
    d_encoded = jnp.dot(d_source, b_ckv.T, preferred_element_type=jnp.float32)
    grad_cq_w = jnp.dot(h_second.T, d_cross_q, preferred_element_type=jnp.float32)
    d_h_second = jnp.dot(d_cross_q, b_cq.T, preferred_element_type=jnp.float32)
    d_middle_part, d_shift_two, d_scale_two = pull_two(d_h_second)
    d_middle_one = d_middle_two + d_middle_part
    d_branch_one = d_middle_one.astype(jnp.bfloat16)
    grad_o_w = jnp.dot(attn_low.T, d_branch_one, preferred_element_type=jnp.float32)
    d_attn = (
        jnp.dot(d_branch_one, b_o.T, preferred_element_type=jnp.float32)
        .astype(jnp.bfloat16)
        .reshape(row_count, HEADS, HEAD)
    )
    keys_back, values_back = (
        lax.all_gather(projected[:, D : 2 * D], "blk", axis=0, tiled=True),
        lax.all_gather(projected[:, 2 * D :], "blk", axis=0, tiled=True),
    )
    d_queries, key_terms = tree_backward_attention(
        queries, keys_back, values_back, reach_rows, first_block, log_total, d_attn
    )
    d_key_value = lax.psum_scatter(
        key_terms.astype(jnp.bfloat16), "blk", scatter_dimension=0, tiled=True
    ).astype(jnp.float32)
    d_projected = jnp.concatenate((d_queries.reshape(row_count, D), d_key_value), axis=1).astype(
        jnp.bfloat16
    )
    grad_qkv_w = jnp.dot(h_first.T, d_projected, preferred_element_type=jnp.float32)
    d_h_first = jnp.dot(d_projected, b_qkv.T, preferred_element_type=jnp.float32)
    d_input_part, d_shift_one, d_scale_one = pull_one(d_h_first)
    d_tokens = d_middle_one + d_input_part
    d_modulate = jnp.concatenate(
        (d_shift_one, d_scale_one, d_shift_two, d_scale_two, d_shift_three, d_scale_three)
    )
    grad_table_w = select[:, None] * d_modulate[None, :]
    gradients = (
        lax.psum_scatter(grad_qkv_w, ("leaf", "blk"), scatter_dimension=0, tiled=True),
        lax.psum_scatter(grad_o_w, ("leaf", "blk"), scatter_dimension=0, tiled=True),
        lax.psum_scatter(grad_cq_w, ("leaf", "blk"), scatter_dimension=0, tiled=True),
        lax.psum_scatter(grad_ckv_w, ("leaf", "blk"), scatter_dimension=0, tiled=True),
        lax.psum_scatter(grad_co_w, ("leaf", "blk"), scatter_dimension=0, tiled=True),
        lax.psum_scatter(grad_in_w, ("leaf", "blk"), scatter_dimension=0, tiled=True),
        lax.psum_scatter(grad_out_w, ("leaf", "blk"), scatter_dimension=0, tiled=True),
        lax.psum_scatter(grad_table_w, ("leaf", "blk"), scatter_dimension=1, tiled=True),
    )
    return (
        mixed_out,
        d_tokens,
        d_encoded,
        gradients[0],
        gradients[1],
        gradients[2],
        gradients[3],
        gradients[4],
        gradients[5],
        gradients[6],
        gradients[7],
    )


MESH = pl.DeviceIdType.MESH
BF = jnp.bfloat16
F32 = jnp.float32


class Place:
    def __init__(self, levels):
        leaf = lax.axis_index("leaf")
        blk = lax.axis_index("blk")
        self.levels = levels
        self.leaf = leaf
        self.blk = blk
        self.z = leaf // 2
        self.core = leaf % 2
        self.near = blk + 1 - 2 * (blk % 2)
        self.far = (blk + 2) % 4
        self.first = self.core * self.near + (1 - self.core) * self.far
        self.second = self.core * self.far + (1 - self.core) * self.near
        self.opposite = 3 - blk
        self.sibling = self.z * 2 + 1 - self.core
        self.has_up = self.z < levels - 1
        self.has_down = self.z > 0

    def greet(self):
        barrier = pltpu.get_barrier_semaphore()

        def hello(leaf, blk):
            pl.semaphore_signal(barrier, inc=1, device_id=(leaf, blk), device_id_type=MESH)

        hello(self.sibling, self.blk)
        hello(self.leaf, self.near)
        hello(self.leaf, self.far)
        hello(self.leaf, self.opposite)
        pl.when(self.has_up)(lambda: hello(self.leaf + 2, self.blk))
        pl.when(self.has_down)(lambda: hello(self.leaf - 2, self.blk))
        ends = self.has_up.astype(jnp.int32) + self.has_down.astype(jnp.int32)
        pl.semaphore_wait(barrier, 4 + ends)


def remote(src, dst, send, recv, leaf, blk):
    return pltpu.make_async_remote_copy(
        src_ref=src, dst_ref=dst, send_sem=send, recv_sem=recv,
        device_id=(leaf, blk), device_id_type=MESH,
    )


def under(cond, action):
    if cond is None:
        action()
    else:
        pl.when(cond)(action)


def both(one, two):
    if one is None:
        return two
    if two is None:
        return one
    return jnp.logical_and(one, two)


def rows_of(start, count):
    return pl.ds(pl.multiple_of(start * count, count), count)


class Gather:
    def __init__(self, place, own, full, rows, columns, send_sem, recv_sem):
        self.place, self.own, self.full, self.rows, self.columns = place, own, full, rows, columns
        self.send_sem, self.recv_sem = send_sem, recv_sem
        self.sent = []
        self.count = 0

    def view(self, leaf, blk):
        return self.full.at[rows_of(leaf * 4 + blk, self.rows), self.columns]

    def push(self, leaf, blk, targets, cond, own=False):
        for to_leaf, to_blk, needs in targets:
            number = self.count
            self.count += 1

            def build(number=number, to_leaf=to_leaf, to_blk=to_blk):
                there = self.view(leaf, blk)
                return remote(
                    self.own if own else there, there, self.send_sem.at[number],
                    self.recv_sem.at[leaf * 4 + blk], to_leaf, to_blk,
                )

            ok = both(cond, needs)
            under(ok, lambda: build().start())
            self.sent.append((ok, build))

    def arrive(self, leaf, blk, cond=None):
        p = self.place

        def wait():
            there = self.view(leaf, blk)
            remote(there, there, self.send_sem.at[0], self.recv_sem.at[leaf * 4 + blk], p.leaf, p.second).wait_recv()

        under(cond, wait)

    def to(self, *names):
        p = self.place
        table = {
            "sibling": (p.sibling, p.blk, None),
            "first": (p.leaf, p.first, None),
            "second": (p.leaf, p.second, None),
            "up": (p.leaf + 2, p.blk, p.has_up),
            "down": (p.leaf - 2, p.blk, p.has_down),
        }
        return [table[name] for name in names]

    def steps(self):
        p = self.place
        self.push(p.leaf, p.blk, self.to("first", "up", "down", "second", "sibling"), None, own=True)
        yield
        self.arrive(p.leaf, p.first)
        self.push(p.leaf, p.first, self.to("up", "down", "second", "sibling"), None)
        yield
        for k in range(1, p.levels):
            below, above = p.leaf - 2 * k, p.leaf + 2 * k
            has_below, has_above = p.z >= k, p.z + k < p.levels
            for blk in (p.blk, p.first):
                self.arrive(below, blk, has_below)
                self.push(below, blk, self.to("up", "second", "sibling"), has_below)
                self.arrive(above, blk, has_above)
                self.push(above, blk, self.to("down", "second", "sibling"), has_above)
            yield
        for k in range(p.levels):
            for leaf, cond in ((p.leaf - 2 * k, p.z >= k), (p.leaf + 2 * k, p.z + k < p.levels)):
                if k == 0 and leaf is not None:
                    cond = None
                for blk in (p.second, p.opposite):
                    self.arrive(leaf, blk, cond)
                    self.push(leaf, blk, self.to("sibling"), cond)
                if k == 0:
                    break
            yield
        for level in range(p.levels):
            for blk in range(4):
                self.arrive(2 * level + 1 - p.core, blk)
        yield

    def finish(self):
        for ok, build in self.sent:
            under(ok, lambda build=build: build().wait_send())

    @staticmethod
    def sends(levels):
        return 5 + 4 + (levels - 1) * 12 + 2 + (levels - 1) * 4


class Share:
    def __init__(self, place, own, full, rows, send_sem, recv_sem):
        self.place, self.own, self.full, self.rows = place, own, full, rows
        self.send_sem, self.recv_sem = send_sem, recv_sem
        self.half = rows // 2

    def view(self, blk, half):
        return self.full.at[pl.ds(pl.multiple_of(blk * self.rows + half * self.half, self.half), self.half), :]

    def build(self, blk, half, to_blk, number, own=False):
        there = self.view(blk, half)
        src = self.own.at[pl.ds(half * self.half, self.half), :] if own else there
        return remote(src, there, self.send_sem.at[number], self.recv_sem.at[blk * 2 + half], self.place.leaf, to_blk)

    def steps(self):
        p = self.place
        self.copies = [
            self.build(p.blk, 0, p.near, 0, True),
            self.build(p.blk, 1, p.far, 1, True),
            self.build(p.blk, 1, p.near, 2, True),
            self.build(p.blk, 0, p.far, 3, True),
        ]
        for copy in self.copies:
            copy.start()
        yield
        for blk, half, to_blk, number in ((p.near, 0, p.far, 4), (p.far, 1, p.near, 5)):
            copy = self.build(blk, half, to_blk, number)
            copy.wait_recv()
            copy.start()
            self.copies.append(copy)
        yield
        self.build(p.near, 1, p.near, 0).wait_recv()
        self.build(p.far, 0, p.near, 0).wait_recv()
        yield
        self.build(p.opposite, 0, p.near, 0).wait_recv()
        self.build(p.opposite, 1, p.near, 0).wait_recv()
        yield

    def finish(self):
        for copy in self.copies:
            copy.wait_send()


class Spread:
    def __init__(self, place, own, full, rows, send_sem, recv_sem):
        self.place, self.own, self.full, self.rows = place, own, full, rows
        self.send_sem, self.recv_sem = send_sem, recv_sem

    def build(self, src, blk, to_blk, number):
        there = self.full.at[rows_of(blk, self.rows), :]
        return remote(there if src is None else src, there, self.send_sem.at[number], self.recv_sem.at[blk], self.place.leaf, to_blk)

    def start(self):
        p = self.place
        self.copies = [self.build(self.own, p.blk, to, n) for n, to in enumerate((p.near, p.far, p.opposite))]
        for copy in self.copies:
            copy.start()

    def arrive(self):
        p = self.place
        for blk in (p.near, p.far, p.opposite):
            self.build(None, blk, p.near, 0).wait_recv()

    def finish(self):
        for copy in self.copies:
            copy.wait_send()


class Reduce:
    def __init__(self, place, total, rows, columns, out, boxes, send_sem, recv_sem):
        self.place, self.total, self.rows, self.columns, self.out = place, total, rows, columns, out
        self.from_sibling, self.from_second, self.from_below, self.from_above, self.from_first = boxes
        self.send_sem, self.recv_sem = send_sem, recv_sem
        self.sent = []

    @staticmethod
    def slots(levels):
        return 7 * levels + 1

    @staticmethod
    def boxes(levels, rows, width, kind):
        return [
            pltpu.VMEM((levels * 4 * rows, width), kind),
            pltpu.VMEM((levels * 2 * rows, width), kind),
            pltpu.VMEM((levels * 2 * rows, width), kind),
            pltpu.VMEM((levels * 2 * rows, width), kind),
            pltpu.VMEM((rows, width), kind),
        ]

    def part(self, leaf, blk, count=1):
        return self.total.at[pl.ds(pl.multiple_of((leaf * 4 + blk) * self.rows, self.rows), self.rows * count), self.columns]

    def copy(self, src, box, position, count, number, leaf, blk):
        there = box.at[pl.ds(pl.multiple_of(position * self.rows, self.rows), self.rows * count), :]
        return remote(there if src is None else src, there, self.send_sem.at[number], self.recv_sem.at[number], leaf, blk)

    def send(self, cond, *parts):
        under(cond, lambda: self.copy(*parts).start())
        self.sent.append((cond, parts))

    def arrived(self, box, position, count, number):
        self.copy(None, box, position, count, number, self.place.leaf, self.place.first).wait_recv()

    def add(self, leaf, blk, box, position, count=1):
        unit = 16 if self.rows % 16 == 0 else self.rows
        into = (leaf * 4 + blk) * self.rows
        source = position * self.rows

        def one(step, carry):
            here = pl.ds(pl.multiple_of(into + step * unit, unit), unit)
            there = pl.ds(pl.multiple_of(source + step * unit, unit), unit)
            value = self.total[here, self.columns].astype(F32) + box[there, :].astype(F32)
            self.total[here, self.columns] = value.astype(self.total.dtype)
            return carry

        lax.fori_loop(0, count * self.rows // unit, one, 0)

    def steps(self):
        p = self.place
        levels = p.levels
        for level in range(levels):
            self.send(None, self.part(2 * level + 1 - p.core, 0, 4), self.from_sibling, 4 * level, 4, level, p.sibling, p.blk)
        yield
        for level in range(levels):
            self.arrived(self.from_sibling, 4 * level, 4, level)
            leaf = 2 * level + p.core
            self.add(leaf, 0, self.from_sibling, 4 * level, 4)
            for which, blk in enumerate((p.second, p.opposite)):
                slot = 2 * level + which
                self.send(None, self.part(leaf, blk), self.from_second, slot, 1, levels + slot, p.leaf, p.second)
        yield
        for level in range(levels):
            leaf = 2 * level + p.core
            for which, blk in enumerate((p.blk, p.first)):
                slot = 2 * level + which
                self.arrived(self.from_second, slot, 1, levels + slot)
                self.add(leaf, blk, self.from_second, slot)
        yield
        for k in range(levels - 1, -1, -1):
            for which, blk in enumerate((p.blk, p.first)):
                up, down = 2 * (p.z + k) + which, 2 * (p.z - k) + which

                def climb(up=up, blk=blk):
                    def more():
                        self.arrived(self.from_below, up, 1, 3 * levels + up)
                        self.add(p.leaf + 2 * k, blk, self.from_below, up)

                    pl.when(p.has_down)(more)

                def fall(down=down, blk=blk):
                    def more():
                        self.arrived(self.from_above, down, 1, 5 * levels + down)
                        self.add(p.leaf - 2 * k, blk, self.from_above, down)

                    pl.when(p.has_up)(more)

                if k == 0:
                    climb()
                    fall()
                else:
                    can_up, can_down = p.z + k < levels, p.z >= k
                    under(can_up, climb)
                    self.send(can_up, self.part(p.leaf + 2 * k, blk), self.from_below, up, 1, 3 * levels + up, p.leaf + 2, p.blk)
                    under(can_down, fall)
                    self.send(can_down, self.part(p.leaf - 2 * k, blk), self.from_above, down, 1, 5 * levels + down, p.leaf - 2, p.blk)
            yield
        self.send(None, self.part(p.leaf, p.first), self.from_first, 0, 1, 7 * levels, p.leaf, p.first)
        yield
        self.arrived(self.from_first, 0, 1, 7 * levels)
        unit = 16 if self.rows % 16 == 0 else self.rows
        for step in range(self.rows // unit):
            here = pl.ds(pl.multiple_of((p.leaf * 4 + p.blk) * self.rows + step * unit, unit), unit)
            there = pl.ds(step * unit, unit)
            self.out(there, self.total[here, self.columns].astype(F32) + self.from_first[there, :].astype(F32))
        yield

    def finish(self):
        for cond, parts in self.sent:
            under(cond, lambda parts=parts: self.copy(*parts).wait_send())


def run_all(sequences):
    live = [item.steps() for item in sequences]
    while live:
        live = [item for item in live if next(item, "end") != "end"]


ANY = pl.BlockSpec(memory_space=pl.ANY)


def copy_in(pairs, sem):
    copies = [pltpu.make_async_copy(src, dst, sem.at[n]) for n, (src, dst) in enumerate(pairs)]
    for copy in copies:
        copy.start()
    for copy in copies:
        copy.wait()


def gather_kernel(levels, cuts, refs):
    (pack, w_out, table, tokens, source, full_pack, full_out, full_table, full_tokens, full_source,
     send, recv, share_send, share_recv, spread_send, spread_recv, local) = refs
    place = Place(levels)
    rows = pack.shape[0]
    index = place.leaf * 4 + place.blk
    pairs = [
        (pack, full_pack.at[rows_of(index, rows), :]),
        (w_out, full_out.at[rows_of(index, w_out.shape[0]), :]),
        (table, full_table.at[rows_of(index, table.shape[0]), :]),
        (tokens, full_tokens.at[rows_of(place.blk, tokens.shape[0]), :]),
        (source, full_source.at[rows_of(place.blk, source.shape[0]), :]),
    ]
    locals_ = [pltpu.make_async_copy(src, dst, local.at[n]) for n, (src, dst) in enumerate(pairs)]
    for copy in locals_:
        copy.start()
    place.greet()
    jobs = [Gather(place, table, full_table, table.shape[0], slice(None), send.at[0], recv.at[0])]
    for n, (start, width) in enumerate(cuts):
        columns = pl.ds(start, width)
        jobs.append(Gather(place, pack.at[:, columns], full_pack, rows, columns, send.at[n + 1], recv.at[n + 1]))
    last = len(jobs)
    jobs.append(Gather(place, w_out, full_out, w_out.shape[0], slice(None), send.at[last], recv.at[last]))
    spread = Spread(place, source, full_source, source.shape[0], spread_send, spread_recv)
    spread.start()
    share = Share(place, tokens, full_tokens, tokens.shape[0], share_send, share_recv)
    run_all([share] + jobs)
    spread.arrive()
    for job in jobs + [share, spread]:
        job.finish()
    for copy in locals_:
        copy.wait()


def gather_all(levels, cuts, pack, w_out, table, tokens, source):
    count = levels * 8
    shape = lambda rows, like: jax.ShapeDtypeStruct((rows, like.shape[1]), like.dtype)
    jobs = len(cuts) + 2
    dma = pltpu.SemaphoreType.DMA
    return pl.pallas_call(
        lambda *refs: gather_kernel(levels, cuts, refs),
        out_shape=[
            shape(count * pack.shape[0], pack), shape(count * w_out.shape[0], w_out),
            shape(count * table.shape[0], table), shape(4 * tokens.shape[0], tokens), shape(4 * source.shape[0], source),
        ],
        in_specs=[ANY] * 5,
        out_specs=[ANY] * 5,
        scratch_shapes=[
            dma((jobs, Gather.sends(levels))), dma((jobs, count)),
            dma((6,)), dma((8,)), dma((3,)), dma((4,)), dma((5,)),
        ],
        compiler_params=pltpu.CompilerParams(collective_id=0, has_side_effects=True),
    )(pack, w_out, table, tokens, source)


def reduce_kernel(levels, cuts, sources, refs):
    inputs, refs = refs[:sources], refs[sources:]
    totals_out, refs = refs[:len(cuts)], refs[len(cuts):]
    totals, refs = refs[:sources], refs[sources:]
    boxes, refs = refs[:5 * len(cuts)], refs[5 * len(cuts):]
    send, recv, local = refs
    copies = [pltpu.make_async_copy(inputs[n], totals[n], local.at[n]) for n in range(sources)]
    for copy in copies:
        copy.start()
    place = Place(levels)
    place.greet()
    for copy in copies:
        copy.wait()
    jobs = []
    for n, (which, rows, columns) in enumerate(cuts):
        out = totals_out[n]

        def store(there, value, out=out):
            out[there, :] = value

        jobs.append(Reduce(place, totals[which], rows, columns, store, boxes[5 * n:5 * n + 5], send.at[n], recv.at[n]))
    run_all(jobs)
    for job in jobs:
        job.finish()


def reduce_all(levels, partials):
    count = levels * 8
    cuts = []
    for n, partial in enumerate(partials):
        cuts.append((n, partial.shape[0] // count, slice(None)))
    dma = pltpu.SemaphoreType.DMA
    boxes = []
    for partial in partials:
        boxes += Reduce.boxes(levels, partial.shape[0] // count, partial.shape[1], partial.dtype)
    return pl.pallas_call(
        lambda *refs: reduce_kernel(levels, cuts, len(partials), refs),
        out_shape=[jax.ShapeDtypeStruct((p.shape[0] // count, p.shape[1]), F32) for p in partials],
        in_specs=[ANY] * len(partials),
        out_specs=[pl.BlockSpec(memory_space=pltpu.VMEM)] * len(partials),
        scratch_shapes=[pltpu.VMEM(p.shape, p.dtype) for p in partials] + boxes + [
            dma((len(cuts), Reduce.slots(levels))), dma((len(cuts), Reduce.slots(levels))), dma((len(partials),)),
        ],
        compiler_params=pltpu.CompilerParams(collective_id=1, has_side_effects=True, vmem_limit_bytes=60 << 20),
    )(*partials)


def per_device(
    tokens,
    cotangent,
    encoded,
    parents,
    timestep,
    w_qkv,
    w_o,
    w_cq,
    w_ckv,
    w_co,
    w_in,
    w_out,
    mod_table,
):
    levels = lax.axis_size("leaf") // 2
    pack = jnp.concatenate((w_qkv, w_o, w_cq, w_ckv, w_co, w_in), axis=1)
    aux = jnp.concatenate(
        (
            jnp.pad(mod_table, ((0, 0), (0, 128 - mod_table.shape[1]))),
            jnp.full((64 - STEPS, 128), timestep[0], jnp.int32).astype(BF),
        ),
        axis=0,
    )
    full_pack, g_out, full_aux, all_tokens, all_source = gather_all(
        levels, [(0, 1536), (1536, 2560), (4096, 2048)], pack, w_out, aux, tokens, encoded
    )
    g_qkv, g_o, g_cq, g_ckv, g_co, g_in = jnp.split(full_pack, (1536, 2048, 2560, 3584, 4096), axis=1)
    full_aux = full_aux.reshape(-1, 64, 128)
    g_table = full_aux[:, :STEPS, : mod_table.shape[1]].transpose(1, 0, 2).reshape(STEPS, -1)
    steps_all = full_aux[::4, STEPS, 0].astype(jnp.int32)
    select = (jnp.arange(STEPS, dtype=jnp.int32) == timestep[0]).astype(jnp.float32)
    modulate = jnp.dot(
        select.astype(jnp.bfloat16)[None, :], g_table, preferred_element_type=jnp.float32
    )[0]
    pieces = [modulate[i * D : (i + 1) * D] for i in range(6)]
    inputs = tokens.astype(jnp.float32)
    row_count = tokens.shape[0]
    local_blocks = row_count // BLOCK
    first_block = lax.axis_index("blk") * local_blocks
    reach_map = ancestors(parents[0])
    reach_rows = lax.dynamic_slice_in_dim(reach_map, first_block, local_blocks, 0)
    scaling = HEAD ** (-0.5)
    normed_one, pull_one = jax.vjp(normalize, inputs, pieces[0], pieces[1])
    h_first = normed_one.astype(jnp.bfloat16)
    projected = jnp.dot(h_first, g_qkv, preferred_element_type=jnp.float32).astype(jnp.bfloat16)
    queries = projected[:, :D].reshape(row_count, HEADS, HEAD)
    all_normed = normalize(all_tokens.astype(jnp.float32), pieces[0], pieces[1]).astype(BF)
    all_kv = jnp.dot(all_normed, g_qkv[:, D:], preferred_element_type=jnp.float32).astype(BF)
    keys, values = all_kv[:, :D], all_kv[:, D:]
    attended, log_total = tree_forward_attention(queries, keys, values, reach_rows, first_block)
    attn_low = attended.reshape(row_count, D).astype(jnp.bfloat16)
    middle_one = inputs + jnp.dot(attn_low, g_o, preferred_element_type=jnp.float32)
    normed_two, pull_two = jax.vjp(normalize, middle_one, pieces[2], pieces[3])
    h_second = normed_two.astype(jnp.bfloat16)
    cross_q = (
        jnp.dot(h_second, g_cq, preferred_element_type=jnp.float32)
        .astype(jnp.bfloat16)
        .reshape(row_count, HEADS, HEAD)
    )
    source_all = jnp.dot(all_source, g_ckv, preferred_element_type=jnp.float32).astype(jnp.bfloat16)
    cross_k = source_all[:, :D].reshape(-1, HEADS, HEAD)
    cross_v = source_all[:, D:].reshape(-1, HEADS, HEAD)
    cross_raw = (
        jnp.einsum("qhd,khd->hqk", cross_q, cross_k, preferred_element_type=jnp.float32) * scaling
    )
    cross_prob = jax.nn.softmax(cross_raw, axis=-1)
    cross_low = cross_prob.astype(jnp.bfloat16)
    cross_out = (
        jnp.einsum("hqk,khd->qhd", cross_low, cross_v, preferred_element_type=jnp.float32)
        .reshape(row_count, D)
        .astype(jnp.bfloat16)
    )
    middle_two = middle_one + jnp.dot(cross_out, g_co, preferred_element_type=jnp.float32)
    normed_three, pull_three = jax.vjp(normalize, middle_two, pieces[4], pieces[5])
    h_third = normed_three.astype(jnp.bfloat16)
    hidden_pre = jnp.dot(h_third, g_in, preferred_element_type=jnp.float32)
    activated, pull_gelu = jax.vjp(
        lambda values_in: jax.nn.gelu(values_in, approximate=True), hidden_pre
    )
    act_low = activated.astype(jnp.bfloat16)
    result = middle_two + jnp.dot(act_low, g_out, preferred_element_type=jnp.float32)
    mixed_out = result.astype(jnp.bfloat16)
    b_qkv, b_o, b_cq, b_ckv, b_co, b_in, b_out = g_qkv, g_o, g_cq, g_ckv, g_co, g_in, g_out
    d_act = jnp.dot(cotangent, b_out.T, preferred_element_type=jnp.float32)
    d_hidden = pull_gelu(d_act)[0].astype(jnp.bfloat16)
    grad_out_w = jnp.dot(act_low.T, cotangent, preferred_element_type=jnp.float32)
    grad_in_w = jnp.dot(h_third.T, d_hidden, preferred_element_type=jnp.float32)
    d_h_third = jnp.dot(d_hidden, b_in.T, preferred_element_type=jnp.float32)
    d_middle_part, d_shift_three, d_scale_three = pull_three(d_h_third)
    d_middle_two = cotangent.astype(jnp.float32) + d_middle_part
    d_branch_two = d_middle_two.astype(jnp.bfloat16)
    grad_co_w = jnp.dot(cross_out.T, d_branch_two, preferred_element_type=jnp.float32)
    d_cross_out = (
        jnp.dot(d_branch_two, b_co.T, preferred_element_type=jnp.float32)
        .astype(jnp.bfloat16)
        .reshape(row_count, HEADS, HEAD)
    )
    d_cross_prob = jnp.einsum(
        "qhd,khd->hqk", d_cross_out, cross_v, preferred_element_type=jnp.float32
    )
    d_cross_raw = (
        cross_prob * (d_cross_prob - jnp.sum(cross_prob * d_cross_prob, axis=-1, keepdims=True))
    ).astype(jnp.bfloat16)
    d_cross_q = (
        (
            jnp.einsum("hqk,khd->qhd", d_cross_raw, cross_k, preferred_element_type=jnp.float32)
            * scaling
        )
        .reshape(row_count, D)
        .astype(jnp.bfloat16)
    )
    d_cross_k = (
        jnp.einsum("hqk,qhd->khd", d_cross_raw, cross_q, preferred_element_type=jnp.float32)
        * scaling
    )
    d_cross_v = jnp.einsum(
        "hqk,qhd->khd", cross_low, d_cross_out, preferred_element_type=jnp.float32
    )
    source_terms = jnp.concatenate((d_cross_k.reshape(-1, D), d_cross_v.reshape(-1, D)), axis=1)
    d_source = lax.psum_scatter(
        source_terms.astype(jnp.bfloat16), "blk", scatter_dimension=0, tiled=True
    )
    grad_ckv_w = jnp.dot(encoded.T, d_source, preferred_element_type=jnp.float32)
    d_encoded = jnp.dot(d_source, b_ckv.T, preferred_element_type=jnp.float32)
    grad_cq_w = jnp.dot(h_second.T, d_cross_q, preferred_element_type=jnp.float32)
    d_h_second = jnp.dot(d_cross_q, b_cq.T, preferred_element_type=jnp.float32)
    d_middle_part, d_shift_two, d_scale_two = pull_two(d_h_second)
    d_middle_one = d_middle_two + d_middle_part
    d_branch_one = d_middle_one.astype(jnp.bfloat16)
    grad_o_w = jnp.dot(attn_low.T, d_branch_one, preferred_element_type=jnp.float32)
    d_attn = (
        jnp.dot(d_branch_one, b_o.T, preferred_element_type=jnp.float32)
        .astype(jnp.bfloat16)
        .reshape(row_count, HEADS, HEAD)
    )
    d_queries, key_terms = tree_backward_attention(
        queries, keys, values, reach_rows, first_block, log_total, d_attn
    )
    d_key_value = lax.psum_scatter(
        key_terms.astype(jnp.bfloat16), "blk", scatter_dimension=0, tiled=True
    ).astype(jnp.float32)
    d_projected = jnp.concatenate((d_queries.reshape(row_count, D), d_key_value), axis=1).astype(
        jnp.bfloat16
    )
    grad_qkv_w = jnp.dot(h_first.T, d_projected, preferred_element_type=jnp.float32)
    d_h_first = jnp.dot(d_projected, b_qkv.T, preferred_element_type=jnp.float32)
    d_input_part, d_shift_one, d_scale_one = pull_one(d_h_first)
    d_tokens = d_middle_one + d_input_part
    d_modulate = jnp.concatenate(
        (d_shift_one, d_scale_one, d_shift_two, d_scale_two, d_shift_three, d_scale_three)
    )
    wide = mod_table.shape[1]
    own = jnp.arange(8)[None, :, None] == lax.axis_index("leaf")
    table_part = jnp.where(own, jnp.pad(d_modulate.reshape(-1, 1, wide), ((0, 0), (0, 0), (0, 128 - wide))), 0.0)
    low = [g.astype(BF) for g in (grad_qkv_w, grad_o_w, grad_cq_w, grad_ckv_w, grad_co_w, grad_in_w, grad_out_w)]
    *gradients, table_sum = reduce_all(levels, low + [table_part.reshape(-1, 128)])
    chosen = (jnp.arange(STEPS)[:, None] == steps_all[None, :]).astype(jnp.float32)
    table_grad = jnp.dot(chosen, table_sum[:, :wide], precision=PRECISE)
    return (mixed_out, d_tokens, d_encoded, *gradients, table_grad)


def solution(mesh):
    fits = mesh.shape["blk"] == 4 and mesh.shape["leaf"] == 8
    return jax.shard_map(
        per_device if fits else generic_device,
        mesh=mesh,
        in_specs=(
            P(("leaf", "blk"), None),
            P(("leaf", "blk"), None),
            P(("leaf", "blk"), None),
            P("leaf", None),
            P("leaf"),
            P(("leaf", "blk"), None),
            P(("leaf", "blk"), None),
            P(("leaf", "blk"), None),
            P(("leaf", "blk"), None),
            P(("leaf", "blk"), None),
            P(("leaf", "blk"), None),
            P(("leaf", "blk"), None),
            P(None, ("leaf", "blk")),
        ),
        out_specs=(
            P(("leaf", "blk"), None),
            P(("leaf", "blk"), None),
            P(("leaf", "blk"), None),
            P(("leaf", "blk"), None),
            P(("leaf", "blk"), None),
            P(("leaf", "blk"), None),
            P(("leaf", "blk"), None),
            P(("leaf", "blk"), None),
            P(("leaf", "blk"), None),
            P(("leaf", "blk"), None),
            P(None, ("leaf", "blk")),
        ),
        check_vma=False,
    )
```

```python
import functools

import jax
import jax.numpy as jnp
from jax import lax
from jax.experimental import pallas as pl
from jax.experimental.pallas import tpu as pltpu
from jax.sharding import PartitionSpec as P

D = 512
HEADS = 8
HEAD = 64
BLOCK = 128
FF = 2048
ENC = 64
STEPS = 50


PRECISE = lax.Precision.HIGHEST
MASKED = -1e30


def ancestors(parent_row):
    count = parent_row.shape[0]
    indices = jnp.arange(count, dtype=jnp.int32)
    reach_map = (indices[:, None] == indices[None, :]).astype(jnp.float32)
    reach_map = jnp.minimum(
        reach_map + (parent_row[:, None] == indices[None, :]).astype(jnp.float32), 1.0
    )
    for rounds in range(max(1, (count - 1).bit_length())):
        reach_map = jnp.minimum(jnp.dot(reach_map, reach_map, precision=PRECISE), 1.0)
    return reach_map


def normalize(values, shift, scaling):
    centred = values - jnp.mean(values, axis=-1, keepdims=True)
    spread = jnp.mean(centred * centred, axis=-1, keepdims=True)
    return centred * lax.rsqrt(spread + 1e-05) * (1.0 + scaling) + shift


def span_link(reach_rows, span):
    return lax.dynamic_slice_in_dim(reach_rows, span * 4, 4, 1)


def span_reached(reach_rows, span):
    return jnp.max(span_link(reach_rows, span)) > 0.5


def span_mask(reach_rows, first_block, span, row_count, width):
    query_index = jnp.arange(row_count, dtype=jnp.int32)
    key_index = jnp.arange(width, dtype=jnp.int32)
    query_block = first_block + query_index // BLOCK
    key_block = span * 4 + key_index // BLOCK
    link = span_link(reach_rows, span)
    link = jnp.repeat(jnp.repeat(link, BLOCK, axis=0), BLOCK, axis=1)
    same = query_block[:, None] == key_block[None, :]
    return (link > 0.5) & (
        jnp.logical_not(same) | (key_index[None, :] % BLOCK <= query_index[:, None] % BLOCK)
    )


def scores_of(queries, key_rows, allowed):
    raw = jnp.einsum(
        "qhd,khd->hqk", queries, key_rows, preferred_element_type=jnp.float32
    ) * HEAD ** (-0.5)
    return jnp.where(allowed[None], raw, MASKED)


def split_spans(keys, values):
    width = 4 * BLOCK
    count = keys.shape[0] // width
    return (
        jnp.arange(count, dtype=jnp.int32),
        keys.reshape(count, width, HEADS, HEAD),
        values.reshape(count, width, HEADS, HEAD),
    )


def tree_forward_attention(queries, keys, values, reach_rows, first_block):
    row_count = queries.shape[0]
    width = 4 * BLOCK
    spans, key_spans, value_spans = split_spans(keys, values)

    def stats(carry, item):
        span, key_rows = item

        def stats_visit(state):
            top, total = state
            allowed = span_mask(reach_rows, first_block, span, row_count, width)
            score = scores_of(queries, key_rows, allowed)
            new_top = jnp.maximum(top, jnp.max(score, axis=-1))
            weight = jnp.where(allowed[None], jnp.exp(score - new_top[..., None]), 0.0)
            return (new_top, total * jnp.exp(top - new_top) + jnp.sum(weight, axis=-1))

        return (
            lax.cond(span_reached(reach_rows, span), stats_visit, lambda state: state, carry),
            None,
        )

    start = (
        jnp.full((HEADS, row_count), MASKED, jnp.float32),
        jnp.zeros((HEADS, row_count), jnp.float32),
    )
    (top, total), unused = lax.scan(stats, start, (spans, key_spans))
    log_total = top + jnp.log(total)

    def collect(accum, item):
        span, key_rows, value_rows = item

        def collect_visit(current):
            allowed = span_mask(reach_rows, first_block, span, row_count, width)
            weight = jnp.where(
                allowed[None],
                jnp.exp(scores_of(queries, key_rows, allowed) - log_total[..., None]),
                0.0,
            )
            return current + jnp.einsum(
                "hqk,khd->qhd",
                weight.astype(jnp.bfloat16),
                value_rows,
                preferred_element_type=jnp.float32,
            )

        return (
            lax.cond(span_reached(reach_rows, span), collect_visit, lambda current: current, accum),
            None,
        )

    attended, unused = lax.scan(
        collect, jnp.zeros((row_count, HEADS, HEAD), jnp.float32), (spans, key_spans, value_spans)
    )
    return (attended, log_total)


def tree_backward_attention(queries, keys, values, reach_rows, first_block, log_total, grad_attn):
    row_count = queries.shape[0]
    width = 4 * BLOCK
    spans, key_spans, value_spans = split_spans(keys, values)

    def probs_of(span, key_rows):
        allowed = span_mask(reach_rows, first_block, span, row_count, width)
        return jnp.where(
            allowed[None],
            jnp.exp(scores_of(queries, key_rows, allowed) - log_total[..., None]),
            0.0,
        )

    def inner_pass(total, item):
        span, key_rows, value_rows = item

        def inner_visit(current):
            weight = probs_of(span, key_rows)
            d_weight = jnp.einsum(
                "qhd,khd->hqk", grad_attn, value_rows, preferred_element_type=jnp.float32
            )
            return current + jnp.sum(weight * d_weight, axis=-1)

        return (
            lax.cond(span_reached(reach_rows, span), inner_visit, lambda current: current, total),
            None,
        )

    delta, unused = lax.scan(
        inner_pass, jnp.zeros((HEADS, row_count), jnp.float32), (spans, key_spans, value_spans)
    )

    def grad_pass(d_queries, item):
        span, key_rows, value_rows = item

        def grad_visit(current):
            weight = probs_of(span, key_rows)
            d_weight = jnp.einsum(
                "qhd,khd->hqk", grad_attn, value_rows, preferred_element_type=jnp.float32
            )
            d_score = (weight * (d_weight - delta[..., None])).astype(jnp.bfloat16)
            current = current + jnp.einsum(
                "hqk,khd->qhd", d_score, key_rows, preferred_element_type=jnp.float32
            )
            d_keys = jnp.einsum(
                "hqk,qhd->khd", d_score, queries, preferred_element_type=jnp.float32
            ) * HEAD ** (-0.5)
            d_values = jnp.einsum(
                "hqk,qhd->khd",
                weight.astype(jnp.bfloat16),
                grad_attn,
                preferred_element_type=jnp.float32,
            )
            return (
                current,
                jnp.concatenate((d_keys.reshape(width, D), d_values.reshape(width, D)), axis=1),
            )

        def skip(current):
            return (current, jnp.zeros((width, 2 * D), jnp.float32))

        return lax.cond(span_reached(reach_rows, span), grad_visit, skip, d_queries)

    d_queries, terms = lax.scan(
        grad_pass, jnp.zeros((row_count, HEADS, HEAD), jnp.float32), (spans, key_spans, value_spans)
    )
    return (d_queries * HEAD ** (-0.5), terms.reshape(-1, 2 * D))


def generic_device(
    tokens,
    cotangent,
    encoded,
    parents,
    timestep,
    w_qkv,
    w_o,
    w_cq,
    w_ckv,
    w_co,
    w_in,
    w_out,
    mod_table,
):
    gathered = (
        lax.all_gather(w_qkv, ("leaf", "blk"), axis=0, tiled=True),
        lax.all_gather(w_o, ("leaf", "blk"), axis=0, tiled=True),
        lax.all_gather(w_cq, ("leaf", "blk"), axis=0, tiled=True),
        lax.all_gather(w_ckv, ("leaf", "blk"), axis=0, tiled=True),
        lax.all_gather(w_co, ("leaf", "blk"), axis=0, tiled=True),
        lax.all_gather(w_in, ("leaf", "blk"), axis=0, tiled=True),
        lax.all_gather(w_out, ("leaf", "blk"), axis=0, tiled=True),
        lax.all_gather(mod_table, ("leaf", "blk"), axis=1, tiled=True),
    )
    g_qkv, g_o, g_cq, g_ckv, g_co, g_in, g_out, g_table = gathered
    select = (jnp.arange(STEPS, dtype=jnp.int32) == timestep[0]).astype(jnp.float32)
    modulate = jnp.dot(
        select.astype(jnp.bfloat16)[None, :], g_table, preferred_element_type=jnp.float32
    )[0]
    pieces = [modulate[i * D : (i + 1) * D] for i in range(6)]
    inputs = tokens.astype(jnp.float32)
    row_count = tokens.shape[0]
    local_blocks = row_count // BLOCK
    first_block = lax.axis_index("blk") * local_blocks
    reach_map = ancestors(parents[0])
    reach_rows = lax.dynamic_slice_in_dim(reach_map, first_block, local_blocks, 0)
    scaling = HEAD ** (-0.5)
    normed_one, pull_one = jax.vjp(normalize, inputs, pieces[0], pieces[1])
    h_first = normed_one.astype(jnp.bfloat16)
    projected = jnp.dot(h_first, g_qkv, preferred_element_type=jnp.float32).astype(jnp.bfloat16)
    queries = projected[:, :D].reshape(row_count, HEADS, HEAD)
    keys, values = (
        lax.all_gather(projected[:, D : 2 * D], "blk", axis=0, tiled=True),
        lax.all_gather(projected[:, 2 * D :], "blk", axis=0, tiled=True),
    )
    attended, log_total = tree_forward_attention(queries, keys, values, reach_rows, first_block)
    attn_low = attended.reshape(row_count, D).astype(jnp.bfloat16)
    middle_one = inputs + jnp.dot(attn_low, g_o, preferred_element_type=jnp.float32)
    normed_two, pull_two = jax.vjp(normalize, middle_one, pieces[2], pieces[3])
    h_second = normed_two.astype(jnp.bfloat16)
    cross_q = (
        jnp.dot(h_second, g_cq, preferred_element_type=jnp.float32)
        .astype(jnp.bfloat16)
        .reshape(row_count, HEADS, HEAD)
    )
    source_local = jnp.dot(encoded, g_ckv, preferred_element_type=jnp.float32).astype(jnp.bfloat16)
    source_all = lax.all_gather(source_local, "blk", axis=0, tiled=True)
    cross_k = source_all[:, :D].reshape(-1, HEADS, HEAD)
    cross_v = source_all[:, D:].reshape(-1, HEADS, HEAD)
    cross_raw = (
        jnp.einsum("qhd,khd->hqk", cross_q, cross_k, preferred_element_type=jnp.float32) * scaling
    )
    cross_prob = jax.nn.softmax(cross_raw, axis=-1)
    cross_low = cross_prob.astype(jnp.bfloat16)
    cross_out = (
        jnp.einsum("hqk,khd->qhd", cross_low, cross_v, preferred_element_type=jnp.float32)
        .reshape(row_count, D)
        .astype(jnp.bfloat16)
    )
    middle_two = middle_one + jnp.dot(cross_out, g_co, preferred_element_type=jnp.float32)
    normed_three, pull_three = jax.vjp(normalize, middle_two, pieces[4], pieces[5])
    h_third = normed_three.astype(jnp.bfloat16)
    hidden_pre = jnp.dot(h_third, g_in, preferred_element_type=jnp.float32)
    activated, pull_gelu = jax.vjp(
        lambda values_in: jax.nn.gelu(values_in, approximate=True), hidden_pre
    )
    act_low = activated.astype(jnp.bfloat16)
    result = middle_two + jnp.dot(act_low, g_out, preferred_element_type=jnp.float32)
    mixed_out = result.astype(jnp.bfloat16)
    back_weights = (
        lax.all_gather(w_qkv, ("leaf", "blk"), axis=0, tiled=True),
        lax.all_gather(w_o, ("leaf", "blk"), axis=0, tiled=True),
        lax.all_gather(w_cq, ("leaf", "blk"), axis=0, tiled=True),
        lax.all_gather(w_ckv, ("leaf", "blk"), axis=0, tiled=True),
        lax.all_gather(w_co, ("leaf", "blk"), axis=0, tiled=True),
        lax.all_gather(w_in, ("leaf", "blk"), axis=0, tiled=True),
        lax.all_gather(w_out, ("leaf", "blk"), axis=0, tiled=True),
        lax.all_gather(mod_table, ("leaf", "blk"), axis=1, tiled=True),
    )
    b_qkv, b_o, b_cq, b_ckv, b_co, b_in, b_out = back_weights[:7]
    d_act = jnp.dot(cotangent, b_out.T, preferred_element_type=jnp.float32)
    d_hidden = pull_gelu(d_act)[0].astype(jnp.bfloat16)
    grad_out_w = jnp.dot(act_low.T, cotangent, preferred_element_type=jnp.float32)
    grad_in_w = jnp.dot(h_third.T, d_hidden, preferred_element_type=jnp.float32)
    d_h_third = jnp.dot(d_hidden, b_in.T, preferred_element_type=jnp.float32)
    d_middle_part, d_shift_three, d_scale_three = pull_three(d_h_third)
    d_middle_two = cotangent.astype(jnp.float32) + d_middle_part
    d_branch_two = d_middle_two.astype(jnp.bfloat16)
    grad_co_w = jnp.dot(cross_out.T, d_branch_two, preferred_element_type=jnp.float32)
    d_cross_out = (
        jnp.dot(d_branch_two, b_co.T, preferred_element_type=jnp.float32)
        .astype(jnp.bfloat16)
        .reshape(row_count, HEADS, HEAD)
    )
    d_cross_prob = jnp.einsum(
        "qhd,khd->hqk", d_cross_out, cross_v, preferred_element_type=jnp.float32
    )
    d_cross_raw = (
        cross_prob * (d_cross_prob - jnp.sum(cross_prob * d_cross_prob, axis=-1, keepdims=True))
    ).astype(jnp.bfloat16)
    d_cross_q = (
        (
            jnp.einsum("hqk,khd->qhd", d_cross_raw, cross_k, preferred_element_type=jnp.float32)
            * scaling
        )
        .reshape(row_count, D)
        .astype(jnp.bfloat16)
    )
    d_cross_k = (
        jnp.einsum("hqk,qhd->khd", d_cross_raw, cross_q, preferred_element_type=jnp.float32)
        * scaling
    )
    d_cross_v = jnp.einsum(
        "hqk,qhd->khd", cross_low, d_cross_out, preferred_element_type=jnp.float32
    )
    source_terms = jnp.concatenate((d_cross_k.reshape(-1, D), d_cross_v.reshape(-1, D)), axis=1)
    d_source = lax.psum_scatter(
        source_terms.astype(jnp.bfloat16), "blk", scatter_dimension=0, tiled=True
    )
    grad_ckv_w = jnp.dot(encoded.T, d_source, preferred_element_type=jnp.float32)
    d_encoded = jnp.dot(d_source, b_ckv.T, preferred_element_type=jnp.float32)
    grad_cq_w = jnp.dot(h_second.T, d_cross_q, preferred_element_type=jnp.float32)
    d_h_second = jnp.dot(d_cross_q, b_cq.T, preferred_element_type=jnp.float32)
    d_middle_part, d_shift_two, d_scale_two = pull_two(d_h_second)
    d_middle_one = d_middle_two + d_middle_part
    d_branch_one = d_middle_one.astype(jnp.bfloat16)
    grad_o_w = jnp.dot(attn_low.T, d_branch_one, preferred_element_type=jnp.float32)
    d_attn = (
        jnp.dot(d_branch_one, b_o.T, preferred_element_type=jnp.float32)
        .astype(jnp.bfloat16)
        .reshape(row_count, HEADS, HEAD)
    )
    keys_back, values_back = (
        lax.all_gather(projected[:, D : 2 * D], "blk", axis=0, tiled=True),
        lax.all_gather(projected[:, 2 * D :], "blk", axis=0, tiled=True),
    )
    d_queries, key_terms = tree_backward_attention(
        queries, keys_back, values_back, reach_rows, first_block, log_total, d_attn
    )
    d_key_value = lax.psum_scatter(
        key_terms.astype(jnp.bfloat16), "blk", scatter_dimension=0, tiled=True
    ).astype(jnp.float32)
    d_projected = jnp.concatenate((d_queries.reshape(row_count, D), d_key_value), axis=1).astype(
        jnp.bfloat16
    )
    grad_qkv_w = jnp.dot(h_first.T, d_projected, preferred_element_type=jnp.float32)
    d_h_first = jnp.dot(d_projected, b_qkv.T, preferred_element_type=jnp.float32)
    d_input_part, d_shift_one, d_scale_one = pull_one(d_h_first)
    d_tokens = d_middle_one + d_input_part
    d_modulate = jnp.concatenate(
        (d_shift_one, d_scale_one, d_shift_two, d_scale_two, d_shift_three, d_scale_three)
    )
    grad_table_w = select[:, None] * d_modulate[None, :]
    gradients = (
        lax.psum_scatter(grad_qkv_w, ("leaf", "blk"), scatter_dimension=0, tiled=True),
        lax.psum_scatter(grad_o_w, ("leaf", "blk"), scatter_dimension=0, tiled=True),
        lax.psum_scatter(grad_cq_w, ("leaf", "blk"), scatter_dimension=0, tiled=True),
        lax.psum_scatter(grad_ckv_w, ("leaf", "blk"), scatter_dimension=0, tiled=True),
        lax.psum_scatter(grad_co_w, ("leaf", "blk"), scatter_dimension=0, tiled=True),
        lax.psum_scatter(grad_in_w, ("leaf", "blk"), scatter_dimension=0, tiled=True),
        lax.psum_scatter(grad_out_w, ("leaf", "blk"), scatter_dimension=0, tiled=True),
        lax.psum_scatter(grad_table_w, ("leaf", "blk"), scatter_dimension=1, tiled=True),
    )
    return (
        mixed_out,
        d_tokens,
        d_encoded,
        gradients[0],
        gradients[1],
        gradients[2],
        gradients[3],
        gradients[4],
        gradients[5],
        gradients[6],
        gradients[7],
    )


MESH = pl.DeviceIdType.MESH
BF = jnp.bfloat16
F32 = jnp.float32


class Place:
    def __init__(self, levels):
        leaf = lax.axis_index("leaf")
        blk = lax.axis_index("blk")
        self.levels = levels
        self.leaf = leaf
        self.blk = blk
        self.z = leaf // 2
        self.core = leaf % 2
        self.near = blk + 1 - 2 * (blk % 2)
        self.far = (blk + 2) % 4
        self.first = self.core * self.near + (1 - self.core) * self.far
        self.second = self.core * self.far + (1 - self.core) * self.near
        self.opposite = 3 - blk
        self.sibling = self.z * 2 + 1 - self.core
        self.has_up = self.z < levels - 1
        self.has_down = self.z > 0

    def greet(self):
        barrier = pltpu.get_barrier_semaphore()

        def hello(leaf, blk):
            pl.semaphore_signal(barrier, inc=1, device_id=(leaf, blk), device_id_type=MESH)

        hello(self.sibling, self.blk)
        hello(self.leaf, self.near)
        hello(self.leaf, self.far)
        hello(self.leaf, self.opposite)
        pl.when(self.has_up)(lambda: hello(self.leaf + 2, self.blk))
        pl.when(self.has_down)(lambda: hello(self.leaf - 2, self.blk))
        ends = self.has_up.astype(jnp.int32) + self.has_down.astype(jnp.int32)
        pl.semaphore_wait(barrier, 4 + ends)


def remote(src, dst, send, recv, leaf, blk):
    return pltpu.make_async_remote_copy(
        src_ref=src, dst_ref=dst, send_sem=send, recv_sem=recv,
        device_id=(leaf, blk), device_id_type=MESH,
    )


def under(cond, action):
    if cond is None:
        action()
    else:
        pl.when(cond)(action)


def both(one, two):
    if one is None:
        return two
    if two is None:
        return one
    return jnp.logical_and(one, two)


def rows_of(start, count):
    return pl.ds(pl.multiple_of(start * count, count), count)


class Gather:
    def __init__(self, place, own, full, rows, columns, send_sem, recv_sem):
        self.place, self.own, self.full, self.rows, self.columns = place, own, full, rows, columns
        self.send_sem, self.recv_sem = send_sem, recv_sem
        self.sent = []
        self.count = 0

    def view(self, leaf, blk):
        return self.full.at[rows_of(leaf * 4 + blk, self.rows), self.columns]

    def push(self, leaf, blk, targets, cond, own=False):
        for to_leaf, to_blk, needs in targets:
            number = self.count
            self.count += 1

            def build(number=number, to_leaf=to_leaf, to_blk=to_blk):
                there = self.view(leaf, blk)
                return remote(
                    self.own if own else there, there, self.send_sem.at[number],
                    self.recv_sem.at[leaf * 4 + blk], to_leaf, to_blk,
                )

            ok = both(cond, needs)
            under(ok, lambda: build().start())
            self.sent.append((ok, build))

    def arrive(self, leaf, blk, cond=None):
        p = self.place

        def wait():
            there = self.view(leaf, blk)
            remote(there, there, self.send_sem.at[0], self.recv_sem.at[leaf * 4 + blk], p.leaf, p.second).wait_recv()

        under(cond, wait)

    def to(self, *names):
        p = self.place
        table = {
            "sibling": (p.sibling, p.blk, None),
            "first": (p.leaf, p.first, None),
            "second": (p.leaf, p.second, None),
            "up": (p.leaf + 2, p.blk, p.has_up),
            "down": (p.leaf - 2, p.blk, p.has_down),
        }
        return [table[name] for name in names]

    def steps(self):
        p = self.place
        self.push(p.leaf, p.blk, self.to("first", "up", "down", "second", "sibling"), None, own=True)
        yield
        self.arrive(p.leaf, p.first)
        self.push(p.leaf, p.first, self.to("up", "down", "second", "sibling"), None)
        yield
        for k in range(1, p.levels):
            below, above = p.leaf - 2 * k, p.leaf + 2 * k
            has_below, has_above = p.z >= k, p.z + k < p.levels
            for blk in (p.blk, p.first):
                self.arrive(below, blk, has_below)
                self.push(below, blk, self.to("up", "second", "sibling"), has_below)
                self.arrive(above, blk, has_above)
                self.push(above, blk, self.to("down", "second", "sibling"), has_above)
            yield
        for k in range(p.levels):
            for leaf, cond in ((p.leaf - 2 * k, p.z >= k), (p.leaf + 2 * k, p.z + k < p.levels)):
                if k == 0 and leaf is not None:
                    cond = None
                for blk in (p.second, p.opposite):
                    self.arrive(leaf, blk, cond)
                    self.push(leaf, blk, self.to("sibling"), cond)
                if k == 0:
                    break
            yield
        for level in range(p.levels):
            for blk in range(4):
                self.arrive(2 * level + 1 - p.core, blk)
        yield

    def finish(self):
        for ok, build in self.sent:
            under(ok, lambda build=build: build().wait_send())

    @staticmethod
    def sends(levels):
        return 5 + 4 + (levels - 1) * 12 + 2 + (levels - 1) * 4


class Share:
    def __init__(self, place, own, full, rows, send_sem, recv_sem):
        self.place, self.own, self.full, self.rows = place, own, full, rows
        self.send_sem, self.recv_sem = send_sem, recv_sem
        self.half = rows // 2

    def view(self, blk, half):
        return self.full.at[pl.ds(pl.multiple_of(blk * self.rows + half * self.half, self.half), self.half), :]

    def build(self, blk, half, to_blk, number, own=False):
        there = self.view(blk, half)
        src = self.own.at[pl.ds(half * self.half, self.half), :] if own else there
        return remote(src, there, self.send_sem.at[number], self.recv_sem.at[blk * 2 + half], self.place.leaf, to_blk)

    def steps(self):
        p = self.place
        self.copies = [
            self.build(p.blk, 0, p.near, 0, True),
            self.build(p.blk, 1, p.far, 1, True),
            self.build(p.blk, 1, p.near, 2, True),
            self.build(p.blk, 0, p.far, 3, True),
        ]
        for copy in self.copies:
            copy.start()
        yield
        for blk, half, to_blk, number in ((p.near, 0, p.far, 4), (p.far, 1, p.near, 5)):
            copy = self.build(blk, half, to_blk, number)
            copy.wait_recv()
            copy.start()
            self.copies.append(copy)
        yield
        self.build(p.near, 1, p.near, 0).wait_recv()
        self.build(p.far, 0, p.near, 0).wait_recv()
        yield
        self.build(p.opposite, 0, p.near, 0).wait_recv()
        self.build(p.opposite, 1, p.near, 0).wait_recv()
        yield

    def finish(self):
        for copy in self.copies:
            copy.wait_send()


class Spread:
    def __init__(self, place, own, full, rows, send_sem, recv_sem):
        self.place, self.own, self.full, self.rows = place, own, full, rows
        self.send_sem, self.recv_sem = send_sem, recv_sem

    def build(self, src, blk, to_blk, number):
        there = self.full.at[rows_of(blk, self.rows), :]
        return remote(there if src is None else src, there, self.send_sem.at[number], self.recv_sem.at[blk], self.place.leaf, to_blk)

    def start(self):
        p = self.place
        self.copies = [self.build(self.own, p.blk, to, n) for n, to in enumerate((p.near, p.far, p.opposite))]
        for copy in self.copies:
            copy.start()

    def arrive(self):
        p = self.place
        for blk in (p.near, p.far, p.opposite):
            self.build(None, blk, p.near, 0).wait_recv()

    def finish(self):
        for copy in self.copies:
            copy.wait_send()


class Reduce:
    def __init__(self, place, total, rows, columns, out, boxes, send_sem, recv_sem):
        self.place, self.total, self.rows, self.columns, self.out = place, total, rows, columns, out
        self.from_sibling, self.from_second, self.from_below, self.from_above, self.from_first = boxes
        self.send_sem, self.recv_sem = send_sem, recv_sem
        self.sent = []

    @staticmethod
    def slots(levels):
        return 7 * levels + 1

    @staticmethod
    def boxes(levels, rows, width, kind):
        return [
            pltpu.VMEM((levels * 4 * rows, width), kind),
            pltpu.VMEM((levels * 2 * rows, width), kind),
            pltpu.VMEM((levels * 2 * rows, width), kind),
            pltpu.VMEM((levels * 2 * rows, width), kind),
            pltpu.VMEM((rows, width), kind),
        ]

    def part(self, leaf, blk, count=1):
        return self.total.at[pl.ds(pl.multiple_of((leaf * 4 + blk) * self.rows, self.rows), self.rows * count), self.columns]

    def copy(self, src, box, position, count, number, leaf, blk):
        there = box.at[pl.ds(pl.multiple_of(position * self.rows, self.rows), self.rows * count), :]
        return remote(there if src is None else src, there, self.send_sem.at[number], self.recv_sem.at[number], leaf, blk)

    def send(self, cond, *parts):
        under(cond, lambda: self.copy(*parts).start())
        self.sent.append((cond, parts))

    def arrived(self, box, position, count, number):
        self.copy(None, box, position, count, number, self.place.leaf, self.place.first).wait_recv()

    def add(self, leaf, blk, box, position, count=1):
        unit = 16 if self.rows % 16 == 0 else self.rows
        into = (leaf * 4 + blk) * self.rows
        source = position * self.rows

        def one(step, carry):
            here = pl.ds(pl.multiple_of(into + step * unit, unit), unit)
            there = pl.ds(pl.multiple_of(source + step * unit, unit), unit)
            value = self.total[here, self.columns].astype(F32) + box[there, :].astype(F32)
            self.total[here, self.columns] = value.astype(self.total.dtype)
            return carry

        lax.fori_loop(0, count * self.rows // unit, one, 0)

    def steps(self):
        p = self.place
        levels = p.levels
        for level in range(levels):
            self.send(None, self.part(2 * level + 1 - p.core, 0, 4), self.from_sibling, 4 * level, 4, level, p.sibling, p.blk)
        yield
        for level in range(levels):
            self.arrived(self.from_sibling, 4 * level, 4, level)
            leaf = 2 * level + p.core
            self.add(leaf, 0, self.from_sibling, 4 * level, 4)
            for which, blk in enumerate((p.second, p.opposite)):
                slot = 2 * level + which
                self.send(None, self.part(leaf, blk), self.from_second, slot, 1, levels + slot, p.leaf, p.second)
        yield
        for level in range(levels):
            leaf = 2 * level + p.core
            for which, blk in enumerate((p.blk, p.first)):
                slot = 2 * level + which
                self.arrived(self.from_second, slot, 1, levels + slot)
                self.add(leaf, blk, self.from_second, slot)
        yield
        for k in range(levels - 1, -1, -1):
            for which, blk in enumerate((p.blk, p.first)):
                up, down = 2 * (p.z + k) + which, 2 * (p.z - k) + which

                def climb(up=up, blk=blk):
                    def more():
                        self.arrived(self.from_below, up, 1, 3 * levels + up)
                        self.add(p.leaf + 2 * k, blk, self.from_below, up)

                    pl.when(p.has_down)(more)

                def fall(down=down, blk=blk):
                    def more():
                        self.arrived(self.from_above, down, 1, 5 * levels + down)
                        self.add(p.leaf - 2 * k, blk, self.from_above, down)

                    pl.when(p.has_up)(more)

                if k == 0:
                    climb()
                    fall()
                else:
                    can_up, can_down = p.z + k < levels, p.z >= k
                    under(can_up, climb)
                    self.send(can_up, self.part(p.leaf + 2 * k, blk), self.from_below, up, 1, 3 * levels + up, p.leaf + 2, p.blk)
                    under(can_down, fall)
                    self.send(can_down, self.part(p.leaf - 2 * k, blk), self.from_above, down, 1, 5 * levels + down, p.leaf - 2, p.blk)
            yield
        self.send(None, self.part(p.leaf, p.first), self.from_first, 0, 1, 7 * levels, p.leaf, p.first)
        yield
        self.arrived(self.from_first, 0, 1, 7 * levels)
        unit = 16 if self.rows % 16 == 0 else self.rows
        for step in range(self.rows // unit):
            here = pl.ds(pl.multiple_of((p.leaf * 4 + p.blk) * self.rows + step * unit, unit), unit)
            there = pl.ds(step * unit, unit)
            self.out(there, self.total[here, self.columns].astype(F32) + self.from_first[there, :].astype(F32))
        yield

    def finish(self):
        for cond, parts in self.sent:
            under(cond, lambda parts=parts: self.copy(*parts).wait_send())


def run_all(sequences):
    live = [item.steps() for item in sequences]
    while live:
        live = [item for item in live if next(item, "end") != "end"]


class GatherPair:
    def __init__(self, place, own, full, send_sem, recv_sem):
        self.place, self.own, self.full = place, own, full
        self.rows, self.width = own.shape[0], full.shape[1]
        self.send_sem, self.recv_sem = send_sem, recv_sem
        self.sent = []
        self.count = 0

    def start(self, cond, make):
        under(cond, lambda: make().start())
        self.sent.append((cond, make))

    def piece(self, src_blk, to_blk, number, own):
        p = self.place
        there = self.full.at[rows_of(p.leaf * 4 + src_blk, self.rows), :]
        src = self.own.at[:, pl.ds(pl.multiple_of(to_blk * self.width, self.width), self.width)] if own else there
        return remote(src, there, self.send_sem.at[number], self.recv_sem.at[src_blk], p.leaf, to_blk)

    def block(self, leaf, number, to_leaf):
        there = self.full.at[rows_of(leaf, 4 * self.rows), :]
        return remote(there, there, self.send_sem.at[number], self.recv_sem.at[4 + leaf], to_leaf, self.place.blk)

    def push(self, leaf, cond, names):
        p = self.place
        table = {"sibling": (p.sibling, None), "up": (p.leaf + 2, p.has_up), "down": (p.leaf - 2, p.has_down)}
        for name in names:
            to_leaf, needs = table[name]
            number = 3 + self.count
            self.count += 1
            self.start(both(cond, needs), lambda number=number, to_leaf=to_leaf: self.block(leaf, number, to_leaf))

    def wait(self, leaf, cond):
        under(cond, lambda: self.block(leaf, 0, self.place.sibling).wait_recv())

    def local(self, sem):
        p = self.place
        mine = self.own.at[:, pl.ds(pl.multiple_of(p.blk * self.width, self.width), self.width)]
        return pltpu.make_async_copy(mine, self.full.at[rows_of(p.leaf * 4 + p.blk, self.rows), :], sem)

    def steps(self):
        p = self.place
        for number, to_blk in enumerate((p.near, p.far, p.opposite)):
            self.start(None, lambda to_blk=to_blk, number=number: self.piece(p.blk, to_blk, number, True))
        yield
        for blk in (p.near, p.far, p.opposite):
            self.piece(blk, p.near, 0, False).wait_recv()
        self.push(p.leaf, None, ("up", "down", "sibling"))
        yield
        for k in range(1, p.levels):
            below, above = p.leaf - 2 * k, p.leaf + 2 * k
            has_below, has_above = p.z >= k, p.z + k < p.levels
            self.wait(below, has_below)
            self.push(below, has_below, ("up", "sibling"))
            self.wait(above, has_above)
            self.push(above, has_above, ("down", "sibling"))
            yield
        for level in range(p.levels):
            self.wait(2 * level + 1 - p.core, None)
        yield

    def finish(self):
        for cond, make in self.sent:
            under(cond, lambda make=make: make().wait_send())

    @staticmethod
    def sends(levels):
        return 6 + 4 * (levels - 1)


class ReducePair:
    def __init__(self, place, total, out, boxes, send_sem, recv_sem):
        self.place, self.total, self.out = place, total, out
        self.rows = total.shape[0] // (place.levels * 8)
        self.from_sibling, self.from_below, self.from_above, self.from_pair = boxes
        self.send_sem, self.recv_sem = send_sem, recv_sem
        self.sent = []

    @staticmethod
    def slots(levels):
        return 3 * levels + 4

    @staticmethod
    def boxes(levels, rows, width, kind):
        return [pltpu.VMEM((levels * 4 * rows, width), kind) for n in range(3)] + [pltpu.VMEM((4 * rows, width), kind)]

    def send(self, cond, src, box, slot, rows, number, leaf, blk):
        def make():
            there = box.at[rows_of(slot, rows), :]
            return remote(there if src is None else src, there, self.send_sem.at[number], self.recv_sem.at[number], leaf, blk)

        under(cond, lambda: make().start())
        self.sent.append((cond, make))

    def arrived(self, box, slot, rows, number):
        there = box.at[rows_of(slot, rows), :]
        p = self.place
        remote(there, there, self.send_sem.at[0], self.recv_sem.at[number], p.sibling, p.blk).wait_recv()

    def part(self, leaf):
        return self.total.at[rows_of(leaf, 4 * self.rows), :]

    def add(self, leaf, box, slot):
        here, there = rows_of(leaf, 4 * self.rows), rows_of(slot, 4 * self.rows)
        value = self.total[here, :].astype(F32) + box[there, :].astype(F32)
        self.total[here, :] = value.astype(self.total.dtype)

    def steps(self):
        p = self.place
        levels, rows = p.levels, 4 * self.rows
        for level in range(levels):
            self.send(None, self.part(2 * level + 1 - p.core), self.from_sibling, level, rows, level, p.sibling, p.blk)
        yield
        for level in range(levels):
            self.arrived(self.from_sibling, level, rows, level)
            self.add(2 * level + p.core, self.from_sibling, level)
        yield
        for k in range(levels - 1, -1, -1):
            up, down = p.z + k, p.z - k

            def climb():
                def more():
                    self.arrived(self.from_below, up, rows, levels + up)
                    self.add(p.leaf + 2 * k, self.from_below, up)

                pl.when(p.has_down)(more)

            def fall():
                def more():
                    self.arrived(self.from_above, down, rows, 2 * levels + down)
                    self.add(p.leaf - 2 * k, self.from_above, down)

                pl.when(p.has_up)(more)

            if k == 0:
                climb()
                fall()
            else:
                under(up < levels, climb)
                self.send(up < levels, self.part(p.leaf + 2 * k), self.from_below, up, rows, levels + up, p.leaf + 2, p.blk)
                under(down >= 0, fall)
                self.send(down >= 0, self.part(p.leaf - 2 * k), self.from_above, down, rows, 2 * levels + down, p.leaf - 2, p.blk)
            yield
        for to_blk in (p.near, p.far, p.opposite):
            src = self.total.at[rows_of(p.leaf * 4 + to_blk, self.rows), :]
            self.pair_send(src, to_blk)
        yield
        self.store(p.blk, self.total[rows_of(p.leaf * 4 + p.blk, self.rows), :])
        for blk in (p.near, p.far, p.opposite):
            there = self.from_pair.at[rows_of(blk, self.rows), :]
            remote(there, there, self.send_sem.at[0], self.recv_sem.at[3 * levels + blk], p.leaf, p.near).wait_recv()
            self.store(blk, self.from_pair[rows_of(blk, self.rows), :])
        yield

    def pair_send(self, src, to_blk):
        p = self.place

        def make():
            there = self.from_pair.at[rows_of(p.blk, self.rows), :]
            return remote(src, there, self.send_sem.at[3 * p.levels + to_blk], self.recv_sem.at[3 * p.levels + p.blk], p.leaf, to_blk)

        make().start()
        self.sent.append((None, make))

    def store(self, blk, value):
        for third in range(3):
            lanes = pl.ds(pl.multiple_of(third * D + blk * 128, 128), 128)
            self.out[:, lanes] = value[:, third * 128:third * 128 + 128].astype(F32)

    def finish(self):
        for cond, make in self.sent:
            under(cond, lambda make=make: make().wait_send())


class Settle:
    def __init__(self, place, part, out, box, send_sem, recv_sem):
        self.place, self.part, self.out, self.box = place, part, out, box
        self.send_sem, self.recv_sem = send_sem, recv_sem
        self.rows = out.shape[0]

    def build(self, src_blk, to_blk):
        p = self.place
        return remote(self.part.at[rows_of(to_blk, self.rows), :], self.box.at[rows_of(src_blk, self.rows), :],
                      self.send_sem.at[to_blk], self.recv_sem.at[src_blk], p.leaf, to_blk)

    def steps(self):
        p = self.place
        self.copies = [self.build(p.blk, to) for to in (p.near, p.far, p.opposite)]
        for copy in self.copies:
            copy.start()
        yield
        total = self.part[rows_of(p.blk, self.rows), :]
        for blk in (p.near, p.far, p.opposite):
            self.build(blk, p.near).wait_recv()
            total = total + self.box[rows_of(blk, self.rows), :]
        self.out[...] = total
        yield

    def finish(self):
        for copy in self.copies:
            copy.wait_send()


SPAN = 256
TINY = 1e-05


def dot(left, right):
    return lax.dot_general(left, right, (((1,), (0,)), ((), ())), preferred_element_type=F32)


def dot_nt(left, right):
    return lax.dot_general(left, right, (((1,), (1,)), ((), ())), preferred_element_type=F32)


def dot_tn(left, right):
    return lax.dot_general(left, right, (((0,), (0,)), ((), ())), preferred_element_type=F32)


def iota(shape, axis):
    return lax.broadcasted_iota(jnp.int32, shape, axis)


def span(start, count=SPAN):
    return pl.ds(pl.multiple_of(start * count, count), count)


def loop(count, body):
    def step(index, carry):
        body(index)
        return carry

    lax.fori_loop(0, count, step, 0)


def unit_rows(values):
    centred = values - jnp.mean(values, axis=-1, keepdims=True)
    root = lax.rsqrt(jnp.mean(centred * centred, axis=-1, keepdims=True) + TINY)
    return centred * root, root


def norm_back(grad, unit, root, scale):
    inner = grad * (1.0 + scale)
    return (
        inner
        - jnp.mean(inner, axis=-1, keepdims=True)
        - unit * jnp.mean(inner * unit, axis=-1, keepdims=True)
    ) * root


def spread_pattern(wide, group):
    column = iota((128, group), 1)
    turn = jnp.zeros((128, group), jnp.int32)
    for step in range(1, group // wide):
        turn = turn + (column >= step * wide).astype(jnp.int32)
    return (column - turn * wide == iota((128, group), 0)).astype(F32)


def shard_of_column(count, wide, group):
    column = iota((count, group), 1)
    turn = jnp.zeros((count, group), jnp.int32)
    for step in range(1, group // wide):
        turn = turn + (column >= step * wide).astype(jnp.int32)
    return turn


def read_modulation(aux, timestep, mod, wide):
    count = aux.shape[0] // 64
    row = iota((count, aux.shape[0]), 0)
    column = iota((count, aux.shape[0]), 1)
    chosen = (column == row * 64 + timestep).astype(BF)
    picked = dot(chosen, aux[...])
    group = wide * 4
    laid = dot(picked.astype(BF), spread_pattern(wide, group).astype(BF))
    offset = iota((count, group), 0) - shard_of_column(count, wide, group)
    for part in range(count // 4):
        mod[0:1, part * group:(part + 1) * group] = jnp.sum(
            jnp.where(offset == 4 * part, laid, 0.0), axis=0, keepdims=True
        )


def table_payload(sums, leaf, wide, count):
    group = wide * 4
    offset = iota((count, group), 0) - shard_of_column(count, wide, group)
    held = jnp.zeros((count, group), F32)
    for part in range(count // 4):
        held = held + jnp.where(offset == 4 * part, sums[0:1, part * group:(part + 1) * group], 0.0)
    cut = lax.dot_general(held, spread_pattern(wide, group), (((1,), (1,)), ((), ())),
                          preferred_element_type=F32, precision=lax.Precision.HIGHEST)
    row = iota((count * 8, count), 0)
    chosen = (row == iota((count * 8, count), 1) * 8 + leaf).astype(F32)
    return lax.dot_general(chosen, cut, (((1,), (0,)), ((), ())),
                           preferred_element_type=F32, precision=lax.Precision.HIGHEST)


def block_bias(parents, bias, blocks):
    row, column = iota((128, 128), 0), iota((128, 128), 1)
    reach = (row == column).astype(F32)
    for block in range(blocks):
        reach = jnp.maximum(reach, ((column == block) & (row == parents[0, block])).astype(F32))
    for step in range((blocks - 1).bit_length()):
        low_reach = reach.astype(BF)
        reach = jnp.minimum(dot(low_reach, low_reach), 1.0)
    held = (reach[:blocks, :] - 1.0) * 1e30
    for block in range(blocks):
        bias[:, block * BLOCK:(block + 1) * BLOCK] = jnp.broadcast_to(held[:, block:block + 1], (blocks, BLOCK))


class Layer:
    def __init__(self, place, refs):
        self.place = place
        self.__dict__.update(refs)

    def project(self, chunk):
        rows = span(chunk)
        unit, root = unit_rows(self.tokens_all[rows, :].astype(F32))
        first = (unit * (1.0 + self.mod[0:1, D:2 * D]) + self.mod[0:1, 0:D]).astype(BF)
        self.h1[rows, :] = first
        made = dot(first, self.w_pair[...])
        lane = iota((SPAN, 128), 1)
        query = made[:, 0:128].astype(BF).astype(F32) * HEAD ** (-0.5)
        self.q_masked[0, rows, :] = jnp.where(lane < HEAD, query, 0.0).astype(BF)
        self.q_masked[1, rows, :] = jnp.where(lane >= HEAD, query, 0.0).astype(BF)
        key = made[:, 128:256]
        value = made[:, 256:384]
        self.key[rows, :] = key.astype(BF)
        self.value[rows, :] = value.astype(BF)
        self.key_t[:, rows] = key.T.astype(BF)
        value_t = value.T.astype(BF)
        ones = jnp.ones((16, SPAN), BF)
        self.value_t[0, 0:HEAD, rows] = value_t[:HEAD]
        self.value_t[1, 0:HEAD, rows] = value_t[HEAD:]
        self.value_t[0, HEAD:HEAD + 16, rows] = ones
        self.value_t[1, HEAD:HEAD + 16, rows] = ones

    def attend(self, tile):
        queries = span(tile)
        base = tile * (tile + 1) // 2
        self.top[...] = jnp.full_like(self.top, -3e30)

        def score(j, diagonal):
            keys = span(j)
            for head in range(2):
                raw = dot_nt(self.key[keys, :], self.q_masked[head, queries, :])
                upper = raw[:BLOCK] + self.bias[pl.ds(2 * j, 1), queries]
                lower = raw[BLOCK:] + self.bias[pl.ds(2 * j + 1, 1), queries]
                kept = jnp.concatenate((upper, lower), axis=0)
                if diagonal:
                    kept = kept + self.corner[...]
                self.scores[head, keys, :] = kept
                self.top[head] = jnp.maximum(self.top[head], jnp.max(kept.reshape(SPAN // 8, 8, SPAN), axis=0))

        loop(tile, lambda j: score(j, False))
        score(tile, True)
        top = [jnp.max(self.top[head], axis=0, keepdims=True) for head in range(2)]
        self.mix[...] = jnp.zeros_like(self.mix)

        def weigh(j):
            keys = span(j)
            for head in range(2):
                weight = jnp.exp(self.scores[head, keys, :] - top[head]).astype(BF)
                self.weights[base + j, head] = weight
                self.mix[head] += dot(self.value_t[head, :, keys], weight)

        loop(tile + 1, weigh)
        halves = []
        for head in range(2):
            inverse = 1.0 / self.mix[head, HEAD:HEAD + 8, :]
            self.inverse[head, :, queries] = inverse
            halves.append(self.mix[head, :HEAD, :] * inverse[0:1])
        attended_t = jnp.concatenate(halves, axis=0)
        self.attended_t[:, queries] = attended_t
        self.attended[queries, :] = attended_t.T.astype(BF)

    def cross_keys(self):
        made = dot(self.source_all[...], self.w_ckv).astype(BF)
        lane = iota((2 * ENC, 128), 1)
        row = iota((2 * ENC, 128), 0)
        own = (lane < HEAD) == (row < ENC)
        for pair in range(4):
            for box, start in ((self.cross_k, 0), (self.cross_v, D)):
                part = made[:, start + 128 * pair:start + 128 * pair + 128].astype(F32)
                box[pair] = jnp.where(own, jnp.concatenate((part, part), axis=0), 0.0).astype(BF)

    def middle(self, chunk):
        rows = span(chunk)
        own = span(self.place.blk * (self.tokens_rows // SPAN) + chunk)
        y1 = self.tokens_all[own, :].astype(F32) + dot(self.gathered[rows, :], self.w_o)
        self.y1[rows, :] = y1
        unit, root = unit_rows(y1)
        h2 = (unit * (1.0 + self.mod[0:1, 3 * D:4 * D]) + self.mod[0:1, 2 * D:3 * D]).astype(BF)
        self.h2[rows, :] = h2
        query = (dot(h2, self.w_cq).astype(BF).astype(F32) * HEAD ** (-0.5)).astype(BF)
        self.cross_q[rows, :] = query
        lane = iota((SPAN, 128), 1)
        same = ((iota((128, 128), 0) < ENC) == (iota((128, 128), 1) < ENC)).astype(BF)
        out = []
        for pair in range(4):
            raw = dot_nt(query[:, 128 * pair:128 * pair + 128], self.cross_k[pair])
            left = jnp.max(jnp.where(lane < ENC, raw, -3e38), axis=-1, keepdims=True)
            right = jnp.max(jnp.where(lane >= ENC, raw, -3e38), axis=-1, keepdims=True)
            weight = jnp.exp(raw - jnp.where(lane < ENC, left, right))
            weight = weight / dot(weight.astype(BF), same)
            self.cross_p[pair, rows, :] = weight
            out.append(dot(weight.astype(BF), self.cross_v[pair]))
        cross = jnp.concatenate(out, axis=1).astype(BF)
        self.cross_out[rows, :] = cross
        y2 = y1 + dot(cross, self.w_co)
        self.y2[rows, :] = y2
        unit, root = unit_rows(y2)
        self.h3[rows, :] = (unit * (1.0 + self.mod[0:1, 5 * D:6 * D]) + self.mod[0:1, 4 * D:5 * D]).astype(BF)

    def hidden(self, chunk):
        units = span(chunk)
        u = dot(self.h3[...], self.w_in(units))
        dg = dot_nt(self.cotangent[...], self.w_out[units, :])
        square = u * u
        slope = 0.7978845608028654
        bend = jnp.tanh(u * (slope + slope * 0.044715 * square))
        half = 0.5 + 0.5 * bend
        self.act[:, units] = (u * half).astype(BF)
        turn = half + 0.5 * u * (1.0 - bend * bend) * (slope + 3.0 * slope * 0.044715 * square)
        self.d_hidden[:, units] = (dg * turn).astype(BF)
        self.grad_out(units, dot_tn(self.act[:, units], self.cotangent[...]).astype(BF))
        self.grad_in(units, dot_tn(self.h3[...], self.d_hidden[:, units]).astype(BF))

    def finish_forward(self, chunk):
        rows = span(chunk)
        self.mixed[rows, :] = (self.y2[rows, :] + dot(self.act[rows, :], self.w_out[...])).astype(BF)

    def sums(self, piece, shift, scale):
        self.mod_grad[0:1, 2 * piece * D:(2 * piece + 1) * D] += jnp.sum(shift, axis=0, keepdims=True)
        self.mod_grad[0:1, (2 * piece + 1) * D:(2 * piece + 2) * D] += jnp.sum(scale, axis=0, keepdims=True)

    def back_three(self, chunk):
        rows = span(chunk)
        dh3 = dot_nt(self.d_hidden[rows, :], self.w_in(slice(None)))
        unit, root = unit_rows(self.y2[rows, :])
        self.sums(2, dh3, dh3 * unit)
        dy2 = self.cotangent[rows, :].astype(F32) + norm_back(dh3, unit, root, self.mod[0:1, 5 * D:6 * D])
        self.dy[rows, :] = dy2
        self.db[rows, :] = dy2.astype(BF)

    def back_cross(self, chunk):
        rows = span(chunk)
        dca = dot_nt(self.db[rows, :], self.w_co).astype(BF)
        lane = iota((SPAN, 128), 1)
        row = iota((128, 128), 0)
        own = (row < ENC) == (iota((128, 128), 1) < HEAD)
        parts = []
        for pair in range(4):
            lanes = slice(128 * pair, 128 * pair + 128)
            weight = self.cross_p[pair, rows, :]
            dc = dot_nt(dca[:, lanes], self.cross_v[pair])
            both_ = weight * dc
            left = jnp.sum(jnp.where(lane < ENC, both_, 0.0), axis=-1, keepdims=True)
            right = jnp.sum(jnp.where(lane >= ENC, both_, 0.0), axis=-1, keepdims=True)
            ds = (weight * (dc - jnp.where(lane < ENC, left, right))).astype(BF)
            parts.append((dot(ds, self.cross_k[pair]) * HEAD ** (-0.5)).astype(BF))
            dk = jnp.where(own, dot_tn(ds, self.cross_q[rows, lanes]), 0.0)
            dv = jnp.where(own, dot_tn(weight.astype(BF), dca[:, lanes]), 0.0)
            self.d_cross[:, lanes] += dk[:ENC] + dk[ENC:]
            self.d_cross[:, 128 * pair + D:128 * pair + D + 128] += dv[:ENC] + dv[ENC:]
        dcq = jnp.concatenate(parts, axis=1)
        self.dcq[rows, :] = dcq
        dh2 = dot_nt(dcq, self.w_cq)
        unit, root = unit_rows(self.y1[rows, :])
        self.sums(1, dh2, dh2 * unit)
        dy1 = self.dy[rows, :] + norm_back(dh2, unit, root, self.mod[0:1, 3 * D:4 * D])
        self.dy[rows, :] = dy1
        low_dy1 = dy1.astype(BF)
        self.db1[rows, :] = low_dy1
        self.d_attn[rows, :] = dot_nt(low_dy1, self.w_o).astype(BF)

    def attend_back(self, tile):
        queries = span(tile)
        base = tile * (tile + 1) // 2
        d_att_t = self.d_att_all[queries, :].astype(F32).T
        scaled = [d_att_t[HEAD * h:HEAD * h + HEAD] * self.inverse[h, 0:1, queries] for h in range(2)]
        delta = [
            jnp.sum(scaled[h] * self.attended_t[HEAD * h:HEAD * h + HEAD, queries], axis=0, keepdims=True)
            for h in range(2)
        ]
        flat = jnp.concatenate(scaled, axis=0).T
        lane = iota((SPAN, 128), 1)
        self.d_masked[0] = jnp.where(lane < HEAD, flat, 0.0).astype(BF)
        self.d_masked[1] = jnp.where(lane >= HEAD, flat, 0.0).astype(BF)
        self.dq_t[...] = jnp.zeros_like(self.dq_t)

        def visit(j):
            keys = span(j)
            dk = dv = 0.0
            for head in range(2):
                dp = dot_nt(self.value[keys, :], self.d_masked[head])
                weight = self.weights[base + j, head]
                ds = (weight.astype(F32) * (dp - delta[head])).astype(BF)
                dk = dk + dot(ds, self.q_masked[head, queries, :])
                dv = dv + dot(weight, self.d_masked[head])
                self.dq_t[HEAD * head:HEAD * head + HEAD, :] += dot(self.key_t[HEAD * head:HEAD * head + HEAD, keys], ds)
            self.dk[keys, :] += dk
            self.dv[keys, :] += dv

        loop(tile + 1, visit)
        self.d_pair[queries, 0:128] = (self.dq_t[...] * HEAD ** (-0.5)).T.astype(BF)
        self.d_pair[queries, 128:256] = self.dk[queries, :].astype(BF)
        self.d_pair[queries, 256:384] = self.dv[queries, :].astype(BF)
        self.dh1_part[queries, :] = dot_nt(self.d_pair[queries, :], self.w_pair[...]).astype(BF)


ANY = pl.BlockSpec(memory_space=pl.ANY)
VMEM = pl.BlockSpec(memory_space=pltpu.VMEM)
SMEM = pl.BlockSpec(memory_space=pltpu.SMEM)
CUTS = ((0, 2560), (2560, FF))


def gather_kernel(levels, refs):
    (pair, pack, w_out, table, tokens, source, full_pair, full_pack, full_out, full_table, full_tokens, full_source,
     send, recv, pair_send, pair_recv, share_send, share_recv, spread_send, spread_recv, local) = refs
    place = Place(levels)
    rows = pack.shape[0]
    index = place.leaf * 4 + place.blk
    pairs = [
        (pack, full_pack.at[rows_of(index, rows), :]),
        (w_out, full_out.at[rows_of(index, w_out.shape[0]), :]),
        (table, full_table.at[rows_of(index, table.shape[0]), :]),
        (tokens, full_tokens.at[rows_of(place.blk, tokens.shape[0]), :]),
        (source, full_source.at[rows_of(place.blk, source.shape[0]), :]),
    ]
    weave = GatherPair(place, pair, full_pair, pair_send, pair_recv)
    mine = weave.local(local.at[5])
    mine.start()
    locals_ = [pltpu.make_async_copy(src, dst, local.at[n]) for n, (src, dst) in enumerate(pairs)]
    for copy in locals_:
        copy.start()
    place.greet()
    mine.wait()
    jobs = [Gather(place, table, full_table, table.shape[0], slice(None), send.at[0], recv.at[0])]
    for n, (start, width) in enumerate(CUTS):
        columns = pl.ds(start, width)
        jobs.append(Gather(place, pack.at[:, columns], full_pack, rows, columns, send.at[n + 1], recv.at[n + 1]))
    last = len(jobs)
    jobs.append(Gather(place, w_out, full_out, w_out.shape[0], slice(None), send.at[last], recv.at[last]))
    spread = Spread(place, source, full_source, source.shape[0], spread_send, spread_recv)
    spread.start()
    share = Share(place, tokens, full_tokens, tokens.shape[0], share_send, share_recv)
    run_all([weave, share] + jobs)
    spread.arrive()
    for job in jobs + [share, spread, weave]:
        job.finish()
    for copy in locals_:
        copy.wait()


def gather_all(levels, pair, pack, w_out, table, tokens, source):
    count = levels * 8
    shape = lambda rows, like: jax.ShapeDtypeStruct((rows, like.shape[1]), like.dtype)
    jobs = len(CUTS) + 2
    dma = pltpu.SemaphoreType.DMA
    return pl.pallas_call(
        lambda *refs: gather_kernel(levels, refs),
        out_shape=[
            jax.ShapeDtypeStruct((count * pair.shape[0], pair.shape[1] // 4), BF),
            shape(count * pack.shape[0], pack), shape(count * w_out.shape[0], w_out),
            shape(count * table.shape[0], table), shape(4 * tokens.shape[0], tokens), shape(4 * source.shape[0], source),
        ],
        in_specs=[ANY] * 6,
        out_specs=[ANY] * 6,
        scratch_shapes=[
            dma((jobs, Gather.sends(levels))), dma((jobs, count)),
            dma((GatherPair.sends(levels),)), dma((4 + 2 * levels,)),
            dma((6,)), dma((8,)), dma((3,)), dma((4,)), dma((6,)),
        ],
        compiler_params=pltpu.CompilerParams(collective_id=0, has_side_effects=True),
    )(pair, pack, w_out, table, tokens, source)


class Weights(Layer):
    w_o = property(lambda self: self.pack[:, 0:D])
    w_cq = property(lambda self: self.pack[:, D:2 * D])
    w_ckv = property(lambda self: self.pack[:, 2 * D:4 * D])
    w_co = property(lambda self: self.pack[:, 4 * D:5 * D])

    def w_in(self, units):
        return self.pack.at[:, 5 * D:5 * D + FF][:, units]

    def grad_in(self, units, value):
        self.grad_pack.at[:, 5 * D:5 * D + FF][:, units] = value

    def grad_out(self, units, value):
        self.grad_w_out[units, :] = value

    def grad_into(self, start, left, right):
        for step in range(right.shape[1] // SPAN):
            columns = slice(start + step * SPAN, start + (step + 1) * SPAN)
            self.grad_pack[:, columns] = dot_tn(left[...], right[:, step * SPAN:(step + 1) * SPAN]).astype(BF)


INS = ("w_pair", "pack", "w_out", "aux", "tokens_all", "source_all", "cotangent", "parents", "timestep")
OUTS = ("mixed", "grad_tokens", "source_grad", "grad_pair", "grad_pack", "grad_w_out", "table_part")


def layer_scratch(rows, tree, blocks):
    tiles = tree // SPAN
    plain = lambda *shape: pltpu.VMEM(shape, F32)
    short = lambda *shape: pltpu.VMEM(shape, BF)
    dma = pltpu.SemaphoreType.DMA
    return dict(
        mod=plain(8, 6 * D), mod_grad=plain(8, 6 * D), bias=plain(blocks, tree), corner=plain(SPAN, SPAN),
        h1=short(tree, D), q_masked=short(2, tree, 128), key=short(tree, 128), value=short(tree, 128),
        key_t=short(128, tree), value_t=short(2, HEAD + 16, tree),
        scores=plain(2, tree, SPAN), top=plain(2, 8, SPAN), mix=plain(2, HEAD + 16, SPAN),
        weights=short(tiles * (tiles + 1) // 2, 2, SPAN, SPAN), inverse=plain(2, 8, tree),
        attended_t=plain(128, tree), attended=short(tree, 128), gathered=short(rows, D),
        cross_k=short(4, 2 * ENC, 128), cross_v=short(4, 2 * ENC, 128), cross_q=short(rows, D), cross_p=plain(4, rows, 128),
        cross_out=short(rows, D), y1=plain(rows, D), y2=plain(rows, D), h2=short(rows, D), h3=short(rows, D),
        act=short(rows, FF), d_hidden=short(rows, FF), dy=plain(rows, D), db=short(rows, D), db1=short(rows, D),
        d_cross=plain(ENC, 2 * D), dcq=short(rows, D), d_attn=short(rows, D), d_att_all=short(tree, 128),
        d_masked=short(2, SPAN, 128), dq_t=plain(128, SPAN), dk=plain(tree, 128), dv=plain(tree, 128),
        d_pair=short(tree, 384), dh1_part=short(tree, D), dh1_box=short(4, rows, D),
        a_send=dma((tiles,)), a_recv=dma((tiles,)), d_send=dma((4,)), d_recv=dma((4,)), h_send=dma((tiles,)), h_recv=dma((tiles,)),
    )


def layer_kernel(levels, names, refs):
    place = Place(levels)
    refs = dict(zip(names, refs))
    refs["tokens_rows"] = refs["cotangent"].shape[0]
    w = Weights(place, refs)
    blk, leaf = place.blk, place.leaf
    peers = (place.near, place.far, place.opposite)
    barrier = pltpu.get_barrier_semaphore()
    for peer in peers:
        pl.semaphore_signal(barrier, inc=1, device_id=(leaf, peer), device_id_type=MESH)
    pl.semaphore_wait(barrier, 3)

    rows = w.tokens_rows
    tree = w.tokens_all.shape[0]
    tiles = tree // SPAN
    halves = rows // SPAN
    blocks = tree // BLOCK
    wide = 6 * D // (levels * 8)
    own_lanes = pl.ds(pl.multiple_of(blk * 128, 128), 128)

    read_modulation(w.aux, w.timestep[0], w.mod, wide)
    block_bias(w.parents, w.bias, blocks)
    row, column = iota((SPAN, SPAN), 0), iota((SPAN, SPAN), 1)
    same = (row < BLOCK) == (column < BLOCK)
    w.corner[...] = jnp.where(same & (row > column), -1e30, 0.0)
    w.mod_grad[...] = jnp.zeros_like(w.mod_grad)
    w.d_cross[...] = jnp.zeros_like(w.d_cross)
    w.dk[...] = jnp.zeros_like(w.dk)
    w.dv[...] = jnp.zeros_like(w.dv)
    loop(tiles, w.project)

    def attended_copy(tile, src):
        there = w.gathered.at[span(tile % halves), pl.ds(pl.multiple_of(src * 128, 128), 128)]
        return remote(w.attended.at[span(tile), :], there, w.a_send.at[tile], w.a_recv.at[src * halves + tile % halves], leaf, tile // halves)

    def forward(tile):
        w.attend(tile)
        away = tile // halves != blk
        pl.when(away)(lambda: attended_copy(tile, blk).start())

        def keep():
            w.gathered[span(tile % halves), own_lanes] = w.attended[span(tile), :]

        pl.when(jnp.logical_not(away))(keep)

    loop(tiles, forward)
    w.cross_keys()
    for peer in peers:
        for half in range(halves):
            attended_copy(blk * halves + half, peer).wait_recv()
    loop(halves, w.middle)
    loop(FF // SPAN, w.hidden)
    loop(halves, w.finish_forward)
    loop(halves, w.back_three)
    w.grad_into(4 * D, w.cross_out, w.db)
    loop(halves, w.back_cross)

    def da_copy(src, to):
        return remote(w.d_attn.at[:, pl.ds(pl.multiple_of(to * 128, 128), 128)], w.d_att_all.at[rows_of(src, rows), :],
                      w.d_send.at[to], w.d_recv.at[src], leaf, to)

    for peer in peers:
        da_copy(blk, peer).start()
    w.d_att_all[rows_of(blk, rows), :] = w.d_attn[:, own_lanes]
    w.grad_into(0, w.gathered, w.db1)
    w.grad_into(D, w.h2, w.dcq)
    low_cross = w.d_cross[...].astype(BF)
    for step in range(2 * D // SPAN):
        columns = slice(2 * D + step * SPAN, 2 * D + (step + 1) * SPAN)
        w.grad_pack[:, columns] = dot_tn(w.source_all[...], low_cross[:, step * SPAN:(step + 1) * SPAN]).astype(BF)
    w.source_grad[...] = dot_nt(low_cross, w.w_ckv)
    for peer in peers:
        da_copy(peer, peer).wait_recv()

    def part_copy(tile, src):
        there = w.dh1_box.at[src, span(tile % halves), :]
        return remote(w.dh1_part.at[span(tile), :], there, w.h_send.at[tile], w.h_recv.at[src * halves + tile % halves], leaf, tile // halves)

    def backward(step):
        tile = tiles - 1 - step
        w.attend_back(tile)
        pl.when(tile // halves != blk)(lambda: part_copy(tile, blk).start())

    loop(tiles, backward)

    def pair_grad(step):
        w.grad_pair[span(step), :] = dot_tn(w.h1[:, span(step)], w.d_pair[...]).astype(BF)

    loop(D // SPAN, pair_grad)
    for peer in peers:
        for half in range(halves):
            part_copy(blk * halves + half, peer).wait_recv()

    def last(chunk):
        here, own = span(chunk), span(blk * halves + chunk)
        dh1 = w.dh1_part[own, :].astype(F32)
        for peer in peers:
            dh1 = dh1 + w.dh1_box[peer, here, :].astype(F32)
        unit, root = unit_rows(w.tokens_all[own, :].astype(F32))
        w.sums(0, dh1, dh1 * unit)
        w.grad_tokens[here, :] = w.dy[here, :] + norm_back(dh1, unit, root, w.mod[0:1, D:2 * D])

    loop(halves, last)
    w.table_part[...] = table_payload(w.mod_grad[0:1, :], leaf, wide, levels * 8)

    def drain(tile):
        def gone():
            attended_copy(tile, blk).wait_send()
            part_copy(tile, blk).wait_send()

        pl.when(tile // halves != blk)(gone)

    loop(tiles, drain)
    for peer in peers:
        da_copy(blk, peer).wait_send()


def layer_all(levels, blocks, ins):
    rows, tree = ins["cotangent"].shape[0], ins["tokens_all"].shape[0]
    scratch = layer_scratch(rows, tree, blocks)
    outs = dict(
        mixed=((rows, D), BF), grad_tokens=((rows, D), F32), source_grad=((ENC, D), F32), grad_pair=((D, 384), BF),
        grad_pack=((D, 5 * D + FF), BF), grad_w_out=((FF, D), BF), table_part=((levels * 64, 128), F32),
    )
    names = INS + OUTS + tuple(scratch)
    return pl.pallas_call(
        lambda *refs: layer_kernel(levels, names, refs),
        out_shape=[jax.ShapeDtypeStruct(*outs[name]) for name in OUTS],
        in_specs=[SMEM if name in ("parents", "timestep") else VMEM for name in INS],
        out_specs=[VMEM] * len(OUTS),
        scratch_shapes=list(scratch.values()),
        compiler_params=pltpu.CompilerParams(collective_id=2, has_side_effects=True, vmem_limit_bytes=63 << 20),
    )(*[ins[name] for name in INS])


def reduce_kernel(levels, refs):
    (pair, pack, w_out, table, source, pair_out, pack_a, pack_b, w_out_out, table_out, source_out,
     pair_total, pack_total, out_total, table_total) = refs[:15]
    boxes, (send, recv, pair_send, pair_recv, settle_send, settle_recv, local, settle_box) = refs[15:-8], refs[-8:]
    moves = [(pair, pair_total), (pack, pack_total), (w_out, out_total), (table, table_total)]
    copies = [pltpu.make_async_copy(src, dst, local.at[n]) for n, (src, dst) in enumerate(moves)]
    for copy in copies:
        copy.start()
    place = Place(levels)
    place.greet()
    for copy in copies:
        copy.wait()

    def writer(out):
        def store(there, value):
            out[there, :] = value

        return store

    jobs = []
    count = levels * 8
    plan = [(out_total, slice(None), w_out_out), (pack_total, slice(*CUTS[0]), pack_a),
            (pack_total, slice(CUTS[1][0], sum(CUTS[1])), pack_b), (table_total, slice(None), table_out)]
    for n, (total, columns, out) in enumerate(plan):
        jobs.append(Reduce(place, total, total.shape[0] // count, columns, writer(out), boxes[5 * n:5 * n + 5], send.at[n], recv.at[n]))
    jobs.append(ReducePair(place, pair_total, pair_out, boxes[20:24], pair_send, pair_recv))
    jobs.append(Settle(place, source, source_out, settle_box, settle_send, settle_recv))
    run_all(jobs)
    for job in jobs:
        job.finish()


def reduce_all(levels, pair, pack, w_out, table, source):
    count = levels * 8
    dma = pltpu.SemaphoreType.DMA
    rows = pack.shape[0] // count
    out = lambda *shape: jax.ShapeDtypeStruct(shape, F32)
    boxes = []
    for each, width, kind in ((w_out.shape[0] // count, D, BF), (rows, CUTS[0][1], BF), (rows, CUTS[1][1], BF), (8, 128, F32)):
        boxes += Reduce.boxes(levels, each, width, kind)
    boxes += ReducePair.boxes(levels, rows, pair.shape[1], BF)
    return pl.pallas_call(
        lambda *refs: reduce_kernel(levels, refs),
        out_shape=[out(rows, 3 * D), out(rows, CUTS[0][1]), out(rows, CUTS[1][1]), out(w_out.shape[0] // count, D), out(8, 128),
                   out(source.shape[0] // 4, D)],
        in_specs=[ANY] * 4 + [VMEM],
        out_specs=[VMEM] * 6,
        scratch_shapes=[pltpu.VMEM(p.shape, p.dtype) for p in (pair, pack, w_out, table)] + boxes + [
            dma((4, Reduce.slots(levels))), dma((4, Reduce.slots(levels))),
            dma((ReducePair.slots(levels),)), dma((ReducePair.slots(levels),)), dma((4,)), dma((4,)), dma((4,)),
            pltpu.VMEM((source.shape[0], D), F32),
        ],
        compiler_params=pltpu.CompilerParams(collective_id=1, has_side_effects=True, vmem_limit_bytes=60 << 20),
    )(pair, pack, w_out, table, source)


def per_device(tokens, cotangent, encoded, parents, timestep, w_qkv, w_o, w_cq, w_ckv, w_co, w_in, w_out, mod_table):
    levels = lax.axis_size("leaf") // 2
    rows, wide = w_qkv.shape[0], mod_table.shape[1]
    pair = w_qkv.reshape(rows, 3, 4, 128).swapaxes(1, 2).reshape(rows, 3 * D)
    pack = jnp.concatenate((w_o, w_cq, w_ckv, w_co, w_in), axis=1)
    aux = jnp.concatenate(
        (
            jnp.pad(mod_table, ((0, 0), (0, 128 - wide))),
            jnp.full((64 - STEPS, 128), timestep[0], jnp.int32).astype(BF),
        ),
        axis=0,
    )
    w_pair, full_pack, full_out, full_aux, all_tokens, all_source = gather_all(levels, pair, pack, w_out, aux, tokens, encoded)
    ins = dict(
        w_pair=w_pair, pack=full_pack, w_out=full_out, aux=full_aux, tokens_all=all_tokens, source_all=all_source,
        cotangent=cotangent, parents=parents, timestep=timestep,
    )
    mixed, grad_tokens, source_part, pair_part, pack_part, out_part, table_part = layer_all(levels, parents.shape[1], ins)
    g_qkv, g_pack, g_in, g_out, table_sum, d_encoded = reduce_all(levels, pair_part, pack_part, out_part, table_part, source_part)
    steps_all = full_aux.reshape(-1, 64, 128)[::4, STEPS, 0].astype(jnp.int32)
    chosen = (jnp.arange(STEPS)[:, None] == steps_all[None, :]).astype(jnp.float32)
    table_grad = jnp.dot(chosen, table_sum[:, :wide], precision=PRECISE)
    return (
        mixed, grad_tokens, d_encoded, g_qkv, g_pack[:, :D], g_pack[:, D:2 * D], g_pack[:, 2 * D:4 * D],
        g_pack[:, 4 * D:5 * D], g_in, g_out, table_grad,
    )


def solution(mesh):
    fits = mesh.shape["blk"] == 4 and mesh.shape["leaf"] == 8
    return jax.shard_map(
        per_device if fits else generic_device,
        mesh=mesh,
        in_specs=(
            P(("leaf", "blk"), None),
            P(("leaf", "blk"), None),
            P(("leaf", "blk"), None),
            P("leaf", None),
            P("leaf"),
            P(("leaf", "blk"), None),
            P(("leaf", "blk"), None),
            P(("leaf", "blk"), None),
            P(("leaf", "blk"), None),
            P(("leaf", "blk"), None),
            P(("leaf", "blk"), None),
            P(("leaf", "blk"), None),
            P(None, ("leaf", "blk")),
        ),
        out_specs=(
            P(("leaf", "blk"), None),
            P(("leaf", "blk"), None),
            P(("leaf", "blk"), None),
            P(("leaf", "blk"), None),
            P(("leaf", "blk"), None),
            P(("leaf", "blk"), None),
            P(("leaf", "blk"), None),
            P(("leaf", "blk"), None),
            P(("leaf", "blk"), None),
            P(("leaf", "blk"), None),
            P(None, ("leaf", "blk")),
        ),
        check_vma=False,
    )
```

```python
import functools

import jax
import jax.numpy as jnp
from jax import lax
from jax.experimental import pallas as pl
from jax.experimental.pallas import tpu as pltpu
from jax.sharding import PartitionSpec as P

D = 512
HEADS = 8
HEAD = 64
BLOCK = 128
FF = 2048
ENC = 64
STEPS = 50


PRECISE = lax.Precision.HIGHEST
MASKED = -1e30


def ancestors(parent_row):
    count = parent_row.shape[0]
    indices = jnp.arange(count, dtype=jnp.int32)
    reach_map = (indices[:, None] == indices[None, :]).astype(jnp.float32)
    reach_map = jnp.minimum(
        reach_map + (parent_row[:, None] == indices[None, :]).astype(jnp.float32), 1.0
    )
    for rounds in range(max(1, (count - 1).bit_length())):
        reach_map = jnp.minimum(jnp.dot(reach_map, reach_map, precision=PRECISE), 1.0)
    return reach_map


def normalize(values, shift, scaling):
    centred = values - jnp.mean(values, axis=-1, keepdims=True)
    spread = jnp.mean(centred * centred, axis=-1, keepdims=True)
    return centred * lax.rsqrt(spread + 1e-05) * (1.0 + scaling) + shift


def span_link(reach_rows, span):
    return lax.dynamic_slice_in_dim(reach_rows, span * 4, 4, 1)


def span_reached(reach_rows, span):
    return jnp.max(span_link(reach_rows, span)) > 0.5


def span_mask(reach_rows, first_block, span, row_count, width):
    query_index = jnp.arange(row_count, dtype=jnp.int32)
    key_index = jnp.arange(width, dtype=jnp.int32)
    query_block = first_block + query_index // BLOCK
    key_block = span * 4 + key_index // BLOCK
    link = span_link(reach_rows, span)
    link = jnp.repeat(jnp.repeat(link, BLOCK, axis=0), BLOCK, axis=1)
    same = query_block[:, None] == key_block[None, :]
    return (link > 0.5) & (
        jnp.logical_not(same) | (key_index[None, :] % BLOCK <= query_index[:, None] % BLOCK)
    )


def scores_of(queries, key_rows, allowed):
    raw = jnp.einsum(
        "qhd,khd->hqk", queries, key_rows, preferred_element_type=jnp.float32
    ) * HEAD ** (-0.5)
    return jnp.where(allowed[None], raw, MASKED)


def split_spans(keys, values):
    width = 4 * BLOCK
    count = keys.shape[0] // width
    return (
        jnp.arange(count, dtype=jnp.int32),
        keys.reshape(count, width, HEADS, HEAD),
        values.reshape(count, width, HEADS, HEAD),
    )


def tree_forward_attention(queries, keys, values, reach_rows, first_block):
    row_count = queries.shape[0]
    width = 4 * BLOCK
    spans, key_spans, value_spans = split_spans(keys, values)

    def stats(carry, item):
        span, key_rows = item

        def stats_visit(state):
            top, total = state
            allowed = span_mask(reach_rows, first_block, span, row_count, width)
            score = scores_of(queries, key_rows, allowed)
            new_top = jnp.maximum(top, jnp.max(score, axis=-1))
            weight = jnp.where(allowed[None], jnp.exp(score - new_top[..., None]), 0.0)
            return (new_top, total * jnp.exp(top - new_top) + jnp.sum(weight, axis=-1))

        return (
            lax.cond(span_reached(reach_rows, span), stats_visit, lambda state: state, carry),
            None,
        )

    start = (
        jnp.full((HEADS, row_count), MASKED, jnp.float32),
        jnp.zeros((HEADS, row_count), jnp.float32),
    )
    (top, total), unused = lax.scan(stats, start, (spans, key_spans))
    log_total = top + jnp.log(total)

    def collect(accum, item):
        span, key_rows, value_rows = item

        def collect_visit(current):
            allowed = span_mask(reach_rows, first_block, span, row_count, width)
            weight = jnp.where(
                allowed[None],
                jnp.exp(scores_of(queries, key_rows, allowed) - log_total[..., None]),
                0.0,
            )
            return current + jnp.einsum(
                "hqk,khd->qhd",
                weight.astype(jnp.bfloat16),
                value_rows,
                preferred_element_type=jnp.float32,
            )

        return (
            lax.cond(span_reached(reach_rows, span), collect_visit, lambda current: current, accum),
            None,
        )

    attended, unused = lax.scan(
        collect, jnp.zeros((row_count, HEADS, HEAD), jnp.float32), (spans, key_spans, value_spans)
    )
    return (attended, log_total)


def tree_backward_attention(queries, keys, values, reach_rows, first_block, log_total, grad_attn):
    row_count = queries.shape[0]
    width = 4 * BLOCK
    spans, key_spans, value_spans = split_spans(keys, values)

    def probs_of(span, key_rows):
        allowed = span_mask(reach_rows, first_block, span, row_count, width)
        return jnp.where(
            allowed[None],
            jnp.exp(scores_of(queries, key_rows, allowed) - log_total[..., None]),
            0.0,
        )

    def inner_pass(total, item):
        span, key_rows, value_rows = item

        def inner_visit(current):
            weight = probs_of(span, key_rows)
            d_weight = jnp.einsum(
                "qhd,khd->hqk", grad_attn, value_rows, preferred_element_type=jnp.float32
            )
            return current + jnp.sum(weight * d_weight, axis=-1)

        return (
            lax.cond(span_reached(reach_rows, span), inner_visit, lambda current: current, total),
            None,
        )

    delta, unused = lax.scan(
        inner_pass, jnp.zeros((HEADS, row_count), jnp.float32), (spans, key_spans, value_spans)
    )

    def grad_pass(d_queries, item):
        span, key_rows, value_rows = item

        def grad_visit(current):
            weight = probs_of(span, key_rows)
            d_weight = jnp.einsum(
                "qhd,khd->hqk", grad_attn, value_rows, preferred_element_type=jnp.float32
            )
            d_score = (weight * (d_weight - delta[..., None])).astype(jnp.bfloat16)
            current = current + jnp.einsum(
                "hqk,khd->qhd", d_score, key_rows, preferred_element_type=jnp.float32
            )
            d_keys = jnp.einsum(
                "hqk,qhd->khd", d_score, queries, preferred_element_type=jnp.float32
            ) * HEAD ** (-0.5)
            d_values = jnp.einsum(
                "hqk,qhd->khd",
                weight.astype(jnp.bfloat16),
                grad_attn,
                preferred_element_type=jnp.float32,
            )
            return (
                current,
                jnp.concatenate((d_keys.reshape(width, D), d_values.reshape(width, D)), axis=1),
            )

        def skip(current):
            return (current, jnp.zeros((width, 2 * D), jnp.float32))

        return lax.cond(span_reached(reach_rows, span), grad_visit, skip, d_queries)

    d_queries, terms = lax.scan(
        grad_pass, jnp.zeros((row_count, HEADS, HEAD), jnp.float32), (spans, key_spans, value_spans)
    )
    return (d_queries * HEAD ** (-0.5), terms.reshape(-1, 2 * D))


def generic_device(
    tokens,
    cotangent,
    encoded,
    parents,
    timestep,
    w_qkv,
    w_o,
    w_cq,
    w_ckv,
    w_co,
    w_in,
    w_out,
    mod_table,
):
    gathered = (
        lax.all_gather(w_qkv, ("leaf", "blk"), axis=0, tiled=True),
        lax.all_gather(w_o, ("leaf", "blk"), axis=0, tiled=True),
        lax.all_gather(w_cq, ("leaf", "blk"), axis=0, tiled=True),
        lax.all_gather(w_ckv, ("leaf", "blk"), axis=0, tiled=True),
        lax.all_gather(w_co, ("leaf", "blk"), axis=0, tiled=True),
        lax.all_gather(w_in, ("leaf", "blk"), axis=0, tiled=True),
        lax.all_gather(w_out, ("leaf", "blk"), axis=0, tiled=True),
        lax.all_gather(mod_table, ("leaf", "blk"), axis=1, tiled=True),
    )
    g_qkv, g_o, g_cq, g_ckv, g_co, g_in, g_out, g_table = gathered
    select = (jnp.arange(STEPS, dtype=jnp.int32) == timestep[0]).astype(jnp.float32)
    modulate = jnp.dot(
        select.astype(jnp.bfloat16)[None, :], g_table, preferred_element_type=jnp.float32
    )[0]
    pieces = [modulate[i * D : (i + 1) * D] for i in range(6)]
    inputs = tokens.astype(jnp.float32)
    row_count = tokens.shape[0]
    local_blocks = row_count // BLOCK
    first_block = lax.axis_index("blk") * local_blocks
    reach_map = ancestors(parents[0])
    reach_rows = lax.dynamic_slice_in_dim(reach_map, first_block, local_blocks, 0)
    scaling = HEAD ** (-0.5)
    normed_one, pull_one = jax.vjp(normalize, inputs, pieces[0], pieces[1])
    h_first = normed_one.astype(jnp.bfloat16)
    projected = jnp.dot(h_first, g_qkv, preferred_element_type=jnp.float32).astype(jnp.bfloat16)
    queries = projected[:, :D].reshape(row_count, HEADS, HEAD)
    keys, values = (
        lax.all_gather(projected[:, D : 2 * D], "blk", axis=0, tiled=True),
        lax.all_gather(projected[:, 2 * D :], "blk", axis=0, tiled=True),
    )
    attended, log_total = tree_forward_attention(queries, keys, values, reach_rows, first_block)
    attn_low = attended.reshape(row_count, D).astype(jnp.bfloat16)
    middle_one = inputs + jnp.dot(attn_low, g_o, preferred_element_type=jnp.float32)
    normed_two, pull_two = jax.vjp(normalize, middle_one, pieces[2], pieces[3])
    h_second = normed_two.astype(jnp.bfloat16)
    cross_q = (
        jnp.dot(h_second, g_cq, preferred_element_type=jnp.float32)
        .astype(jnp.bfloat16)
        .reshape(row_count, HEADS, HEAD)
    )
    source_local = jnp.dot(encoded, g_ckv, preferred_element_type=jnp.float32).astype(jnp.bfloat16)
    source_all = lax.all_gather(source_local, "blk", axis=0, tiled=True)
    cross_k = source_all[:, :D].reshape(-1, HEADS, HEAD)
    cross_v = source_all[:, D:].reshape(-1, HEADS, HEAD)
    cross_raw = (
        jnp.einsum("qhd,khd->hqk", cross_q, cross_k, preferred_element_type=jnp.float32) * scaling
    )
    cross_prob = jax.nn.softmax(cross_raw, axis=-1)
    cross_low = cross_prob.astype(jnp.bfloat16)
    cross_out = (
        jnp.einsum("hqk,khd->qhd", cross_low, cross_v, preferred_element_type=jnp.float32)
        .reshape(row_count, D)
        .astype(jnp.bfloat16)
    )
    middle_two = middle_one + jnp.dot(cross_out, g_co, preferred_element_type=jnp.float32)
    normed_three, pull_three = jax.vjp(normalize, middle_two, pieces[4], pieces[5])
    h_third = normed_three.astype(jnp.bfloat16)
    hidden_pre = jnp.dot(h_third, g_in, preferred_element_type=jnp.float32)
    activated, pull_gelu = jax.vjp(
        lambda values_in: jax.nn.gelu(values_in, approximate=True), hidden_pre
    )
    act_low = activated.astype(jnp.bfloat16)
    result = middle_two + jnp.dot(act_low, g_out, preferred_element_type=jnp.float32)
    mixed_out = result.astype(jnp.bfloat16)
    back_weights = (
        lax.all_gather(w_qkv, ("leaf", "blk"), axis=0, tiled=True),
        lax.all_gather(w_o, ("leaf", "blk"), axis=0, tiled=True),
        lax.all_gather(w_cq, ("leaf", "blk"), axis=0, tiled=True),
        lax.all_gather(w_ckv, ("leaf", "blk"), axis=0, tiled=True),
        lax.all_gather(w_co, ("leaf", "blk"), axis=0, tiled=True),
        lax.all_gather(w_in, ("leaf", "blk"), axis=0, tiled=True),
        lax.all_gather(w_out, ("leaf", "blk"), axis=0, tiled=True),
        lax.all_gather(mod_table, ("leaf", "blk"), axis=1, tiled=True),
    )
    b_qkv, b_o, b_cq, b_ckv, b_co, b_in, b_out = back_weights[:7]
    d_act = jnp.dot(cotangent, b_out.T, preferred_element_type=jnp.float32)
    d_hidden = pull_gelu(d_act)[0].astype(jnp.bfloat16)
    grad_out_w = jnp.dot(act_low.T, cotangent, preferred_element_type=jnp.float32)
    grad_in_w = jnp.dot(h_third.T, d_hidden, preferred_element_type=jnp.float32)
    d_h_third = jnp.dot(d_hidden, b_in.T, preferred_element_type=jnp.float32)
    d_middle_part, d_shift_three, d_scale_three = pull_three(d_h_third)
    d_middle_two = cotangent.astype(jnp.float32) + d_middle_part
    d_branch_two = d_middle_two.astype(jnp.bfloat16)
    grad_co_w = jnp.dot(cross_out.T, d_branch_two, preferred_element_type=jnp.float32)
    d_cross_out = (
        jnp.dot(d_branch_two, b_co.T, preferred_element_type=jnp.float32)
        .astype(jnp.bfloat16)
        .reshape(row_count, HEADS, HEAD)
    )
    d_cross_prob = jnp.einsum(
        "qhd,khd->hqk", d_cross_out, cross_v, preferred_element_type=jnp.float32
    )
    d_cross_raw = (
        cross_prob * (d_cross_prob - jnp.sum(cross_prob * d_cross_prob, axis=-1, keepdims=True))
    ).astype(jnp.bfloat16)
    d_cross_q = (
        (
            jnp.einsum("hqk,khd->qhd", d_cross_raw, cross_k, preferred_element_type=jnp.float32)
            * scaling
        )
        .reshape(row_count, D)
        .astype(jnp.bfloat16)
    )
    d_cross_k = (
        jnp.einsum("hqk,qhd->khd", d_cross_raw, cross_q, preferred_element_type=jnp.float32)
        * scaling
    )
    d_cross_v = jnp.einsum(
        "hqk,qhd->khd", cross_low, d_cross_out, preferred_element_type=jnp.float32
    )
    source_terms = jnp.concatenate((d_cross_k.reshape(-1, D), d_cross_v.reshape(-1, D)), axis=1)
    d_source = lax.psum_scatter(
        source_terms.astype(jnp.bfloat16), "blk", scatter_dimension=0, tiled=True
    )
    grad_ckv_w = jnp.dot(encoded.T, d_source, preferred_element_type=jnp.float32)
    d_encoded = jnp.dot(d_source, b_ckv.T, preferred_element_type=jnp.float32)
    grad_cq_w = jnp.dot(h_second.T, d_cross_q, preferred_element_type=jnp.float32)
    d_h_second = jnp.dot(d_cross_q, b_cq.T, preferred_element_type=jnp.float32)
    d_middle_part, d_shift_two, d_scale_two = pull_two(d_h_second)
    d_middle_one = d_middle_two + d_middle_part
    d_branch_one = d_middle_one.astype(jnp.bfloat16)
    grad_o_w = jnp.dot(attn_low.T, d_branch_one, preferred_element_type=jnp.float32)
    d_attn = (
        jnp.dot(d_branch_one, b_o.T, preferred_element_type=jnp.float32)
        .astype(jnp.bfloat16)
        .reshape(row_count, HEADS, HEAD)
    )
    keys_back, values_back = (
        lax.all_gather(projected[:, D : 2 * D], "blk", axis=0, tiled=True),
        lax.all_gather(projected[:, 2 * D :], "blk", axis=0, tiled=True),
    )
    d_queries, key_terms = tree_backward_attention(
        queries, keys_back, values_back, reach_rows, first_block, log_total, d_attn
    )
    d_key_value = lax.psum_scatter(
        key_terms.astype(jnp.bfloat16), "blk", scatter_dimension=0, tiled=True
    ).astype(jnp.float32)
    d_projected = jnp.concatenate((d_queries.reshape(row_count, D), d_key_value), axis=1).astype(
        jnp.bfloat16
    )
    grad_qkv_w = jnp.dot(h_first.T, d_projected, preferred_element_type=jnp.float32)
    d_h_first = jnp.dot(d_projected, b_qkv.T, preferred_element_type=jnp.float32)
    d_input_part, d_shift_one, d_scale_one = pull_one(d_h_first)
    d_tokens = d_middle_one + d_input_part
    d_modulate = jnp.concatenate(
        (d_shift_one, d_scale_one, d_shift_two, d_scale_two, d_shift_three, d_scale_three)
    )
    grad_table_w = select[:, None] * d_modulate[None, :]
    gradients = (
        lax.psum_scatter(grad_qkv_w, ("leaf", "blk"), scatter_dimension=0, tiled=True),
        lax.psum_scatter(grad_o_w, ("leaf", "blk"), scatter_dimension=0, tiled=True),
        lax.psum_scatter(grad_cq_w, ("leaf", "blk"), scatter_dimension=0, tiled=True),
        lax.psum_scatter(grad_ckv_w, ("leaf", "blk"), scatter_dimension=0, tiled=True),
        lax.psum_scatter(grad_co_w, ("leaf", "blk"), scatter_dimension=0, tiled=True),
        lax.psum_scatter(grad_in_w, ("leaf", "blk"), scatter_dimension=0, tiled=True),
        lax.psum_scatter(grad_out_w, ("leaf", "blk"), scatter_dimension=0, tiled=True),
        lax.psum_scatter(grad_table_w, ("leaf", "blk"), scatter_dimension=1, tiled=True),
    )
    return (
        mixed_out,
        d_tokens,
        d_encoded,
        gradients[0],
        gradients[1],
        gradients[2],
        gradients[3],
        gradients[4],
        gradients[5],
        gradients[6],
        gradients[7],
    )


MESH = pl.DeviceIdType.MESH
BF = jnp.bfloat16
F32 = jnp.float32


class Place:
    def __init__(self, levels):
        leaf = lax.axis_index("leaf")
        blk = lax.axis_index("blk")
        self.levels = levels
        self.leaf = leaf
        self.blk = blk
        self.z = leaf // 2
        self.core = leaf % 2
        self.near = blk + 1 - 2 * (blk % 2)
        self.far = (blk + 2) % 4
        self.first = self.core * self.near + (1 - self.core) * self.far
        self.second = self.core * self.far + (1 - self.core) * self.near
        self.opposite = 3 - blk
        self.sibling = self.z * 2 + 1 - self.core
        self.has_up = self.z < levels - 1
        self.has_down = self.z > 0

    def greet(self):
        barrier = pltpu.get_barrier_semaphore()

        count = self.levels * 2

        def hello(leaf, blk):
            pl.semaphore_signal(barrier, inc=1, device_id=(leaf, blk), device_id_type=MESH)

        for blk in (self.near, self.far, self.opposite):
            hello(self.leaf, blk)
        for step in range(1, count):
            hello((self.leaf + step) % count, self.blk)
        pl.semaphore_wait(barrier, count + 2)


def remote(src, dst, send, recv, leaf, blk):
    return pltpu.make_async_remote_copy(
        src_ref=src, dst_ref=dst, send_sem=send, recv_sem=recv,
        device_id=(leaf, blk), device_id_type=MESH,
    )


def under(cond, action):
    if cond is None:
        action()
    else:
        pl.when(cond)(action)


def both(one, two):
    if one is None:
        return two
    if two is None:
        return one
    return jnp.logical_and(one, two)


def rows_of(start, count):
    return pl.ds(pl.multiple_of(start * count, count), count)


class Gather:
    def __init__(self, place, full, rows, columns, send_sem, recv_sem):
        self.place, self.full, self.rows, self.columns = place, full, rows, columns
        self.send_sem, self.recv_sem = send_sem, recv_sem
        self.sent = []
        self.count = 0

    def view(self, leaf, blk):
        return self.full.at[rows_of(leaf * 4 + blk, self.rows), self.columns]

    def push(self, leaf, blk, targets, cond):
        for to_leaf, to_blk, needs in targets:
            number = self.count
            self.count += 1

            def build(number=number, to_leaf=to_leaf, to_blk=to_blk):
                there = self.view(leaf, blk)
                return remote(there, there, self.send_sem.at[number], self.recv_sem.at[leaf * 4 + blk], to_leaf, to_blk)

            ok = both(cond, needs)
            under(ok, lambda: build().start())
            self.sent.append((ok, build))

    def arrive(self, leaf, blk, cond=None):
        p = self.place

        def wait():
            there = self.view(leaf, blk)
            remote(there, there, self.send_sem.at[0], self.recv_sem.at[leaf * 4 + blk], p.leaf, p.second).wait_recv()

        under(cond, wait)

    def to(self, *names):
        p = self.place
        table = {
            "sibling": (p.sibling, p.blk, None),
            "first": (p.leaf, p.first, None),
            "second": (p.leaf, p.second, None),
            "up": (p.leaf + 2, p.blk, p.has_up),
            "down": (p.leaf - 2, p.blk, p.has_down),
        }
        return [table[name] for name in names]

    def steps(self):
        p = self.place
        self.push(p.leaf, p.blk, self.to("first", "up", "down", "sibling"), None)
        yield
        self.arrive(p.leaf, p.first)
        self.push(p.leaf, p.first, self.to("up", "down", "sibling"), None)
        yield
        self.push(p.leaf, p.blk, self.to("second"), None)
        self.push(p.leaf, p.first, self.to("second"), None)
        yield
        for k in range(1, p.levels):
            below, above = p.leaf - 2 * k, p.leaf + 2 * k
            has_below, has_above = p.z >= k, p.z + k < p.levels
            for blk in (p.blk, p.first):
                self.arrive(below, blk, has_below)
                self.push(below, blk, self.to("up", "second", "sibling"), has_below)
                self.arrive(above, blk, has_above)
                self.push(above, blk, self.to("down", "second", "sibling"), has_above)
            yield
        for k in range(p.levels):
            for leaf, cond in ((p.leaf - 2 * k, p.z >= k), (p.leaf + 2 * k, p.z + k < p.levels)):
                if k == 0 and leaf is not None:
                    cond = None
                for blk in (p.second, p.opposite):
                    self.arrive(leaf, blk, cond)
                    self.push(leaf, blk, self.to("sibling"), cond)
                if k == 0:
                    break
            yield
        for level in range(p.levels):
            for blk in range(4):
                self.arrive(2 * level + 1 - p.core, blk)
        yield

    def finish(self):
        for ok, build in self.sent:
            under(ok, lambda build=build: build().wait_send())

    @staticmethod
    def sends(levels):
        return 5 + 4 + (levels - 1) * 12 + 2 + (levels - 1) * 4


class Share:
    def __init__(self, place, full, rows, send_sem, recv_sem):
        self.place, self.full, self.rows = place, full, rows
        self.send_sem, self.recv_sem = send_sem, recv_sem
        self.half = rows // 2

    def view(self, blk, half):
        return self.full.at[pl.ds(pl.multiple_of(blk * self.rows + half * self.half, self.half), self.half), :]

    def build(self, blk, half, to_blk, number):
        there = self.view(blk, half)
        return remote(there, there, self.send_sem.at[number], self.recv_sem.at[blk * 2 + half], self.place.leaf, to_blk)

    def steps(self):
        p = self.place
        self.copies = [
            self.build(p.blk, 0, p.near, 0),
            self.build(p.blk, 1, p.far, 1),
            self.build(p.blk, 1, p.near, 2),
            self.build(p.blk, 0, p.far, 3),
        ]
        for copy in self.copies:
            copy.start()
        yield
        for blk, half, to_blk, number in ((p.near, 0, p.far, 4), (p.far, 1, p.near, 5)):
            copy = self.build(blk, half, to_blk, number)
            copy.wait_recv()
            copy.start()
            self.copies.append(copy)
        yield
        self.build(p.near, 1, p.near, 0).wait_recv()
        self.build(p.far, 0, p.near, 0).wait_recv()
        yield
        self.build(p.opposite, 0, p.near, 0).wait_recv()
        self.build(p.opposite, 1, p.near, 0).wait_recv()
        yield

    def finish(self):
        for copy in self.copies:
            copy.wait_send()


class Spread:
    def __init__(self, place, full, rows, send_sem, recv_sem):
        self.place, self.full, self.rows = place, full, rows
        self.send_sem, self.recv_sem = send_sem, recv_sem

    def build(self, blk, to_blk, number):
        there = self.full.at[rows_of(blk, self.rows), :]
        return remote(there, there, self.send_sem.at[number], self.recv_sem.at[blk], self.place.leaf, to_blk)

    def start(self):
        p = self.place
        self.copies = [self.build(p.blk, to, n) for n, to in enumerate((p.near, p.far, p.opposite))]
        for copy in self.copies:
            copy.start()

    def arrive(self):
        p = self.place
        for blk in (p.near, p.far, p.opposite):
            self.build(blk, p.near, 0).wait_recv()

    def finish(self):
        for copy in self.copies:
            copy.wait_send()


class Reduce:
    def __init__(self, place, total, rows, columns, out, boxes, send_sem, recv_sem):
        self.place, self.total, self.rows, self.columns, self.out = place, total, rows, columns, out
        self.from_sibling, self.from_second, self.from_line, self.from_first = boxes
        self.send_sem, self.recv_sem = send_sem, recv_sem
        self.sent = []

    @staticmethod
    def slots(levels):
        return 7 * levels + 1

    @staticmethod
    def boxes(levels, rows, width, kind):
        return [
            pltpu.VMEM((levels * 4 * rows, width), kind),
            pltpu.VMEM((levels * 2 * rows, width), kind),
            pltpu.VMEM(((levels + 1) * 2 * rows, width), kind),
            pltpu.VMEM((rows, width), kind),
        ]

    def part(self, leaf, blk, count=1):
        return self.total.at[pl.ds(pl.multiple_of((leaf * 4 + blk) * self.rows, self.rows), self.rows * count), self.columns]

    def copy(self, src, box, position, count, number, leaf, blk):
        there = box.at[pl.ds(pl.multiple_of(position * self.rows, self.rows), self.rows * count), :]
        return remote(there if src is None else src, there, self.send_sem.at[number], self.recv_sem.at[number], leaf, blk)

    def send(self, cond, *parts):
        under(cond, lambda: self.copy(*parts).start())
        self.sent.append((cond, parts))

    def arrived(self, box, position, count, number):
        self.copy(None, box, position, count, number, self.place.leaf, self.place.first).wait_recv()

    def add(self, leaf, blk, box, position, count=1):
        unit = 16 if self.rows % 16 == 0 else self.rows
        into = (leaf * 4 + blk) * self.rows
        source = position * self.rows

        def one(step, carry):
            here = pl.ds(pl.multiple_of(into + step * unit, unit), unit)
            there = pl.ds(pl.multiple_of(source + step * unit, unit), unit)
            value = self.total[here, self.columns].astype(F32) + box[there, :].astype(F32)
            self.total[here, self.columns] = value.astype(self.total.dtype)
            return carry

        lax.fori_loop(0, count * self.rows // unit, one, 0)

    def steps(self):
        p = self.place
        levels = p.levels
        for level in range(levels):
            self.send(None, self.part(2 * level + 1 - p.core, 0, 4), self.from_sibling, 4 * level, 4, level, p.sibling, p.blk)
        yield
        for level in range(levels):
            self.arrived(self.from_sibling, 4 * level, 4, level)
            leaf = 2 * level + p.core
            self.add(leaf, 0, self.from_sibling, 4 * level, 4)
            for which, blk in enumerate((p.second, p.opposite)):
                slot = 2 * level + which
                self.send(None, self.part(leaf, blk), self.from_second, slot, 1, levels + slot, p.leaf, p.second)
        yield
        for level in range(levels):
            leaf = 2 * level + p.core
            for which, blk in enumerate((p.blk, p.first)):
                slot = 2 * level + which
                self.arrived(self.from_second, slot, 1, levels + slot)
                self.add(leaf, blk, self.from_second, slot)
        yield
        for k in range(levels - 1, -1, -1):
            for which, blk in enumerate((p.blk, p.first)):
                up, down = 2 * (p.z + k) + which, 2 * (p.z - k) + which

                here = 2 * p.levels + which if k == 0 else down
                there = 2 * p.levels + which if k == 1 else down

                def climb(up=up, blk=blk):
                    def more():
                        self.arrived(self.from_line, up, 1, 3 * levels + up)
                        self.add(p.leaf + 2 * k, blk, self.from_line, up)

                    pl.when(p.has_down)(more)

                def fall(down=down, here=here, blk=blk):
                    def more():
                        self.arrived(self.from_line, here, 1, 5 * levels + down)
                        self.add(p.leaf - 2 * k, blk, self.from_line, here)

                    pl.when(p.has_up)(more)

                if k == 0:
                    climb()
                    fall()
                else:
                    can_up, can_down = p.z + k < levels, p.z >= k
                    under(can_up, climb)
                    self.send(can_up, self.part(p.leaf + 2 * k, blk), self.from_line, up, 1, 3 * levels + up, p.leaf + 2, p.blk)
                    under(can_down, fall)
                    self.send(can_down, self.part(p.leaf - 2 * k, blk), self.from_line, there, 1, 5 * levels + down, p.leaf - 2, p.blk)
            yield
        self.send(None, self.part(p.leaf, p.first), self.from_first, 0, 1, 7 * levels, p.leaf, p.first)
        yield
        self.arrived(self.from_first, 0, 1, 7 * levels)
        unit = 16 if self.rows % 16 == 0 else self.rows
        for step in range(self.rows // unit):
            here = pl.ds(pl.multiple_of((p.leaf * 4 + p.blk) * self.rows + step * unit, unit), unit)
            there = pl.ds(step * unit, unit)
            self.out(there, self.total[here, self.columns].astype(F32) + self.from_first[there, :].astype(F32))
        yield

    def finish(self):
        for cond, parts in self.sent:
            under(cond, lambda parts=parts: self.copy(*parts).wait_send())


def run_all(sequences):
    live = [item.steps() for item in sequences]
    while live:
        live = [item for item in live if next(item, "end") != "end"]


class GatherPair:
    def __init__(self, place, own, full, send_sem, recv_sem):
        self.place, self.own, self.full = place, own, full
        self.rows, self.width = own.shape[0], full.shape[1]
        self.send_sem, self.recv_sem = send_sem, recv_sem
        self.sent = []
        self.count = 0

    def start(self, cond, make):
        under(cond, lambda: make().start())
        self.sent.append((cond, make))

    def piece(self, src_blk, to_blk, number, own):
        p = self.place
        there = self.full.at[rows_of(p.leaf * 4 + src_blk, self.rows), :]
        src = self.own.at[:, pl.ds(pl.multiple_of(to_blk * self.width, self.width), self.width)] if own else there
        return remote(src, there, self.send_sem.at[number], self.recv_sem.at[src_blk], p.leaf, to_blk)

    def block(self, leaf, number, to_leaf):
        there = self.full.at[rows_of(leaf, 4 * self.rows), :]
        return remote(there, there, self.send_sem.at[number], self.recv_sem.at[4 + leaf], to_leaf, self.place.blk)

    def push(self, leaf, cond, names):
        p = self.place
        table = {"sibling": (p.sibling, None), "up": (p.leaf + 2, p.has_up), "down": (p.leaf - 2, p.has_down)}
        for name in names:
            to_leaf, needs = table[name]
            number = 3 + self.count
            self.count += 1
            self.start(both(cond, needs), lambda number=number, to_leaf=to_leaf: self.block(leaf, number, to_leaf))

    def wait(self, leaf, cond):
        under(cond, lambda: self.block(leaf, 0, self.place.sibling).wait_recv())

    def local(self, sem):
        p = self.place
        mine = self.own.at[:, pl.ds(pl.multiple_of(p.blk * self.width, self.width), self.width)]
        return pltpu.make_async_copy(mine, self.full.at[rows_of(p.leaf * 4 + p.blk, self.rows), :], sem)

    def steps(self):
        p = self.place
        for number, to_blk in enumerate((p.near, p.far, p.opposite)):
            self.start(None, lambda to_blk=to_blk, number=number: self.piece(p.blk, to_blk, number, True))
        yield
        for blk in (p.near, p.far, p.opposite):
            self.piece(blk, p.near, 0, False).wait_recv()
        self.push(p.leaf, None, ("up", "down", "sibling"))
        yield
        for k in range(1, p.levels):
            below, above = p.leaf - 2 * k, p.leaf + 2 * k
            has_below, has_above = p.z >= k, p.z + k < p.levels
            self.wait(below, has_below)
            self.push(below, has_below, ("up", "sibling"))
            self.wait(above, has_above)
            self.push(above, has_above, ("down", "sibling"))
            yield
        for level in range(p.levels):
            self.wait(2 * level + 1 - p.core, None)
        yield

    def finish(self):
        for cond, make in self.sent:
            under(cond, lambda make=make: make().wait_send())

    @staticmethod
    def sends(levels):
        return 6 + 4 * (levels - 1)


class ReducePair:
    def __init__(self, place, total, out, boxes, send_sem, recv_sem):
        self.place, self.total, self.out = place, total, out
        self.rows = total.shape[0] // (place.levels * 8)
        self.from_sibling, self.from_below, self.from_above, self.from_pair = boxes
        self.send_sem, self.recv_sem = send_sem, recv_sem
        self.sent = []

    @staticmethod
    def slots(levels):
        return 3 * levels + 4

    @staticmethod
    def boxes(levels, rows, width, kind):
        return [pltpu.VMEM((levels * 4 * rows, width), kind) for n in range(3)] + [pltpu.VMEM((4 * rows, width), kind)]

    def send(self, cond, src, box, slot, rows, number, leaf, blk):
        def make():
            there = box.at[rows_of(slot, rows), :]
            return remote(there if src is None else src, there, self.send_sem.at[number], self.recv_sem.at[number], leaf, blk)

        under(cond, lambda: make().start())
        self.sent.append((cond, make))

    def arrived(self, box, slot, rows, number):
        there = box.at[rows_of(slot, rows), :]
        p = self.place
        remote(there, there, self.send_sem.at[0], self.recv_sem.at[number], p.sibling, p.blk).wait_recv()

    def part(self, leaf):
        return self.total.at[rows_of(leaf, 4 * self.rows), :]

    def add(self, leaf, box, slot):
        here, there = rows_of(leaf, 4 * self.rows), rows_of(slot, 4 * self.rows)
        value = self.total[here, :].astype(F32) + box[there, :].astype(F32)
        self.total[here, :] = value.astype(self.total.dtype)

    def steps(self):
        p = self.place
        levels, rows = p.levels, 4 * self.rows
        for level in range(levels):
            self.send(None, self.part(2 * level + 1 - p.core), self.from_sibling, level, rows, level, p.sibling, p.blk)
        yield
        for level in range(levels):
            self.arrived(self.from_sibling, level, rows, level)
            self.add(2 * level + p.core, self.from_sibling, level)
        yield
        for k in range(levels - 1, -1, -1):
            up, down = p.z + k, p.z - k

            def climb():
                def more():
                    self.arrived(self.from_below, up, rows, levels + up)
                    self.add(p.leaf + 2 * k, self.from_below, up)

                pl.when(p.has_down)(more)

            def fall():
                def more():
                    self.arrived(self.from_above, down, rows, 2 * levels + down)
                    self.add(p.leaf - 2 * k, self.from_above, down)

                pl.when(p.has_up)(more)

            if k == 0:
                climb()
                fall()
            else:
                under(up < levels, climb)
                self.send(up < levels, self.part(p.leaf + 2 * k), self.from_below, up, rows, levels + up, p.leaf + 2, p.blk)
                under(down >= 0, fall)
                self.send(down >= 0, self.part(p.leaf - 2 * k), self.from_above, down, rows, 2 * levels + down, p.leaf - 2, p.blk)
            yield
        for to_blk in (p.near, p.far, p.opposite):
            src = self.total.at[rows_of(p.leaf * 4 + to_blk, self.rows), :]
            self.pair_send(src, to_blk)
        yield
        self.store(p.blk, self.total[rows_of(p.leaf * 4 + p.blk, self.rows), :])
        for blk in (p.near, p.far, p.opposite):
            there = self.from_pair.at[rows_of(blk, self.rows), :]
            remote(there, there, self.send_sem.at[0], self.recv_sem.at[3 * levels + blk], p.leaf, p.near).wait_recv()
            self.store(blk, self.from_pair[rows_of(blk, self.rows), :])
        yield

    def pair_send(self, src, to_blk):
        p = self.place

        def make():
            there = self.from_pair.at[rows_of(p.blk, self.rows), :]
            return remote(src, there, self.send_sem.at[3 * p.levels + to_blk], self.recv_sem.at[3 * p.levels + p.blk], p.leaf, to_blk)

        make().start()
        self.sent.append((None, make))

    def store(self, blk, value):
        for third in range(3):
            lanes = pl.ds(pl.multiple_of(third * D + blk * 128, 128), 128)
            self.out[:, lanes] = value[:, third * 128:third * 128 + 128].astype(F32)

    def finish(self):
        for cond, make in self.sent:
            under(cond, lambda make=make: make().wait_send())


class Settle:
    def __init__(self, place, part, out, box, send_sem, recv_sem):
        self.place, self.part, self.out, self.box = place, part, out, box
        self.send_sem, self.recv_sem = send_sem, recv_sem
        self.rows = out.shape[0]

    def build(self, src_blk, to_blk):
        p = self.place
        return remote(self.part.at[rows_of(to_blk, self.rows), :], self.box.at[rows_of(src_blk, self.rows), :],
                      self.send_sem.at[to_blk], self.recv_sem.at[src_blk], p.leaf, to_blk)

    def steps(self):
        p = self.place
        self.copies = [self.build(p.blk, to) for to in (p.near, p.far, p.opposite)]
        for copy in self.copies:
            copy.start()
        yield
        total = self.part[rows_of(p.blk, self.rows), :]
        for blk in (p.near, p.far, p.opposite):
            self.build(blk, p.near).wait_recv()
            total = total + self.box[rows_of(blk, self.rows), :]
        self.out[...] = total
        yield

    def finish(self):
        for copy in self.copies:
            copy.wait_send()


class TableSum:
    def __init__(self, place, payload, box, rows_box, send_sem, recv_sem):
        self.place, self.payload, self.box, self.rows_box = place, payload, box, rows_box
        self.send_sem, self.recv_sem = send_sem, recv_sem
        self.leaves = place.levels * 2
        self.rows = self.leaves * 8

    def first(self, src_blk, to_blk):
        return remote(self.payload.at[rows_of(to_blk, self.rows), :], self.box.at[rows_of(src_blk, self.rows), :],
                      self.send_sem.at[to_blk], self.recv_sem.at[src_blk], self.place.leaf, to_blk)

    def second(self, src_leaf, to_leaf):
        p = self.place
        start = p.blk * self.leaves + to_leaf
        return remote(self.payload.at[rows_of(start, 8), :], self.rows_box.at[rows_of(src_leaf, 8), :],
                      self.send_sem.at[4 + to_leaf], self.recv_sem.at[4 + src_leaf], to_leaf, p.blk)

    def steps(self):
        p = self.place
        peers = (p.near, p.far, p.opposite)
        others = [(p.leaf + step) % self.leaves for step in range(1, self.leaves)]
        for to in peers:
            self.first(p.blk, to).start()
        yield
        here = rows_of(p.blk, self.rows)
        total = self.payload[here, :]
        for src in peers:
            self.first(src, p.near).wait_recv()
            total = total + self.box[rows_of(src, self.rows), :]
        self.payload[here, :] = total
        for to in others:
            self.second(p.leaf, to).start()
        self.rows_box[rows_of(p.leaf, 8), :] = self.payload[rows_of(p.blk * self.leaves + p.leaf, 8), :]
        yield
        for src in others:
            self.second(src, others[0]).wait_recv()
        yield

    def finish(self):
        p = self.place
        for to in (p.near, p.far, p.opposite):
            self.first(p.blk, to).wait_send()
        for step in range(1, self.leaves):
            self.second(p.leaf, (p.leaf + step) % self.leaves).wait_send()


class TreeReduce:
    def __init__(self, place, part, relay, box, send_sem, relay_sem, recv_sem):
        self.place, self.part, self.relay, self.box = place, part, relay, box
        self.send_sem, self.relay_sem, self.recv_sem = send_sem, relay_sem, recv_sem

    def roles(self, tile):
        owner, half = tile // 2, tile % 2
        near, far = owner + 1 - 2 * (owner % 2), (owner + 2) % 4
        direct, relayed = (near, far) if half == 0 else (far, near)
        return owner, half, direct, relayed, 3 - owner

    def to_owner(self, tile, which):
        owner, half = tile // 2, tile % 2
        return remote(self.part.at[span(tile), :], self.box.at[half, which], self.send_sem.at[tile],
                      self.recv_sem.at[half * 2 + which], self.place.leaf, owner)

    def to_relay(self, tile):
        owner, half, direct, relayed, opposite = self.roles(tile)
        return remote(self.part.at[span(tile), :], self.relay.at[half], self.send_sem.at[tile],
                      self.relay_sem.at[half], self.place.leaf, relayed)

    def offer(self, tile):
        owner, half, direct, relayed, opposite = self.roles(tile)
        pl.when(self.place.blk == opposite)(lambda: self.to_relay(tile).start())
        pl.when(self.place.blk == direct)(lambda: self.to_owner(tile, 0).start())

    def forward(self, tile):
        owner, half, direct, relayed, opposite = self.roles(tile)

        def go():
            self.to_relay(tile).wait_recv()
            total = self.part[span(tile), :].astype(F32) + self.relay[half].astype(F32)
            self.part[span(tile), :] = total.astype(BF)
            self.to_owner(tile, 1).start()

        pl.when(self.place.blk == relayed)(go)

    def arrive(self, half):
        for which in range(2):
            self.to_owner(half, which).wait_recv()

    def finish(self, tile):
        owner, half, direct, relayed, opposite = self.roles(tile)
        pl.when(self.place.blk == opposite)(lambda: self.to_relay(tile).wait_send())
        pl.when(self.place.blk == direct)(lambda: self.to_owner(tile, 0).wait_send())
        pl.when(self.place.blk == relayed)(lambda: self.to_owner(tile, 1).wait_send())


SPAN = 256
TINY = 1e-05


def dot(left, right):
    return lax.dot_general(left, right, (((1,), (0,)), ((), ())), preferred_element_type=F32)


def dot_nt(left, right):
    return lax.dot_general(left, right, (((1,), (1,)), ((), ())), preferred_element_type=F32)


def dot_tn(left, right):
    return lax.dot_general(left, right, (((0,), (0,)), ((), ())), preferred_element_type=F32)


def iota(shape, axis):
    return lax.broadcasted_iota(jnp.int32, shape, axis)


def span(start, count=SPAN):
    return pl.ds(pl.multiple_of(start * count, count), count)


def loop(count, body):
    def step(index, carry):
        body(index)
        return carry

    lax.fori_loop(0, count, step, 0)


def unit_rows(values):
    centred = values - jnp.mean(values, axis=-1, keepdims=True)
    root = lax.rsqrt(jnp.mean(centred * centred, axis=-1, keepdims=True) + TINY)
    return centred * root, root


def norm_back(grad, unit, root, scale):
    inner = grad * (1.0 + scale)
    return (
        inner
        - jnp.mean(inner, axis=-1, keepdims=True)
        - unit * jnp.mean(inner * unit, axis=-1, keepdims=True)
    ) * root


def spread_pattern(wide, group):
    column = iota((128, group), 1)
    turn = jnp.zeros((128, group), jnp.int32)
    for step in range(1, group // wide):
        turn = turn + (column >= step * wide).astype(jnp.int32)
    return (column - turn * wide == iota((128, group), 0)).astype(F32)


def shard_of_column(count, wide, group):
    column = iota((count, group), 1)
    turn = jnp.zeros((count, group), jnp.int32)
    for step in range(1, group // wide):
        turn = turn + (column >= step * wide).astype(jnp.int32)
    return turn


def read_modulation(aux, timestep, mod, wide):
    count = aux.shape[0] // 64
    row = iota((count, aux.shape[0]), 0)
    column = iota((count, aux.shape[0]), 1)
    chosen = (column == row * 64 + timestep).astype(BF)
    picked = dot(chosen, aux[...])
    group = wide * 4
    laid = dot(picked.astype(BF), spread_pattern(wide, group).astype(BF))
    offset = iota((count, group), 0) - shard_of_column(count, wide, group)
    for part in range(count // 4):
        mod[0:1, part * group:(part + 1) * group] = jnp.sum(
            jnp.where(offset == 4 * part, laid, 0.0), axis=0, keepdims=True
        )


def table_payload(sums, wide, count):
    group = wide * 4
    offset = iota((count, group), 0) - shard_of_column(count, wide, group)
    held = jnp.zeros((count, group), F32)
    for part in range(count // 4):
        held = held + jnp.where(offset == 4 * part, sums[0:1, part * group:(part + 1) * group], 0.0)
    cut = lax.dot_general(held, spread_pattern(wide, group), (((1,), (1,)), ((), ())),
                          preferred_element_type=F32, precision=lax.Precision.HIGHEST)
    leaves = count // 4
    row = iota((count * 8, count), 0)
    tile = sum((row >= 8 * step).astype(jnp.int32) for step in range(1, count))
    block = sum((row >= 8 * leaves * step).astype(jnp.int32) for step in range(1, 4))
    chosen = (iota((count * 8, count), 1) == (tile - block * leaves) * 4 + block).astype(F32)
    return lax.dot_general(chosen, cut, (((1,), (0,)), ((), ())),
                           preferred_element_type=F32, precision=lax.Precision.HIGHEST)


def block_bias(parents, bias, blocks):
    row, column = iota((128, 128), 0), iota((128, 128), 1)
    reach = (row == column).astype(F32)
    for block in range(blocks):
        reach = jnp.maximum(reach, ((column == block) & (row == parents[0, block])).astype(F32))
    for step in range((blocks - 1).bit_length()):
        low_reach = reach.astype(BF)
        reach = jnp.minimum(dot(low_reach, low_reach), 1.0)
    held = (reach[:blocks, :] - 1.0) * 1e30
    for block in range(blocks):
        bias[:, block * BLOCK:(block + 1) * BLOCK] = jnp.broadcast_to(held[:, block:block + 1], (blocks, BLOCK))


class Layer:
    def __init__(self, place, refs):
        self.place = place
        self.__dict__.update(refs)

    def project(self, chunk):
        rows = span(chunk)
        unit, root = unit_rows(self.tokens_all[rows, :].astype(F32))
        first = (unit * (1.0 + self.mod[0:1, D:2 * D]) + self.mod[0:1, 0:D]).astype(BF)
        self.h1[rows, :] = first
        made = dot(first, self.w_pair[...])
        lane = iota((SPAN, 128), 1)
        query = made[:, 0:128].astype(BF).astype(F32) * HEAD ** (-0.5)
        self.q_masked[0, rows, :] = jnp.where(lane < HEAD, query, 0.0).astype(BF)
        self.q_masked[1, rows, :] = jnp.where(lane >= HEAD, query, 0.0).astype(BF)
        key = made[:, 128:256]
        value = made[:, 256:384]
        self.key[rows, :] = key.astype(BF)
        self.value[rows, :] = value.astype(BF)
        self.key_t[:, rows] = key.T.astype(BF)
        value_t = value.T.astype(BF)
        ones = jnp.ones((16, SPAN), BF)
        self.value_t[0, 0:HEAD, rows] = value_t[:HEAD]
        self.value_t[1, 0:HEAD, rows] = value_t[HEAD:]
        self.value_t[0, HEAD:HEAD + 16, rows] = ones
        self.value_t[1, HEAD:HEAD + 16, rows] = ones

    def attend(self, tile):
        queries = span(tile)
        base = tile * (tile + 1) // 2
        self.top[...] = jnp.full_like(self.top, -3e30)

        def score(j, head, diagonal):
            raw = dot_nt(self.key[span(j), :], self.q_masked[head, queries, :])
            upper = raw[:BLOCK] + self.bias[pl.ds(2 * j, 1), queries]
            lower = raw[BLOCK:] + self.bias[pl.ds(2 * j + 1, 1), queries]
            kept = jnp.concatenate((upper, lower), axis=0)
            return kept + self.corner[...] if diagonal else kept

        def highest(j, diagonal):
            for head in range(2):
                kept = score(j, head, diagonal)
                self.top[head] = jnp.maximum(self.top[head], jnp.max(kept.reshape(SPAN // 8, 8, SPAN), axis=0))

        loop(tile, lambda j: highest(j, False))
        highest(tile, True)
        top = [jnp.max(self.top[head], axis=0, keepdims=True) for head in range(2)]
        self.mix[...] = jnp.zeros_like(self.mix)

        def weigh(j, diagonal):
            for head in range(2):
                weight = jnp.exp(score(j, head, diagonal) - top[head]).astype(BF)
                self.weights[base + j, head] = weight
                self.mix[head] += dot(self.value_t[head, :, span(j)], weight)

        loop(tile, lambda j: weigh(j, False))
        weigh(tile, True)
        halves = []
        for head in range(2):
            inverse = 1.0 / self.mix[head, HEAD:HEAD + 8, :]
            self.inverse[head, :, queries] = inverse
            halves.append(self.mix[head, :HEAD, :] * inverse[0:1])
        attended_t = jnp.concatenate(halves, axis=0)
        self.attended_t[:, queries] = attended_t
        self.attended[queries, :] = attended_t.T.astype(BF)

    def cross_keys(self):
        made = dot(self.source_all[...], self.w_ckv).astype(BF)
        lane = iota((2 * ENC, 128), 1)
        row = iota((2 * ENC, 128), 0)
        own = (lane < HEAD) == (row < ENC)
        for pair in range(4):
            for box, start in ((self.cross_k, 0), (self.cross_v, D)):
                part = made[:, start + 128 * pair:start + 128 * pair + 128].astype(F32)
                box[pair] = jnp.where(own, jnp.concatenate((part, part), axis=0), 0.0).astype(BF)

    def middle(self, chunk):
        rows = span(chunk)
        y1 = self.tokens[rows, :].astype(F32) + dot(self.gathered[rows, :], self.w_o)
        self.y1[rows, :] = y1
        unit, root = unit_rows(y1)
        h2 = (unit * (1.0 + self.mod[0:1, 3 * D:4 * D]) + self.mod[0:1, 2 * D:3 * D]).astype(BF)
        self.h2[rows, :] = h2
        query = (dot(h2, self.w_cq).astype(BF).astype(F32) * HEAD ** (-0.5)).astype(BF)
        self.cross_q[rows, :] = query
        lane = iota((SPAN, 128), 1)
        same = ((iota((128, 128), 0) < ENC) == (iota((128, 128), 1) < ENC)).astype(BF)
        out = []
        for pair in range(4):
            raw = dot_nt(query[:, 128 * pair:128 * pair + 128], self.cross_k[pair])
            left = jnp.max(jnp.where(lane < ENC, raw, -3e38), axis=-1, keepdims=True)
            right = jnp.max(jnp.where(lane >= ENC, raw, -3e38), axis=-1, keepdims=True)
            weight = jnp.exp(raw - jnp.where(lane < ENC, left, right))
            weight = weight / dot(weight.astype(BF), same)
            self.cross_p[pair, rows, :] = weight.astype(BF)
            out.append(dot(weight.astype(BF), self.cross_v[pair]))
        cross = jnp.concatenate(out, axis=1).astype(BF)
        self.cross_out[rows, :] = cross
        y2 = y1 + dot(cross, self.w_co)
        self.y2[rows, :] = y2
        unit, root = unit_rows(y2)
        self.h3[rows, :] = (unit * (1.0 + self.mod[0:1, 5 * D:6 * D]) + self.mod[0:1, 4 * D:5 * D]).astype(BF)

    def hidden(self, chunk):
        units = span(chunk)
        u = dot(self.h3[...], self.w_in(units))
        dg = dot_nt(self.cotangent[...], self.w_out[units, :])
        square = u * u
        slope = 0.7978845608028654
        bend = jnp.tanh(u * (slope + slope * 0.044715 * square))
        half = 0.5 + 0.5 * bend
        self.act[:, units] = (u * half).astype(BF)
        turn = half + 0.5 * u * (1.0 - bend * bend) * (slope + 3.0 * slope * 0.044715 * square)
        self.d_hidden[:, units] = (dg * turn).astype(BF)
        self.grad_out(units, dot_tn(self.act[:, units], self.cotangent[...]).astype(BF))
        self.grad_in(units, dot_tn(self.h3[...], self.d_hidden[:, units]).astype(BF))

    def finish_forward(self, chunk):
        rows = span(chunk)
        self.mixed[rows, :] = (self.y2[rows, :] + dot(self.act[rows, :], self.w_out[...])).astype(BF)

    def sums(self, piece, shift, scale):
        self.mod_grad[0:1, 2 * piece * D:(2 * piece + 1) * D] += jnp.sum(shift, axis=0, keepdims=True)
        self.mod_grad[0:1, (2 * piece + 1) * D:(2 * piece + 2) * D] += jnp.sum(scale, axis=0, keepdims=True)

    def back_three(self, chunk):
        rows = span(chunk)
        dh3 = dot_nt(self.d_hidden[rows, :], self.w_in(slice(None)))
        unit, root = unit_rows(self.y2[rows, :])
        self.sums(2, dh3, dh3 * unit)
        dy2 = self.cotangent[rows, :].astype(F32) + norm_back(dh3, unit, root, self.mod[0:1, 5 * D:6 * D])
        self.dy[rows, :] = dy2
        self.db[rows, :] = dy2.astype(BF)

    def back_cross(self, chunk):
        rows = span(chunk)
        dca = dot_nt(self.db[rows, :], self.w_co).astype(BF)
        lane = iota((SPAN, 128), 1)
        row = iota((128, 128), 0)
        own = (row < ENC) == (iota((128, 128), 1) < HEAD)
        parts = []
        for pair in range(4):
            lanes = slice(128 * pair, 128 * pair + 128)
            low_weight = self.cross_p[pair, rows, :]
            weight = low_weight.astype(F32)
            dc = dot_nt(dca[:, lanes], self.cross_v[pair])
            both_ = weight * dc
            left = jnp.sum(jnp.where(lane < ENC, both_, 0.0), axis=-1, keepdims=True)
            right = jnp.sum(jnp.where(lane >= ENC, both_, 0.0), axis=-1, keepdims=True)
            ds = (weight * (dc - jnp.where(lane < ENC, left, right))).astype(BF)
            parts.append((dot(ds, self.cross_k[pair]) * HEAD ** (-0.5)).astype(BF))
            dk = jnp.where(own, dot_tn(ds, self.cross_q[rows, lanes]), 0.0)
            dv = jnp.where(own, dot_tn(low_weight, dca[:, lanes]), 0.0)
            self.d_cross[:, lanes] += dk[:ENC] + dk[ENC:]
            self.d_cross[:, 128 * pair + D:128 * pair + D + 128] += dv[:ENC] + dv[ENC:]
        dcq = jnp.concatenate(parts, axis=1)
        self.dcq[rows, :] = dcq
        dh2 = dot_nt(dcq, self.w_cq)
        unit, root = unit_rows(self.y1[rows, :])
        self.sums(1, dh2, dh2 * unit)
        dy1 = self.dy[rows, :] + norm_back(dh2, unit, root, self.mod[0:1, 3 * D:4 * D])
        self.dy[rows, :] = dy1
        low_dy1 = dy1.astype(BF)
        self.db1[rows, :] = low_dy1
        self.d_attn[rows, :] = dot_nt(low_dy1, self.w_o).astype(BF)

    def attend_back(self, tile):
        queries = span(tile)
        base = tile * (tile + 1) // 2
        d_att_t = self.d_att_all[queries, :].astype(F32).T
        scaled = [d_att_t[HEAD * h:HEAD * h + HEAD] * self.inverse[h, 0:1, queries] for h in range(2)]
        delta = [
            jnp.sum(scaled[h] * self.attended_t[HEAD * h:HEAD * h + HEAD, queries], axis=0, keepdims=True)
            for h in range(2)
        ]
        flat = jnp.concatenate(scaled, axis=0).T
        lane = iota((SPAN, 128), 1)
        self.d_masked[0] = jnp.where(lane < HEAD, flat, 0.0).astype(BF)
        self.d_masked[1] = jnp.where(lane >= HEAD, flat, 0.0).astype(BF)
        self.dq_t[...] = jnp.zeros_like(self.dq_t)

        def visit(j):
            keys = span(j)
            dk = dv = 0.0
            for head in range(2):
                dp = dot_nt(self.value[keys, :], self.d_masked[head])
                weight = self.weights[base + j, head]
                ds = (weight.astype(F32) * (dp - delta[head])).astype(BF)
                dk = dk + dot(ds, self.q_masked[head, queries, :])
                dv = dv + dot(weight, self.d_masked[head])
                self.dq_t[HEAD * head:HEAD * head + HEAD, :] += dot(self.key_t[HEAD * head:HEAD * head + HEAD, keys], ds)
            self.dk[keys, :] += dk
            self.dv[keys, :] += dv

        loop(tile + 1, visit)
        self.d_pair[queries, 0:128] = (self.dq_t[...] * HEAD ** (-0.5)).T.astype(BF)
        self.d_pair[queries, 128:256] = self.dk[queries, :].astype(BF)
        self.d_pair[queries, 256:384] = self.dv[queries, :].astype(BF)
        self.dh1_part[queries, :] = dot_nt(self.d_pair[queries, :], self.w_pair[...]).astype(BF)


VMEM = pl.BlockSpec(memory_space=pltpu.VMEM)
SMEM = pl.BlockSpec(memory_space=pltpu.SMEM)
CROSS = 5 * D


class Weights(Layer):
    w_o = property(lambda self: self.pack[:, 0:D])
    w_cq = property(lambda self: self.pack[:, D:2 * D])
    w_ckv = property(lambda self: self.pack[:, 2 * D:4 * D])
    w_co = property(lambda self: self.pack[:, 4 * D:CROSS])

    def w_in(self, units):
        return self.pack.at[:, CROSS:CROSS + FF][:, units]

    def grad_in(self, units, value):
        self.grad_pack.at[:, CROSS:CROSS + FF][:, units] = value

    def grad_out(self, units, value):
        self.grad_w_out[units, :] = value

    def grad_into(self, start, left, right):
        for step in range(right.shape[1] // SPAN):
            columns = slice(start + step * SPAN, start + (step + 1) * SPAN)
            self.grad_pack[:, columns] = dot_tn(left[...], right[:, step * SPAN:(step + 1) * SPAN]).astype(BF)


INS = ("tokens", "cotangent", "encoded", "parents", "timestep", "i_qkv", "i_o", "i_cq", "i_ckv", "i_co", "i_in", "i_out", "aux_own")
OUTS = ("mixed", "grad_tokens", "g_encoded", "g_qkv", "g_o", "g_cq", "g_ckv", "g_co", "g_in", "g_out", "g_table")


def layer_scratch(rows, tree, blocks, levels, wide):
    tiles = tree // SPAN
    count = levels * 8
    each = D // count
    plain = lambda *shape: pltpu.VMEM(shape, F32)
    short = lambda *shape: pltpu.VMEM(shape, BF)
    dma = pltpu.SemaphoreType.DMA
    scratch = dict(
        pair_own=short(each, 3 * D), w_pair=short(D, 384), pack=short(D, CROSS + FF), w_out=short(FF, D),
        aux=short(count * 64, 128), tokens_all=short(tree, D), source_all=short(ENC, D),
        mod=plain(8, 6 * D), mod_grad=plain(8, 6 * D), bias=plain(blocks, tree), corner=plain(SPAN, SPAN),
        h1=short(tree, D), q_masked=short(2, tree, 128), key=short(tree, 128), value=short(tree, 128),
        key_t=short(128, tree), value_t=short(2, HEAD + 16, tree),
        top=plain(2, 8, SPAN), mix=plain(2, HEAD + 16, SPAN),
        weights=short(tiles * (tiles + 1) // 2, 2, SPAN, SPAN), inverse=plain(2, 8, tree),
        attended_t=plain(128, tree), attended=short(tree, 128), gathered=short(rows, D),
        cross_k=short(4, 2 * ENC, 128), cross_v=short(4, 2 * ENC, 128), cross_q=short(rows, D), cross_p=short(4, rows, 128),
        cross_out=short(rows, D), y1=plain(rows, D), h2=short(rows, D), h3=short(rows, D),
        act=short(rows, FF), d_hidden=short(rows, FF),
        d_cross=plain(ENC, 2 * D), dcq=short(rows, D), d_att_all=short(tree, 128),
        d_masked=short(2, SPAN, 128), dq_t=plain(128, SPAN), dk=plain(tree, 128), dv=plain(tree, 128),
        d_pair=short(tree, 384), relay=short(2, SPAN, D), dh1_box=short(2, 2, SPAN, D),
        grad_pack=short(D, CROSS + FF), grad_w_out=short(FF, D), grad_pair=short(D, 384), source_part=plain(ENC, D),
        payload=plain(count * 8, 128), table_box=plain(count * 8, 128), table_rows=plain(levels * 16, 128), settle_box=plain(ENC, D),
        a_send=dma((tiles,)), a_recv=dma((tiles,)), d_send=dma((4,)), d_recv=dma((4,)),
        h_send=dma((tiles,)), h_relay=dma((2,)), h_recv=dma((4,)),
        send=dma((4, Gather.sends(levels))), recv=dma((4, count)),
        pair_send=dma((GatherPair.sends(levels),)), pair_recv=dma((4 + 2 * levels,)),
        share_send=dma((6,)), share_recv=dma((8,)), spread_send=dma((3,)), spread_recv=dma((4,)),
        r_send=dma((3, Reduce.slots(levels))), r_recv=dma((3, Reduce.slots(levels))),
        rp_send=dma((ReducePair.slots(levels),)), rp_recv=dma((ReducePair.slots(levels),)),
        settle_send=dma((4,)), settle_recv=dma((4,)), t_send=dma((4 + 2 * levels,)), t_recv=dma((4 + 2 * levels,)),
    )
    for name, height, width in (("box_out", FF // count, D), ("box_in", each, FF), ("box_cross", each, CROSS)):
        for n, box in enumerate(Reduce.boxes(levels, height, width, BF)):
            scratch[f"{name}{n}"] = box
    for n, box in enumerate(ReducePair.boxes(levels, each, 384, BF)):
        scratch[f"box_pair{n}"] = box
    return scratch


def layer_kernel(levels, wide, names, refs):
    place = Place(levels)
    refs = dict(zip(names, refs))
    refs["y2"] = refs["dy"] = refs["grad_tokens"]
    refs["db"] = refs["db1"] = refs["h3"]
    refs["d_attn"] = refs["cross_q"]
    refs["dh1_part"] = refs["tokens_all"]
    w = Weights(place, refs)
    blk, leaf = place.blk, place.leaf
    peers = (place.near, place.far, place.opposite)
    rows = w.tokens.shape[0]
    tree = w.tokens_all.shape[0]
    tiles = tree // SPAN
    halves = rows // SPAN
    blocks = tree // BLOCK
    count = levels * 8
    each = D // count
    index = leaf * 4 + blk
    own_lanes = pl.ds(pl.multiple_of(blk * 128, 128), 128)

    w.tokens_all[rows_of(blk, rows), :] = w.tokens[...]
    w.source_all[rows_of(blk, w.encoded.shape[0]), :] = w.encoded[...]
    mine = rows_of(index, each)
    start = 0
    for name in ("i_o", "i_cq", "i_ckv", "i_co", "i_in"):
        width = refs[name].shape[1]
        w.pack[mine, start:start + width] = refs[name][...]
        start += width
    w.w_out[rows_of(index, w.i_out.shape[0]), :] = w.i_out[...]
    w.aux[rows_of(index, 64), :] = w.aux_own[...]
    for pair in range(4):
        for third in range(3):
            w.pair_own[:, 384 * pair + 128 * third:384 * pair + 128 * third + 128] = (
                w.i_qkv[:, D * third + 128 * pair:D * third + 128 * pair + 128])
    w.w_pair[mine, :] = w.pair_own[:, pl.ds(pl.multiple_of(blk * 384, 128), 384)]
    place.greet()

    weave = GatherPair(place, w.pair_own, w.w_pair, w.pair_send, w.pair_recv)
    table = Gather(place, w.aux, 64, slice(None), w.send.at[0], w.recv.at[0])
    share = Share(place, w.tokens_all, rows, w.share_send, w.share_recv)
    spread = Spread(place, w.source_all, w.encoded.shape[0], w.spread_send, w.spread_recv)
    loads = [
        Gather(place, w.pack, each, slice(0, CROSS), w.send.at[1], w.recv.at[1]),
        Gather(place, w.pack, each, slice(CROSS, CROSS + FF), w.send.at[2], w.recv.at[2]),
        Gather(place, w.w_out, FF // count, slice(None), w.send.at[3], w.recv.at[3]),
    ]
    weave_steps, table_steps, share_steps = weave.steps(), table.steps(), share.steps()
    load_steps = [load.steps() for load in loads]

    def ticks(steps, number=1):
        for turn in range(number):
            for step in steps:
                next(step, None)

    ticks([weave_steps, table_steps, share_steps])
    spread.start()
    ticks(load_steps)
    w.mod_grad[...] = jnp.zeros_like(w.mod_grad)
    w.d_cross[...] = jnp.zeros_like(w.d_cross)
    w.dk[...] = jnp.zeros_like(w.dk)
    w.dv[...] = jnp.zeros_like(w.dv)
    block_bias(w.parents, w.bias, blocks)
    row, column = iota((SPAN, SPAN), 0), iota((SPAN, SPAN), 1)
    w.corner[...] = jnp.where(((row < BLOCK) == (column < BLOCK)) & (row > column), -1e30, 0.0)
    ticks([weave_steps, table_steps], 2)
    ticks([share_steps])
    ticks(load_steps)
    ticks([weave_steps, table_steps], 10)
    read_modulation(w.aux, w.timestep[0], w.mod, wide)

    def project(block):
        for half in range(halves):
            w.project(block * halves + half)

    project(blk)
    ticks(load_steps)
    ticks([share_steps])
    project(place.near)
    project(place.far)
    ticks([share_steps])
    project(place.opposite)
    ticks(load_steps)

    def attended_copy(tile, src):
        there = w.gathered.at[span(tile % halves), pl.ds(pl.multiple_of(src * 128, 128), 128)]
        return remote(w.attended.at[span(tile), :], there, w.a_send.at[tile], w.a_recv.at[src * halves + tile % halves], leaf, tile // halves)

    for tile in range(tiles):
        w.attend(tile)
        away = tile // halves != blk
        pl.when(away)(lambda tile=tile: attended_copy(tile, blk).start())

        def keep(tile=tile):
            w.gathered[span(tile % halves), own_lanes] = w.attended[span(tile), :]

        pl.when(jnp.logical_not(away))(keep)
        ticks(load_steps)
    ticks(load_steps, 20)
    spread.arrive()
    w.cross_keys()
    for peer in peers:
        for half in range(halves):
            attended_copy(blk * halves + half, peer).wait_recv()
    loop(halves, w.middle)
    loop(FF // SPAN, w.hidden)
    for job in loads + [weave, table, share, spread]:
        job.finish()

    def boxes(name, number=4):
        return [refs[f"{name}{n}"] for n in range(number)]

    def store_out(there, value):
        w.g_out[there, :] = value

    def store_in(there, value):
        w.g_in[there, :] = value

    def store_cross(there, value):
        w.g_o[there, :] = value[:, 0:D]
        w.g_cq[there, :] = value[:, D:2 * D]
        w.g_ckv[there, :] = value[:, 2 * D:4 * D]
        w.g_co[there, :] = value[:, 4 * D:5 * D]

    sums = [
        Reduce(place, w.grad_w_out, FF // count, slice(None), store_out, boxes("box_out"), w.r_send.at[0], w.r_recv.at[0]),
        Reduce(place, w.grad_pack, each, slice(CROSS, CROSS + FF), store_in, boxes("box_in"), w.r_send.at[1], w.r_recv.at[1]),
    ]
    sum_steps = [job.steps() for job in sums]
    ticks(sum_steps)
    loop(halves, w.finish_forward)
    ticks(sum_steps)
    loop(halves, w.back_three)
    ticks(sum_steps)
    w.grad_into(4 * D, w.cross_out, w.db)
    loop(halves, w.back_cross)

    def da_copy(src, to):
        return remote(w.d_attn.at[:, pl.ds(pl.multiple_of(to * 128, 128), 128)], w.d_att_all.at[rows_of(src, rows), :],
                      w.d_send.at[to], w.d_recv.at[src], leaf, to)

    for peer in peers:
        da_copy(blk, peer).start()
    w.d_att_all[rows_of(blk, rows), :] = w.d_attn[:, own_lanes]
    ticks(sum_steps)
    w.grad_into(0, w.gathered, w.db1)
    w.grad_into(D, w.h2, w.dcq)
    low_cross = w.d_cross[...].astype(BF)
    for step in range(2 * D // SPAN):
        columns = slice(2 * D + step * SPAN, 2 * D + (step + 1) * SPAN)
        w.grad_pack[:, columns] = dot_tn(w.source_all[...], low_cross[:, step * SPAN:(step + 1) * SPAN]).astype(BF)
    w.source_part[...] = dot_nt(low_cross, w.w_ckv)
    sums.append(Reduce(place, w.grad_pack, each, slice(0, CROSS), store_cross, boxes("box_cross"), w.r_send.at[2], w.r_recv.at[2]))
    settle = Settle(place, w.source_part, w.g_encoded, w.settle_box, w.settle_send, w.settle_recv)
    later_steps = [sums[2].steps(), settle.steps()]
    ticks(later_steps)
    for peer in peers:
        da_copy(peer, peer).wait_recv()

    tree_sum = TreeReduce(place, w.dh1_part, w.relay, w.dh1_box, w.h_send, w.h_relay, w.h_recv)
    for tile in range(tiles - 1, -1, -1):
        w.attend_back(tile)
        tree_sum.offer(tile)
        if tile + 1 < tiles:
            tree_sum.forward(tile + 1)
        ticks(sum_steps)
        ticks(later_steps)
    tree_sum.forward(0)

    def pair_grad(step):
        w.grad_pair[span(step), :] = dot_tn(w.h1[:, span(step)], w.d_pair[...]).astype(BF)

    loop(D // SPAN, pair_grad)
    pair_sum = ReducePair(place, w.grad_pair, w.g_qkv, boxes("box_pair", 4), w.rp_send, w.rp_recv)
    pair_steps = pair_sum.steps()
    ticks([pair_steps])
    ticks(sum_steps + later_steps, 10)
    ticks([pair_steps], 3)

    def last(half):
        tree_sum.arrive(half)
        here, own = span(half), span(blk * halves + half)
        dh1 = w.dh1_part[own, :].astype(F32) + w.dh1_box[half, 0].astype(F32) + w.dh1_box[half, 1].astype(F32)
        unit, root = unit_rows(w.tokens[here, :].astype(F32))
        w.sums(0, dh1, dh1 * unit)
        w.grad_tokens[here, :] = w.dy[here, :] + norm_back(dh1, unit, root, w.mod[0:1, D:2 * D])

    for half in range(halves):
        last(half)
    w.payload[...] = table_payload(w.mod_grad[0:1, :], wide, count)
    table_sum = TableSum(place, w.payload, w.table_box, w.table_rows, w.t_send, w.t_recv)
    ticks([table_sum.steps(), pair_steps], 0)
    table_steps = table_sum.steps()
    ticks([table_steps, pair_steps], 10)

    leaves = levels * 2
    chosen = (iota((leaves, count * 64), 1) == iota((leaves, count * 64), 0) * 256 + STEPS).astype(BF)
    steps_all = dot(chosen, w.aux[...])
    line = iota((64, 128), 0).astype(F32)
    grad_table = jnp.zeros((64, 128), F32)
    for tree_at in range(leaves):
        grad_table = grad_table + jnp.where(line == steps_all[tree_at:tree_at + 1, :], w.table_rows[8 * tree_at:8 * tree_at + 1, :], 0.0)
    w.g_table[...] = grad_table[:STEPS, :wide]

    for tile in range(tiles):
        pl.when(tile // halves != blk)(lambda tile=tile: attended_copy(tile, blk).wait_send())
        tree_sum.finish(tile)
    for peer in peers:
        da_copy(blk, peer).wait_send()
    for job in sums + [settle, pair_sum, table_sum]:
        job.finish()


def per_device(tokens, cotangent, encoded, parents, timestep, w_qkv, w_o, w_cq, w_ckv, w_co, w_in, w_out, mod_table):
    levels = lax.axis_size("leaf") // 2
    rows, wide = tokens.shape[0], mod_table.shape[1]
    blocks = parents.shape[1]
    tree = blocks * BLOCK
    aux = jnp.concatenate(
        (
            jnp.pad(mod_table, ((0, 0), (0, 128 - wide))),
            jnp.full((64 - STEPS, 128), timestep[0], jnp.int32).astype(BF),
        ),
        axis=0,
    )
    ins = (tokens, cotangent, encoded, parents, timestep, w_qkv, w_o, w_cq, w_ckv, w_co, w_in, w_out, aux)
    scratch = layer_scratch(rows, tree, blocks, levels, wide)
    out = lambda like: jax.ShapeDtypeStruct(like.shape, F32)
    names = INS + OUTS + tuple(scratch)
    return pl.pallas_call(
        lambda *refs: layer_kernel(levels, wide, names, refs),
        out_shape=[jax.ShapeDtypeStruct((rows, D), BF), out(tokens), out(encoded)]
        + [out(weight) for weight in (w_qkv, w_o, w_cq, w_ckv, w_co, w_in, w_out, mod_table)],
        in_specs=[SMEM if name in ("parents", "timestep") else VMEM for name in INS],
        out_specs=[VMEM] * len(OUTS),
        scratch_shapes=list(scratch.values()),
        compiler_params=pltpu.CompilerParams(collective_id=0, has_side_effects=True, vmem_limit_bytes=(64 << 20) - (64 << 10)),
    )(*ins)


def solution(mesh):
    fits = mesh.shape["blk"] == 4 and mesh.shape["leaf"] == 8
    return jax.shard_map(
        per_device if fits else generic_device,
        mesh=mesh,
        in_specs=(
            P(("leaf", "blk"), None),
            P(("leaf", "blk"), None),
            P(("leaf", "blk"), None),
            P("leaf", None),
            P("leaf"),
            P(("leaf", "blk"), None),
            P(("leaf", "blk"), None),
            P(("leaf", "blk"), None),
            P(("leaf", "blk"), None),
            P(("leaf", "blk"), None),
            P(("leaf", "blk"), None),
            P(("leaf", "blk"), None),
            P(None, ("leaf", "blk")),
        ),
        out_specs=(
            P(("leaf", "blk"), None),
            P(("leaf", "blk"), None),
            P(("leaf", "blk"), None),
            P(("leaf", "blk"), None),
            P(("leaf", "blk"), None),
            P(("leaf", "blk"), None),
            P(("leaf", "blk"), None),
            P(("leaf", "blk"), None),
            P(("leaf", "blk"), None),
            P(("leaf", "blk"), None),
            P(None, ("leaf", "blk")),
        ),
        check_vma=False,
    )
```

```python
import functools

import jax
import jax.numpy as jnp
from jax import lax
from jax.experimental import pallas as pl
from jax.experimental.pallas import tpu as pltpu
from jax.sharding import PartitionSpec as P

D = 512
HEADS = 8
HEAD = 64
BLOCK = 128
FF = 2048
ENC = 64
STEPS = 50


PRECISE = lax.Precision.HIGHEST
MASKED = -1e30


def ancestors(parent_row):
    count = parent_row.shape[0]
    indices = jnp.arange(count, dtype=jnp.int32)
    reach_map = (indices[:, None] == indices[None, :]).astype(jnp.float32)
    reach_map = jnp.minimum(
        reach_map + (parent_row[:, None] == indices[None, :]).astype(jnp.float32), 1.0
    )
    for rounds in range(max(1, (count - 1).bit_length())):
        reach_map = jnp.minimum(jnp.dot(reach_map, reach_map, precision=PRECISE), 1.0)
    return reach_map


def normalize(values, shift, scaling):
    centred = values - jnp.mean(values, axis=-1, keepdims=True)
    spread = jnp.mean(centred * centred, axis=-1, keepdims=True)
    return centred * lax.rsqrt(spread + 1e-05) * (1.0 + scaling) + shift


def span_link(reach_rows, span):
    return lax.dynamic_slice_in_dim(reach_rows, span * 4, 4, 1)


def span_reached(reach_rows, span):
    return jnp.max(span_link(reach_rows, span)) > 0.5


def span_mask(reach_rows, first_block, span, row_count, width):
    query_index = jnp.arange(row_count, dtype=jnp.int32)
    key_index = jnp.arange(width, dtype=jnp.int32)
    query_block = first_block + query_index // BLOCK
    key_block = span * 4 + key_index // BLOCK
    link = span_link(reach_rows, span)
    link = jnp.repeat(jnp.repeat(link, BLOCK, axis=0), BLOCK, axis=1)
    same = query_block[:, None] == key_block[None, :]
    return (link > 0.5) & (
        jnp.logical_not(same) | (key_index[None, :] % BLOCK <= query_index[:, None] % BLOCK)
    )


def scores_of(queries, key_rows, allowed):
    raw = jnp.einsum(
        "qhd,khd->hqk", queries, key_rows, preferred_element_type=jnp.float32
    ) * HEAD ** (-0.5)
    return jnp.where(allowed[None], raw, MASKED)


def split_spans(keys, values):
    width = 4 * BLOCK
    count = keys.shape[0] // width
    return (
        jnp.arange(count, dtype=jnp.int32),
        keys.reshape(count, width, HEADS, HEAD),
        values.reshape(count, width, HEADS, HEAD),
    )


def tree_forward_attention(queries, keys, values, reach_rows, first_block):
    row_count = queries.shape[0]
    width = 4 * BLOCK
    spans, key_spans, value_spans = split_spans(keys, values)

    def stats(carry, item):
        span, key_rows = item

        def stats_visit(state):
            top, total = state
            allowed = span_mask(reach_rows, first_block, span, row_count, width)
            score = scores_of(queries, key_rows, allowed)
            new_top = jnp.maximum(top, jnp.max(score, axis=-1))
            weight = jnp.where(allowed[None], jnp.exp(score - new_top[..., None]), 0.0)
            return (new_top, total * jnp.exp(top - new_top) + jnp.sum(weight, axis=-1))

        return (
            lax.cond(span_reached(reach_rows, span), stats_visit, lambda state: state, carry),
            None,
        )

    start = (
        jnp.full((HEADS, row_count), MASKED, jnp.float32),
        jnp.zeros((HEADS, row_count), jnp.float32),
    )
    (top, total), unused = lax.scan(stats, start, (spans, key_spans))
    log_total = top + jnp.log(total)

    def collect(accum, item):
        span, key_rows, value_rows = item

        def collect_visit(current):
            allowed = span_mask(reach_rows, first_block, span, row_count, width)
            weight = jnp.where(
                allowed[None],
                jnp.exp(scores_of(queries, key_rows, allowed) - log_total[..., None]),
                0.0,
            )
            return current + jnp.einsum(
                "hqk,khd->qhd",
                weight.astype(jnp.bfloat16),
                value_rows,
                preferred_element_type=jnp.float32,
            )

        return (
            lax.cond(span_reached(reach_rows, span), collect_visit, lambda current: current, accum),
            None,
        )

    attended, unused = lax.scan(
        collect, jnp.zeros((row_count, HEADS, HEAD), jnp.float32), (spans, key_spans, value_spans)
    )
    return (attended, log_total)


def tree_backward_attention(queries, keys, values, reach_rows, first_block, log_total, grad_attn):
    row_count = queries.shape[0]
    width = 4 * BLOCK
    spans, key_spans, value_spans = split_spans(keys, values)

    def probs_of(span, key_rows):
        allowed = span_mask(reach_rows, first_block, span, row_count, width)
        return jnp.where(
            allowed[None],
            jnp.exp(scores_of(queries, key_rows, allowed) - log_total[..., None]),
            0.0,
        )

    def inner_pass(total, item):
        span, key_rows, value_rows = item

        def inner_visit(current):
            weight = probs_of(span, key_rows)
            d_weight = jnp.einsum(
                "qhd,khd->hqk", grad_attn, value_rows, preferred_element_type=jnp.float32
            )
            return current + jnp.sum(weight * d_weight, axis=-1)

        return (
            lax.cond(span_reached(reach_rows, span), inner_visit, lambda current: current, total),
            None,
        )

    delta, unused = lax.scan(
        inner_pass, jnp.zeros((HEADS, row_count), jnp.float32), (spans, key_spans, value_spans)
    )

    def grad_pass(d_queries, item):
        span, key_rows, value_rows = item

        def grad_visit(current):
            weight = probs_of(span, key_rows)
            d_weight = jnp.einsum(
                "qhd,khd->hqk", grad_attn, value_rows, preferred_element_type=jnp.float32
            )
            d_score = (weight * (d_weight - delta[..., None])).astype(jnp.bfloat16)
            current = current + jnp.einsum(
                "hqk,khd->qhd", d_score, key_rows, preferred_element_type=jnp.float32
            )
            d_keys = jnp.einsum(
                "hqk,qhd->khd", d_score, queries, preferred_element_type=jnp.float32
            ) * HEAD ** (-0.5)
            d_values = jnp.einsum(
                "hqk,qhd->khd",
                weight.astype(jnp.bfloat16),
                grad_attn,
                preferred_element_type=jnp.float32,
            )
            return (
                current,
                jnp.concatenate((d_keys.reshape(width, D), d_values.reshape(width, D)), axis=1),
            )

        def skip(current):
            return (current, jnp.zeros((width, 2 * D), jnp.float32))

        return lax.cond(span_reached(reach_rows, span), grad_visit, skip, d_queries)

    d_queries, terms = lax.scan(
        grad_pass, jnp.zeros((row_count, HEADS, HEAD), jnp.float32), (spans, key_spans, value_spans)
    )
    return (d_queries * HEAD ** (-0.5), terms.reshape(-1, 2 * D))


def generic_device(
    tokens,
    cotangent,
    encoded,
    parents,
    timestep,
    w_qkv,
    w_o,
    w_cq,
    w_ckv,
    w_co,
    w_in,
    w_out,
    mod_table,
):
    gathered = (
        lax.all_gather(w_qkv, ("leaf", "blk"), axis=0, tiled=True),
        lax.all_gather(w_o, ("leaf", "blk"), axis=0, tiled=True),
        lax.all_gather(w_cq, ("leaf", "blk"), axis=0, tiled=True),
        lax.all_gather(w_ckv, ("leaf", "blk"), axis=0, tiled=True),
        lax.all_gather(w_co, ("leaf", "blk"), axis=0, tiled=True),
        lax.all_gather(w_in, ("leaf", "blk"), axis=0, tiled=True),
        lax.all_gather(w_out, ("leaf", "blk"), axis=0, tiled=True),
        lax.all_gather(mod_table, ("leaf", "blk"), axis=1, tiled=True),
    )
    g_qkv, g_o, g_cq, g_ckv, g_co, g_in, g_out, g_table = gathered
    select = (jnp.arange(STEPS, dtype=jnp.int32) == timestep[0]).astype(jnp.float32)
    modulate = jnp.dot(
        select.astype(jnp.bfloat16)[None, :], g_table, preferred_element_type=jnp.float32
    )[0]
    pieces = [modulate[i * D : (i + 1) * D] for i in range(6)]
    inputs = tokens.astype(jnp.float32)
    row_count = tokens.shape[0]
    local_blocks = row_count // BLOCK
    first_block = lax.axis_index("blk") * local_blocks
    reach_map = ancestors(parents[0])
    reach_rows = lax.dynamic_slice_in_dim(reach_map, first_block, local_blocks, 0)
    scaling = HEAD ** (-0.5)
    normed_one, pull_one = jax.vjp(normalize, inputs, pieces[0], pieces[1])
    h_first = normed_one.astype(jnp.bfloat16)
    projected = jnp.dot(h_first, g_qkv, preferred_element_type=jnp.float32).astype(jnp.bfloat16)
    queries = projected[:, :D].reshape(row_count, HEADS, HEAD)
    keys, values = (
        lax.all_gather(projected[:, D : 2 * D], "blk", axis=0, tiled=True),
        lax.all_gather(projected[:, 2 * D :], "blk", axis=0, tiled=True),
    )
    attended, log_total = tree_forward_attention(queries, keys, values, reach_rows, first_block)
    attn_low = attended.reshape(row_count, D).astype(jnp.bfloat16)
    middle_one = inputs + jnp.dot(attn_low, g_o, preferred_element_type=jnp.float32)
    normed_two, pull_two = jax.vjp(normalize, middle_one, pieces[2], pieces[3])
    h_second = normed_two.astype(jnp.bfloat16)
    cross_q = (
        jnp.dot(h_second, g_cq, preferred_element_type=jnp.float32)
        .astype(jnp.bfloat16)
        .reshape(row_count, HEADS, HEAD)
    )
    source_local = jnp.dot(encoded, g_ckv, preferred_element_type=jnp.float32).astype(jnp.bfloat16)
    source_all = lax.all_gather(source_local, "blk", axis=0, tiled=True)
    cross_k = source_all[:, :D].reshape(-1, HEADS, HEAD)
    cross_v = source_all[:, D:].reshape(-1, HEADS, HEAD)
    cross_raw = (
        jnp.einsum("qhd,khd->hqk", cross_q, cross_k, preferred_element_type=jnp.float32) * scaling
    )
    cross_prob = jax.nn.softmax(cross_raw, axis=-1)
    cross_low = cross_prob.astype(jnp.bfloat16)
    cross_out = (
        jnp.einsum("hqk,khd->qhd", cross_low, cross_v, preferred_element_type=jnp.float32)
        .reshape(row_count, D)
        .astype(jnp.bfloat16)
    )
    middle_two = middle_one + jnp.dot(cross_out, g_co, preferred_element_type=jnp.float32)
    normed_three, pull_three = jax.vjp(normalize, middle_two, pieces[4], pieces[5])
    h_third = normed_three.astype(jnp.bfloat16)
    hidden_pre = jnp.dot(h_third, g_in, preferred_element_type=jnp.float32)
    activated, pull_gelu = jax.vjp(
        lambda values_in: jax.nn.gelu(values_in, approximate=True), hidden_pre
    )
    act_low = activated.astype(jnp.bfloat16)
    result = middle_two + jnp.dot(act_low, g_out, preferred_element_type=jnp.float32)
    mixed_out = result.astype(jnp.bfloat16)
    back_weights = (
        lax.all_gather(w_qkv, ("leaf", "blk"), axis=0, tiled=True),
        lax.all_gather(w_o, ("leaf", "blk"), axis=0, tiled=True),
        lax.all_gather(w_cq, ("leaf", "blk"), axis=0, tiled=True),
        lax.all_gather(w_ckv, ("leaf", "blk"), axis=0, tiled=True),
        lax.all_gather(w_co, ("leaf", "blk"), axis=0, tiled=True),
        lax.all_gather(w_in, ("leaf", "blk"), axis=0, tiled=True),
        lax.all_gather(w_out, ("leaf", "blk"), axis=0, tiled=True),
        lax.all_gather(mod_table, ("leaf", "blk"), axis=1, tiled=True),
    )
    b_qkv, b_o, b_cq, b_ckv, b_co, b_in, b_out = back_weights[:7]
    d_act = jnp.dot(cotangent, b_out.T, preferred_element_type=jnp.float32)
    d_hidden = pull_gelu(d_act)[0].astype(jnp.bfloat16)
    grad_out_w = jnp.dot(act_low.T, cotangent, preferred_element_type=jnp.float32)
    grad_in_w = jnp.dot(h_third.T, d_hidden, preferred_element_type=jnp.float32)
    d_h_third = jnp.dot(d_hidden, b_in.T, preferred_element_type=jnp.float32)
    d_middle_part, d_shift_three, d_scale_three = pull_three(d_h_third)
    d_middle_two = cotangent.astype(jnp.float32) + d_middle_part
    d_branch_two = d_middle_two.astype(jnp.bfloat16)
    grad_co_w = jnp.dot(cross_out.T, d_branch_two, preferred_element_type=jnp.float32)
    d_cross_out = (
        jnp.dot(d_branch_two, b_co.T, preferred_element_type=jnp.float32)
        .astype(jnp.bfloat16)
        .reshape(row_count, HEADS, HEAD)
    )
    d_cross_prob = jnp.einsum(
        "qhd,khd->hqk", d_cross_out, cross_v, preferred_element_type=jnp.float32
    )
    d_cross_raw = (
        cross_prob * (d_cross_prob - jnp.sum(cross_prob * d_cross_prob, axis=-1, keepdims=True))
    ).astype(jnp.bfloat16)
    d_cross_q = (
        (
            jnp.einsum("hqk,khd->qhd", d_cross_raw, cross_k, preferred_element_type=jnp.float32)
            * scaling
        )
        .reshape(row_count, D)
        .astype(jnp.bfloat16)
    )
    d_cross_k = (
        jnp.einsum("hqk,qhd->khd", d_cross_raw, cross_q, preferred_element_type=jnp.float32)
        * scaling
    )
    d_cross_v = jnp.einsum(
        "hqk,qhd->khd", cross_low, d_cross_out, preferred_element_type=jnp.float32
    )
    source_terms = jnp.concatenate((d_cross_k.reshape(-1, D), d_cross_v.reshape(-1, D)), axis=1)
    d_source = lax.psum_scatter(
        source_terms.astype(jnp.bfloat16), "blk", scatter_dimension=0, tiled=True
    )
    grad_ckv_w = jnp.dot(encoded.T, d_source, preferred_element_type=jnp.float32)
    d_encoded = jnp.dot(d_source, b_ckv.T, preferred_element_type=jnp.float32)
    grad_cq_w = jnp.dot(h_second.T, d_cross_q, preferred_element_type=jnp.float32)
    d_h_second = jnp.dot(d_cross_q, b_cq.T, preferred_element_type=jnp.float32)
    d_middle_part, d_shift_two, d_scale_two = pull_two(d_h_second)
    d_middle_one = d_middle_two + d_middle_part
    d_branch_one = d_middle_one.astype(jnp.bfloat16)
    grad_o_w = jnp.dot(attn_low.T, d_branch_one, preferred_element_type=jnp.float32)
    d_attn = (
        jnp.dot(d_branch_one, b_o.T, preferred_element_type=jnp.float32)
        .astype(jnp.bfloat16)
        .reshape(row_count, HEADS, HEAD)
    )
    keys_back, values_back = (
        lax.all_gather(projected[:, D : 2 * D], "blk", axis=0, tiled=True),
        lax.all_gather(projected[:, 2 * D :], "blk", axis=0, tiled=True),
    )
    d_queries, key_terms = tree_backward_attention(
        queries, keys_back, values_back, reach_rows, first_block, log_total, d_attn
    )
    d_key_value = lax.psum_scatter(
        key_terms.astype(jnp.bfloat16), "blk", scatter_dimension=0, tiled=True
    ).astype(jnp.float32)
    d_projected = jnp.concatenate((d_queries.reshape(row_count, D), d_key_value), axis=1).astype(
        jnp.bfloat16
    )
    grad_qkv_w = jnp.dot(h_first.T, d_projected, preferred_element_type=jnp.float32)
    d_h_first = jnp.dot(d_projected, b_qkv.T, preferred_element_type=jnp.float32)
    d_input_part, d_shift_one, d_scale_one = pull_one(d_h_first)
    d_tokens = d_middle_one + d_input_part
    d_modulate = jnp.concatenate(
        (d_shift_one, d_scale_one, d_shift_two, d_scale_two, d_shift_three, d_scale_three)
    )
    grad_table_w = select[:, None] * d_modulate[None, :]
    gradients = (
        lax.psum_scatter(grad_qkv_w, ("leaf", "blk"), scatter_dimension=0, tiled=True),
        lax.psum_scatter(grad_o_w, ("leaf", "blk"), scatter_dimension=0, tiled=True),
        lax.psum_scatter(grad_cq_w, ("leaf", "blk"), scatter_dimension=0, tiled=True),
        lax.psum_scatter(grad_ckv_w, ("leaf", "blk"), scatter_dimension=0, tiled=True),
        lax.psum_scatter(grad_co_w, ("leaf", "blk"), scatter_dimension=0, tiled=True),
        lax.psum_scatter(grad_in_w, ("leaf", "blk"), scatter_dimension=0, tiled=True),
        lax.psum_scatter(grad_out_w, ("leaf", "blk"), scatter_dimension=0, tiled=True),
        lax.psum_scatter(grad_table_w, ("leaf", "blk"), scatter_dimension=1, tiled=True),
    )
    return (
        mixed_out,
        d_tokens,
        d_encoded,
        gradients[0],
        gradients[1],
        gradients[2],
        gradients[3],
        gradients[4],
        gradients[5],
        gradients[6],
        gradients[7],
    )


MESH = pl.DeviceIdType.MESH
BF = jnp.bfloat16
F32 = jnp.float32


class Place:
    def __init__(self, levels):
        leaf = lax.axis_index("leaf")
        blk = lax.axis_index("blk")
        self.levels = levels
        self.leaf = leaf
        self.blk = blk
        self.z = leaf // 2
        self.core = leaf % 2
        self.near = blk + 1 - 2 * (blk % 2)
        self.far = (blk + 2) % 4
        self.first = self.core * self.near + (1 - self.core) * self.far
        self.second = self.core * self.far + (1 - self.core) * self.near
        self.opposite = 3 - blk
        self.sibling = self.z * 2 + 1 - self.core
        self.line = [(leaf + 2 * step) % (2 * levels) for step in range(1, levels)]

    def greet(self):
        barrier = pltpu.get_barrier_semaphore()

        count = self.levels * 2

        def hello(leaf, blk):
            pl.semaphore_signal(barrier, inc=1, device_id=(leaf, blk), device_id_type=MESH)

        for blk in (self.near, self.far, self.opposite):
            hello(self.leaf, blk)
        for step in range(1, count):
            hello((self.leaf + step) % count, self.blk)
        pl.semaphore_wait(barrier, count + 2)


def remote(src, dst, send, recv, leaf, blk):
    return pltpu.make_async_remote_copy(
        src_ref=src, dst_ref=dst, send_sem=send, recv_sem=recv,
        device_id=(leaf, blk), device_id_type=MESH,
    )


def rows_of(start, count):
    return pl.ds(pl.multiple_of(start * count, count), count)


class Gather:
    def __init__(self, place, full, rows, columns, send_sem, recv_sem):
        self.place, self.full, self.rows, self.columns = place, full, rows, columns
        self.send_sem, self.recv_sem = send_sem, recv_sem
        self.sent = []

    def build(self, leaf, blk, to_leaf, to_blk, number):
        there = self.full.at[rows_of(leaf * 4 + blk, self.rows), self.columns]
        return remote(there, there, self.send_sem.at[number], self.recv_sem.at[leaf * 4 + blk], to_leaf, to_blk)

    def push(self, leaf, blk, *targets):
        for to_leaf, to_blk in targets:
            copy = self.build(leaf, blk, to_leaf, to_blk, len(self.sent))
            copy.start()
            self.sent.append(copy)

    def arrive(self, leaf, blk):
        p = self.place
        self.build(leaf, blk, p.leaf, p.second, 0).wait_recv()

    def steps(self):
        p = self.place
        sibling, second = (p.sibling, p.blk), (p.leaf, p.second)
        line = [(leaf, p.blk) for leaf in p.line]
        self.push(p.leaf, p.blk, (p.leaf, p.first), *line, sibling)
        yield
        self.arrive(p.leaf, p.first)
        self.push(p.leaf, p.first, *line, sibling)
        yield
        self.push(p.leaf, p.blk, second)
        self.push(p.leaf, p.first, second)
        for leaf in p.line:
            self.arrive(leaf, p.blk)
            self.push(leaf, p.blk, second, sibling)
        yield
        for leaf in p.line:
            self.arrive(leaf, p.first)
            self.push(leaf, p.first, second, sibling)
        yield
        for leaf in (p.leaf, *p.line):
            for blk in (p.second, p.opposite):
                self.arrive(leaf, blk)
                self.push(leaf, blk, sibling)
        yield
        for level in range(p.levels):
            for blk in range(4):
                self.arrive(2 * level + 1 - p.core, blk)
        yield

    def finish(self):
        for copy in self.sent:
            copy.wait_send()

    @staticmethod
    def sends(levels):
        return 8 * levels


class Share:
    def __init__(self, place, full, rows, send_sem, recv_sem):
        self.place, self.full, self.rows = place, full, rows
        self.send_sem, self.recv_sem = send_sem, recv_sem
        self.half = rows // 2

    def view(self, blk, half):
        return self.full.at[pl.ds(pl.multiple_of(blk * self.rows + half * self.half, self.half), self.half), :]

    def build(self, blk, half, to_blk, number):
        there = self.view(blk, half)
        return remote(there, there, self.send_sem.at[number], self.recv_sem.at[blk * 2 + half], self.place.leaf, to_blk)

    def steps(self):
        p = self.place
        self.copies = [
            self.build(p.blk, 0, p.near, 0),
            self.build(p.blk, 1, p.far, 1),
            self.build(p.blk, 1, p.near, 2),
            self.build(p.blk, 0, p.far, 3),
        ]
        for copy in self.copies:
            copy.start()
        yield
        for blk, half, to_blk, number in ((p.near, 0, p.far, 4), (p.far, 1, p.near, 5)):
            copy = self.build(blk, half, to_blk, number)
            copy.wait_recv()
            copy.start()
            self.copies.append(copy)
        yield
        self.build(p.near, 1, p.near, 0).wait_recv()
        self.build(p.far, 0, p.near, 0).wait_recv()
        yield
        self.build(p.opposite, 0, p.near, 0).wait_recv()
        self.build(p.opposite, 1, p.near, 0).wait_recv()
        yield

    def finish(self):
        for copy in self.copies:
            copy.wait_send()


class Spread:
    def __init__(self, place, full, rows, send_sem, recv_sem):
        self.place, self.full, self.rows = place, full, rows
        self.send_sem, self.recv_sem = send_sem, recv_sem

    def build(self, blk, to_blk, number):
        there = self.full.at[rows_of(blk, self.rows), :]
        return remote(there, there, self.send_sem.at[number], self.recv_sem.at[blk], self.place.leaf, to_blk)

    def start(self):
        p = self.place
        self.copies = [self.build(p.blk, to, n) for n, to in enumerate((p.near, p.far, p.opposite))]
        for copy in self.copies:
            copy.start()

    def arrive(self):
        p = self.place
        for blk in (p.near, p.far, p.opposite):
            self.build(blk, p.near, 0).wait_recv()

    def finish(self):
        for copy in self.copies:
            copy.wait_send()


class Reduce:
    def __init__(self, place, total, rows, columns, store, boxes, send_sem, recv_sem, line_last):
        self.place, self.total, self.rows, self.columns, self.store = place, total, rows, columns, store
        self.from_sibling, self.from_second, self.from_line, self.from_first = boxes
        self.send_sem, self.recv_sem = send_sem, recv_sem
        self.line_last = line_last
        self.sent = []

    @staticmethod
    def slots(levels):
        return 6 * levels

    @staticmethod
    def boxes(levels, rows, width, kind, line_last):
        line, first = (levels, levels) if line_last else (2 * levels, 1)
        return [pltpu.VMEM((slots * rows, width), kind) for slots in (4 * levels, 2 * levels, line, first)]

    def here(self, leaf, blk):
        return (leaf * 4 + blk) * self.rows

    def part(self, leaf, blk, count=1):
        return self.total.at[pl.ds(pl.multiple_of(self.here(leaf, blk), self.rows), self.rows * count), self.columns]

    def copy(self, src, box, position, count, number, leaf, blk, sender=None):
        there = box.at[pl.ds(pl.multiple_of(position * self.rows, self.rows), self.rows * count), :]
        sender = number if sender is None else sender
        return remote(there if src is None else src, there, self.send_sem.at[sender], self.recv_sem.at[number], leaf, blk)

    def send(self, *parts):
        copy = self.copy(*parts)
        copy.start()
        self.sent.append(copy)

    def arrived(self, box, position, count, number):
        self.copy(None, box, position, count, number, self.place.leaf, self.place.first).wait_recv()

    def value(self, start, *sources):
        unit = pl.ds(pl.multiple_of(start, 16), 16)
        value = self.total[unit, self.columns].astype(F32)
        for box, position in sources:
            value = value + box[pl.ds(pl.multiple_of(position, 16), 16), :].astype(F32)
        return unit, value

    def add(self, leaf, blk, *sources, count=1):
        def one(step):
            unit, value = self.value(self.here(leaf, blk) + 16 * step, *[(box, slot * self.rows + 16 * step) for box, slot in sources])
            self.total[unit, self.columns] = value.astype(self.total.dtype)

        loop(count * self.rows // 16, one)

    def give(self, *sources):
        for step in range(self.rows // 16):
            unit, value = self.value(self.here(self.place.leaf, self.place.blk) + 16 * step,
                                     *[(box, slot * self.rows + 16 * step) for box, slot in sources])
            self.store(pl.ds(16 * step, 16), value)

    def steps(self):
        p = self.place
        levels = p.levels
        for level in range(levels):
            self.send(self.part(2 * level + 1 - p.core, 0, 4), self.from_sibling, 4 * level, 4, level, p.sibling, p.blk)
        yield
        for level in range(levels):
            self.arrived(self.from_sibling, 4 * level, 4, level)
            leaf = 2 * level + p.core
            self.add(leaf, 0, (self.from_sibling, 4 * level), count=4)
            for which, blk in enumerate((p.second, p.opposite)):
                slot = 2 * level + which
                self.send(self.part(leaf, blk), self.from_second, slot, 1, levels + slot, p.leaf, p.second)
        yield
        for level in range(levels):
            leaf = 2 * level + p.core
            for which, blk in enumerate((p.blk, p.first)):
                slot = 2 * level + which
                self.arrived(self.from_second, slot, 1, levels + slot)
                self.add(leaf, blk, (self.from_second, slot))
                if self.line_last and which == 1:
                    self.send(self.part(leaf, p.first), self.from_first, level, 1, 5 * levels + level, p.leaf, p.first)
        if self.line_last:
            yield
            for level in range(levels):
                self.arrived(self.from_first, level, 1, 5 * levels + level)
                self.add(2 * level + p.core, p.blk, (self.from_first, level))
        shards = (p.blk,) if self.line_last else (p.blk, p.first)
        slots = len(shards)
        for leaf in p.line:
            for which, blk in enumerate(shards):
                self.send(self.part(leaf, blk), self.from_line, slots * p.z + which, 1, 3 * levels + slots * p.z + which,
                          leaf, p.blk, 3 * levels + slots * (leaf // 2) + which)
        yield
        came = []
        for which, blk in enumerate(shards):
            slots_of = [slots * (leaf // 2) + which for leaf in p.line]
            for slot in slots_of:
                self.arrived(self.from_line, slot, 1, 3 * levels + slot)
            came.append([(self.from_line, slot) for slot in slots_of])
        if self.line_last:
            self.give(*came[0])
            yield
            return
        self.add(p.leaf, p.first, *came[1])
        self.send(self.part(p.leaf, p.first), self.from_first, 0, 1, 5 * levels, p.leaf, p.first)
        yield
        self.arrived(self.from_first, 0, 1, 5 * levels)
        self.give(*came[0], (self.from_first, 0))
        yield

    def finish(self):
        for copy in self.sent:
            copy.wait_send()


class GatherPair:
    def __init__(self, place, own, full, send_sem, recv_sem):
        self.place, self.own, self.full = place, own, full
        self.rows, self.width = own.shape[0], full.shape[1]
        self.send_sem, self.recv_sem = send_sem, recv_sem
        self.sent = []

    def start(self, copy):
        copy.start()
        self.sent.append(copy)

    def piece(self, src_blk, to_blk):
        p = self.place
        there = self.full.at[rows_of(p.leaf * 4 + src_blk, self.rows), :]
        src = self.own.at[:, pl.ds(pl.multiple_of(to_blk * self.width, 128), self.width)]
        return remote(src, there, self.send_sem.at[len(self.sent)], self.recv_sem.at[src_blk], p.leaf, to_blk)

    def block(self, leaf, to_leaf):
        there = self.full.at[rows_of(leaf, 4 * self.rows), :]
        return remote(there, there, self.send_sem.at[len(self.sent)], self.recv_sem.at[4 + leaf], to_leaf, self.place.blk)

    def steps(self):
        p = self.place
        for to_blk in (p.near, p.far, p.opposite):
            self.start(self.piece(p.blk, to_blk))
        yield
        for blk in (p.near, p.far, p.opposite):
            self.piece(blk, p.near).wait_recv()
        for to_leaf in (*p.line, p.sibling):
            self.start(self.block(p.leaf, to_leaf))
        yield
        for leaf in p.line:
            self.block(leaf, p.sibling).wait_recv()
            self.start(self.block(leaf, p.sibling))
        yield
        for level in range(p.levels):
            self.block(2 * level + 1 - p.core, p.sibling).wait_recv()
        yield

    def finish(self):
        for copy in self.sent:
            copy.wait_send()

    @staticmethod
    def sends(levels):
        return 2 * levels + 3


class ReducePair:
    def __init__(self, place, total, out, boxes, send_sem, recv_sem):
        self.place, self.total, self.out = place, total, out
        self.rows = total.shape[0] // (place.levels * 8)
        self.from_sibling, self.from_line, self.from_pair = boxes
        self.send_sem, self.recv_sem = send_sem, recv_sem
        self.sent = []

    @staticmethod
    def slots(levels):
        return 2 * levels + 4

    @staticmethod
    def boxes(levels, rows, width, kind):
        return [pltpu.VMEM((levels * 4 * rows, width), kind) for n in range(2)] + [pltpu.VMEM((4 * rows, width), kind)]

    def build(self, src, box, slot, rows, number, leaf, blk):
        there = box.at[rows_of(slot, rows), :]
        return remote(there if src is None else src, there, self.send_sem.at[len(self.sent)], self.recv_sem.at[number], leaf, blk)

    def send(self, *parts):
        copy = self.build(*parts)
        copy.start()
        self.sent.append(copy)

    def arrived(self, box, slot, rows, number):
        self.build(None, box, slot, rows, number, self.place.sibling, self.place.blk).wait_recv()

    def part(self, leaf):
        return self.total.at[rows_of(leaf, 4 * self.rows), :]

    def add(self, leaf, *sources):
        here = rows_of(leaf, 4 * self.rows)
        value = self.total[here, :].astype(F32)
        for box, slot in sources:
            value = value + box[rows_of(slot, 4 * self.rows), :].astype(F32)
        self.total[here, :] = value.astype(self.total.dtype)

    def steps(self):
        p = self.place
        levels, rows = p.levels, 4 * self.rows
        for level in range(levels):
            self.send(self.part(2 * level + 1 - p.core), self.from_sibling, level, rows, level, p.sibling, p.blk)
        yield
        for level in range(levels):
            self.arrived(self.from_sibling, level, rows, level)
            self.add(2 * level + p.core, (self.from_sibling, level))
        for leaf in p.line:
            self.send(self.part(leaf), self.from_line, p.z, rows, levels + p.z, leaf, p.blk)
        yield
        for leaf in p.line:
            self.arrived(self.from_line, leaf // 2, rows, levels + leaf // 2)
        self.add(p.leaf, *[(self.from_line, leaf // 2) for leaf in p.line])
        peers = (p.near, p.far, p.opposite)
        for to_blk in peers:
            src = self.total.at[rows_of(p.leaf * 4 + to_blk, self.rows), :]
            self.send(src, self.from_pair, p.blk, self.rows, 2 * levels + p.blk, p.leaf, to_blk)
        self.store(p.blk, self.total[rows_of(p.leaf * 4 + p.blk, self.rows), :])
        yield
        for blk in peers:
            self.arrived(self.from_pair, blk, self.rows, 2 * levels + blk)
            self.store(blk, self.from_pair[rows_of(blk, self.rows), :])
        yield

    def store(self, blk, value):
        for third in range(3):
            lanes = pl.ds(pl.multiple_of(third * D + blk * 128, 128), 128)
            self.out[:, lanes] = value[:, third * 128:third * 128 + 128].astype(F32)

    def finish(self):
        for copy in self.sent:
            copy.wait_send()


class Settle:
    def __init__(self, place, part, out, box, send_sem, recv_sem):
        self.place, self.part, self.out, self.box = place, part, out, box
        self.send_sem, self.recv_sem = send_sem, recv_sem
        self.rows = out.shape[0]

    def build(self, src_blk, to_blk):
        p = self.place
        return remote(self.part.at[rows_of(to_blk, self.rows), :], self.box.at[rows_of(src_blk, self.rows), :],
                      self.send_sem.at[to_blk], self.recv_sem.at[src_blk], p.leaf, to_blk)

    def steps(self):
        p = self.place
        self.copies = [self.build(p.blk, to) for to in (p.near, p.far, p.opposite)]
        for copy in self.copies:
            copy.start()
        yield
        total = self.part[rows_of(p.blk, self.rows), :]
        for blk in (p.near, p.far, p.opposite):
            self.build(blk, p.near).wait_recv()
            total = total + self.box[rows_of(blk, self.rows), :]
        self.out[...] = total
        yield

    def finish(self):
        for copy in self.copies:
            copy.wait_send()


class TableSum:
    def __init__(self, place, payload, box, rows_box, send_sem, recv_sem):
        self.place, self.payload, self.box, self.rows_box = place, payload, box, rows_box
        self.send_sem, self.recv_sem = send_sem, recv_sem
        self.leaves = place.levels * 2
        self.rows = self.leaves * 8

    def first(self, src_blk, to_blk):
        return remote(self.payload.at[rows_of(to_blk, self.rows), :], self.box.at[rows_of(src_blk, self.rows), :],
                      self.send_sem.at[to_blk], self.recv_sem.at[src_blk], self.place.leaf, to_blk)

    def second(self, src_leaf, to_leaf):
        p = self.place
        start = p.blk * self.leaves + to_leaf
        return remote(self.payload.at[rows_of(start, 8), :], self.rows_box.at[rows_of(src_leaf, 8), :],
                      self.send_sem.at[4 + to_leaf], self.recv_sem.at[4 + src_leaf], to_leaf, p.blk)

    def steps(self):
        p = self.place
        peers = (p.near, p.far, p.opposite)
        others = [(p.leaf + step) % self.leaves for step in range(1, self.leaves)]
        for to in peers:
            self.first(p.blk, to).start()
        yield
        here = rows_of(p.blk, self.rows)
        total = self.payload[here, :]
        for src in peers:
            self.first(src, p.near).wait_recv()
            total = total + self.box[rows_of(src, self.rows), :]
        self.payload[here, :] = total
        for to in others:
            self.second(p.leaf, to).start()
        self.rows_box[rows_of(p.leaf, 8), :] = self.payload[rows_of(p.blk * self.leaves + p.leaf, 8), :]
        yield
        for src in others:
            self.second(src, others[0]).wait_recv()
        yield

    def finish(self):
        p = self.place
        for to in (p.near, p.far, p.opposite):
            self.first(p.blk, to).wait_send()
        for step in range(1, self.leaves):
            self.second(p.leaf, (p.leaf + step) % self.leaves).wait_send()


class TreeReduce:
    def __init__(self, place, part, relay, box, send_sem, relay_sem, recv_sem):
        self.place, self.part, self.relay, self.box = place, part, relay, box
        self.send_sem, self.relay_sem, self.recv_sem = send_sem, relay_sem, recv_sem

    def roles(self, tile):
        owner, half = tile // 2, tile % 2
        near, far = owner + 1 - 2 * (owner % 2), (owner + 2) % 4
        direct, relayed = (near, far) if half == 0 else (far, near)
        return owner, half, direct, relayed, 3 - owner

    def to_owner(self, tile, which):
        owner, half = tile // 2, tile % 2
        return remote(self.part.at[span(tile), :], self.box.at[half, which], self.send_sem.at[tile],
                      self.recv_sem.at[half * 2 + which], self.place.leaf, owner)

    def to_relay(self, tile):
        owner, half, direct, relayed, opposite = self.roles(tile)
        return remote(self.part.at[span(tile), :], self.relay.at[half], self.send_sem.at[tile],
                      self.relay_sem.at[half], self.place.leaf, relayed)

    def offer(self, tile):
        owner, half, direct, relayed, opposite = self.roles(tile)
        pl.when(self.place.blk == opposite)(lambda: self.to_relay(tile).start())
        pl.when(self.place.blk == direct)(lambda: self.to_owner(tile, 0).start())

    def forward(self, tile):
        owner, half, direct, relayed, opposite = self.roles(tile)

        def go():
            self.to_relay(tile).wait_recv()
            total = self.part[span(tile), :].astype(F32) + self.relay[half].astype(F32)
            self.part[span(tile), :] = total.astype(BF)
            self.to_owner(tile, 1).start()

        pl.when(self.place.blk == relayed)(go)

    def arrive(self, half):
        for which in range(2):
            self.to_owner(half, which).wait_recv()

    def finish(self, tile):
        owner, half, direct, relayed, opposite = self.roles(tile)
        pl.when(self.place.blk == opposite)(lambda: self.to_relay(tile).wait_send())
        pl.when(self.place.blk == direct)(lambda: self.to_owner(tile, 0).wait_send())
        pl.when(self.place.blk == relayed)(lambda: self.to_owner(tile, 1).wait_send())


SPAN = 256
TINY = 1e-05


def dot(left, right):
    return lax.dot_general(left, right, (((1,), (0,)), ((), ())), preferred_element_type=F32)


def dot_nt(left, right):
    return lax.dot_general(left, right, (((1,), (1,)), ((), ())), preferred_element_type=F32)


def dot_tn(left, right):
    return lax.dot_general(left, right, (((0,), (0,)), ((), ())), preferred_element_type=F32)


def iota(shape, axis):
    return lax.broadcasted_iota(jnp.int32, shape, axis)


def span(start, count=SPAN):
    return pl.ds(pl.multiple_of(start * count, count), count)


def loop(count, body):
    def step(index, carry):
        body(index)
        return carry

    lax.fori_loop(0, count, step, 0)


def unit_rows(values):
    centred = values - jnp.mean(values, axis=-1, keepdims=True)
    root = lax.rsqrt(jnp.mean(centred * centred, axis=-1, keepdims=True) + TINY)
    return centred * root, root


def norm_back(grad, unit, root, scale):
    inner = grad * (1.0 + scale)
    return (
        inner
        - jnp.mean(inner, axis=-1, keepdims=True)
        - unit * jnp.mean(inner * unit, axis=-1, keepdims=True)
    ) * root


def spread_pattern(wide, group):
    column = iota((128, group), 1)
    turn = jnp.zeros((128, group), jnp.int32)
    for step in range(1, group // wide):
        turn = turn + (column >= step * wide).astype(jnp.int32)
    return (column - turn * wide == iota((128, group), 0)).astype(F32)


def shard_of_column(count, wide, group):
    column = iota((count, group), 1)
    turn = jnp.zeros((count, group), jnp.int32)
    for step in range(1, group // wide):
        turn = turn + (column >= step * wide).astype(jnp.int32)
    return turn


def read_modulation(aux, timestep, mod, wide):
    count = aux.shape[0] // 64
    row = iota((count, aux.shape[0]), 0)
    column = iota((count, aux.shape[0]), 1)
    chosen = (column == row * 64 + timestep).astype(BF)
    picked = dot(chosen, aux[...])
    group = wide * 4
    laid = dot(picked.astype(BF), spread_pattern(wide, group).astype(BF))
    offset = iota((count, group), 0) - shard_of_column(count, wide, group)
    for part in range(count // 4):
        mod[0:1, part * group:(part + 1) * group] = jnp.sum(
            jnp.where(offset == 4 * part, laid, 0.0), axis=0, keepdims=True
        )


def table_payload(sums, wide, count):
    group = wide * 4
    offset = iota((count, group), 0) - shard_of_column(count, wide, group)
    held = jnp.zeros((count, group), F32)
    for part in range(count // 4):
        held = held + jnp.where(offset == 4 * part, sums[0:1, part * group:(part + 1) * group], 0.0)
    cut = lax.dot_general(held, spread_pattern(wide, group), (((1,), (1,)), ((), ())),
                          preferred_element_type=F32, precision=lax.Precision.HIGHEST)
    leaves = count // 4
    row = iota((count * 8, count), 0)
    tile = sum((row >= 8 * step).astype(jnp.int32) for step in range(1, count))
    block = sum((row >= 8 * leaves * step).astype(jnp.int32) for step in range(1, 4))
    chosen = (iota((count * 8, count), 1) == (tile - block * leaves) * 4 + block).astype(F32)
    return lax.dot_general(chosen, cut, (((1,), (0,)), ((), ())),
                           preferred_element_type=F32, precision=lax.Precision.HIGHEST)


def block_bias(parents, bias, blocks):
    row, column = iota((128, 128), 0), iota((128, 128), 1)
    reach = (row == column).astype(F32)
    for block in range(blocks):
        reach = jnp.maximum(reach, ((column == block) & (row == parents[0, block])).astype(F32))
    for step in range((blocks - 1).bit_length()):
        low_reach = reach.astype(BF)
        reach = jnp.minimum(dot(low_reach, low_reach), 1.0)
    held = (reach[:blocks, :] - 1.0) * 1e30
    for block in range(blocks):
        bias[:, block * BLOCK:(block + 1) * BLOCK] = jnp.broadcast_to(held[:, block:block + 1], (blocks, BLOCK))


class Layer:
    def __init__(self, place, refs):
        self.place = place
        self.__dict__.update(refs)

    def project(self, chunk):
        rows = span(chunk)
        unit, root = unit_rows(self.tokens_all[rows, :].astype(F32))
        first = (unit * (1.0 + self.mod[0:1, D:2 * D]) + self.mod[0:1, 0:D]).astype(BF)
        self.h1[rows, :] = first
        made = dot(first, self.w_pair[...])
        lane = iota((SPAN, 128), 1)
        query = made[:, 0:128].astype(BF).astype(F32) * HEAD ** (-0.5)
        self.q_masked[0, rows, :] = jnp.where(lane < HEAD, query, 0.0).astype(BF)
        self.q_masked[1, rows, :] = jnp.where(lane >= HEAD, query, 0.0).astype(BF)
        key = made[:, 128:256]
        value = made[:, 256:384]
        self.key[rows, :] = key.astype(BF)
        self.value[rows, :] = value.astype(BF)
        self.key_t[:, rows] = key.T.astype(BF)
        value_t = value.T.astype(BF)
        ones = jnp.ones((16, SPAN), BF)
        self.value_t[0, 0:HEAD, rows] = value_t[:HEAD]
        self.value_t[1, 0:HEAD, rows] = value_t[HEAD:]
        self.value_t[0, HEAD:HEAD + 16, rows] = ones
        self.value_t[1, HEAD:HEAD + 16, rows] = ones

    def attend(self, tile):
        queries = slice(tile * SPAN, (tile + 1) * SPAN)
        base = tile * (tile + 1) // 2

        def score(j, head):
            raw = dot_nt(self.key[j * SPAN:(j + 1) * SPAN, :], self.q_masked[head, queries, :])
            upper = raw[:BLOCK] + self.bias[2 * j:2 * j + 1, queries]
            lower = raw[BLOCK:] + self.bias[2 * j + 1:2 * j + 2, queries]
            kept = jnp.concatenate((upper, lower), axis=0)
            return kept + self.corner[...] if j == tile else kept

        top = [jnp.full((8, SPAN), -3e30, F32) for head in range(2)]
        for j in range(tile + 1):
            for head in range(2):
                top[head] = jnp.maximum(top[head], jnp.max(score(j, head).reshape(SPAN // 8, 8, SPAN), axis=0))
        top = [jnp.max(each, axis=0, keepdims=True) for each in top]
        mix = [0.0, 0.0]
        for j in range(tile + 1):
            for head in range(2):
                weight = jnp.exp(score(j, head) - top[head]).astype(BF)
                self.weights[base + j, head] = weight
                mix[head] = mix[head] + dot(self.value_t[head, :, j * SPAN:(j + 1) * SPAN], weight)
        halves = []
        for head in range(2):
            inverse = 1.0 / mix[head][HEAD:HEAD + 8, :]
            self.inverse[head, :, queries] = inverse
            halves.append(mix[head][:HEAD, :] * inverse[0:1])
        attended_t = jnp.concatenate(halves, axis=0)
        self.attended_t[:, queries] = attended_t
        self.attended[queries, :] = attended_t.T.astype(BF)

    def cross_keys(self):
        made = dot(self.source_all[...], self.w_ckv).astype(BF)
        lane = iota((2 * ENC, 128), 1)
        row = iota((2 * ENC, 128), 0)
        own = (lane < HEAD) == (row < ENC)
        for pair in range(4):
            for box, start in ((self.cross_k, 0), (self.cross_v, D)):
                part = made[:, start + 128 * pair:start + 128 * pair + 128].astype(F32)
                box[pair] = jnp.where(own, jnp.concatenate((part, part), axis=0), 0.0).astype(BF)

    def middle(self, chunk):
        rows = span(chunk)
        y1 = self.tokens[rows, :].astype(F32) + dot(self.gathered[rows, :], self.w_o)
        self.y1[rows, :] = y1
        unit, root = unit_rows(y1)
        h2 = (unit * (1.0 + self.mod[0:1, 3 * D:4 * D]) + self.mod[0:1, 2 * D:3 * D]).astype(BF)
        self.h2[rows, :] = h2
        query = (dot(h2, self.w_cq).astype(BF).astype(F32) * HEAD ** (-0.5)).astype(BF)
        self.cross_q[rows, :] = query
        lane = iota((SPAN, 128), 1)
        same = ((iota((128, 128), 0) < ENC) == (iota((128, 128), 1) < ENC)).astype(BF)
        out = []
        for pair in range(4):
            raw = dot_nt(query[:, 128 * pair:128 * pair + 128], self.cross_k[pair])
            left = jnp.max(jnp.where(lane < ENC, raw, -3e38), axis=-1, keepdims=True)
            right = jnp.max(jnp.where(lane >= ENC, raw, -3e38), axis=-1, keepdims=True)
            weight = jnp.exp(raw - jnp.where(lane < ENC, left, right))
            weight = weight / dot(weight.astype(BF), same)
            self.cross_p[pair, rows, :] = weight.astype(BF)
            out.append(dot(weight.astype(BF), self.cross_v[pair]))
        cross = jnp.concatenate(out, axis=1).astype(BF)
        self.cross_out[rows, :] = cross
        y2 = y1 + dot(cross, self.w_co)
        self.y2[rows, :] = y2
        unit, root = unit_rows(y2)
        self.h3[rows, :] = (unit * (1.0 + self.mod[0:1, 5 * D:6 * D]) + self.mod[0:1, 4 * D:5 * D]).astype(BF)

    def hidden(self, chunk):
        units = span(chunk)
        u = dot(self.h3[...], self.w_in(units))
        dg = dot_nt(self.cotangent[...], self.w_out[units, :])
        square = u * u
        slope = 0.7978845608028654
        bend = jnp.tanh(u * (slope + slope * 0.044715 * square))
        half = 0.5 + 0.5 * bend
        self.act[:, units] = (u * half).astype(BF)
        turn = half + 0.5 * u * (1.0 - bend * bend) * (slope + 3.0 * slope * 0.044715 * square)
        self.d_hidden[:, units] = (dg * turn).astype(BF)
        self.grad_out(units, dot_tn(self.act[:, units], self.cotangent[...]).astype(BF))
        self.grad_in(units, dot_tn(self.h3[...], self.d_hidden[:, units]).astype(BF))

    def finish_forward(self, chunk):
        rows = span(chunk)
        self.mixed[rows, :] = (self.y2[rows, :] + dot(self.act[rows, :], self.w_out[...])).astype(BF)

    def sums(self, piece, shift, scale):
        self.mod_grad[0:1, 2 * piece * D:(2 * piece + 1) * D] += jnp.sum(shift, axis=0, keepdims=True)
        self.mod_grad[0:1, (2 * piece + 1) * D:(2 * piece + 2) * D] += jnp.sum(scale, axis=0, keepdims=True)

    def back_three(self, chunk):
        rows = span(chunk)
        dh3 = dot_nt(self.d_hidden[rows, :], self.w_in(slice(None)))
        unit, root = unit_rows(self.y2[rows, :])
        self.sums(2, dh3, dh3 * unit)
        dy2 = self.cotangent[rows, :].astype(F32) + norm_back(dh3, unit, root, self.mod[0:1, 5 * D:6 * D])
        self.dy[rows, :] = dy2
        self.db[rows, :] = dy2.astype(BF)

    def back_cross(self, chunk):
        rows = span(chunk)
        dca = dot_nt(self.db[rows, :], self.w_co).astype(BF)
        lane = iota((SPAN, 128), 1)
        row = iota((128, 128), 0)
        own = (row < ENC) == (iota((128, 128), 1) < HEAD)
        parts = []
        for pair in range(4):
            lanes = slice(128 * pair, 128 * pair + 128)
            low_weight = self.cross_p[pair, rows, :]
            weight = low_weight.astype(F32)
            dc = dot_nt(dca[:, lanes], self.cross_v[pair])
            both_ = weight * dc
            left = jnp.sum(jnp.where(lane < ENC, both_, 0.0), axis=-1, keepdims=True)
            right = jnp.sum(jnp.where(lane >= ENC, both_, 0.0), axis=-1, keepdims=True)
            ds = (weight * (dc - jnp.where(lane < ENC, left, right))).astype(BF)
            parts.append((dot(ds, self.cross_k[pair]) * HEAD ** (-0.5)).astype(BF))
            dk = jnp.where(own, dot_tn(ds, self.cross_q[rows, lanes]), 0.0)
            dv = jnp.where(own, dot_tn(low_weight, dca[:, lanes]), 0.0)
            self.d_cross[:, lanes] += dk[:ENC] + dk[ENC:]
            self.d_cross[:, 128 * pair + D:128 * pair + D + 128] += dv[:ENC] + dv[ENC:]
        dcq = jnp.concatenate(parts, axis=1)
        self.dcq[rows, :] = dcq
        dh2 = dot_nt(dcq, self.w_cq)
        unit, root = unit_rows(self.y1[rows, :])
        self.sums(1, dh2, dh2 * unit)
        dy1 = self.dy[rows, :] + norm_back(dh2, unit, root, self.mod[0:1, 3 * D:4 * D])
        self.dy[rows, :] = dy1
        low_dy1 = dy1.astype(BF)
        self.db1[rows, :] = low_dy1
        self.d_attn[rows, :] = dot_nt(low_dy1, self.w_o).astype(BF)

    def attend_back(self, tile):
        queries = slice(tile * SPAN, (tile + 1) * SPAN)
        base = tile * (tile + 1) // 2
        d_att_t = self.d_att_all[queries, :].astype(F32).T
        scaled = [d_att_t[HEAD * h:HEAD * h + HEAD] * self.inverse[h, 0:1, queries] for h in range(2)]
        delta = [
            jnp.sum(scaled[h] * self.attended_t[HEAD * h:HEAD * h + HEAD, queries], axis=0, keepdims=True)
            for h in range(2)
        ]
        flat = jnp.concatenate(scaled, axis=0).T
        lane = iota((SPAN, 128), 1)
        masked = [jnp.where((lane < HEAD) == (h == 0), flat, 0.0).astype(BF) for h in range(2)]
        dq_t = [0.0, 0.0]
        for j in range(tile + 1):
            keys = slice(j * SPAN, (j + 1) * SPAN)
            dk = dv = 0.0
            for head in range(2):
                dp = dot_nt(self.value[keys, :], masked[head])
                weight = self.weights[base + j, head]
                ds = (weight.astype(F32) * (dp - delta[head])).astype(BF)
                dk = dk + dot(ds, self.q_masked[head, queries, :])
                dv = dv + dot(weight, masked[head])
                dq_t[head] = dq_t[head] + dot(self.key_t[HEAD * head:HEAD * head + HEAD, keys], ds)
            self.dk[keys, :] += dk
            self.dv[keys, :] += dv
        self.d_pair[queries, 0:128] = (jnp.concatenate(dq_t, axis=0) * HEAD ** (-0.5)).T.astype(BF)
        self.d_pair[queries, 128:256] = self.dk[queries, :].astype(BF)
        self.d_pair[queries, 256:384] = self.dv[queries, :].astype(BF)
        self.dh1_part[queries, :] = dot_nt(self.d_pair[queries, :], self.w_pair[...]).astype(BF)


VMEM = pl.BlockSpec(memory_space=pltpu.VMEM)
SMEM = pl.BlockSpec(memory_space=pltpu.SMEM)
CROSS = 5 * D


class Weights(Layer):
    w_o = property(lambda self: self.pack[:, 0:D])
    w_cq = property(lambda self: self.pack[:, D:2 * D])
    w_ckv = property(lambda self: self.pack[:, 2 * D:4 * D])
    w_co = property(lambda self: self.pack[:, 4 * D:CROSS])

    def w_in(self, units):
        return self.pack.at[:, CROSS:CROSS + FF][:, units]

    def grad_in(self, units, value):
        self.grad_pack.at[:, CROSS:CROSS + FF][:, units] = value

    def grad_out(self, units, value):
        self.grad_w_out[units, :] = value

    def grad_into(self, start, left, right):
        for step in range(right.shape[1] // SPAN):
            columns = slice(start + step * SPAN, start + (step + 1) * SPAN)
            self.grad_pack[:, columns] = dot_tn(left[...], right[:, step * SPAN:(step + 1) * SPAN]).astype(BF)


ANY = pl.BlockSpec(memory_space=pl.ANY)
INS = ("i_tokens", "i_cotangent", "i_encoded", "parents", "timestep", "i_qkv", "i_o", "i_cq", "i_ckv", "i_co", "i_in", "i_out", "i_aux")
OUTS = ("mixed", "grad_tokens", "g_encoded", "g_qkv", "g_o", "g_cq", "g_ckv", "g_co", "g_in", "g_out", "g_table")


def layer_scratch(rows, tree, blocks, levels, wide):
    tiles = tree // SPAN
    count = levels * 8
    each = D // count
    plain = lambda *shape: pltpu.VMEM(shape, F32)
    short = lambda *shape: pltpu.VMEM(shape, BF)
    dma = pltpu.SemaphoreType.DMA
    scratch = dict(
        tokens=short(rows, D), cotangent=short(rows, D), qkv_own=short(each, 3 * D), mixed=short(rows, D), grad_tokens=plain(rows, D),
        g_encoded=plain(ENC // 4, D), g_qkv=plain(each, 3 * D), g_o=plain(each, D), g_cq=plain(each, D), g_ckv=plain(each, 2 * D),
        g_co=plain(each, D), g_in=plain(each, FF), g_out=plain(FF // count, D), g_table=plain(STEPS, wide),
        in_sem=dma((11,)), out_sem=dma((11,)),
        pair_own=short(each, 3 * D), w_pair=short(D, 384), pack=short(D, CROSS + FF), w_out=short(FF, D),
        aux=short(count * 64, 128), tokens_all=short(tree, D), source_all=short(ENC, D),
        mod=plain(8, 6 * D), mod_grad=plain(8, 6 * D), bias=plain(blocks, tree), corner=plain(SPAN, SPAN),
        h1=short(tree, D), q_masked=short(2, tree, 128), key=short(tree, 128), value=short(tree, 128),
        key_t=short(128, tree), value_t=short(2, HEAD + 16, tree),
        weights=short(tiles * (tiles + 1) // 2, 2, SPAN, SPAN), inverse=plain(2, 8, tree),
        attended_t=plain(128, tree), attended=short(tree, 128), gathered=short(rows, D),
        cross_k=short(4, 2 * ENC, 128), cross_v=short(4, 2 * ENC, 128), cross_q=short(rows, D), cross_p=short(4, rows, 128),
        cross_out=short(rows, D), y1=plain(rows, D), h2=short(rows, D), h3=short(rows, D),
        act=short(rows, FF), d_hidden=short(rows, FF),
        d_cross=plain(ENC, 2 * D), dcq=short(rows, D), d_att_all=short(tree, 128),
        dk=plain(tree, 128), dv=plain(tree, 128),
        d_pair=short(tree, 384), relay=short(2, SPAN, D), dh1_box=short(2, 2, SPAN, D),
        grad_pack=short(D, CROSS + FF), grad_w_out=short(FF, D), grad_pair=short(D, 384), source_part=plain(ENC, D),
        payload=plain(count * 8, 128), table_box=plain(count * 8, 128), table_rows=plain(levels * 16, 128), settle_box=plain(ENC, D),
        a_send=dma((tiles,)), a_recv=dma((tiles,)), d_send=dma((4,)), d_recv=dma((4,)),
        h_send=dma((tiles,)), h_relay=dma((2,)), h_recv=dma((4,)),
        send=dma((4, Gather.sends(levels))), recv=dma((4, count)),
        pair_send=dma((GatherPair.sends(levels),)), pair_recv=dma((4 + 2 * levels,)),
        share_send=dma((6,)), share_recv=dma((8,)), spread_send=dma((3,)), spread_recv=dma((4,)),
        r_send=dma((3, Reduce.slots(levels))), r_recv=dma((3, Reduce.slots(levels))),
        rp_send=dma((ReducePair.slots(levels),)), rp_recv=dma((ReducePair.slots(levels),)),
        settle_send=dma((4,)), settle_recv=dma((4,)), t_send=dma((4 + 2 * levels,)), t_recv=dma((4 + 2 * levels,)),
    )
    for name, height, width, line_last in (("box_out", FF // count, D, True), ("box_in", each, FF, True), ("box_cross", each, CROSS, False)):
        for n, box in enumerate(Reduce.boxes(levels, height, width, BF, line_last)):
            scratch[f"{name}{n}"] = box
    for n, box in enumerate(ReducePair.boxes(levels, each, 384, BF)):
        scratch[f"box_pair{n}"] = box
    return scratch


def layer_kernel(levels, wide, names, refs):
    place = Place(levels)
    refs = dict(zip(names, refs))
    refs["y2"] = refs["dy"] = refs["grad_tokens"]
    refs["db"] = refs["db1"] = refs["h3"]
    refs["d_attn"] = refs["cross_q"]
    refs["dh1_part"] = refs["tokens_all"]
    w = Weights(place, refs)
    blk, leaf = place.blk, place.leaf
    peers = (place.near, place.far, place.opposite)
    rows = w.tokens.shape[0]
    tree = w.tokens_all.shape[0]
    tiles = tree // SPAN
    halves = rows // SPAN
    blocks = tree // BLOCK
    count = levels * 8
    each = D // count
    index = leaf * 4 + blk
    own_lanes = pl.ds(pl.multiple_of(blk * 128, 128), 128)

    mine = rows_of(index, each)
    moves = [
        (w.i_tokens, w.tokens_all.at[rows_of(blk, rows), :]), (w.i_qkv, w.qkv_own), (w.i_aux, w.aux.at[rows_of(index, 64), :]),
        (w.i_encoded, w.source_all.at[rows_of(blk, w.i_encoded.shape[0]), :]),
        (w.i_out, w.w_out.at[rows_of(index, w.i_out.shape[0]), :]),
    ]
    start = 0
    for name in ("i_o", "i_cq", "i_ckv", "i_co", "i_in"):
        width = refs[name].shape[1]
        moves.append((refs[name], w.pack.at[mine, start:start + width]))
        start += width
    copies = [pltpu.make_async_copy(src, dst, w.in_sem.at[n]) for n, (src, dst) in enumerate(moves)]
    for copy in copies:
        copy.start()
    place.greet()
    for copy in copies:
        copy.wait()
    late = pltpu.make_async_copy(w.i_cotangent, w.cotangent, w.in_sem.at[10])
    late.start()
    w.tokens[...] = w.tokens_all[rows_of(blk, rows), :]
    for pair in range(4):
        for third in range(3):
            w.pair_own[:, 384 * pair + 128 * third:384 * pair + 128 * third + 128] = (
                w.qkv_own[:, D * third + 128 * pair:D * third + 128 * pair + 128])
    w.w_pair[mine, :] = w.pair_own[:, pl.ds(pl.multiple_of(blk * 384, 128), 384)]
    given = []

    def give(*outs):
        for name in outs:
            copy = pltpu.make_async_copy(refs[name], refs["o_" + name], w.out_sem.at[OUTS.index(name)])
            copy.start()
            given.append(copy)

    weave = GatherPair(place, w.pair_own, w.w_pair, w.pair_send, w.pair_recv)
    table = Gather(place, w.aux, 64, slice(None), w.send.at[0], w.recv.at[0])
    share = Share(place, w.tokens_all, rows, w.share_send, w.share_recv)
    spread = Spread(place, w.source_all, w.i_encoded.shape[0], w.spread_send, w.spread_recv)
    loads = [
        Gather(place, w.pack, each, slice(0, CROSS), w.send.at[1], w.recv.at[1]),
        Gather(place, w.pack, each, slice(CROSS, CROSS + FF), w.send.at[2], w.recv.at[2]),
        Gather(place, w.w_out, FF // count, slice(None), w.send.at[3], w.recv.at[3]),
    ]
    weave_steps, table_steps, share_steps = weave.steps(), table.steps(), share.steps()
    load_steps = [load.steps() for load in loads]

    def ticks(steps, number=1):
        for turn in range(number):
            for step in steps:
                next(step, None)

    ticks([weave_steps, table_steps, share_steps])
    spread.start()
    w.mod_grad[...] = jnp.zeros_like(w.mod_grad)
    w.d_cross[...] = jnp.zeros_like(w.d_cross)
    w.dk[...] = jnp.zeros_like(w.dk)
    w.dv[...] = jnp.zeros_like(w.dv)
    block_bias(w.parents, w.bias, blocks)
    row, column = iota((SPAN, SPAN), 0), iota((SPAN, SPAN), 1)
    w.corner[...] = jnp.where(((row < BLOCK) == (column < BLOCK)) & (row > column), -1e30, 0.0)
    ticks([weave_steps, table_steps])
    ticks([weave_steps, table_steps])
    ticks(load_steps)
    ticks([weave_steps, table_steps, share_steps])
    ticks([weave_steps, table_steps])
    ticks(load_steps)
    ticks([weave_steps, table_steps], 5)
    read_modulation(w.aux, w.timestep[0], w.mod, wide)

    def project(block):
        for half in range(halves):
            w.project(block * halves + half)

    project(blk)
    ticks([share_steps])
    project(place.near)
    project(place.far)
    ticks([share_steps])
    ticks(load_steps)
    project(place.opposite)

    def attended_copy(tile, src):
        there = w.gathered.at[span(tile % halves), pl.ds(pl.multiple_of(src * 128, 128), 128)]
        return remote(w.attended.at[span(tile), :], there, w.a_send.at[tile], w.a_recv.at[src * halves + tile % halves], leaf, tile // halves)

    for tile in range(tiles):
        w.attend(tile)
        away = tile // halves != blk
        pl.when(away)(lambda tile=tile: attended_copy(tile, blk).start())

        def keep(tile=tile):
            w.gathered[span(tile % halves), own_lanes] = w.attended[span(tile), :]

        pl.when(jnp.logical_not(away))(keep)
        if tile == tiles - 2:
            ticks(load_steps)
    ticks(load_steps[:1])
    spread.arrive()
    ticks(load_steps[:1])
    w.cross_keys()
    for peer in peers:
        for half in range(halves):
            attended_copy(blk * halves + half, peer).wait_recv()
    loop(halves, w.middle)
    late.wait()
    ticks(load_steps, 2)
    loop(FF // SPAN, w.hidden)
    for job in loads + [weave, table, share, spread]:
        job.finish()

    def boxes(name, number=4):
        return [refs[f"{name}{n}"] for n in range(number)]

    def store_out(there, value):
        w.g_out[there, :] = value

    def store_in(there, value):
        w.g_in[there, :] = value

    def store_cross(there, value):
        w.g_o[there, :] = value[:, 0:D]
        w.g_cq[there, :] = value[:, D:2 * D]
        w.g_ckv[there, :] = value[:, 2 * D:4 * D]
        w.g_co[there, :] = value[:, 4 * D:5 * D]

    sums = [
        Reduce(place, w.grad_w_out, FF // count, slice(None), store_out, boxes("box_out"), w.r_send.at[0], w.r_recv.at[0], True),
        Reduce(place, w.grad_pack, each, slice(CROSS, CROSS + FF), store_in, boxes("box_in"), w.r_send.at[1], w.r_recv.at[1], True),
    ]
    sum_steps = [job.steps() for job in sums]
    ticks(sum_steps)
    loop(halves, w.finish_forward)
    give("mixed")
    ticks(sum_steps)
    loop(halves, w.back_three)
    w.grad_into(4 * D, w.cross_out, w.db)
    loop(halves, w.back_cross)

    def da_copy(src, to):
        return remote(w.d_attn.at[:, pl.ds(pl.multiple_of(to * 128, 128), 128)], w.d_att_all.at[rows_of(src, rows), :],
                      w.d_send.at[to], w.d_recv.at[src], leaf, to)

    for peer in peers:
        da_copy(blk, peer).start()
    w.d_att_all[rows_of(blk, rows), :] = w.d_attn[:, own_lanes]
    w.grad_into(0, w.gathered, w.db1)
    w.grad_into(D, w.h2, w.dcq)
    low_cross = w.d_cross[...].astype(BF)
    for step in range(2 * D // SPAN):
        columns = slice(2 * D + step * SPAN, 2 * D + (step + 1) * SPAN)
        w.grad_pack[:, columns] = dot_tn(w.source_all[...], low_cross[:, step * SPAN:(step + 1) * SPAN]).astype(BF)
    w.source_part[...] = dot_nt(low_cross, w.w_ckv)
    sums.append(Reduce(place, w.grad_pack, each, slice(0, CROSS), store_cross, boxes("box_cross"), w.r_send.at[2], w.r_recv.at[2], False))
    settle = Settle(place, w.source_part, w.g_encoded, w.settle_box, w.settle_send, w.settle_recv)
    later_steps = [sums[2].steps(), settle.steps()]
    ticks(later_steps)
    for peer in peers:
        da_copy(peer, peer).wait_recv()

    tree_sum = TreeReduce(place, w.dh1_part, w.relay, w.dh1_box, w.h_send, w.h_relay, w.h_recv)
    plan = [(tiles - 1, sum_steps), (tiles - 1, later_steps), (tiles - 2, sum_steps), (tiles - 3, later_steps),
            (tiles - 4, sum_steps), (tiles - 5, later_steps)]
    for tile in range(tiles - 1, -1, -1):
        w.attend_back(tile)
        tree_sum.offer(tile)
        if tile + 3 < tiles:
            tree_sum.forward(tile + 3)
        for when, steps in plan:
            if when == tile:
                ticks(steps)
    for tile in (2, 1, 0):
        tree_sum.forward(tile)

    def pair_grad(step):
        w.grad_pair[span(step), :] = dot_tn(w.h1[:, span(step)], w.d_pair[...]).astype(BF)

    loop(D // SPAN, pair_grad)
    pair_sum = ReducePair(place, w.grad_pair, w.g_qkv, boxes("box_pair", 3), w.rp_send, w.rp_recv)
    pair_steps = pair_sum.steps()
    ticks([pair_steps])
    ticks(sum_steps + later_steps, 10)
    give("g_encoded", "g_o", "g_cq", "g_ckv", "g_co", "g_in", "g_out")
    ticks([pair_steps])

    def last(half):
        tree_sum.arrive(half)
        here, own = span(half), span(blk * halves + half)
        dh1 = w.dh1_part[own, :].astype(F32) + w.dh1_box[half, 0].astype(F32) + w.dh1_box[half, 1].astype(F32)
        unit, root = unit_rows(w.tokens[here, :].astype(F32))
        w.sums(0, dh1, dh1 * unit)
        w.grad_tokens[here, :] = w.dy[here, :] + norm_back(dh1, unit, root, w.mod[0:1, D:2 * D])

    for half in range(halves):
        last(half)
    give("grad_tokens")
    w.payload[...] = table_payload(w.mod_grad[0:1, :], wide, count)
    table_sum = TableSum(place, w.payload, w.table_box, w.table_rows, w.t_send, w.t_recv)
    table_steps = table_sum.steps()
    ticks([table_steps, pair_steps], 10)
    give("g_qkv")

    leaves = levels * 2
    chosen = (iota((leaves, count * 64), 1) == iota((leaves, count * 64), 0) * 256 + STEPS).astype(BF)
    steps_all = dot(chosen, w.aux[...])
    line = iota((64, 128), 0).astype(F32)
    grad_table = jnp.zeros((64, 128), F32)
    for tree_at in range(leaves):
        grad_table = grad_table + jnp.where(line == steps_all[tree_at:tree_at + 1, :], w.table_rows[8 * tree_at:8 * tree_at + 1, :], 0.0)
    w.g_table[...] = grad_table[:STEPS, :wide]
    give("g_table")

    for tile in range(tiles):
        pl.when(tile // halves != blk)(lambda tile=tile: attended_copy(tile, blk).wait_send())
        tree_sum.finish(tile)
    for peer in peers:
        da_copy(blk, peer).wait_send()
    for job in sums + [settle, pair_sum, table_sum]:
        job.finish()
    for copy in given:
        copy.wait()


def copy_kernel(count, refs):
    ins, outs, held, sems = refs[:count], refs[count:2 * count], refs[2 * count:3 * count], refs[3 * count]
    inward = [pltpu.make_async_copy(ins[n], held[n], sems.at[0, n]) for n in range(count)]
    outward = [pltpu.make_async_copy(held[n], outs[n], sems.at[1, n]) for n in range(count)]
    for copy in inward:
        copy.start()
    for copy, then in zip(inward, outward):
        copy.wait()
        then.start()
    for copy in outward:
        copy.wait()


def copy_all(arrays):
    return pl.pallas_call(
        lambda *refs: copy_kernel(len(arrays), refs),
        out_shape=[jax.ShapeDtypeStruct(array.shape, array.dtype) for array in arrays],
        in_specs=[ANY] * len(arrays),
        out_specs=[ANY] * len(arrays),
        scratch_shapes=[pltpu.VMEM(array.shape, array.dtype) for array in arrays] + [pltpu.SemaphoreType.DMA((2, len(arrays)))],
    )(*arrays)


def per_device(tokens, cotangent, encoded, parents, timestep, w_qkv, w_o, w_cq, w_ckv, w_co, w_in, w_out, mod_table):
    levels = lax.axis_size("leaf") // 2
    rows, wide = tokens.shape[0], mod_table.shape[1]
    blocks = parents.shape[1]
    tree = blocks * BLOCK
    aux = jnp.concatenate(
        (
            jnp.pad(mod_table, ((0, 0), (0, 128 - wide))),
            jnp.full((64 - STEPS, 128), timestep[0], jnp.int32).astype(BF),
        ),
        axis=0,
    )
    ins = (tokens, cotangent, encoded, parents, timestep, w_qkv, w_o, w_cq, w_ckv, w_co, w_in, w_out, aux)
    scratch = layer_scratch(rows, tree, blocks, levels, wide)
    out = lambda like: jax.ShapeDtypeStruct(like.shape, F32)
    names = INS + tuple("o_" + name for name in OUTS) + tuple(scratch)
    return copy_all(pl.pallas_call(
        lambda *refs: layer_kernel(levels, wide, names, refs),
        out_shape=[jax.ShapeDtypeStruct((rows, D), BF), out(tokens), out(encoded)]
        + [out(weight) for weight in (w_qkv, w_o, w_cq, w_ckv, w_co, w_in, w_out, mod_table)],
        in_specs=[SMEM if name in ("parents", "timestep") else ANY for name in INS],
        out_specs=[ANY] * len(OUTS),
        scratch_shapes=list(scratch.values()),
        compiler_params=pltpu.CompilerParams(collective_id=0, has_side_effects=True, vmem_limit_bytes=(64 << 20) - (64 << 10)),
    )(*ins))


def solution(mesh):
    fits = mesh.shape["blk"] == 4 and mesh.shape["leaf"] == 8
    return jax.shard_map(
        per_device if fits else generic_device,
        mesh=mesh,
        in_specs=(
            P(("leaf", "blk"), None),
            P(("leaf", "blk"), None),
            P(("leaf", "blk"), None),
            P("leaf", None),
            P("leaf"),
            P(("leaf", "blk"), None),
            P(("leaf", "blk"), None),
            P(("leaf", "blk"), None),
            P(("leaf", "blk"), None),
            P(("leaf", "blk"), None),
            P(("leaf", "blk"), None),
            P(("leaf", "blk"), None),
            P(None, ("leaf", "blk")),
        ),
        out_specs=(
            P(("leaf", "blk"), None),
            P(("leaf", "blk"), None),
            P(("leaf", "blk"), None),
            P(("leaf", "blk"), None),
            P(("leaf", "blk"), None),
            P(("leaf", "blk"), None),
            P(("leaf", "blk"), None),
            P(("leaf", "blk"), None),
            P(("leaf", "blk"), None),
            P(("leaf", "blk"), None),
            P(None, ("leaf", "blk")),
        ),
        check_vma=False,
    )
```

```python
import functools

import jax
import jax.numpy as jnp
from jax import lax
from jax.experimental import pallas as pl
from jax.experimental.pallas import tpu as pltpu
from jax.sharding import PartitionSpec as P

D = 512
HEADS = 8
HEAD = 64
BLOCK = 128
FF = 2048
ENC = 64
STEPS = 50


PRECISE = lax.Precision.HIGHEST
MASKED = -1e30


def ancestors(parent_row):
    count = parent_row.shape[0]
    indices = jnp.arange(count, dtype=jnp.int32)
    reach_map = (indices[:, None] == indices[None, :]).astype(jnp.float32)
    reach_map = jnp.minimum(
        reach_map + (parent_row[:, None] == indices[None, :]).astype(jnp.float32), 1.0
    )
    for rounds in range(max(1, (count - 1).bit_length())):
        reach_map = jnp.minimum(jnp.dot(reach_map, reach_map, precision=PRECISE), 1.0)
    return reach_map


def normalize(values, shift, scaling):
    centred = values - jnp.mean(values, axis=-1, keepdims=True)
    spread = jnp.mean(centred * centred, axis=-1, keepdims=True)
    return centred * lax.rsqrt(spread + 1e-05) * (1.0 + scaling) + shift


def span_link(reach_rows, span):
    return lax.dynamic_slice_in_dim(reach_rows, span * 4, 4, 1)


def span_reached(reach_rows, span):
    return jnp.max(span_link(reach_rows, span)) > 0.5


def span_mask(reach_rows, first_block, span, row_count, width):
    query_index = jnp.arange(row_count, dtype=jnp.int32)
    key_index = jnp.arange(width, dtype=jnp.int32)
    query_block = first_block + query_index // BLOCK
    key_block = span * 4 + key_index // BLOCK
    link = span_link(reach_rows, span)
    link = jnp.repeat(jnp.repeat(link, BLOCK, axis=0), BLOCK, axis=1)
    same = query_block[:, None] == key_block[None, :]
    return (link > 0.5) & (
        jnp.logical_not(same) | (key_index[None, :] % BLOCK <= query_index[:, None] % BLOCK)
    )


def scores_of(queries, key_rows, allowed):
    raw = jnp.einsum(
        "qhd,khd->hqk", queries, key_rows, preferred_element_type=jnp.float32
    ) * HEAD ** (-0.5)
    return jnp.where(allowed[None], raw, MASKED)


def split_spans(keys, values):
    width = 4 * BLOCK
    count = keys.shape[0] // width
    return (
        jnp.arange(count, dtype=jnp.int32),
        keys.reshape(count, width, HEADS, HEAD),
        values.reshape(count, width, HEADS, HEAD),
    )


def tree_forward_attention(queries, keys, values, reach_rows, first_block):
    row_count = queries.shape[0]
    width = 4 * BLOCK
    spans, key_spans, value_spans = split_spans(keys, values)

    def stats(carry, item):
        span, key_rows = item

        def stats_visit(state):
            top, total = state
            allowed = span_mask(reach_rows, first_block, span, row_count, width)
            score = scores_of(queries, key_rows, allowed)
            new_top = jnp.maximum(top, jnp.max(score, axis=-1))
            weight = jnp.where(allowed[None], jnp.exp(score - new_top[..., None]), 0.0)
            return (new_top, total * jnp.exp(top - new_top) + jnp.sum(weight, axis=-1))

        return (
            lax.cond(span_reached(reach_rows, span), stats_visit, lambda state: state, carry),
            None,
        )

    start = (
        jnp.full((HEADS, row_count), MASKED, jnp.float32),
        jnp.zeros((HEADS, row_count), jnp.float32),
    )
    (top, total), unused = lax.scan(stats, start, (spans, key_spans))
    log_total = top + jnp.log(total)

    def collect(accum, item):
        span, key_rows, value_rows = item

        def collect_visit(current):
            allowed = span_mask(reach_rows, first_block, span, row_count, width)
            weight = jnp.where(
                allowed[None],
                jnp.exp(scores_of(queries, key_rows, allowed) - log_total[..., None]),
                0.0,
            )
            return current + jnp.einsum(
                "hqk,khd->qhd",
                weight.astype(jnp.bfloat16),
                value_rows,
                preferred_element_type=jnp.float32,
            )

        return (
            lax.cond(span_reached(reach_rows, span), collect_visit, lambda current: current, accum),
            None,
        )

    attended, unused = lax.scan(
        collect, jnp.zeros((row_count, HEADS, HEAD), jnp.float32), (spans, key_spans, value_spans)
    )
    return (attended, log_total)


def tree_backward_attention(queries, keys, values, reach_rows, first_block, log_total, grad_attn):
    row_count = queries.shape[0]
    width = 4 * BLOCK
    spans, key_spans, value_spans = split_spans(keys, values)

    def probs_of(span, key_rows):
        allowed = span_mask(reach_rows, first_block, span, row_count, width)
        return jnp.where(
            allowed[None],
            jnp.exp(scores_of(queries, key_rows, allowed) - log_total[..., None]),
            0.0,
        )

    def inner_pass(total, item):
        span, key_rows, value_rows = item

        def inner_visit(current):
            weight = probs_of(span, key_rows)
            d_weight = jnp.einsum(
                "qhd,khd->hqk", grad_attn, value_rows, preferred_element_type=jnp.float32
            )
            return current + jnp.sum(weight * d_weight, axis=-1)

        return (
            lax.cond(span_reached(reach_rows, span), inner_visit, lambda current: current, total),
            None,
        )

    delta, unused = lax.scan(
        inner_pass, jnp.zeros((HEADS, row_count), jnp.float32), (spans, key_spans, value_spans)
    )

    def grad_pass(d_queries, item):
        span, key_rows, value_rows = item

        def grad_visit(current):
            weight = probs_of(span, key_rows)
            d_weight = jnp.einsum(
                "qhd,khd->hqk", grad_attn, value_rows, preferred_element_type=jnp.float32
            )
            d_score = (weight * (d_weight - delta[..., None])).astype(jnp.bfloat16)
            current = current + jnp.einsum(
                "hqk,khd->qhd", d_score, key_rows, preferred_element_type=jnp.float32
            )
            d_keys = jnp.einsum(
                "hqk,qhd->khd", d_score, queries, preferred_element_type=jnp.float32
            ) * HEAD ** (-0.5)
            d_values = jnp.einsum(
                "hqk,qhd->khd",
                weight.astype(jnp.bfloat16),
                grad_attn,
                preferred_element_type=jnp.float32,
            )
            return (
                current,
                jnp.concatenate((d_keys.reshape(width, D), d_values.reshape(width, D)), axis=1),
            )

        def skip(current):
            return (current, jnp.zeros((width, 2 * D), jnp.float32))

        return lax.cond(span_reached(reach_rows, span), grad_visit, skip, d_queries)

    d_queries, terms = lax.scan(
        grad_pass, jnp.zeros((row_count, HEADS, HEAD), jnp.float32), (spans, key_spans, value_spans)
    )
    return (d_queries * HEAD ** (-0.5), terms.reshape(-1, 2 * D))


def generic_device(
    tokens,
    cotangent,
    encoded,
    parents,
    timestep,
    w_qkv,
    w_o,
    w_cq,
    w_ckv,
    w_co,
    w_in,
    w_out,
    mod_table,
):
    gathered = (
        lax.all_gather(w_qkv, ("leaf", "blk"), axis=0, tiled=True),
        lax.all_gather(w_o, ("leaf", "blk"), axis=0, tiled=True),
        lax.all_gather(w_cq, ("leaf", "blk"), axis=0, tiled=True),
        lax.all_gather(w_ckv, ("leaf", "blk"), axis=0, tiled=True),
        lax.all_gather(w_co, ("leaf", "blk"), axis=0, tiled=True),
        lax.all_gather(w_in, ("leaf", "blk"), axis=0, tiled=True),
        lax.all_gather(w_out, ("leaf", "blk"), axis=0, tiled=True),
        lax.all_gather(mod_table, ("leaf", "blk"), axis=1, tiled=True),
    )
    g_qkv, g_o, g_cq, g_ckv, g_co, g_in, g_out, g_table = gathered
    select = (jnp.arange(STEPS, dtype=jnp.int32) == timestep[0]).astype(jnp.float32)
    modulate = jnp.dot(
        select.astype(jnp.bfloat16)[None, :], g_table, preferred_element_type=jnp.float32
    )[0]
    pieces = [modulate[i * D : (i + 1) * D] for i in range(6)]
    inputs = tokens.astype(jnp.float32)
    row_count = tokens.shape[0]
    local_blocks = row_count // BLOCK
    first_block = lax.axis_index("blk") * local_blocks
    reach_map = ancestors(parents[0])
    reach_rows = lax.dynamic_slice_in_dim(reach_map, first_block, local_blocks, 0)
    scaling = HEAD ** (-0.5)
    normed_one, pull_one = jax.vjp(normalize, inputs, pieces[0], pieces[1])
    h_first = normed_one.astype(jnp.bfloat16)
    projected = jnp.dot(h_first, g_qkv, preferred_element_type=jnp.float32).astype(jnp.bfloat16)
    queries = projected[:, :D].reshape(row_count, HEADS, HEAD)
    keys, values = (
        lax.all_gather(projected[:, D : 2 * D], "blk", axis=0, tiled=True),
        lax.all_gather(projected[:, 2 * D :], "blk", axis=0, tiled=True),
    )
    attended, log_total = tree_forward_attention(queries, keys, values, reach_rows, first_block)
    attn_low = attended.reshape(row_count, D).astype(jnp.bfloat16)
    middle_one = inputs + jnp.dot(attn_low, g_o, preferred_element_type=jnp.float32)
    normed_two, pull_two = jax.vjp(normalize, middle_one, pieces[2], pieces[3])
    h_second = normed_two.astype(jnp.bfloat16)
    cross_q = (
        jnp.dot(h_second, g_cq, preferred_element_type=jnp.float32)
        .astype(jnp.bfloat16)
        .reshape(row_count, HEADS, HEAD)
    )
    source_local = jnp.dot(encoded, g_ckv, preferred_element_type=jnp.float32).astype(jnp.bfloat16)
    source_all = lax.all_gather(source_local, "blk", axis=0, tiled=True)
    cross_k = source_all[:, :D].reshape(-1, HEADS, HEAD)
    cross_v = source_all[:, D:].reshape(-1, HEADS, HEAD)
    cross_raw = (
        jnp.einsum("qhd,khd->hqk", cross_q, cross_k, preferred_element_type=jnp.float32) * scaling
    )
    cross_prob = jax.nn.softmax(cross_raw, axis=-1)
    cross_low = cross_prob.astype(jnp.bfloat16)
    cross_out = (
        jnp.einsum("hqk,khd->qhd", cross_low, cross_v, preferred_element_type=jnp.float32)
        .reshape(row_count, D)
        .astype(jnp.bfloat16)
    )
    middle_two = middle_one + jnp.dot(cross_out, g_co, preferred_element_type=jnp.float32)
    normed_three, pull_three = jax.vjp(normalize, middle_two, pieces[4], pieces[5])
    h_third = normed_three.astype(jnp.bfloat16)
    hidden_pre = jnp.dot(h_third, g_in, preferred_element_type=jnp.float32)
    activated, pull_gelu = jax.vjp(
        lambda values_in: jax.nn.gelu(values_in, approximate=True), hidden_pre
    )
    act_low = activated.astype(jnp.bfloat16)
    result = middle_two + jnp.dot(act_low, g_out, preferred_element_type=jnp.float32)
    mixed_out = result.astype(jnp.bfloat16)
    back_weights = (
        lax.all_gather(w_qkv, ("leaf", "blk"), axis=0, tiled=True),
        lax.all_gather(w_o, ("leaf", "blk"), axis=0, tiled=True),
        lax.all_gather(w_cq, ("leaf", "blk"), axis=0, tiled=True),
        lax.all_gather(w_ckv, ("leaf", "blk"), axis=0, tiled=True),
        lax.all_gather(w_co, ("leaf", "blk"), axis=0, tiled=True),
        lax.all_gather(w_in, ("leaf", "blk"), axis=0, tiled=True),
        lax.all_gather(w_out, ("leaf", "blk"), axis=0, tiled=True),
        lax.all_gather(mod_table, ("leaf", "blk"), axis=1, tiled=True),
    )
    b_qkv, b_o, b_cq, b_ckv, b_co, b_in, b_out = back_weights[:7]
    d_act = jnp.dot(cotangent, b_out.T, preferred_element_type=jnp.float32)
    d_hidden = pull_gelu(d_act)[0].astype(jnp.bfloat16)
    grad_out_w = jnp.dot(act_low.T, cotangent, preferred_element_type=jnp.float32)
    grad_in_w = jnp.dot(h_third.T, d_hidden, preferred_element_type=jnp.float32)
    d_h_third = jnp.dot(d_hidden, b_in.T, preferred_element_type=jnp.float32)
    d_middle_part, d_shift_three, d_scale_three = pull_three(d_h_third)
    d_middle_two = cotangent.astype(jnp.float32) + d_middle_part
    d_branch_two = d_middle_two.astype(jnp.bfloat16)
    grad_co_w = jnp.dot(cross_out.T, d_branch_two, preferred_element_type=jnp.float32)
    d_cross_out = (
        jnp.dot(d_branch_two, b_co.T, preferred_element_type=jnp.float32)
        .astype(jnp.bfloat16)
        .reshape(row_count, HEADS, HEAD)
    )
    d_cross_prob = jnp.einsum(
        "qhd,khd->hqk", d_cross_out, cross_v, preferred_element_type=jnp.float32
    )
    d_cross_raw = (
        cross_prob * (d_cross_prob - jnp.sum(cross_prob * d_cross_prob, axis=-1, keepdims=True))
    ).astype(jnp.bfloat16)
    d_cross_q = (
        (
            jnp.einsum("hqk,khd->qhd", d_cross_raw, cross_k, preferred_element_type=jnp.float32)
            * scaling
        )
        .reshape(row_count, D)
        .astype(jnp.bfloat16)
    )
    d_cross_k = (
        jnp.einsum("hqk,qhd->khd", d_cross_raw, cross_q, preferred_element_type=jnp.float32)
        * scaling
    )
    d_cross_v = jnp.einsum(
        "hqk,qhd->khd", cross_low, d_cross_out, preferred_element_type=jnp.float32
    )
    source_terms = jnp.concatenate((d_cross_k.reshape(-1, D), d_cross_v.reshape(-1, D)), axis=1)
    d_source = lax.psum_scatter(
        source_terms.astype(jnp.bfloat16), "blk", scatter_dimension=0, tiled=True
    )
    grad_ckv_w = jnp.dot(encoded.T, d_source, preferred_element_type=jnp.float32)
    d_encoded = jnp.dot(d_source, b_ckv.T, preferred_element_type=jnp.float32)
    grad_cq_w = jnp.dot(h_second.T, d_cross_q, preferred_element_type=jnp.float32)
    d_h_second = jnp.dot(d_cross_q, b_cq.T, preferred_element_type=jnp.float32)
    d_middle_part, d_shift_two, d_scale_two = pull_two(d_h_second)
    d_middle_one = d_middle_two + d_middle_part
    d_branch_one = d_middle_one.astype(jnp.bfloat16)
    grad_o_w = jnp.dot(attn_low.T, d_branch_one, preferred_element_type=jnp.float32)
    d_attn = (
        jnp.dot(d_branch_one, b_o.T, preferred_element_type=jnp.float32)
        .astype(jnp.bfloat16)
        .reshape(row_count, HEADS, HEAD)
    )
    keys_back, values_back = (
        lax.all_gather(projected[:, D : 2 * D], "blk", axis=0, tiled=True),
        lax.all_gather(projected[:, 2 * D :], "blk", axis=0, tiled=True),
    )
    d_queries, key_terms = tree_backward_attention(
        queries, keys_back, values_back, reach_rows, first_block, log_total, d_attn
    )
    d_key_value = lax.psum_scatter(
        key_terms.astype(jnp.bfloat16), "blk", scatter_dimension=0, tiled=True
    ).astype(jnp.float32)
    d_projected = jnp.concatenate((d_queries.reshape(row_count, D), d_key_value), axis=1).astype(
        jnp.bfloat16
    )
    grad_qkv_w = jnp.dot(h_first.T, d_projected, preferred_element_type=jnp.float32)
    d_h_first = jnp.dot(d_projected, b_qkv.T, preferred_element_type=jnp.float32)
    d_input_part, d_shift_one, d_scale_one = pull_one(d_h_first)
    d_tokens = d_middle_one + d_input_part
    d_modulate = jnp.concatenate(
        (d_shift_one, d_scale_one, d_shift_two, d_scale_two, d_shift_three, d_scale_three)
    )
    grad_table_w = select[:, None] * d_modulate[None, :]
    gradients = (
        lax.psum_scatter(grad_qkv_w, ("leaf", "blk"), scatter_dimension=0, tiled=True),
        lax.psum_scatter(grad_o_w, ("leaf", "blk"), scatter_dimension=0, tiled=True),
        lax.psum_scatter(grad_cq_w, ("leaf", "blk"), scatter_dimension=0, tiled=True),
        lax.psum_scatter(grad_ckv_w, ("leaf", "blk"), scatter_dimension=0, tiled=True),
        lax.psum_scatter(grad_co_w, ("leaf", "blk"), scatter_dimension=0, tiled=True),
        lax.psum_scatter(grad_in_w, ("leaf", "blk"), scatter_dimension=0, tiled=True),
        lax.psum_scatter(grad_out_w, ("leaf", "blk"), scatter_dimension=0, tiled=True),
        lax.psum_scatter(grad_table_w, ("leaf", "blk"), scatter_dimension=1, tiled=True),
    )
    return (
        mixed_out,
        d_tokens,
        d_encoded,
        gradients[0],
        gradients[1],
        gradients[2],
        gradients[3],
        gradients[4],
        gradients[5],
        gradients[6],
        gradients[7],
    )


MESH = pl.DeviceIdType.MESH
BF = jnp.bfloat16
F32 = jnp.float32


class Place:
    def __init__(self, levels):
        leaf = lax.axis_index("leaf")
        blk = lax.axis_index("blk")
        self.levels = levels
        self.leaf = leaf
        self.blk = blk
        self.z = leaf // 2
        self.core = leaf % 2
        self.near = blk + 1 - 2 * (blk % 2)
        self.far = (blk + 2) % 4
        self.first = self.core * self.near + (1 - self.core) * self.far
        self.second = self.core * self.far + (1 - self.core) * self.near
        self.opposite = 3 - blk
        self.sibling = self.z * 2 + 1 - self.core
        self.side = blk // 2
        self.served = self.z * 2 + self.side
        self.pair = blk % 2 * 2 + self.core
        self.main = self.side == self.core
        self.line = [(leaf + 2 * step) % (2 * levels) for step in range(1, levels)]

    def greet(self):
        barrier = pltpu.get_barrier_semaphore()

        count = self.levels * 2

        def hello(leaf, blk):
            pl.semaphore_signal(barrier, inc=1, device_id=(leaf, blk), device_id_type=MESH)

        for blk in (self.near, self.far, self.opposite):
            hello(self.leaf, blk)
            hello(self.sibling, blk)
        for step in range(1, count):
            hello((self.leaf + step) % count, self.blk)
        pl.semaphore_wait(barrier, count + 5)


def remote(src, dst, send, recv, leaf, blk):
    return pltpu.make_async_remote_copy(
        src_ref=src, dst_ref=dst, send_sem=send, recv_sem=recv,
        device_id=(leaf, blk), device_id_type=MESH,
    )


def rows_of(start, count):
    return pl.ds(pl.multiple_of(start * count, count), count)


class Gather:
    def __init__(self, place, full, rows, columns, send_sem, recv_sem):
        self.place, self.full, self.rows, self.columns = place, full, rows, columns
        self.send_sem, self.recv_sem = send_sem, recv_sem
        self.sent = []

    def build(self, leaf, blk, to_leaf, to_blk, number):
        there = self.full.at[rows_of(leaf * 4 + blk, self.rows), self.columns]
        return remote(there, there, self.send_sem.at[number], self.recv_sem.at[leaf * 4 + blk], to_leaf, to_blk)

    def push(self, leaf, blk, *targets):
        for to_leaf, to_blk in targets:
            copy = self.build(leaf, blk, to_leaf, to_blk, len(self.sent))
            copy.start()
            self.sent.append(copy)

    def arrive(self, leaf, blk):
        p = self.place
        self.build(leaf, blk, p.leaf, p.second, 0).wait_recv()

    def steps(self):
        p = self.place
        sibling, second = (p.sibling, p.blk), (p.leaf, p.second)
        line = [(leaf, p.blk) for leaf in p.line]
        self.push(p.leaf, p.blk, (p.leaf, p.first), *line, sibling)
        yield
        self.arrive(p.leaf, p.first)
        self.push(p.leaf, p.first, *line, sibling)
        yield
        self.push(p.leaf, p.blk, second)
        self.push(p.leaf, p.first, second)
        for leaf in p.line:
            self.arrive(leaf, p.blk)
            self.push(leaf, p.blk, second, sibling)
        yield
        for leaf in p.line:
            self.arrive(leaf, p.first)
            self.push(leaf, p.first, second, sibling)
        yield
        for leaf in (p.leaf, *p.line):
            for blk in (p.second, p.opposite):
                self.arrive(leaf, blk)
                self.push(leaf, blk, sibling)
        yield
        for level in range(p.levels):
            for blk in range(4):
                self.arrive(2 * level + 1 - p.core, blk)
        yield

    def finish(self):
        for copy in self.sent:
            copy.wait_send()

    @staticmethod
    def sends(levels):
        return 8 * levels


class Spread:
    def __init__(self, place, full, rows, send_sem, recv_sem):
        self.place, self.full, self.rows = place, full, rows
        self.send_sem, self.recv_sem = send_sem, recv_sem

    def build(self, blk, to_blk, number):
        there = self.full.at[rows_of(blk, self.rows), :]
        return remote(there, there, self.send_sem.at[number], self.recv_sem.at[blk], self.place.leaf, to_blk)

    def start(self):
        p = self.place
        self.copies = [self.build(p.blk, to, n) for n, to in enumerate((p.near, p.far, p.opposite))]
        for copy in self.copies:
            copy.start()

    def arrive(self):
        p = self.place
        for blk in (p.near, p.far, p.opposite):
            self.build(blk, p.near, 0).wait_recv()

    def finish(self):
        for copy in self.copies:
            copy.wait_send()


class Reduce:
    def __init__(self, place, total, rows, columns, store, boxes, send_sem, recv_sem, line_last):
        self.place, self.total, self.rows, self.columns, self.store = place, total, rows, columns, store
        self.from_sibling, self.from_second, self.from_line, self.from_first = boxes
        self.send_sem, self.recv_sem = send_sem, recv_sem
        self.line_last = line_last
        self.sent = []

    @staticmethod
    def slots(levels):
        return 6 * levels

    @staticmethod
    def boxes(levels, rows, width, kind, line_last):
        line, first = (levels, levels) if line_last else (2 * levels, 1)
        return [pltpu.VMEM((slots * rows, width), kind) for slots in (4 * levels, 2 * levels, line, first)]

    def here(self, leaf, blk):
        return (leaf * 4 + blk) * self.rows

    def part(self, leaf, blk, count=1):
        return self.total.at[pl.ds(pl.multiple_of(self.here(leaf, blk), self.rows), self.rows * count), self.columns]

    def copy(self, src, box, position, count, number, leaf, blk, sender=None):
        there = box.at[pl.ds(pl.multiple_of(position * self.rows, self.rows), self.rows * count), :]
        sender = number if sender is None else sender
        return remote(there if src is None else src, there, self.send_sem.at[sender], self.recv_sem.at[number], leaf, blk)

    def send(self, *parts):
        copy = self.copy(*parts)
        copy.start()
        self.sent.append(copy)

    def arrived(self, box, position, count, number):
        self.copy(None, box, position, count, number, self.place.leaf, self.place.first).wait_recv()

    def value(self, start, *sources):
        unit = pl.ds(pl.multiple_of(start, 16), 16)
        value = self.total[unit, self.columns].astype(F32)
        for box, position in sources:
            value = value + box[pl.ds(pl.multiple_of(position, 16), 16), :].astype(F32)
        return unit, value

    def add(self, leaf, blk, *sources, count=1):
        def one(step):
            unit, value = self.value(self.here(leaf, blk) + 16 * step, *[(box, slot * self.rows + 16 * step) for box, slot in sources])
            self.total[unit, self.columns] = value.astype(self.total.dtype)

        loop(count * self.rows // 16, one)

    def give(self, *sources):
        for step in range(self.rows // 16):
            unit, value = self.value(self.here(self.place.leaf, self.place.blk) + 16 * step,
                                     *[(box, slot * self.rows + 16 * step) for box, slot in sources])
            self.store(pl.ds(16 * step, 16), value)

    def steps(self):
        p = self.place
        levels = p.levels
        for level in range(levels):
            self.send(self.part(2 * level + 1 - p.core, 0, 4), self.from_sibling, 4 * level, 4, level, p.sibling, p.blk)
        yield
        for level in range(levels):
            self.arrived(self.from_sibling, 4 * level, 4, level)
            leaf = 2 * level + p.core
            self.add(leaf, 0, (self.from_sibling, 4 * level), count=4)
            for which, blk in enumerate((p.second, p.opposite)):
                slot = 2 * level + which
                self.send(self.part(leaf, blk), self.from_second, slot, 1, levels + slot, p.leaf, p.second)
        yield
        for level in range(levels):
            leaf = 2 * level + p.core
            for which, blk in enumerate((p.blk, p.first)):
                slot = 2 * level + which
                self.arrived(self.from_second, slot, 1, levels + slot)
                self.add(leaf, blk, (self.from_second, slot))
                if self.line_last and which == 1:
                    self.send(self.part(leaf, p.first), self.from_first, level, 1, 5 * levels + level, p.leaf, p.first)
        if self.line_last:
            yield
            for level in range(levels):
                self.arrived(self.from_first, level, 1, 5 * levels + level)
                self.add(2 * level + p.core, p.blk, (self.from_first, level))
        shards = (p.blk,) if self.line_last else (p.blk, p.first)
        slots = len(shards)
        for leaf in p.line:
            for which, blk in enumerate(shards):
                self.send(self.part(leaf, blk), self.from_line, slots * p.z + which, 1, 3 * levels + slots * p.z + which,
                          leaf, p.blk, 3 * levels + slots * (leaf // 2) + which)
        yield
        came = []
        for which, blk in enumerate(shards):
            slots_of = [slots * (leaf // 2) + which for leaf in p.line]
            for slot in slots_of:
                self.arrived(self.from_line, slot, 1, 3 * levels + slot)
            came.append([(self.from_line, slot) for slot in slots_of])
        if self.line_last:
            self.give(*came[0])
            yield
            return
        self.add(p.leaf, p.first, *came[1])
        self.send(self.part(p.leaf, p.first), self.from_first, 0, 1, 5 * levels, p.leaf, p.first)
        yield
        self.arrived(self.from_first, 0, 1, 5 * levels)
        self.give(*came[0], (self.from_first, 0))
        yield

    def finish(self):
        for copy in self.sent:
            copy.wait_send()


class GatherLine(Gather):
    def steps(self):
        p = self.place
        sibling, first, second = (p.sibling, p.blk), (p.leaf, p.first), (p.leaf, p.second)
        self.push(p.leaf, p.blk, *[(leaf, p.blk) for leaf in p.line], sibling)
        yield
        self.push(p.leaf, p.blk, first, second)
        for leaf in p.line:
            self.arrive(leaf, p.blk)
            self.push(leaf, p.blk, first, second, sibling)
        yield
        for leaf in (p.leaf, *p.line):
            self.arrive(leaf, p.first)
            self.push(leaf, p.first, second, sibling)
        yield
        for leaf in (p.leaf, *p.line):
            for blk in (p.second, p.opposite):
                self.arrive(leaf, blk)
                self.push(leaf, blk, sibling)
        yield
        for level in range(p.levels):
            for blk in range(4):
                self.arrive(2 * level + 1 - p.core, blk)
        yield


class Share:
    def __init__(self, place, own, full, send_sem, recv_sem):
        self.place, self.own, self.full = place, own, full
        self.rows = own.shape[0]
        self.half = self.rows // 2
        self.send_sem, self.recv_sem = send_sem, recv_sem
        self.sent = []

    def build(self, blk, half, to_leaf, to_blk, number, own=False):
        there = self.full.at[pl.ds(pl.multiple_of(blk * self.rows + half * self.half, self.half), self.half), :]
        src = self.own.at[pl.ds(half * self.half, self.half), :] if own else there
        return remote(src, there, self.send_sem.at[number], self.recv_sem.at[blk * 2 + half], to_leaf, to_blk)

    def wait(self, blk, half):
        self.build(blk, half, self.place.sibling, self.place.blk, 0).wait_recv()

    def push(self, cond, *parts):
        number = len(self.sent)
        pl.when(cond)(lambda: self.build(*parts[:4], number, *parts[4:]).start())
        self.sent.append((cond, parts, number))

    def steps(self):
        p = self.place
        helps = jnp.logical_not(p.main)
        sibling = (p.sibling, p.blk)
        for half in range(2):
            self.push(helps, p.blk, half, p.leaf, p.far, True)
            self.push(p.main, p.blk, half, p.leaf, p.near, True)
        for half in range(2):
            self.push(p.main, p.blk, half, *sibling, True)
        yield
        for half in range(2):
            pl.when(p.main)(lambda half=half: self.wait(p.far, half))
            self.push(p.main, p.far, half, p.leaf, p.near)
            self.push(p.main, p.far, half, *sibling)
        yield
        for blk in (p.near, p.opposite):
            for half in range(2):
                pl.when(p.main)(lambda blk=blk, half=half: self.wait(blk, half))
                self.push(p.main, blk, half, *sibling)
            yield

    def arrive(self, blk):
        for half in range(2):
            pl.when(jnp.logical_not(self.place.main))(lambda half=half: self.wait(blk, half))

    def finish(self):
        for cond, parts, number in self.sent:
            pl.when(cond)(lambda parts=parts, number=number: self.build(*parts[:4], number, *parts[4:]).wait_send())

    sends = 14


class GatherPair:
    def __init__(self, place, own, full, transit, send_sem, recv_sem):
        self.place, self.own, self.full, self.transit = place, own, full, transit
        self.rows, self.width = own.shape[0], full.shape[1]
        self.send_sem, self.recv_sem = send_sem, recv_sem
        self.sent = []

    def start(self, copy):
        copy.start()
        self.sent.append(copy)

    def send_of(self):
        return self.send_sem.at[len(self.sent)]

    def columns(self, pair):
        return self.own.at[:, pl.ds(pl.multiple_of(pair * self.width, 128), self.width)]

    def piece(self, src_blk, to_blk, other):
        p = self.place
        there = self.transit.at[rows_of(p.z * 4 + src_blk, self.rows), :] if other else self.full.at[rows_of(p.leaf * 4 + src_blk, self.rows), :]
        src = self.columns(2 * (to_blk % 2) + (1 - p.core if other else p.core))
        return remote(src, there, self.send_of(), self.recv_sem.at[2 * src_blk + other], p.leaf, to_blk)

    def block(self, level, to_leaf, other):
        p = self.place
        there = self.transit.at[rows_of(level, 4 * self.rows), :] if other else self.full.at[rows_of(2 * level + p.core, 4 * self.rows), :]
        return remote(there, there, self.send_of(), self.recv_sem.at[8 + 2 * level + other], to_leaf, p.blk)

    def hand(self, level):
        p = self.place
        there = self.full.at[rows_of(2 * level + p.core, 4 * self.rows), :]
        return remote(self.transit.at[rows_of(level, 4 * self.rows), :], there, self.send_of(),
                      self.recv_sem.at[8 + 2 * p.levels + level], p.sibling, p.blk)

    def handed(self, level):
        p = self.place
        there = self.full.at[rows_of(2 * level + 1 - p.core, 4 * self.rows), :]
        remote(there, there, self.send_sem.at[0], self.recv_sem.at[8 + 2 * p.levels + level], p.sibling, p.blk).wait_recv()

    def fill(self):
        p = self.place
        self.full[rows_of(p.leaf * 4 + p.blk, self.rows), :] = self.columns(p.pair)[...]
        self.transit[rows_of(p.z * 4 + p.blk, self.rows), :] = self.columns(2 * (p.blk % 2) + 1 - p.core)[...]

    def steps(self):
        p = self.place
        for to_blk in (p.near, p.far, p.opposite):
            for other in range(2):
                self.start(self.piece(p.blk, to_blk, other))
        yield
        for blk in (p.near, p.far, p.opposite):
            for other in range(2):
                self.piece(blk, p.near, other).wait_recv()
        for to_leaf in p.line:
            for other in range(2):
                self.start(self.block(p.z, to_leaf, other))
        self.start(self.hand(p.z))
        yield
        for leaf in p.line:
            for other in range(2):
                self.block(leaf // 2, p.sibling, other).wait_recv()
            self.start(self.hand(leaf // 2))
        yield
        for level in range(p.levels):
            self.handed(level)
        yield

    def finish(self):
        for copy in self.sent:
            copy.wait_send()

    @staticmethod
    def sends(levels):
        return 6 + 2 * (levels - 1) + levels

    @staticmethod
    def receives(levels):
        return 8 + 3 * levels


class ReducePair:
    def __init__(self, place, total, out, boxes, send_sem, recv_sem):
        self.place, self.total, self.out = place, total, out
        self.rows = total.shape[0] // (place.levels * 8)
        self.from_far, self.from_line, self.from_pair = boxes
        self.send_sem, self.recv_sem = send_sem, recv_sem
        self.sent = []

    @staticmethod
    def slots(levels):
        return 4 * levels + 4

    @staticmethod
    def boxes(levels, rows, width, kind):
        return [pltpu.VMEM((levels * 4 * rows, width), kind) for n in range(2)] + [pltpu.VMEM((4 * rows, width), kind)]

    def build(self, src, box, slot, rows, number, leaf, blk):
        there = box.at[rows_of(slot, rows), :]
        return remote(there if src is None else src, there, self.send_sem.at[len(self.sent)], self.recv_sem.at[number], leaf, blk)

    def send(self, *parts):
        copy = self.build(*parts)
        copy.start()
        self.sent.append(copy)

    def arrived(self, box, slot, rows, number):
        self.build(None, box, slot, rows, number, self.place.sibling, self.place.blk).wait_recv()

    def twin(self, leaf, side):
        return rows_of(leaf * 2 + side, 2 * self.rows)

    def add(self, leaf, *sources):
        here = self.twin(leaf, self.place.side)
        value = self.total[here, :].astype(F32)
        for box, slot in sources:
            value = value + box[rows_of(slot, 2 * self.rows), :].astype(F32)
        self.total[here, :] = value.astype(self.total.dtype)

    def steps(self):
        p = self.place
        levels, rows = p.levels, 2 * self.rows
        for leaf in range(2 * levels):
            self.send(self.total.at[self.twin(leaf, 1 - p.side), :], self.from_far, leaf, rows, leaf, p.leaf, p.far)
        yield
        for leaf in range(2 * levels):
            self.arrived(self.from_far, leaf, rows, leaf)
            self.add(leaf, (self.from_far, leaf))
        for to_leaf in p.line:
            for core in range(2):
                slot = 2 * p.z + core
                self.send(self.total.at[self.twin(to_leaf // 2 * 2 + core, p.side), :], self.from_line, slot, rows,
                          2 * levels + slot, to_leaf, p.blk)
        yield
        for core in range(2):
            slots = [leaf // 2 * 2 + core for leaf in p.line]
            for slot in slots:
                self.arrived(self.from_line, slot, rows, 2 * levels + slot)
            self.add(2 * p.z + core, *[(self.from_line, slot) for slot in slots])
        for leaf, blk in ((p.sibling, p.blk), (p.leaf, p.near), (p.sibling, p.near)):
            src = self.total.at[rows_of(leaf * 4 + blk, self.rows), :]
            self.send(src, self.from_pair, p.pair, self.rows, 4 * levels + p.pair, leaf, blk)
        self.store(p.pair, self.total[rows_of(p.leaf * 4 + p.blk, self.rows), :])
        yield
        column = p.blk % 2
        for pair in (2 * column + 1 - p.core, 2 * (1 - column) + p.core, 2 * (1 - column) + 1 - p.core):
            self.arrived(self.from_pair, pair, self.rows, 4 * levels + pair)
            self.store(pair, self.from_pair[rows_of(pair, self.rows), :])
        yield

    def store(self, pair, value):
        for third in range(3):
            lanes = pl.ds(pl.multiple_of(third * D + pair * 128, 128), 128)
            self.out[:, lanes] = value[:, third * 128:third * 128 + 128].astype(F32)

    def finish(self):
        for copy in self.sent:
            copy.wait_send()


class TreeReduce:
    def __init__(self, place, part, from_core, from_chip, box, send_sem, core_sem, chip_sem, recv_sem):
        self.place, self.part = place, part
        self.from_core, self.from_chip, self.box = from_core, from_chip, box
        self.send_sem, self.core_sem, self.chip_sem, self.recv_sem = send_sem, core_sem, chip_sem, recv_sem

    def to_core(self, tile):
        p = self.place
        return remote(self.part.at[span(tile), :], self.from_core.at[tile // 2], self.send_sem.at[tile],
                      self.core_sem.at[tile // 2], p.sibling, p.blk)

    def to_chip(self, tile):
        p = self.place
        return remote(self.part.at[span(tile), :], self.from_chip.at[tile // 4], self.send_sem.at[tile],
                      self.chip_sem.at[tile // 4], p.leaf, p.near)

    def to_owner(self, tile):
        p = self.place
        return remote(self.part.at[span(tile), :], self.box.at[tile % 2], self.send_sem.at[tile],
                      self.recv_sem.at[tile % 2], p.served, tile // 2)

    def roles(self, tile):
        p = self.place
        collects = p.core == tile % 2
        gate = p.blk % 2 == tile // 2 % 2
        owner = (p.leaf == p.served) & (p.blk == tile // 2)
        return collects, gate, owner

    def offer(self, tile):
        collects, gate, owner = self.roles(tile)
        pl.when(jnp.logical_not(collects))(lambda: self.to_core(tile).start())

    def add(self, tile, box, slot):
        total = self.part[span(tile), :].astype(F32) + box[slot].astype(F32)
        self.part[span(tile), :] = total.astype(BF)

    def collect(self, tile):
        collects, gate, owner = self.roles(tile)

        def go():
            self.to_core(tile).wait_recv()
            self.add(tile, self.from_core, tile // 2)
            pl.when(jnp.logical_not(gate))(lambda: self.to_chip(tile).start())

        pl.when(collects)(go)

    def forward(self, tile):
        collects, gate, owner = self.roles(tile)

        def go():
            self.to_chip(tile).wait_recv()
            self.add(tile, self.from_chip, tile // 4)
            pl.when(jnp.logical_not(owner))(lambda: self.to_owner(tile).start())

            def keep():
                self.box[tile % 2] = self.part[span(tile), :]

            pl.when(owner)(keep)

        pl.when(collects & gate)(go)

    def arrive(self, half):
        p = self.place
        kept = p.main & (p.core == half)
        pl.when(jnp.logical_not(kept))(lambda: self.to_owner(half).wait_recv())

    def finish(self, tile):
        collects, gate, owner = self.roles(tile)
        pl.when(jnp.logical_not(collects))(lambda: self.to_core(tile).wait_send())
        pl.when(collects & jnp.logical_not(gate))(lambda: self.to_chip(tile).wait_send())
        pl.when(collects & gate & jnp.logical_not(owner))(lambda: self.to_owner(tile).wait_send())


class Settle:
    def __init__(self, place, part, out, box, send_sem, recv_sem):
        self.place, self.part, self.out, self.box = place, part, out, box
        self.send_sem, self.recv_sem = send_sem, recv_sem
        self.rows = out.shape[0]

    def build(self, src_blk, to_blk):
        p = self.place
        return remote(self.part.at[rows_of(to_blk, self.rows), :], self.box.at[rows_of(src_blk, self.rows), :],
                      self.send_sem.at[to_blk], self.recv_sem.at[src_blk], p.leaf, to_blk)

    def steps(self):
        p = self.place
        self.copies = [self.build(p.blk, to) for to in (p.near, p.far, p.opposite)]
        for copy in self.copies:
            copy.start()
        yield
        total = self.part[rows_of(p.blk, self.rows), :]
        for blk in (p.near, p.far, p.opposite):
            self.build(blk, p.near).wait_recv()
            total = total + self.box[rows_of(blk, self.rows), :]
        self.out[...] = total
        yield

    def finish(self):
        for copy in self.copies:
            copy.wait_send()


class TableSum:
    def __init__(self, place, payload, box, rows_box, send_sem, recv_sem):
        self.place, self.payload, self.box, self.rows_box = place, payload, box, rows_box
        self.send_sem, self.recv_sem = send_sem, recv_sem
        self.leaves = place.levels * 2
        self.rows = self.leaves * 8

    def first(self, src_blk, to_blk):
        return remote(self.payload.at[rows_of(to_blk, self.rows), :], self.box.at[rows_of(src_blk, self.rows), :],
                      self.send_sem.at[to_blk], self.recv_sem.at[src_blk], self.place.leaf, to_blk)

    def second(self, src_leaf, to_leaf):
        p = self.place
        start = p.blk * self.leaves + to_leaf
        return remote(self.payload.at[rows_of(start, 8), :], self.rows_box.at[rows_of(src_leaf, 8), :],
                      self.send_sem.at[4 + to_leaf], self.recv_sem.at[4 + src_leaf], to_leaf, p.blk)

    def steps(self):
        p = self.place
        peers = (p.near, p.far, p.opposite)
        others = [(p.leaf + step) % self.leaves for step in range(1, self.leaves)]
        for to in peers:
            self.first(p.blk, to).start()
        yield
        here = rows_of(p.blk, self.rows)
        total = self.payload[here, :]
        for src in peers:
            self.first(src, p.near).wait_recv()
            total = total + self.box[rows_of(src, self.rows), :]
        self.payload[here, :] = total
        for to in others:
            self.second(p.leaf, to).start()
        self.rows_box[rows_of(p.leaf, 8), :] = self.payload[rows_of(p.blk * self.leaves + p.leaf, 8), :]
        yield
        for src in others:
            self.second(src, others[0]).wait_recv()
        yield

    def finish(self):
        p = self.place
        for to in (p.near, p.far, p.opposite):
            self.first(p.blk, to).wait_send()
        for step in range(1, self.leaves):
            self.second(p.leaf, (p.leaf + step) % self.leaves).wait_send()


SPAN = 256
TINY = 1e-05


def dot(left, right):
    return lax.dot_general(left, right, (((1,), (0,)), ((), ())), preferred_element_type=F32)


def dot_nt(left, right):
    return lax.dot_general(left, right, (((1,), (1,)), ((), ())), preferred_element_type=F32)


def dot_tn(left, right):
    return lax.dot_general(left, right, (((0,), (0,)), ((), ())), preferred_element_type=F32)


def iota(shape, axis):
    return lax.broadcasted_iota(jnp.int32, shape, axis)


def span(start, count=SPAN):
    return pl.ds(pl.multiple_of(start * count, count), count)


def loop(count, body):
    def step(index, carry):
        body(index)
        return carry

    lax.fori_loop(0, count, step, 0)


def unit_rows(values):
    centred = values - jnp.mean(values, axis=-1, keepdims=True)
    root = lax.rsqrt(jnp.mean(centred * centred, axis=-1, keepdims=True) + TINY)
    return centred * root, root


def norm_back(grad, unit, root, scale):
    inner = grad * (1.0 + scale)
    return (
        inner
        - jnp.mean(inner, axis=-1, keepdims=True)
        - unit * jnp.mean(inner * unit, axis=-1, keepdims=True)
    ) * root


def spread_pattern(wide, group):
    column = iota((128, group), 1)
    turn = jnp.zeros((128, group), jnp.int32)
    for step in range(1, group // wide):
        turn = turn + (column >= step * wide).astype(jnp.int32)
    return (column - turn * wide == iota((128, group), 0)).astype(F32)


def shard_of_column(count, wide, group):
    column = iota((count, group), 1)
    turn = jnp.zeros((count, group), jnp.int32)
    for step in range(1, group // wide):
        turn = turn + (column >= step * wide).astype(jnp.int32)
    return turn


def aux_row(aux, leaf, row):
    chosen = (iota((8, aux.shape[0]), 1) == leaf * 256 + row).astype(BF)
    return dot(chosen, aux[...])[0:1, :]


def read_modulation(aux, timestep, mod, wide):
    count = aux.shape[0] // 64
    row = iota((count, aux.shape[0]), 0)
    column = iota((count, aux.shape[0]), 1)
    chosen = ((column - row * 64).astype(F32) == timestep).astype(BF)
    picked = dot(chosen, aux[...])
    group = wide * 4
    laid = dot(picked.astype(BF), spread_pattern(wide, group).astype(BF))
    offset = iota((count, group), 0) - shard_of_column(count, wide, group)
    for part in range(count // 4):
        mod[0:1, part * group:(part + 1) * group] = jnp.sum(
            jnp.where(offset == 4 * part, laid, 0.0), axis=0, keepdims=True
        )


def table_payload(sums, wide, count):
    group = wide * 4
    offset = iota((count, group), 0) - shard_of_column(count, wide, group)
    held = jnp.zeros((count, group), F32)
    for part in range(count // 4):
        held = held + jnp.where(offset == 4 * part, sums[0:1, part * group:(part + 1) * group], 0.0)
    cut = lax.dot_general(held, spread_pattern(wide, group), (((1,), (1,)), ((), ())),
                          preferred_element_type=F32, precision=lax.Precision.HIGHEST)
    leaves = count // 4
    row = iota((count * 8, count), 0)
    tile = sum((row >= 8 * step).astype(jnp.int32) for step in range(1, count))
    block = sum((row >= 8 * leaves * step).astype(jnp.int32) for step in range(1, 4))
    chosen = (iota((count * 8, count), 1) == (tile - block * leaves) * 4 + block).astype(F32)
    return lax.dot_general(chosen, cut, (((1,), (0,)), ((), ())),
                           preferred_element_type=F32, precision=lax.Precision.HIGHEST)


def block_bias(parents, bias, blocks):
    row, column = iota((128, 128), 0), iota((128, 128), 1)
    reach = (row == column).astype(F32)
    reach = jnp.maximum(reach, (row.astype(F32) == parents).astype(F32))
    for step in range((blocks - 1).bit_length()):
        low_reach = reach.astype(BF)
        reach = jnp.minimum(dot(low_reach, low_reach), 1.0)
    held = (reach[:blocks, :] - 1.0) * 1e30
    for block in range(blocks):
        bias[:, block * BLOCK:(block + 1) * BLOCK] = jnp.broadcast_to(held[:, block:block + 1], (blocks, BLOCK))


class Layer:
    def __init__(self, place, refs):
        self.place = place
        self.__dict__.update(refs)

    def project(self, chunk):
        rows = span(chunk)
        unit, root = unit_rows(self.tokens_all[rows, :].astype(F32))
        first = (unit * (1.0 + self.mod_served[0:1, D:2 * D]) + self.mod_served[0:1, 0:D]).astype(BF)
        self.h1[rows, :] = first
        made = dot(first, self.w_pair[...])
        lane = iota((SPAN, 128), 1)
        query = made[:, 0:128].astype(BF).astype(F32) * HEAD ** (-0.5)
        self.q_masked[0, rows, :] = jnp.where(lane < HEAD, query, 0.0).astype(BF)
        self.q_masked[1, rows, :] = jnp.where(lane >= HEAD, query, 0.0).astype(BF)
        key = made[:, 128:256]
        value = made[:, 256:384]
        self.key[rows, :] = key.astype(BF)
        self.value[rows, :] = value.astype(BF)
        self.key_t[:, rows] = key.T.astype(BF)
        value_t = value.T.astype(BF)
        ones = jnp.ones((16, SPAN), BF)
        self.value_t[0, 0:HEAD, rows] = value_t[:HEAD]
        self.value_t[1, 0:HEAD, rows] = value_t[HEAD:]
        self.value_t[0, HEAD:HEAD + 16, rows] = ones
        self.value_t[1, HEAD:HEAD + 16, rows] = ones

    def attend(self, tile):
        queries = slice(tile * SPAN, (tile + 1) * SPAN)
        base = tile * (tile + 1) // 2

        def score(j, head):
            raw = dot_nt(self.key[j * SPAN:(j + 1) * SPAN, :], self.q_masked[head, queries, :])
            upper = raw[:BLOCK] + self.bias[2 * j:2 * j + 1, queries]
            lower = raw[BLOCK:] + self.bias[2 * j + 1:2 * j + 2, queries]
            kept = jnp.concatenate((upper, lower), axis=0)
            return kept + self.corner[...] if j == tile else kept

        top = [jnp.full((8, SPAN), -3e30, F32) for head in range(2)]
        for j in range(tile + 1):
            for head in range(2):
                top[head] = jnp.maximum(top[head], jnp.max(score(j, head).reshape(SPAN // 8, 8, SPAN), axis=0))
        top = [jnp.max(each, axis=0, keepdims=True) for each in top]
        mix = [0.0, 0.0]
        for j in range(tile + 1):
            for head in range(2):
                weight = jnp.exp(score(j, head) - top[head]).astype(BF)
                self.weights[base + j, head] = weight
                mix[head] = mix[head] + dot(self.value_t[head, :, j * SPAN:(j + 1) * SPAN], weight)
        halves = []
        for head in range(2):
            inverse = 1.0 / mix[head][HEAD:HEAD + 8, :]
            self.inverse[head, :, queries] = inverse
            halves.append(mix[head][:HEAD, :] * inverse[0:1])
        attended_t = jnp.concatenate(halves, axis=0)
        self.attended_t[:, queries] = attended_t
        self.attended[queries, :] = attended_t.T.astype(BF)

    def cross_keys(self):
        made = dot(self.source_all[...], self.w_ckv).astype(BF)
        lane = iota((2 * ENC, 128), 1)
        row = iota((2 * ENC, 128), 0)
        own = (lane < HEAD) == (row < ENC)
        for pair in range(4):
            for box, start in ((self.cross_k, 0), (self.cross_v, D)):
                part = made[:, start + 128 * pair:start + 128 * pair + 128].astype(F32)
                box[pair] = jnp.where(own, jnp.concatenate((part, part), axis=0), 0.0).astype(BF)

    def middle(self, chunk):
        rows = span(chunk)
        y1 = self.tokens[rows, :].astype(F32) + dot(self.gathered[rows, :], self.w_o)
        self.y1[rows, :] = y1
        unit, root = unit_rows(y1)
        h2 = (unit * (1.0 + self.mod[0:1, 3 * D:4 * D]) + self.mod[0:1, 2 * D:3 * D]).astype(BF)
        self.h2[rows, :] = h2
        query = (dot(h2, self.w_cq).astype(BF).astype(F32) * HEAD ** (-0.5)).astype(BF)
        self.cross_q[rows, :] = query
        lane = iota((SPAN, 128), 1)
        same = ((iota((128, 128), 0) < ENC) == (iota((128, 128), 1) < ENC)).astype(BF)
        out = []
        for pair in range(4):
            raw = dot_nt(query[:, 128 * pair:128 * pair + 128], self.cross_k[pair])
            left = jnp.max(jnp.where(lane < ENC, raw, -3e38), axis=-1, keepdims=True)
            right = jnp.max(jnp.where(lane >= ENC, raw, -3e38), axis=-1, keepdims=True)
            weight = jnp.exp(raw - jnp.where(lane < ENC, left, right))
            weight = weight / dot(weight.astype(BF), same)
            self.cross_p[pair, rows, :] = weight.astype(BF)
            out.append(dot(weight.astype(BF), self.cross_v[pair]))
        cross = jnp.concatenate(out, axis=1).astype(BF)
        self.cross_out[rows, :] = cross
        y2 = y1 + dot(cross, self.w_co)
        self.y2[rows, :] = y2
        unit, root = unit_rows(y2)
        self.h3[rows, :] = (unit * (1.0 + self.mod[0:1, 5 * D:6 * D]) + self.mod[0:1, 4 * D:5 * D]).astype(BF)

    def hidden(self, chunk):
        units = span(chunk)
        u = dot(self.h3[...], self.w_in(units))
        dg = dot_nt(self.cotangent[...], self.w_out[units, :])
        square = u * u
        slope = 0.7978845608028654
        bend = jnp.tanh(u * (slope + slope * 0.044715 * square))
        half = 0.5 + 0.5 * bend
        self.act[:, units] = (u * half).astype(BF)
        turn = half + 0.5 * u * (1.0 - bend * bend) * (slope + 3.0 * slope * 0.044715 * square)
        self.d_hidden[:, units] = (dg * turn).astype(BF)
        self.grad_out(units, dot_tn(self.act[:, units], self.cotangent[...]).astype(BF))
        self.grad_in(units, dot_tn(self.h3[...], self.d_hidden[:, units]).astype(BF))

    def finish_forward(self, chunk):
        rows = span(chunk)
        self.mixed[rows, :] = (self.y2[rows, :] + dot(self.act[rows, :], self.w_out[...])).astype(BF)

    def sums(self, piece, shift, scale):
        self.mod_grad[0:1, 2 * piece * D:(2 * piece + 1) * D] += jnp.sum(shift, axis=0, keepdims=True)
        self.mod_grad[0:1, (2 * piece + 1) * D:(2 * piece + 2) * D] += jnp.sum(scale, axis=0, keepdims=True)

    def back_three(self, chunk):
        rows = span(chunk)
        dh3 = dot_nt(self.d_hidden[rows, :], self.w_in(slice(None)))
        unit, root = unit_rows(self.y2[rows, :])
        self.sums(2, dh3, dh3 * unit)
        dy2 = self.cotangent[rows, :].astype(F32) + norm_back(dh3, unit, root, self.mod[0:1, 5 * D:6 * D])
        self.dy[rows, :] = dy2
        self.db[rows, :] = dy2.astype(BF)

    def back_cross(self, chunk):
        rows = span(chunk)
        dca = dot_nt(self.db[rows, :], self.w_co).astype(BF)
        lane = iota((SPAN, 128), 1)
        row = iota((128, 128), 0)
        own = (row < ENC) == (iota((128, 128), 1) < HEAD)
        parts = []
        for pair in range(4):
            lanes = slice(128 * pair, 128 * pair + 128)
            low_weight = self.cross_p[pair, rows, :]
            weight = low_weight.astype(F32)
            dc = dot_nt(dca[:, lanes], self.cross_v[pair])
            both_ = weight * dc
            left = jnp.sum(jnp.where(lane < ENC, both_, 0.0), axis=-1, keepdims=True)
            right = jnp.sum(jnp.where(lane >= ENC, both_, 0.0), axis=-1, keepdims=True)
            ds = (weight * (dc - jnp.where(lane < ENC, left, right))).astype(BF)
            parts.append((dot(ds, self.cross_k[pair]) * HEAD ** (-0.5)).astype(BF))
            dk = jnp.where(own, dot_tn(ds, self.cross_q[rows, lanes]), 0.0)
            dv = jnp.where(own, dot_tn(low_weight, dca[:, lanes]), 0.0)
            self.d_cross[:, lanes] += dk[:ENC] + dk[ENC:]
            self.d_cross[:, 128 * pair + D:128 * pair + D + 128] += dv[:ENC] + dv[ENC:]
        dcq = jnp.concatenate(parts, axis=1)
        self.dcq[rows, :] = dcq
        dh2 = dot_nt(dcq, self.w_cq)
        unit, root = unit_rows(self.y1[rows, :])
        self.sums(1, dh2, dh2 * unit)
        dy1 = self.dy[rows, :] + norm_back(dh2, unit, root, self.mod[0:1, 3 * D:4 * D])
        self.dy[rows, :] = dy1
        low_dy1 = dy1.astype(BF)
        self.db1[rows, :] = low_dy1
        self.d_attn[rows, :] = dot_nt(low_dy1, self.w_o).astype(BF)

    def attend_back(self, tile):
        queries = slice(tile * SPAN, (tile + 1) * SPAN)
        base = tile * (tile + 1) // 2
        d_att_t = self.d_att_all[queries, :].astype(F32).T
        scaled = [d_att_t[HEAD * h:HEAD * h + HEAD] * self.inverse[h, 0:1, queries] for h in range(2)]
        delta = [
            jnp.sum(scaled[h] * self.attended_t[HEAD * h:HEAD * h + HEAD, queries], axis=0, keepdims=True)
            for h in range(2)
        ]
        flat = jnp.concatenate(scaled, axis=0).T
        lane = iota((SPAN, 128), 1)
        masked = [jnp.where((lane < HEAD) == (h == 0), flat, 0.0).astype(BF) for h in range(2)]
        dq_t = [0.0, 0.0]
        for j in range(tile + 1):
            keys = slice(j * SPAN, (j + 1) * SPAN)
            dk = dv = 0.0
            for head in range(2):
                dp = dot_nt(self.value[keys, :], masked[head])
                weight = self.weights[base + j, head]
                ds = (weight.astype(F32) * (dp - delta[head])).astype(BF)
                dk = dk + dot(ds, self.q_masked[head, queries, :])
                dv = dv + dot(weight, masked[head])
                dq_t[head] = dq_t[head] + dot(self.key_t[HEAD * head:HEAD * head + HEAD, keys], ds)
            self.dk[keys, :] += dk
            self.dv[keys, :] += dv
        self.d_pair[queries, 0:128] = (jnp.concatenate(dq_t, axis=0) * HEAD ** (-0.5)).T.astype(BF)
        self.d_pair[queries, 128:256] = self.dk[queries, :].astype(BF)
        self.d_pair[queries, 256:384] = self.dv[queries, :].astype(BF)
        self.dh1_part[queries, :] = dot_nt(self.d_pair[queries, :], self.w_pair[...]).astype(BF)


VMEM = pl.BlockSpec(memory_space=pltpu.VMEM)
SMEM = pl.BlockSpec(memory_space=pltpu.SMEM)
CROSS = 5 * D
PACKED = ((0, 2 * D), (2 * D, CROSS), (CROSS, CROSS + FF // 2), (CROSS + FF // 2, CROSS + FF))
LAST = ((0, D // 2), (D // 2, D))


class Weights(Layer):
    w_o = property(lambda self: self.pack[:, 0:D])
    w_cq = property(lambda self: self.pack[:, D:2 * D])
    w_ckv = property(lambda self: self.pack[:, 2 * D:4 * D])
    w_co = property(lambda self: self.pack[:, 4 * D:CROSS])

    def w_in(self, units):
        return self.pack.at[:, CROSS:CROSS + FF][:, units]

    def grad_in(self, units, value):
        self.grad_pack.at[:, CROSS:CROSS + FF][:, units] = value

    def grad_out(self, units, value):
        self.grad_w_out[units, :] = value

    def grad_into(self, start, left, right):
        for step in range(right.shape[1] // SPAN):
            columns = slice(start + step * SPAN, start + (step + 1) * SPAN)
            self.grad_pack[:, columns] = dot_tn(left[...], right[:, step * SPAN:(step + 1) * SPAN]).astype(BF)


ANY = pl.BlockSpec(memory_space=pl.ANY)
INS = ("i_tokens", "i_cotangent", "i_encoded", "parents", "timestep", "i_qkv", "i_o", "i_cq", "i_ckv", "i_co", "i_in", "i_out", "i_table")
OUTS = ("mixed", "grad_tokens", "g_encoded", "g_qkv", "g_o", "g_cq", "g_ckv", "g_co", "g_in", "g_out", "g_table")


def layer_scratch(rows, tree, blocks, levels, wide):
    tiles = tree // SPAN
    count = levels * 8
    each = D // count
    plain = lambda *shape: pltpu.VMEM(shape, F32)
    short = lambda *shape: pltpu.VMEM(shape, BF)
    dma = pltpu.SemaphoreType.DMA
    scratch = dict(
        tokens=short(rows, D), cotangent=short(rows, D), qkv_own=short(each, 3 * D), mixed=short(rows, D), grad_tokens=plain(rows, D),
        g_encoded=plain(ENC // 4, D), g_qkv=plain(each, 3 * D), g_o=plain(each, D), g_cq=plain(each, D), g_ckv=plain(each, 2 * D),
        g_co=plain(each, D), g_in=plain(each, FF), g_out=plain(FF // count, D), g_table=plain(STEPS, wide),
        in_sem=dma((11,)), out_sem=dma((11,)),
        pair_own=short(each, 3 * D), w_pair=short(D, 384), transit=short(D // 2, 384), pack=short(D, CROSS + FF), w_out=short(FF, D),
        aux=short(count * 64, 128), tokens_all=short(tree, D), source_all=short(ENC, D),
        mod=plain(8, 6 * D), mod_served=plain(8, 6 * D), mod_grad=plain(8, 6 * D), bias=plain(blocks, tree), corner=plain(SPAN, SPAN),
        h1=short(tree, D), q_masked=short(2, tree, 128), key=short(tree, 128), value=short(tree, 128),
        key_t=short(128, tree), value_t=short(2, HEAD + 16, tree),
        weights=short(tiles * (tiles + 1) // 2, 2, SPAN, SPAN), inverse=plain(2, 8, tree),
        attended_t=plain(128, tree), attended=short(tree, 128), gathered=short(rows, D),
        cross_k=short(4, 2 * ENC, 128), cross_v=short(4, 2 * ENC, 128), cross_q=short(rows, D), cross_p=short(4, rows, 128),
        cross_out=short(rows, D), y1=plain(rows, D), h2=short(rows, D), h3=short(rows, D),
        act=short(rows, FF), d_hidden=short(rows, FF),
        d_cross=plain(ENC, 2 * D), dcq=short(rows, D), d_att_all=short(tree, 128),
        dk=plain(tree, 128), dv=plain(tree, 128),
        d_pair=short(tree, 384), from_core=short(4, SPAN, D), from_chip=short(2, SPAN, D), dh1_box=short(2, SPAN, D),
        grad_pack=short(D, CROSS + FF), grad_w_out=short(FF, D), grad_pair=short(D, 384), source_part=plain(ENC, D),
        payload=plain(count * 8, 128), table_box=plain(count * 8, 128), table_rows=plain(levels * 16, 128), settle_box=plain(ENC, D),
        a_send=dma((tiles,)), a_recv=dma((tiles,)), d_send=dma((4,)), d_recv=dma((4,)),
        h_send=dma((tiles,)), h_core=dma((4,)), h_chip=dma((2,)), h_recv=dma((2,)),
        send=dma((7, Gather.sends(levels))), recv=dma((7, count)),
        pair_send=dma((GatherPair.sends(levels),)), pair_recv=dma((GatherPair.receives(levels),)),
        share_send=dma((Share.sends,)), share_recv=dma((8,)), spread_send=dma((3,)), spread_recv=dma((4,)),
        r_send=dma((6, Reduce.slots(levels))), r_recv=dma((6, Reduce.slots(levels))), line=plain(64, 128),
        rp_send=dma((ReducePair.slots(levels),)), rp_recv=dma((ReducePair.slots(levels),)),
        settle_send=dma((4,)), settle_recv=dma((4,)), t_send=dma((4 + 2 * levels,)), t_recv=dma((4 + 2 * levels,)),
    )
    for piece, (height, width, line_last) in enumerate(
        [(FF // count, end - start, True) for start, end in LAST]
        + [(each, end - start, False) for start, end in PACKED[2:] + PACKED[:2]]
    ):
        for n, box in enumerate(Reduce.boxes(levels, height, width, BF, line_last)):
            scratch[f"box{piece}_{n}"] = box
    for n, box in enumerate(ReducePair.boxes(levels, each, 384, BF)):
        scratch[f"box_pair{n}"] = box
    return scratch


def layer_kernel(levels, wide, names, refs):
    place = Place(levels)
    refs = dict(zip(names, refs))
    refs["y2"] = refs["dy"] = refs["grad_tokens"]
    refs["db"] = refs["db1"] = refs["h3"]
    refs["d_attn"] = refs["cross_q"]
    refs["dh1_part"] = refs["tokens_all"]
    w = Weights(place, refs)
    blk, leaf = place.blk, place.leaf
    rows = w.tokens.shape[0]
    tree = w.tokens_all.shape[0]
    tiles = tree // SPAN
    halves = rows // SPAN
    blocks = tree // BLOCK
    count = levels * 8
    each = D // count
    index = leaf * 4 + blk
    own_lanes = pl.ds(pl.multiple_of(place.pair * 128, 128), 128)

    mine = rows_of(index, each)
    moves = [
        (w.i_tokens, w.tokens), (w.i_qkv, w.qkv_own),
        (w.i_encoded, w.source_all.at[rows_of(blk, w.i_encoded.shape[0]), :]),
        (w.i_out, w.w_out.at[rows_of(index, w.i_out.shape[0]), :]),
    ]
    start = 0
    for name in ("i_o", "i_cq", "i_ckv", "i_co", "i_in"):
        width = refs[name].shape[1]
        moves.append((refs[name], w.pack.at[mine, start:start + width]))
        start += width
    copies = [pltpu.make_async_copy(src, dst, w.in_sem.at[n]) for n, (src, dst) in enumerate(moves)]
    for copy in copies:
        copy.start()
    lane = iota((1, 128), 1)
    parents = jnp.zeros((1, 128), F32)
    for block in range(blocks):
        parents = jnp.where(lane == block, w.parents[0, block].astype(F32), parents)
    w.line[...] = jnp.zeros_like(w.line)
    w.line[:STEPS, :wide] = w.i_table[...].astype(F32)
    w.line[STEPS:STEPS + 1, :] = jnp.full((1, 128), w.timestep[0].astype(F32))
    w.line[STEPS + 1:STEPS + 2, :] = parents
    w.aux[rows_of(index, 64), :] = w.line[...].astype(BF)
    place.greet()
    for copy in copies:
        copy.wait()
    late = pltpu.make_async_copy(w.i_cotangent, w.cotangent, w.in_sem.at[10])
    late.start()

    def keep_tokens():
        w.tokens_all[rows_of(blk, rows), :] = w.tokens[...]

    pl.when(place.main)(keep_tokens)
    for pair in range(4):
        for third in range(3):
            w.pair_own[:, 384 * pair + 128 * third:384 * pair + 128 * third + 128] = (
                w.qkv_own[:, D * third + 128 * pair:D * third + 128 * pair + 128])
    given = []

    def give(*outs):
        for name in outs:
            copy = pltpu.make_async_copy(refs[name], refs["o_" + name], w.out_sem.at[OUTS.index(name)])
            copy.start()
            given.append(copy)

    weave = GatherPair(place, w.pair_own, w.w_pair, w.transit, w.pair_send, w.pair_recv)
    weave.fill()
    table = GatherLine(place, w.aux, 64, slice(None), w.send.at[6], w.recv.at[6])
    share = Share(place, w.tokens, w.tokens_all, w.share_send, w.share_recv)
    spread = Spread(place, w.source_all, w.i_encoded.shape[0], w.spread_send, w.spread_recv)
    loads = [
        GatherLine(place, w.pack, each, slice(*cut), w.send.at[n], w.recv.at[n]) for n, cut in enumerate(PACKED)
    ] + [
        GatherLine(place, w.w_out, FF // count, slice(*cut), w.send.at[4 + n], w.recv.at[4 + n]) for n, cut in enumerate(LAST)
    ]
    weave_steps, table_steps, share_steps = weave.steps(), table.steps(), share.steps()
    load_steps = [load.steps() for load in loads]

    def ticks(steps, number=1):
        for turn in range(number):
            for step in steps:
                next(step, None)

    beat = [0]

    def load_tick():
        beat[0] += 1
        for behind, step in enumerate(load_steps[:beat[0]]):
            if beat[0] - behind <= 4:
                next(step, None)

    ticks([weave_steps, table_steps, share_steps])
    spread.start()
    w.mod_grad[...] = jnp.zeros_like(w.mod_grad)
    w.d_cross[...] = jnp.zeros_like(w.d_cross)
    w.dk[...] = jnp.zeros_like(w.dk)
    w.dv[...] = jnp.zeros_like(w.dv)
    row, column = iota((SPAN, SPAN), 0), iota((SPAN, SPAN), 1)
    w.corner[...] = jnp.where(((row < BLOCK) == (column < BLOCK)) & (row > column), -1e30, 0.0)
    ticks([weave_steps, table_steps])
    ticks(load_steps)
    ticks([table_steps, share_steps, weave_steps])
    ticks([table_steps, weave_steps], 6)
    block_bias(aux_row(w.aux, place.served, STEPS + 1), w.bias, blocks)
    read_modulation(w.aux, w.timestep[0].astype(F32), w.mod, wide)
    read_modulation(w.aux, aux_row(w.aux, place.served, STEPS)[0:1, 0:1], w.mod_served, wide)

    def project(block):
        share.arrive(block)
        for half in range(halves):
            w.project(block * halves + half)

    project(blk)
    project(place.far)
    load_tick()
    ticks([share_steps])
    project(place.near)
    ticks([share_steps])
    load_tick()
    project(place.opposite)

    def attended_copy(tile, pair, here):
        there = w.gathered.at[span(tile % halves), pl.ds(pl.multiple_of(pair * 128, 128), 128)]
        to_leaf, to_blk = (leaf, place.near) if here else (place.served, tile // halves)
        return remote(w.attended.at[span(tile), :], there, w.a_send.at[tile], w.a_recv.at[pair * halves + tile % halves], to_leaf, to_blk)

    def mine_too(tile):
        return (place.served == leaf) & (blk == tile // halves)

    for tile in range(tiles):
        w.attend(tile)
        away = jnp.logical_not(mine_too(tile))
        pl.when(away)(lambda tile=tile: attended_copy(tile, place.pair, False).start())

        def keep(tile=tile):
            w.gathered[span(tile % halves), own_lanes] = w.attended[span(tile), :]

        pl.when(jnp.logical_not(away))(keep)
        if tile in (tiles - 4, tiles - 1):
            load_tick()
    spread.arrive()
    load_tick()
    w.cross_keys()
    for pair in range(4):
        for half in range(halves):
            other = jnp.logical_not(place.main & (place.pair == pair))
            pl.when(other)(lambda pair=pair, half=half: attended_copy(half, pair, True).wait_recv())
    for half in range(halves):
        w.middle(half)
        load_tick()
    late.wait()
    for step in range(2):
        load_tick()
    loop(FF // SPAN, w.hidden)
    for job in loads + [weave, table, share, spread]:
        job.finish()

    def writer(*outs):
        def store(there, value):
            start = 0
            for out, at, width in outs:
                out[there, at:at + width] = value[:, start:start + width]
                start += width

        return store

    writers = [
        writer((w.g_out, 0, D // 2)), writer((w.g_out, D // 2, D // 2)),
        writer((w.g_in, 0, FF // 2)), writer((w.g_in, FF // 2, FF // 2)),
        writer((w.g_o, 0, D), (w.g_cq, 0, D)), writer((w.g_ckv, 0, 2 * D), (w.g_co, 0, D)),
    ]
    sums = []
    for n, (total, height, cut) in enumerate(
        [(w.grad_w_out, FF // count, cut) for cut in LAST] + [(w.grad_pack, each, cut) for cut in PACKED[2:] + PACKED[:2]]
    ):
        sums.append(Reduce(place, total, height, slice(*cut), writers[n], [refs[f"box{n}_{k}"] for k in range(4)],
                           w.r_send.at[n], w.r_recv.at[n], n < 2))
    out0, out1, in0, in1, cross0, cross1 = sum_steps = [job.steps() for job in sums]
    ticks([out0, out1, in0, in1])
    loop(halves, w.finish_forward)
    give("mixed")
    ticks([out0, out1])
    loop(halves, w.back_three)
    ticks([out0])
    w.grad_into(4 * D, w.cross_out, w.db)
    loop(halves, w.back_cross)

    def da_copy(src, pair):
        return remote(w.d_attn.at[:, pair * 128:pair * 128 + 128], w.d_att_all.at[rows_of(src, rows), :],
                      w.d_send.at[pair], w.d_recv.at[src], 2 * place.z + pair % 2, 2 * place.core + pair // 2)

    def stays(pair):
        return place.main & (place.pair == pair)

    for pair in range(4):
        pl.when(jnp.logical_not(stays(pair)))(lambda pair=pair: da_copy(blk, pair).start())

    def keep_da():
        w.d_att_all[rows_of(blk, rows), :] = w.d_attn[:, own_lanes]

    pl.when(place.main)(keep_da)
    ticks([out1, in0, in1])
    w.grad_into(0, w.gathered, w.db1)
    w.grad_into(D, w.h2, w.dcq)
    low_cross = w.d_cross[...].astype(BF)
    for step in range(2 * D // SPAN):
        columns = slice(2 * D + step * SPAN, 2 * D + (step + 1) * SPAN)
        w.grad_pack[:, columns] = dot_tn(w.source_all[...], low_cross[:, step * SPAN:(step + 1) * SPAN]).astype(BF)
    w.source_part[...] = dot_nt(low_cross, w.w_ckv)
    settle = Settle(place, w.source_part, w.g_encoded, w.settle_box, w.settle_send, w.settle_recv)
    settle_steps = settle.steps()
    ticks([cross0, cross1, settle_steps, out0, out1, in0])
    for src in range(4):
        pl.when(jnp.logical_not(place.main & (blk == src)))(lambda src=src: da_copy(src, 0).wait_recv())

    tree_sum = TreeReduce(place, w.dh1_part, w.from_core, w.from_chip, w.dh1_box, w.h_send, w.h_core, w.h_chip, w.h_recv)
    plan = [
        (tiles - 1, [cross0, settle_steps, in1]), (tiles - 2, [out0, cross1]), (tiles - 3, [cross0, out1]),
        (tiles - 4, [in0, cross1]), (tiles - 5, [in1]), (tiles - 6, [cross0]),
    ]
    for tile in range(tiles - 1, -1, -1):
        w.attend_back(tile)
        tree_sum.offer(tile)
        if tile + 1 < tiles:
            tree_sum.collect(tile + 1)
        if tile + 3 < tiles:
            tree_sum.forward(tile + 3)
        for when, steps in plan:
            if when == tile:
                ticks(steps)
    tree_sum.collect(0)
    for tile in (2, 1, 0):
        tree_sum.forward(tile)

    def pair_grad(step):
        w.grad_pair[span(step), :] = dot_tn(w.h1[:, span(step)], w.d_pair[...]).astype(BF)

    loop(D // SPAN, pair_grad)
    pair_sum = ReducePair(place, w.grad_pair, w.g_qkv, [refs[f"box_pair{n}"] for n in range(3)], w.rp_send, w.rp_recv)
    pair_steps = pair_sum.steps()
    ticks([pair_steps])
    ticks(sum_steps, 10)
    give("g_encoded", "g_o", "g_cq", "g_ckv", "g_co", "g_in", "g_out")
    ticks([pair_steps])

    def last(half):
        tree_sum.arrive(half)
        here = span(half)
        dh1 = w.dh1_box[half].astype(F32)
        unit, root = unit_rows(w.tokens[here, :].astype(F32))
        w.sums(0, dh1, dh1 * unit)
        w.grad_tokens[here, :] = w.dy[here, :] + norm_back(dh1, unit, root, w.mod[0:1, D:2 * D])

    for half in range(halves):
        last(half)
    give("grad_tokens")
    w.payload[...] = table_payload(w.mod_grad[0:1, :], wide, count)
    table_sum = TableSum(place, w.payload, w.table_box, w.table_rows, w.t_send, w.t_recv)
    table_steps = table_sum.steps()
    ticks([table_steps, pair_steps], 10)
    give("g_qkv")

    leaves = levels * 2
    chosen = (iota((leaves, count * 64), 1) == iota((leaves, count * 64), 0) * 256 + STEPS).astype(BF)
    steps_all = dot(chosen, w.aux[...])
    line = iota((64, 128), 0).astype(F32)
    grad_table = jnp.zeros((64, 128), F32)
    for tree_at in range(leaves):
        grad_table = grad_table + jnp.where(line == steps_all[tree_at:tree_at + 1, :], w.table_rows[8 * tree_at:8 * tree_at + 1, :], 0.0)
    w.g_table[...] = grad_table[:STEPS, :wide]
    give("g_table")

    for tile in range(tiles):
        pl.when(jnp.logical_not(mine_too(tile)))(lambda tile=tile: attended_copy(tile, place.pair, False).wait_send())
        tree_sum.finish(tile)
    for pair in range(4):
        pl.when(jnp.logical_not(stays(pair)))(lambda pair=pair: da_copy(blk, pair).wait_send())
    for job in sums + [settle, pair_sum, table_sum]:
        job.finish()
    for copy in given:
        copy.wait()


def copy_kernel(count, refs):
    ins, outs, held, sems = refs[:count], refs[count:2 * count], refs[2 * count:3 * count], refs[3 * count]
    inward = [pltpu.make_async_copy(ins[n], held[n], sems.at[0, n]) for n in range(count)]
    outward = [pltpu.make_async_copy(held[n], outs[n], sems.at[1, n]) for n in range(count)]
    for copy in inward:
        copy.start()
    for copy, then in zip(inward, outward):
        copy.wait()
        then.start()
    for copy in outward:
        copy.wait()


def copy_all(arrays):
    return pl.pallas_call(
        lambda *refs: copy_kernel(len(arrays), refs),
        out_shape=[jax.ShapeDtypeStruct(array.shape, array.dtype) for array in arrays],
        in_specs=[ANY] * len(arrays),
        out_specs=[ANY] * len(arrays),
        scratch_shapes=[pltpu.VMEM(array.shape, array.dtype) for array in arrays] + [pltpu.SemaphoreType.DMA((2, len(arrays)))],
    )(*arrays)


def per_device(tokens, cotangent, encoded, parents, timestep, w_qkv, w_o, w_cq, w_ckv, w_co, w_in, w_out, mod_table):
    levels = lax.axis_size("leaf") // 2
    rows, wide = tokens.shape[0], mod_table.shape[1]
    blocks = parents.shape[1]
    tree = blocks * BLOCK
    ins = (tokens, cotangent, encoded, parents, timestep, w_qkv, w_o, w_cq, w_ckv, w_co, w_in, w_out, mod_table)
    scratch = layer_scratch(rows, tree, blocks, levels, wide)
    out = lambda like: jax.ShapeDtypeStruct(like.shape, F32)
    names = INS + tuple("o_" + name for name in OUTS) + tuple(scratch)
    return copy_all(pl.pallas_call(
        lambda *refs: layer_kernel(levels, wide, names, refs),
        out_shape=[jax.ShapeDtypeStruct((rows, D), BF), out(tokens), out(encoded)]
        + [out(weight) for weight in (w_qkv, w_o, w_cq, w_ckv, w_co, w_in, w_out, mod_table)],
        in_specs=[SMEM if name in ("parents", "timestep") else VMEM if name == "i_table" else ANY for name in INS],
        out_specs=[ANY] * len(OUTS),
        scratch_shapes=list(scratch.values()),
        compiler_params=pltpu.CompilerParams(collective_id=0, has_side_effects=True, vmem_limit_bytes=(64 << 20) - (64 << 10)),
    )(*ins))


def solution(mesh):
    fits = mesh.shape["blk"] == 4 and mesh.shape["leaf"] == 8
    return jax.shard_map(
        per_device if fits else generic_device,
        mesh=mesh,
        in_specs=(
            P(("leaf", "blk"), None),
            P(("leaf", "blk"), None),
            P(("leaf", "blk"), None),
            P("leaf", None),
            P("leaf"),
            P(("leaf", "blk"), None),
            P(("leaf", "blk"), None),
            P(("leaf", "blk"), None),
            P(("leaf", "blk"), None),
            P(("leaf", "blk"), None),
            P(("leaf", "blk"), None),
            P(("leaf", "blk"), None),
            P(None, ("leaf", "blk")),
        ),
        out_specs=(
            P(("leaf", "blk"), None),
            P(("leaf", "blk"), None),
            P(("leaf", "blk"), None),
            P(("leaf", "blk"), None),
            P(("leaf", "blk"), None),
            P(("leaf", "blk"), None),
            P(("leaf", "blk"), None),
            P(("leaf", "blk"), None),
            P(("leaf", "blk"), None),
            P(("leaf", "blk"), None),
            P(None, ("leaf", "blk")),
        ),
        check_vma=False,
    )
```

```python
import functools

import jax
import jax.numpy as jnp
from jax import lax
from jax.experimental import pallas as pl
from jax.experimental.pallas import tpu as pltpu
from jax.sharding import PartitionSpec as P

D = 512
HEADS = 8
HEAD = 64
BLOCK = 128
FF = 2048
ENC = 64
STEPS = 50


PRECISE = lax.Precision.HIGHEST
MASKED = -1e30


def ancestors(parent_row):
    count = parent_row.shape[0]
    indices = jnp.arange(count, dtype=jnp.int32)
    reach_map = (indices[:, None] == indices[None, :]).astype(jnp.float32)
    reach_map = jnp.minimum(
        reach_map + (parent_row[:, None] == indices[None, :]).astype(jnp.float32), 1.0
    )
    for rounds in range(max(1, (count - 1).bit_length())):
        reach_map = jnp.minimum(jnp.dot(reach_map, reach_map, precision=PRECISE), 1.0)
    return reach_map


def normalize(values, shift, scaling):
    centred = values - jnp.mean(values, axis=-1, keepdims=True)
    spread = jnp.mean(centred * centred, axis=-1, keepdims=True)
    return centred * lax.rsqrt(spread + 1e-05) * (1.0 + scaling) + shift


def span_link(reach_rows, span):
    return lax.dynamic_slice_in_dim(reach_rows, span * 4, 4, 1)


def span_reached(reach_rows, span):
    return jnp.max(span_link(reach_rows, span)) > 0.5


def span_mask(reach_rows, first_block, span, row_count, width):
    query_index = jnp.arange(row_count, dtype=jnp.int32)
    key_index = jnp.arange(width, dtype=jnp.int32)
    query_block = first_block + query_index // BLOCK
    key_block = span * 4 + key_index // BLOCK
    link = span_link(reach_rows, span)
    link = jnp.repeat(jnp.repeat(link, BLOCK, axis=0), BLOCK, axis=1)
    same = query_block[:, None] == key_block[None, :]
    return (link > 0.5) & (
        jnp.logical_not(same) | (key_index[None, :] % BLOCK <= query_index[:, None] % BLOCK)
    )


def scores_of(queries, key_rows, allowed):
    raw = jnp.einsum(
        "qhd,khd->hqk", queries, key_rows, preferred_element_type=jnp.float32
    ) * HEAD ** (-0.5)
    return jnp.where(allowed[None], raw, MASKED)


def split_spans(keys, values):
    width = 4 * BLOCK
    count = keys.shape[0] // width
    return (
        jnp.arange(count, dtype=jnp.int32),
        keys.reshape(count, width, HEADS, HEAD),
        values.reshape(count, width, HEADS, HEAD),
    )


def tree_forward_attention(queries, keys, values, reach_rows, first_block):
    row_count = queries.shape[0]
    width = 4 * BLOCK
    spans, key_spans, value_spans = split_spans(keys, values)

    def stats(carry, item):
        span, key_rows = item

        def stats_visit(state):
            top, total = state
            allowed = span_mask(reach_rows, first_block, span, row_count, width)
            score = scores_of(queries, key_rows, allowed)
            new_top = jnp.maximum(top, jnp.max(score, axis=-1))
            weight = jnp.where(allowed[None], jnp.exp(score - new_top[..., None]), 0.0)
            return (new_top, total * jnp.exp(top - new_top) + jnp.sum(weight, axis=-1))

        return (
            lax.cond(span_reached(reach_rows, span), stats_visit, lambda state: state, carry),
            None,
        )

    start = (
        jnp.full((HEADS, row_count), MASKED, jnp.float32),
        jnp.zeros((HEADS, row_count), jnp.float32),
    )
    (top, total), unused = lax.scan(stats, start, (spans, key_spans))
    log_total = top + jnp.log(total)

    def collect(accum, item):
        span, key_rows, value_rows = item

        def collect_visit(current):
            allowed = span_mask(reach_rows, first_block, span, row_count, width)
            weight = jnp.where(
                allowed[None],
                jnp.exp(scores_of(queries, key_rows, allowed) - log_total[..., None]),
                0.0,
            )
            return current + jnp.einsum(
                "hqk,khd->qhd",
                weight.astype(jnp.bfloat16),
                value_rows,
                preferred_element_type=jnp.float32,
            )

        return (
            lax.cond(span_reached(reach_rows, span), collect_visit, lambda current: current, accum),
            None,
        )

    attended, unused = lax.scan(
        collect, jnp.zeros((row_count, HEADS, HEAD), jnp.float32), (spans, key_spans, value_spans)
    )
    return (attended, log_total)


def tree_backward_attention(queries, keys, values, reach_rows, first_block, log_total, grad_attn):
    row_count = queries.shape[0]
    width = 4 * BLOCK
    spans, key_spans, value_spans = split_spans(keys, values)

    def probs_of(span, key_rows):
        allowed = span_mask(reach_rows, first_block, span, row_count, width)
        return jnp.where(
            allowed[None],
            jnp.exp(scores_of(queries, key_rows, allowed) - log_total[..., None]),
            0.0,
        )

    def inner_pass(total, item):
        span, key_rows, value_rows = item

        def inner_visit(current):
            weight = probs_of(span, key_rows)
            d_weight = jnp.einsum(
                "qhd,khd->hqk", grad_attn, value_rows, preferred_element_type=jnp.float32
            )
            return current + jnp.sum(weight * d_weight, axis=-1)

        return (
            lax.cond(span_reached(reach_rows, span), inner_visit, lambda current: current, total),
            None,
        )

    delta, unused = lax.scan(
        inner_pass, jnp.zeros((HEADS, row_count), jnp.float32), (spans, key_spans, value_spans)
    )

    def grad_pass(d_queries, item):
        span, key_rows, value_rows = item

        def grad_visit(current):
            weight = probs_of(span, key_rows)
            d_weight = jnp.einsum(
                "qhd,khd->hqk", grad_attn, value_rows, preferred_element_type=jnp.float32
            )
            d_score = (weight * (d_weight - delta[..., None])).astype(jnp.bfloat16)
            current = current + jnp.einsum(
                "hqk,khd->qhd", d_score, key_rows, preferred_element_type=jnp.float32
            )
            d_keys = jnp.einsum(
                "hqk,qhd->khd", d_score, queries, preferred_element_type=jnp.float32
            ) * HEAD ** (-0.5)
            d_values = jnp.einsum(
                "hqk,qhd->khd",
                weight.astype(jnp.bfloat16),
                grad_attn,
                preferred_element_type=jnp.float32,
            )
            return (
                current,
                jnp.concatenate((d_keys.reshape(width, D), d_values.reshape(width, D)), axis=1),
            )

        def skip(current):
            return (current, jnp.zeros((width, 2 * D), jnp.float32))

        return lax.cond(span_reached(reach_rows, span), grad_visit, skip, d_queries)

    d_queries, terms = lax.scan(
        grad_pass, jnp.zeros((row_count, HEADS, HEAD), jnp.float32), (spans, key_spans, value_spans)
    )
    return (d_queries * HEAD ** (-0.5), terms.reshape(-1, 2 * D))


def generic_device(
    tokens,
    cotangent,
    encoded,
    parents,
    timestep,
    w_qkv,
    w_o,
    w_cq,
    w_ckv,
    w_co,
    w_in,
    w_out,
    mod_table,
):
    gathered = (
        lax.all_gather(w_qkv, ("leaf", "blk"), axis=0, tiled=True),
        lax.all_gather(w_o, ("leaf", "blk"), axis=0, tiled=True),
        lax.all_gather(w_cq, ("leaf", "blk"), axis=0, tiled=True),
        lax.all_gather(w_ckv, ("leaf", "blk"), axis=0, tiled=True),
        lax.all_gather(w_co, ("leaf", "blk"), axis=0, tiled=True),
        lax.all_gather(w_in, ("leaf", "blk"), axis=0, tiled=True),
        lax.all_gather(w_out, ("leaf", "blk"), axis=0, tiled=True),
        lax.all_gather(mod_table, ("leaf", "blk"), axis=1, tiled=True),
    )
    g_qkv, g_o, g_cq, g_ckv, g_co, g_in, g_out, g_table = gathered
    select = (jnp.arange(STEPS, dtype=jnp.int32) == timestep[0]).astype(jnp.float32)
    modulate = jnp.dot(
        select.astype(jnp.bfloat16)[None, :], g_table, preferred_element_type=jnp.float32
    )[0]
    pieces = [modulate[i * D : (i + 1) * D] for i in range(6)]
    inputs = tokens.astype(jnp.float32)
    row_count = tokens.shape[0]
    local_blocks = row_count // BLOCK
    first_block = lax.axis_index("blk") * local_blocks
    reach_map = ancestors(parents[0])
    reach_rows = lax.dynamic_slice_in_dim(reach_map, first_block, local_blocks, 0)
    scaling = HEAD ** (-0.5)
    normed_one, pull_one = jax.vjp(normalize, inputs, pieces[0], pieces[1])
    h_first = normed_one.astype(jnp.bfloat16)
    projected = jnp.dot(h_first, g_qkv, preferred_element_type=jnp.float32).astype(jnp.bfloat16)
    queries = projected[:, :D].reshape(row_count, HEADS, HEAD)
    keys, values = (
        lax.all_gather(projected[:, D : 2 * D], "blk", axis=0, tiled=True),
        lax.all_gather(projected[:, 2 * D :], "blk", axis=0, tiled=True),
    )
    attended, log_total = tree_forward_attention(queries, keys, values, reach_rows, first_block)
    attn_low = attended.reshape(row_count, D).astype(jnp.bfloat16)
    middle_one = inputs + jnp.dot(attn_low, g_o, preferred_element_type=jnp.float32)
    normed_two, pull_two = jax.vjp(normalize, middle_one, pieces[2], pieces[3])
    h_second = normed_two.astype(jnp.bfloat16)
    cross_q = (
        jnp.dot(h_second, g_cq, preferred_element_type=jnp.float32)
        .astype(jnp.bfloat16)
        .reshape(row_count, HEADS, HEAD)
    )
    source_local = jnp.dot(encoded, g_ckv, preferred_element_type=jnp.float32).astype(jnp.bfloat16)
    source_all = lax.all_gather(source_local, "blk", axis=0, tiled=True)
    cross_k = source_all[:, :D].reshape(-1, HEADS, HEAD)
    cross_v = source_all[:, D:].reshape(-1, HEADS, HEAD)
    cross_raw = (
        jnp.einsum("qhd,khd->hqk", cross_q, cross_k, preferred_element_type=jnp.float32) * scaling
    )
    cross_prob = jax.nn.softmax(cross_raw, axis=-1)
    cross_low = cross_prob.astype(jnp.bfloat16)
    cross_out = (
        jnp.einsum("hqk,khd->qhd", cross_low, cross_v, preferred_element_type=jnp.float32)
        .reshape(row_count, D)
        .astype(jnp.bfloat16)
    )
    middle_two = middle_one + jnp.dot(cross_out, g_co, preferred_element_type=jnp.float32)
    normed_three, pull_three = jax.vjp(normalize, middle_two, pieces[4], pieces[5])
    h_third = normed_three.astype(jnp.bfloat16)
    hidden_pre = jnp.dot(h_third, g_in, preferred_element_type=jnp.float32)
    activated, pull_gelu = jax.vjp(
        lambda values_in: jax.nn.gelu(values_in, approximate=True), hidden_pre
    )
    act_low = activated.astype(jnp.bfloat16)
    result = middle_two + jnp.dot(act_low, g_out, preferred_element_type=jnp.float32)
    mixed_out = result.astype(jnp.bfloat16)
    back_weights = (
        lax.all_gather(w_qkv, ("leaf", "blk"), axis=0, tiled=True),
        lax.all_gather(w_o, ("leaf", "blk"), axis=0, tiled=True),
        lax.all_gather(w_cq, ("leaf", "blk"), axis=0, tiled=True),
        lax.all_gather(w_ckv, ("leaf", "blk"), axis=0, tiled=True),
        lax.all_gather(w_co, ("leaf", "blk"), axis=0, tiled=True),
        lax.all_gather(w_in, ("leaf", "blk"), axis=0, tiled=True),
        lax.all_gather(w_out, ("leaf", "blk"), axis=0, tiled=True),
        lax.all_gather(mod_table, ("leaf", "blk"), axis=1, tiled=True),
    )
    b_qkv, b_o, b_cq, b_ckv, b_co, b_in, b_out = back_weights[:7]
    d_act = jnp.dot(cotangent, b_out.T, preferred_element_type=jnp.float32)
    d_hidden = pull_gelu(d_act)[0].astype(jnp.bfloat16)
    grad_out_w = jnp.dot(act_low.T, cotangent, preferred_element_type=jnp.float32)
    grad_in_w = jnp.dot(h_third.T, d_hidden, preferred_element_type=jnp.float32)
    d_h_third = jnp.dot(d_hidden, b_in.T, preferred_element_type=jnp.float32)
    d_middle_part, d_shift_three, d_scale_three = pull_three(d_h_third)
    d_middle_two = cotangent.astype(jnp.float32) + d_middle_part
    d_branch_two = d_middle_two.astype(jnp.bfloat16)
    grad_co_w = jnp.dot(cross_out.T, d_branch_two, preferred_element_type=jnp.float32)
    d_cross_out = (
        jnp.dot(d_branch_two, b_co.T, preferred_element_type=jnp.float32)
        .astype(jnp.bfloat16)
        .reshape(row_count, HEADS, HEAD)
    )
    d_cross_prob = jnp.einsum(
        "qhd,khd->hqk", d_cross_out, cross_v, preferred_element_type=jnp.float32
    )
    d_cross_raw = (
        cross_prob * (d_cross_prob - jnp.sum(cross_prob * d_cross_prob, axis=-1, keepdims=True))
    ).astype(jnp.bfloat16)
    d_cross_q = (
        (
            jnp.einsum("hqk,khd->qhd", d_cross_raw, cross_k, preferred_element_type=jnp.float32)
            * scaling
        )
        .reshape(row_count, D)
        .astype(jnp.bfloat16)
    )
    d_cross_k = (
        jnp.einsum("hqk,qhd->khd", d_cross_raw, cross_q, preferred_element_type=jnp.float32)
        * scaling
    )
    d_cross_v = jnp.einsum(
        "hqk,qhd->khd", cross_low, d_cross_out, preferred_element_type=jnp.float32
    )
    source_terms = jnp.concatenate((d_cross_k.reshape(-1, D), d_cross_v.reshape(-1, D)), axis=1)
    d_source = lax.psum_scatter(
        source_terms.astype(jnp.bfloat16), "blk", scatter_dimension=0, tiled=True
    )
    grad_ckv_w = jnp.dot(encoded.T, d_source, preferred_element_type=jnp.float32)
    d_encoded = jnp.dot(d_source, b_ckv.T, preferred_element_type=jnp.float32)
    grad_cq_w = jnp.dot(h_second.T, d_cross_q, preferred_element_type=jnp.float32)
    d_h_second = jnp.dot(d_cross_q, b_cq.T, preferred_element_type=jnp.float32)
    d_middle_part, d_shift_two, d_scale_two = pull_two(d_h_second)
    d_middle_one = d_middle_two + d_middle_part
    d_branch_one = d_middle_one.astype(jnp.bfloat16)
    grad_o_w = jnp.dot(attn_low.T, d_branch_one, preferred_element_type=jnp.float32)
    d_attn = (
        jnp.dot(d_branch_one, b_o.T, preferred_element_type=jnp.float32)
        .astype(jnp.bfloat16)
        .reshape(row_count, HEADS, HEAD)
    )
    keys_back, values_back = (
        lax.all_gather(projected[:, D : 2 * D], "blk", axis=0, tiled=True),
        lax.all_gather(projected[:, 2 * D :], "blk", axis=0, tiled=True),
    )
    d_queries, key_terms = tree_backward_attention(
        queries, keys_back, values_back, reach_rows, first_block, log_total, d_attn
    )
    d_key_value = lax.psum_scatter(
        key_terms.astype(jnp.bfloat16), "blk", scatter_dimension=0, tiled=True
    ).astype(jnp.float32)
    d_projected = jnp.concatenate((d_queries.reshape(row_count, D), d_key_value), axis=1).astype(
        jnp.bfloat16
    )
    grad_qkv_w = jnp.dot(h_first.T, d_projected, preferred_element_type=jnp.float32)
    d_h_first = jnp.dot(d_projected, b_qkv.T, preferred_element_type=jnp.float32)
    d_input_part, d_shift_one, d_scale_one = pull_one(d_h_first)
    d_tokens = d_middle_one + d_input_part
    d_modulate = jnp.concatenate(
        (d_shift_one, d_scale_one, d_shift_two, d_scale_two, d_shift_three, d_scale_three)
    )
    grad_table_w = select[:, None] * d_modulate[None, :]
    gradients = (
        lax.psum_scatter(grad_qkv_w, ("leaf", "blk"), scatter_dimension=0, tiled=True),
        lax.psum_scatter(grad_o_w, ("leaf", "blk"), scatter_dimension=0, tiled=True),
        lax.psum_scatter(grad_cq_w, ("leaf", "blk"), scatter_dimension=0, tiled=True),
        lax.psum_scatter(grad_ckv_w, ("leaf", "blk"), scatter_dimension=0, tiled=True),
        lax.psum_scatter(grad_co_w, ("leaf", "blk"), scatter_dimension=0, tiled=True),
        lax.psum_scatter(grad_in_w, ("leaf", "blk"), scatter_dimension=0, tiled=True),
        lax.psum_scatter(grad_out_w, ("leaf", "blk"), scatter_dimension=0, tiled=True),
        lax.psum_scatter(grad_table_w, ("leaf", "blk"), scatter_dimension=1, tiled=True),
    )
    return (
        mixed_out,
        d_tokens,
        d_encoded,
        gradients[0],
        gradients[1],
        gradients[2],
        gradients[3],
        gradients[4],
        gradients[5],
        gradients[6],
        gradients[7],
    )


MESH = pl.DeviceIdType.MESH
BF = jnp.bfloat16
F32 = jnp.float32


class Place:
    def __init__(self, levels):
        leaf = lax.axis_index("leaf")
        blk = lax.axis_index("blk")
        self.levels = levels
        self.leaf = leaf
        self.blk = blk
        self.z = leaf // 2
        self.core = leaf % 2
        self.near = blk + 1 - 2 * (blk % 2)
        self.far = (blk + 2) % 4
        self.first = self.core * self.near + (1 - self.core) * self.far
        self.second = self.core * self.far + (1 - self.core) * self.near
        self.opposite = 3 - blk
        self.sibling = self.z * 2 + 1 - self.core
        self.side = blk // 2
        self.served = self.z * 2 + self.side
        self.pair = blk % 2 * 2 + self.core
        self.main = self.side == self.core
        self.line = [(leaf + 2 * step) % (2 * levels) for step in range(1, levels)]

    def greet(self):
        barrier = pltpu.get_barrier_semaphore()

        count = self.levels * 2

        def hello(leaf, blk):
            pl.semaphore_signal(barrier, inc=1, device_id=(leaf, blk), device_id_type=MESH)

        for blk in (self.near, self.far, self.opposite):
            hello(self.leaf, blk)
            hello(self.sibling, blk)
        for step in range(1, count):
            hello((self.leaf + step) % count, self.blk)
        pl.semaphore_wait(barrier, count + 5)


def remote(src, dst, send, recv, leaf, blk):
    return pltpu.make_async_remote_copy(
        src_ref=src, dst_ref=dst, send_sem=send, recv_sem=recv,
        device_id=(leaf, blk), device_id_type=MESH,
    )


def rows_of(start, count):
    return pl.ds(pl.multiple_of(start * count, count), count)


class Gather:
    def __init__(self, place, full, rows, columns, send_sem, recv_sem, fixed=False):
        self.place, self.full, self.rows, self.columns = place, full, rows, columns
        self.send_sem, self.recv_sem = send_sem, recv_sem
        self.sent = []
        self.first = place.near if fixed else place.first
        self.second = place.far if fixed else place.second

    def build(self, leaf, blk, to_leaf, to_blk, number):
        there = self.full.at[rows_of(leaf * 4 + blk, self.rows), self.columns]
        return remote(there, there, self.send_sem.at[number], self.recv_sem.at[leaf * 4 + blk], to_leaf, to_blk)

    def push(self, leaf, blk, *targets):
        for to_leaf, to_blk in targets:
            copy = self.build(leaf, blk, to_leaf, to_blk, len(self.sent))
            copy.start()
            self.sent.append(copy)

    def arrive(self, leaf, blk):
        p = self.place
        self.build(leaf, blk, p.leaf, self.second, 0).wait_recv()

    def steps(self):
        p = self.place
        sibling, second = (p.sibling, p.blk), (p.leaf, self.second)
        line = [(leaf, p.blk) for leaf in p.line]
        self.push(p.leaf, p.blk, (p.leaf, self.first), *line, sibling)
        yield
        self.arrive(p.leaf, self.first)
        self.push(p.leaf, self.first, *line, sibling)
        yield
        self.push(p.leaf, p.blk, second)
        self.push(p.leaf, self.first, second)
        for leaf in p.line:
            self.arrive(leaf, p.blk)
            self.push(leaf, p.blk, second, sibling)
        yield
        for leaf in p.line:
            self.arrive(leaf, self.first)
            self.push(leaf, self.first, second, sibling)
        yield
        for leaf in (p.leaf, *p.line):
            for blk in (self.second, p.opposite):
                self.arrive(leaf, blk)
                self.push(leaf, blk, sibling)
        yield
        for level in range(p.levels):
            for blk in range(4):
                self.arrive(2 * level + 1 - p.core, blk)
        yield

    def finish(self):
        for copy in self.sent:
            copy.wait_send()

    @staticmethod
    def sends(levels):
        return 8 * levels


class Spread:
    def __init__(self, place, full, rows, send_sem, recv_sem):
        self.place, self.full, self.rows = place, full, rows
        self.send_sem, self.recv_sem = send_sem, recv_sem

    def build(self, blk, to_blk, number):
        there = self.full.at[rows_of(blk, self.rows), :]
        return remote(there, there, self.send_sem.at[number], self.recv_sem.at[blk], self.place.leaf, to_blk)

    def start(self):
        p = self.place
        self.copies = [self.build(p.blk, to, n) for n, to in enumerate((p.near, p.far, p.opposite))]
        for copy in self.copies:
            copy.start()

    def arrive(self):
        p = self.place
        for blk in (p.near, p.far, p.opposite):
            self.build(blk, p.near, 0).wait_recv()

    def finish(self):
        for copy in self.copies:
            copy.wait_send()


class Reduce:
    def __init__(self, place, total, rows, columns, store, boxes, send_sem, recv_sem, line_last):
        self.place, self.total, self.rows, self.columns, self.store = place, total, rows, columns, store
        self.from_sibling, self.from_second, self.from_line, self.from_first = boxes
        self.send_sem, self.recv_sem = send_sem, recv_sem
        self.line_last = line_last
        self.sent = []

    @staticmethod
    def slots(levels):
        return 6 * levels

    @staticmethod
    def boxes(levels, rows, width, kind, line_last):
        line, first = (levels, levels) if line_last else (2 * levels, 1)
        return [pltpu.VMEM((slots * rows, width), kind) for slots in (4 * levels, 2 * levels, line, first)]

    def here(self, leaf, blk):
        return (leaf * 4 + blk) * self.rows

    def part(self, leaf, blk, count=1):
        return self.total.at[pl.ds(pl.multiple_of(self.here(leaf, blk), self.rows), self.rows * count), self.columns]

    def copy(self, src, box, position, count, number, leaf, blk, sender=None):
        there = box.at[pl.ds(pl.multiple_of(position * self.rows, self.rows), self.rows * count), :]
        sender = number if sender is None else sender
        return remote(there if src is None else src, there, self.send_sem.at[sender], self.recv_sem.at[number], leaf, blk)

    def send(self, *parts):
        copy = self.copy(*parts)
        copy.start()
        self.sent.append(copy)

    def arrived(self, box, position, count, number):
        self.copy(None, box, position, count, number, self.place.leaf, self.place.first).wait_recv()

    def value(self, start, *sources):
        unit = pl.ds(pl.multiple_of(start, 16), 16)
        value = self.total[unit, self.columns].astype(F32)
        for box, position in sources:
            value = value + box[pl.ds(pl.multiple_of(position, 16), 16), :].astype(F32)
        return unit, value

    def add(self, leaf, blk, *sources, count=1):
        def one(step):
            unit, value = self.value(self.here(leaf, blk) + 16 * step, *[(box, slot * self.rows + 16 * step) for box, slot in sources])
            self.total[unit, self.columns] = value.astype(self.total.dtype)

        loop(count * self.rows // 16, one)

    def give(self, *sources):
        for step in range(self.rows // 16):
            unit, value = self.value(self.here(self.place.leaf, self.place.blk) + 16 * step,
                                     *[(box, slot * self.rows + 16 * step) for box, slot in sources])
            self.store(pl.ds(16 * step, 16), value)

    def steps(self):
        p = self.place
        levels = p.levels
        for level in range(levels):
            self.send(self.part(2 * level + 1 - p.core, 0, 4), self.from_sibling, 4 * level, 4, level, p.sibling, p.blk)
        yield
        for level in range(levels):
            self.arrived(self.from_sibling, 4 * level, 4, level)
            leaf = 2 * level + p.core
            self.add(leaf, 0, (self.from_sibling, 4 * level), count=4)
            for which, blk in enumerate((p.second, p.opposite)):
                slot = 2 * level + which
                self.send(self.part(leaf, blk), self.from_second, slot, 1, levels + slot, p.leaf, p.second)
        yield
        for level in range(levels):
            leaf = 2 * level + p.core
            for which, blk in enumerate((p.blk, p.first)):
                slot = 2 * level + which
                self.arrived(self.from_second, slot, 1, levels + slot)
                self.add(leaf, blk, (self.from_second, slot))
                if self.line_last and which == 1:
                    self.send(self.part(leaf, p.first), self.from_first, level, 1, 5 * levels + level, p.leaf, p.first)
        if self.line_last:
            yield
            for level in range(levels):
                self.arrived(self.from_first, level, 1, 5 * levels + level)
                self.add(2 * level + p.core, p.blk, (self.from_first, level))
        shards = (p.blk,) if self.line_last else (p.blk, p.first)
        slots = len(shards)
        for leaf in p.line:
            for which, blk in enumerate(shards):
                self.send(self.part(leaf, blk), self.from_line, slots * p.z + which, 1, 3 * levels + slots * p.z + which,
                          leaf, p.blk, 3 * levels + slots * (leaf // 2) + which)
        yield
        came = []
        for which, blk in enumerate(shards):
            slots_of = [slots * (leaf // 2) + which for leaf in p.line]
            for slot in slots_of:
                self.arrived(self.from_line, slot, 1, 3 * levels + slot)
            came.append([(self.from_line, slot) for slot in slots_of])
        if self.line_last:
            self.give(*came[0])
            yield
            return
        self.add(p.leaf, p.first, *came[1])
        self.send(self.part(p.leaf, p.first), self.from_first, 0, 1, 5 * levels, p.leaf, p.first)
        yield
        self.arrived(self.from_first, 0, 1, 5 * levels)
        self.give(*came[0], (self.from_first, 0))
        yield

    def finish(self):
        for copy in self.sent:
            copy.wait_send()


class GatherLine(Gather):
    def steps(self):
        p = self.place
        sibling, first, second = (p.sibling, p.blk), (p.leaf, self.first), (p.leaf, self.second)
        self.push(p.leaf, p.blk, *[(leaf, p.blk) for leaf in p.line], sibling)
        yield
        self.push(p.leaf, p.blk, first, second)
        for leaf in p.line:
            self.arrive(leaf, p.blk)
            self.push(leaf, p.blk, first, second, sibling)
        yield
        for leaf in (p.leaf, *p.line):
            self.arrive(leaf, self.first)
            self.push(leaf, self.first, second, sibling)
        yield
        for leaf in (p.leaf, *p.line):
            for blk in (self.second, p.opposite):
                self.arrive(leaf, blk)
                self.push(leaf, blk, sibling)
        yield
        for level in range(p.levels):
            for blk in range(4):
                self.arrive(2 * level + 1 - p.core, blk)
        yield


class Share:
    def __init__(self, place, own, full, send_sem, recv_sem):
        self.place, self.own, self.full = place, own, full
        self.rows = own.shape[0]
        self.half = self.rows // 2
        self.send_sem, self.recv_sem = send_sem, recv_sem
        self.sent = []

    def build(self, blk, half, to_leaf, to_blk, number, own=False):
        there = self.full.at[pl.ds(pl.multiple_of(blk * self.rows + half * self.half, self.half), self.half), :]
        src = self.own.at[pl.ds(half * self.half, self.half), :] if own else there
        return remote(src, there, self.send_sem.at[number], self.recv_sem.at[blk * 2 + half], to_leaf, to_blk)

    def wait(self, blk, half):
        self.build(blk, half, self.place.sibling, self.place.blk, 0).wait_recv()

    def push(self, cond, *parts):
        number = len(self.sent)
        pl.when(cond)(lambda: self.build(*parts[:4], number, *parts[4:]).start())
        self.sent.append((cond, parts, number))

    def steps(self):
        p = self.place
        helps = jnp.logical_not(p.main)
        sibling = (p.sibling, p.blk)
        for half in range(2):
            self.push(helps, p.blk, half, p.leaf, p.far, True)
            self.push(p.main, p.blk, half, p.leaf, p.near, True)
        for half in range(2):
            self.push(p.main, p.blk, half, *sibling, True)
        yield
        for half in range(2):
            pl.when(p.main)(lambda half=half: self.wait(p.far, half))
            self.push(p.main, p.far, half, p.leaf, p.near)
            self.push(p.main, p.far, half, *sibling)
        yield
        for blk in (p.near, p.opposite):
            for half in range(2):
                pl.when(p.main)(lambda blk=blk, half=half: self.wait(blk, half))
                self.push(p.main, blk, half, *sibling)
            yield

    def arrive(self, blk):
        for half in range(2):
            pl.when(jnp.logical_not(self.place.main))(lambda half=half: self.wait(blk, half))

    def finish(self):
        for cond, parts, number in self.sent:
            pl.when(cond)(lambda parts=parts, number=number: self.build(*parts[:4], number, *parts[4:]).wait_send())

    sends = 14


class GatherPair:
    def __init__(self, place, held, full, transit, send_sem, recv_sem):
        self.place, self.held, self.full, self.transit = place, held, full, transit
        self.rows, self.width = held.shape[0] // place.levels, full.shape[1]
        self.send_sem, self.recv_sem = send_sem, recv_sem
        self.sent = []

    def start(self, copy):
        copy.start()
        self.sent.append(copy)

    def send_of(self):
        return self.send_sem.at[len(self.sent)]

    def columns(self, level, pair):
        return self.held.at[rows_of(level, self.rows), pl.ds(pl.multiple_of(pair * self.width, 128), self.width)]

    def along(self, level, to_leaf):
        there = self.held.at[rows_of(level, self.rows), :]
        return remote(there, there, self.send_of(), self.recv_sem.at[level], to_leaf, self.place.blk)

    def target(self, level, blk, other):
        p = self.place
        if other:
            return self.transit.at[rows_of(level * 4 + blk, self.rows), :]
        return self.full.at[rows_of((2 * level + p.core) * 4 + blk, self.rows), :]

    def piece(self, level, src_blk, to_blk, other):
        p = self.place
        src = self.columns(level, 2 * (to_blk % 2) + (1 - p.core if other else p.core))
        number = p.levels + (level * 4 + src_blk) * 2 + other
        return remote(src, self.target(level, src_blk, other), self.send_of(), self.recv_sem.at[number], p.leaf, to_blk)

    def hand(self, level, core):
        p = self.place
        there = self.full.at[rows_of(2 * level + core, 4 * self.rows), :]
        return remote(self.transit.at[rows_of(level, 4 * self.rows), :], there, self.send_of(),
                      self.recv_sem.at[9 * p.levels + level], p.sibling, p.blk)

    def offer(self, level):
        p = self.place
        for to_blk in (p.near, p.far, p.opposite):
            for other in range(2):
                self.start(self.piece(level, p.blk, to_blk, other))
        for other in range(2):
            pair = 2 * (p.blk % 2) + (1 - p.core if other else p.core)
            self.target(level, p.blk, other)[...] = self.columns(level, pair)[...]

    def steps(self):
        p = self.place
        for to_leaf in p.line:
            self.start(self.along(p.z, to_leaf))
        self.offer(p.z)
        yield
        for leaf in p.line:
            self.along(leaf // 2, p.sibling).wait_recv()
            self.offer(leaf // 2)
        yield
        for level in (p.z, *[leaf // 2 for leaf in p.line]):
            for blk in (p.near, p.far, p.opposite):
                for other in range(2):
                    self.piece(level, blk, p.near, other).wait_recv()
            self.start(self.hand(level, p.core))
        yield
        for level in range(p.levels):
            self.hand(level, 1 - p.core).wait_recv()
        yield

    def finish(self):
        for copy in self.sent:
            copy.wait_send()

    @staticmethod
    def sends(levels):
        return levels - 1 + 7 * levels

    @staticmethod
    def receives(levels):
        return 10 * levels


class ReducePair:
    def __init__(self, place, total, out, boxes, send_sem, recv_sem):
        self.place, self.total, self.out = place, total, out
        self.rows = total.shape[0] // (place.levels * 8)
        self.from_far, self.from_line, self.from_pair = boxes
        self.send_sem, self.recv_sem = send_sem, recv_sem
        self.sent = []

    @staticmethod
    def slots(levels):
        return 4 * levels + 4

    @staticmethod
    def boxes(levels, rows, width, kind):
        return [pltpu.VMEM((levels * 4 * rows, width), kind) for n in range(2)] + [pltpu.VMEM((4 * rows, width), kind)]

    def build(self, src, box, slot, rows, number, leaf, blk):
        there = box.at[rows_of(slot, rows), :]
        return remote(there if src is None else src, there, self.send_sem.at[len(self.sent)], self.recv_sem.at[number], leaf, blk)

    def send(self, *parts):
        copy = self.build(*parts)
        copy.start()
        self.sent.append(copy)

    def arrived(self, box, slot, rows, number):
        self.build(None, box, slot, rows, number, self.place.sibling, self.place.blk).wait_recv()

    def twin(self, leaf, side):
        return rows_of(leaf * 2 + side, 2 * self.rows)

    def add(self, leaf, *sources):
        here = self.twin(leaf, self.place.side)
        value = self.total[here, :].astype(F32)
        for box, slot in sources:
            value = value + box[rows_of(slot, 2 * self.rows), :].astype(F32)
        self.total[here, :] = value.astype(self.total.dtype)

    def steps(self):
        p = self.place
        levels, rows = p.levels, 2 * self.rows
        for leaf in range(2 * levels):
            self.send(self.total.at[self.twin(leaf, 1 - p.side), :], self.from_far, leaf, rows, leaf, p.leaf, p.far)
        yield
        for leaf in range(2 * levels):
            self.arrived(self.from_far, leaf, rows, leaf)
            self.add(leaf, (self.from_far, leaf))
        for to_leaf in p.line:
            for core in range(2):
                slot = 2 * p.z + core
                self.send(self.total.at[self.twin(to_leaf // 2 * 2 + core, p.side), :], self.from_line, slot, rows,
                          2 * levels + slot, to_leaf, p.blk)
        yield
        for core in range(2):
            slots = [leaf // 2 * 2 + core for leaf in p.line]
            for slot in slots:
                self.arrived(self.from_line, slot, rows, 2 * levels + slot)
            self.add(2 * p.z + core, *[(self.from_line, slot) for slot in slots])
        for leaf, blk in ((p.sibling, p.blk), (p.leaf, p.near), (p.sibling, p.near)):
            src = self.total.at[rows_of(leaf * 4 + blk, self.rows), :]
            self.send(src, self.from_pair, p.pair, self.rows, 4 * levels + p.pair, leaf, blk)
        self.store(p.pair, self.total[rows_of(p.leaf * 4 + p.blk, self.rows), :])
        yield
        column = p.blk % 2
        for pair in (2 * column + 1 - p.core, 2 * (1 - column) + p.core, 2 * (1 - column) + 1 - p.core):
            self.arrived(self.from_pair, pair, self.rows, 4 * levels + pair)
            self.store(pair, self.from_pair[rows_of(pair, self.rows), :])
        yield

    def store(self, pair, value):
        for third in range(3):
            lanes = pl.ds(pl.multiple_of(third * D + pair * 128, 128), 128)
            self.out[:, lanes] = value[:, third * 128:third * 128 + 128].astype(F32)

    def finish(self):
        for copy in self.sent:
            copy.wait_send()


class TreeReduce:
    def __init__(self, place, part, from_core, box, send_sem, core_sem, recv_sem):
        self.place, self.part, self.from_core, self.box = place, part, from_core, box
        self.send_sem, self.core_sem, self.recv_sem = send_sem, core_sem, recv_sem

    def to_core(self, tile):
        p = self.place
        return remote(self.part.at[span(tile), :], self.from_core.at[tile // 2], self.send_sem.at[tile],
                      self.core_sem.at[tile // 2], p.sibling, p.blk)

    def to_owner(self, tile, which):
        p = self.place
        return remote(self.part.at[span(tile), :], self.box.at[tile % 2, which], self.send_sem.at[tile],
                      self.recv_sem.at[tile % 2 * 2 + which], p.served, tile // 2)

    def roles(self, tile):
        p = self.place
        collects = p.core == tile % 2
        gate = p.blk % 2 == tile // 2 % 2
        owner = (p.leaf == p.served) & (p.blk == tile // 2)
        return collects, gate, owner

    def offer(self, tile):
        collects, gate, owner = self.roles(tile)
        pl.when(jnp.logical_not(collects))(lambda: self.to_core(tile).start())

    def collect(self, tile):
        collects, gate, owner = self.roles(tile)

        def go():
            self.to_core(tile).wait_recv()
            total = self.part[span(tile), :].astype(F32) + self.from_core[tile // 2].astype(F32)
            self.part[span(tile), :] = total.astype(BF)
            pl.when(gate & jnp.logical_not(owner))(lambda: self.to_owner(tile, 0).start())
            pl.when(jnp.logical_not(gate))(lambda: self.to_owner(tile, 1).start())

            def keep():
                self.box[tile % 2, 0] = self.part[span(tile), :]

            pl.when(owner)(keep)

        pl.when(collects)(go)

    def arrive(self, half):
        p = self.place
        kept = p.main & (p.core == half)
        pl.when(jnp.logical_not(kept))(lambda: self.to_owner(half, 0).wait_recv())
        self.to_owner(half, 1).wait_recv()

    def finish(self, tile):
        collects, gate, owner = self.roles(tile)
        pl.when(jnp.logical_not(collects))(lambda: self.to_core(tile).wait_send())
        pl.when(collects & gate & jnp.logical_not(owner))(lambda: self.to_owner(tile, 0).wait_send())
        pl.when(collects & jnp.logical_not(gate))(lambda: self.to_owner(tile, 1).wait_send())


class Settle:
    def __init__(self, place, part, out, box, send_sem, recv_sem):
        self.place, self.part, self.out, self.box = place, part, out, box
        self.send_sem, self.recv_sem = send_sem, recv_sem
        self.rows = out.shape[0]

    def build(self, src_blk, to_blk):
        p = self.place
        return remote(self.part.at[rows_of(to_blk, self.rows), :], self.box.at[rows_of(src_blk, self.rows), :],
                      self.send_sem.at[to_blk], self.recv_sem.at[src_blk], p.leaf, to_blk)

    def steps(self):
        p = self.place
        self.copies = [self.build(p.blk, to) for to in (p.near, p.far, p.opposite)]
        for copy in self.copies:
            copy.start()
        yield
        total = self.part[rows_of(p.blk, self.rows), :]
        for blk in (p.near, p.far, p.opposite):
            self.build(blk, p.near).wait_recv()
            total = total + self.box[rows_of(blk, self.rows), :]
        self.out[...] = total
        yield

    def finish(self):
        for copy in self.copies:
            copy.wait_send()


class TableSum:
    def __init__(self, place, payload, box, rows_box, send_sem, recv_sem):
        self.place, self.payload, self.box, self.rows_box = place, payload, box, rows_box
        self.send_sem, self.recv_sem = send_sem, recv_sem
        self.leaves = place.levels * 2
        self.rows = self.leaves * 8

    def first(self, src_blk, to_blk):
        return remote(self.payload.at[rows_of(to_blk, self.rows), :], self.box.at[rows_of(src_blk, self.rows), :],
                      self.send_sem.at[to_blk], self.recv_sem.at[src_blk], self.place.leaf, to_blk)

    def second(self, src_leaf, to_leaf):
        p = self.place
        start = p.blk * self.leaves + to_leaf
        return remote(self.payload.at[rows_of(start, 8), :], self.rows_box.at[rows_of(src_leaf, 8), :],
                      self.send_sem.at[4 + to_leaf], self.recv_sem.at[4 + src_leaf], to_leaf, p.blk)

    def steps(self):
        p = self.place
        peers = (p.near, p.far, p.opposite)
        others = [(p.leaf + step) % self.leaves for step in range(1, self.leaves)]
        for to in peers:
            self.first(p.blk, to).start()
        yield
        here = rows_of(p.blk, self.rows)
        total = self.payload[here, :]
        for src in peers:
            self.first(src, p.near).wait_recv()
            total = total + self.box[rows_of(src, self.rows), :]
        self.payload[here, :] = total
        for to in others:
            self.second(p.leaf, to).start()
        self.rows_box[rows_of(p.leaf, 8), :] = self.payload[rows_of(p.blk * self.leaves + p.leaf, 8), :]
        yield
        for src in others:
            self.second(src, others[0]).wait_recv()
        yield

    def finish(self):
        p = self.place
        for to in (p.near, p.far, p.opposite):
            self.first(p.blk, to).wait_send()
        for step in range(1, self.leaves):
            self.second(p.leaf, (p.leaf + step) % self.leaves).wait_send()


SPAN = 256
TINY = 1e-05


def dot(left, right):
    return lax.dot_general(left, right, (((1,), (0,)), ((), ())), preferred_element_type=F32)


def dot_nt(left, right):
    return lax.dot_general(left, right, (((1,), (1,)), ((), ())), preferred_element_type=F32)


def dot_tn(left, right):
    return lax.dot_general(left, right, (((0,), (0,)), ((), ())), preferred_element_type=F32)


def iota(shape, axis):
    return lax.broadcasted_iota(jnp.int32, shape, axis)


def span(start, count=SPAN):
    return pl.ds(pl.multiple_of(start * count, count), count)


def loop(count, body):
    def step(index, carry):
        body(index)
        return carry

    lax.fori_loop(0, count, step, 0)


def unit_rows(values):
    centred = values - jnp.mean(values, axis=-1, keepdims=True)
    root = lax.rsqrt(jnp.mean(centred * centred, axis=-1, keepdims=True) + TINY)
    return centred * root, root


def norm_back(grad, unit, root, scale):
    inner = grad * (1.0 + scale)
    return (
        inner
        - jnp.mean(inner, axis=-1, keepdims=True)
        - unit * jnp.mean(inner * unit, axis=-1, keepdims=True)
    ) * root


def spread_pattern(wide, group):
    column = iota((128, group), 1)
    turn = jnp.zeros((128, group), jnp.int32)
    for step in range(1, group // wide):
        turn = turn + (column >= step * wide).astype(jnp.int32)
    return (column - turn * wide == iota((128, group), 0)).astype(F32)


def shard_of_column(count, wide, group):
    column = iota((count, group), 1)
    turn = jnp.zeros((count, group), jnp.int32)
    for step in range(1, group // wide):
        turn = turn + (column >= step * wide).astype(jnp.int32)
    return turn


def aux_row(aux, leaf, row):
    chosen = (iota((8, aux.shape[0]), 1) == leaf * 256 + row).astype(BF)
    return dot(chosen, aux[...])[0:1, :]


def read_modulation(aux, timestep, mod, wide):
    count = aux.shape[0] // 64
    row = iota((count, aux.shape[0]), 0)
    column = iota((count, aux.shape[0]), 1)
    chosen = ((column - row * 64).astype(F32) == timestep).astype(BF)
    picked = dot(chosen, aux[...])
    group = wide * 4
    laid = dot(picked.astype(BF), spread_pattern(wide, group).astype(BF))
    offset = iota((count, group), 0) - shard_of_column(count, wide, group)
    for part in range(count // 4):
        mod[0:1, part * group:(part + 1) * group] = jnp.sum(
            jnp.where(offset == 4 * part, laid, 0.0), axis=0, keepdims=True
        )


def table_payload(sums, wide, count):
    group = wide * 4
    offset = iota((count, group), 0) - shard_of_column(count, wide, group)
    held = jnp.zeros((count, group), F32)
    for part in range(count // 4):
        held = held + jnp.where(offset == 4 * part, sums[0:1, part * group:(part + 1) * group], 0.0)
    cut = lax.dot_general(held, spread_pattern(wide, group), (((1,), (1,)), ((), ())),
                          preferred_element_type=F32, precision=lax.Precision.HIGHEST)
    leaves = count // 4
    row = iota((count * 8, count), 0)
    tile = sum((row >= 8 * step).astype(jnp.int32) for step in range(1, count))
    block = sum((row >= 8 * leaves * step).astype(jnp.int32) for step in range(1, 4))
    chosen = (iota((count * 8, count), 1) == (tile - block * leaves) * 4 + block).astype(F32)
    return lax.dot_general(chosen, cut, (((1,), (0,)), ((), ())),
                           preferred_element_type=F32, precision=lax.Precision.HIGHEST)


def block_bias(parents, bias, blocks):
    row, column = iota((128, 128), 0), iota((128, 128), 1)
    reach = (row == column).astype(F32)
    reach = jnp.maximum(reach, (row.astype(F32) == parents).astype(F32))
    for step in range((blocks - 1).bit_length()):
        low_reach = reach.astype(BF)
        reach = jnp.minimum(dot(low_reach, low_reach), 1.0)
    held = (reach[:blocks, :] - 1.0) * 1e30
    for block in range(blocks):
        bias[:, block * BLOCK:(block + 1) * BLOCK] = jnp.broadcast_to(held[:, block:block + 1], (blocks, BLOCK))


class Layer:
    def __init__(self, place, refs):
        self.place = place
        self.__dict__.update(refs)

    def project(self, chunk):
        rows = span(chunk)
        unit, root = unit_rows(self.tokens_all[rows, :].astype(F32))
        first = (unit * (1.0 + self.mod_served[0:1, D:2 * D]) + self.mod_served[0:1, 0:D]).astype(BF)
        self.h1[rows, :] = first
        made = dot(first, self.w_pair[...])
        lane = iota((SPAN, 128), 1)
        query = made[:, 0:128].astype(BF).astype(F32) * HEAD ** (-0.5)
        self.q_masked[0, rows, :] = jnp.where(lane < HEAD, query, 0.0).astype(BF)
        self.q_masked[1, rows, :] = jnp.where(lane >= HEAD, query, 0.0).astype(BF)
        key = made[:, 128:256]
        value = made[:, 256:384]
        self.key[rows, :] = key.astype(BF)
        self.value[rows, :] = value.astype(BF)
        self.key_t[:, rows] = key.T.astype(BF)
        value_t = value.T.astype(BF)
        ones = jnp.ones((16, SPAN), BF)
        self.value_t[0, 0:HEAD, rows] = value_t[:HEAD]
        self.value_t[1, 0:HEAD, rows] = value_t[HEAD:]
        self.value_t[0, HEAD:HEAD + 16, rows] = ones
        self.value_t[1, HEAD:HEAD + 16, rows] = ones

    def attend(self, tile):
        queries = slice(tile * SPAN, (tile + 1) * SPAN)
        base = tile * (tile + 1) // 2

        def score(j, head):
            raw = dot_nt(self.key[j * SPAN:(j + 1) * SPAN, :], self.q_masked[head, queries, :])
            upper = raw[:BLOCK] + self.bias[2 * j:2 * j + 1, queries]
            lower = raw[BLOCK:] + self.bias[2 * j + 1:2 * j + 2, queries]
            kept = jnp.concatenate((upper, lower), axis=0)
            return kept + self.corner[...] if j == tile else kept

        top = [jnp.full((8, SPAN), -3e30, F32) for head in range(2)]
        for j in range(tile + 1):
            for head in range(2):
                top[head] = jnp.maximum(top[head], jnp.max(score(j, head).reshape(SPAN // 8, 8, SPAN), axis=0))
        top = [jnp.max(each, axis=0, keepdims=True) for each in top]
        mix = [0.0, 0.0]
        for j in range(tile + 1):
            for head in range(2):
                weight = jnp.exp(score(j, head) - top[head]).astype(BF)
                self.weights[base + j, head] = weight
                mix[head] = mix[head] + dot(self.value_t[head, :, j * SPAN:(j + 1) * SPAN], weight)
        halves = []
        for head in range(2):
            inverse = 1.0 / mix[head][HEAD:HEAD + 8, :]
            self.inverse[head, :, queries] = inverse
            halves.append(mix[head][:HEAD, :] * inverse[0:1])
        attended_t = jnp.concatenate(halves, axis=0)
        self.attended_t[:, queries] = attended_t
        self.attended[queries, :] = attended_t.T.astype(BF)

    def cross_keys(self):
        made = dot(self.source_all[...], self.w_ckv).astype(BF)
        lane = iota((2 * ENC, 128), 1)
        row = iota((2 * ENC, 128), 0)
        own = (lane < HEAD) == (row < ENC)
        for pair in range(4):
            for box, start in ((self.cross_k, 0), (self.cross_v, D)):
                part = made[:, start + 128 * pair:start + 128 * pair + 128].astype(F32)
                box[pair] = jnp.where(own, jnp.concatenate((part, part), axis=0), 0.0).astype(BF)

    def middle(self, chunk):
        rows = span(chunk)
        y1 = self.tokens[rows, :].astype(F32) + dot(self.gathered[rows, :], self.w_o)
        self.y1[rows, :] = y1
        unit, root = unit_rows(y1)
        h2 = (unit * (1.0 + self.mod[0:1, 3 * D:4 * D]) + self.mod[0:1, 2 * D:3 * D]).astype(BF)
        self.h2[rows, :] = h2
        query = (dot(h2, self.w_cq).astype(BF).astype(F32) * HEAD ** (-0.5)).astype(BF)
        self.cross_q[rows, :] = query
        lane = iota((SPAN, 128), 1)
        same = ((iota((128, 128), 0) < ENC) == (iota((128, 128), 1) < ENC)).astype(BF)
        out = []
        for pair in range(4):
            raw = dot_nt(query[:, 128 * pair:128 * pair + 128], self.cross_k[pair])
            left = jnp.max(jnp.where(lane < ENC, raw, -3e38), axis=-1, keepdims=True)
            right = jnp.max(jnp.where(lane >= ENC, raw, -3e38), axis=-1, keepdims=True)
            weight = jnp.exp(raw - jnp.where(lane < ENC, left, right))
            weight = weight / dot(weight.astype(BF), same)
            self.cross_p[pair, rows, :] = weight.astype(BF)
            out.append(dot(weight.astype(BF), self.cross_v[pair]))
        cross = jnp.concatenate(out, axis=1).astype(BF)
        self.cross_out[rows, :] = cross
        y2 = y1 + dot(cross, self.w_co)
        self.y2[rows, :] = y2
        unit, root = unit_rows(y2)
        self.h3[rows, :] = (unit * (1.0 + self.mod[0:1, 5 * D:6 * D]) + self.mod[0:1, 4 * D:5 * D]).astype(BF)

    def hidden(self, chunk):
        units = span(chunk)
        u = dot(self.h3[...], self.w_in(units))
        dg = dot_nt(self.cotangent[...], self.w_out[units, :])
        square = u * u
        slope = 0.7978845608028654
        bend = jnp.tanh(u * (slope + slope * 0.044715 * square))
        half = 0.5 + 0.5 * bend
        self.act[:, units] = (u * half).astype(BF)
        turn = half + 0.5 * u * (1.0 - bend * bend) * (slope + 3.0 * slope * 0.044715 * square)
        self.d_hidden[:, units] = (dg * turn).astype(BF)
        self.grad_out(units, dot_tn(self.act[:, units], self.cotangent[...]).astype(BF))
        self.grad_in(units, dot_tn(self.h3[...], self.d_hidden[:, units]).astype(BF))

    def finish_forward(self, chunk):
        rows = span(chunk)
        self.mixed[rows, :] = (self.y2[rows, :] + dot(self.act[rows, :], self.w_out[...])).astype(BF)

    def sums(self, piece, shift, scale):
        self.mod_grad[0:1, 2 * piece * D:(2 * piece + 1) * D] += jnp.sum(shift, axis=0, keepdims=True)
        self.mod_grad[0:1, (2 * piece + 1) * D:(2 * piece + 2) * D] += jnp.sum(scale, axis=0, keepdims=True)

    def back_three(self, chunk):
        rows = span(chunk)
        dh3 = dot_nt(self.d_hidden[rows, :], self.w_in(slice(None)))
        unit, root = unit_rows(self.y2[rows, :])
        self.sums(2, dh3, dh3 * unit)
        dy2 = self.cotangent[rows, :].astype(F32) + norm_back(dh3, unit, root, self.mod[0:1, 5 * D:6 * D])
        self.dy[rows, :] = dy2
        self.db[rows, :] = dy2.astype(BF)

    def back_cross(self, chunk):
        rows = span(chunk)
        dca = dot_nt(self.db[rows, :], self.w_co).astype(BF)
        lane = iota((SPAN, 128), 1)
        row = iota((128, 128), 0)
        own = (row < ENC) == (iota((128, 128), 1) < HEAD)
        parts = []
        for pair in range(4):
            lanes = slice(128 * pair, 128 * pair + 128)
            low_weight = self.cross_p[pair, rows, :]
            weight = low_weight.astype(F32)
            dc = dot_nt(dca[:, lanes], self.cross_v[pair])
            both_ = weight * dc
            left = jnp.sum(jnp.where(lane < ENC, both_, 0.0), axis=-1, keepdims=True)
            right = jnp.sum(jnp.where(lane >= ENC, both_, 0.0), axis=-1, keepdims=True)
            ds = (weight * (dc - jnp.where(lane < ENC, left, right))).astype(BF)
            parts.append((dot(ds, self.cross_k[pair]) * HEAD ** (-0.5)).astype(BF))
            dk = jnp.where(own, dot_tn(ds, self.cross_q[rows, lanes]), 0.0)
            dv = jnp.where(own, dot_tn(low_weight, dca[:, lanes]), 0.0)
            self.d_cross[:, lanes] += dk[:ENC] + dk[ENC:]
            self.d_cross[:, 128 * pair + D:128 * pair + D + 128] += dv[:ENC] + dv[ENC:]
        dcq = jnp.concatenate(parts, axis=1)
        self.dcq[rows, :] = dcq
        dh2 = dot_nt(dcq, self.w_cq)
        unit, root = unit_rows(self.y1[rows, :])
        self.sums(1, dh2, dh2 * unit)
        dy1 = self.dy[rows, :] + norm_back(dh2, unit, root, self.mod[0:1, 3 * D:4 * D])
        self.dy[rows, :] = dy1
        low_dy1 = dy1.astype(BF)
        self.db1[rows, :] = low_dy1
        self.d_attn[rows, :] = dot_nt(low_dy1, self.w_o).astype(BF)

    def attend_back(self, tile):
        queries = slice(tile * SPAN, (tile + 1) * SPAN)
        base = tile * (tile + 1) // 2
        d_att_t = self.d_att_all[queries, :].astype(F32).T
        scaled = [d_att_t[HEAD * h:HEAD * h + HEAD] * self.inverse[h, 0:1, queries] for h in range(2)]
        delta = [
            jnp.sum(scaled[h] * self.attended_t[HEAD * h:HEAD * h + HEAD, queries], axis=0, keepdims=True)
            for h in range(2)
        ]
        flat = jnp.concatenate(scaled, axis=0).T
        lane = iota((SPAN, 128), 1)
        masked = [jnp.where((lane < HEAD) == (h == 0), flat, 0.0).astype(BF) for h in range(2)]
        dq_t = [0.0, 0.0]
        for j in range(tile + 1):
            keys = slice(j * SPAN, (j + 1) * SPAN)
            dk = dv = 0.0
            for head in range(2):
                dp = dot_nt(self.value[keys, :], masked[head])
                weight = self.weights[base + j, head]
                ds = (weight.astype(F32) * (dp - delta[head])).astype(BF)
                dk = dk + dot(ds, self.q_masked[head, queries, :])
                dv = dv + dot(weight, masked[head])
                dq_t[head] = dq_t[head] + dot(self.key_t[HEAD * head:HEAD * head + HEAD, keys], ds)
            self.dk[keys, :] += dk
            self.dv[keys, :] += dv
        self.d_pair[queries, 0:128] = (jnp.concatenate(dq_t, axis=0) * HEAD ** (-0.5)).T.astype(BF)
        self.d_pair[queries, 128:256] = self.dk[queries, :].astype(BF)
        self.d_pair[queries, 256:384] = self.dv[queries, :].astype(BF)
        self.dh1_part[queries, :] = dot_nt(self.d_pair[queries, :], self.w_pair[...]).astype(BF)


VMEM = pl.BlockSpec(memory_space=pltpu.VMEM)
SMEM = pl.BlockSpec(memory_space=pltpu.SMEM)
CROSS = 5 * D
PACKED = ((0, 2 * D), (2 * D, CROSS), (CROSS, CROSS + FF // 2), (CROSS + FF // 2, CROSS + FF))
FIXED = True
LAST = ((0, D // 2), (D // 2, D))


class Weights(Layer):
    w_o = property(lambda self: self.pack[:, 0:D])
    w_cq = property(lambda self: self.pack[:, D:2 * D])
    w_ckv = property(lambda self: self.pack[:, 2 * D:4 * D])
    w_co = property(lambda self: self.pack[:, 4 * D:CROSS])

    def w_in(self, units):
        return self.pack.at[:, CROSS:CROSS + FF][:, units]

    def grad_in(self, units, value):
        self.grad_pack.at[:, CROSS:CROSS + FF][:, units] = value

    def grad_out(self, units, value):
        self.grad_w_out[units, :] = value

    def grad_into(self, start, left, right):
        for step in range(right.shape[1] // SPAN):
            columns = slice(start + step * SPAN, start + (step + 1) * SPAN)
            self.grad_pack[:, columns] = dot_tn(left[...], right[:, step * SPAN:(step + 1) * SPAN]).astype(BF)


ANY = pl.BlockSpec(memory_space=pl.ANY)
INS = ("i_tokens", "i_cotangent", "i_encoded", "parents", "timestep", "i_qkv", "i_o", "i_cq", "i_ckv", "i_co", "i_in", "i_out", "i_table")
OUTS = ("mixed", "grad_tokens", "g_encoded", "g_qkv", "g_o", "g_cq", "g_ckv", "g_co", "g_in", "g_out", "g_table")


def layer_scratch(rows, tree, blocks, levels, wide):
    tiles = tree // SPAN
    count = levels * 8
    each = D // count
    plain = lambda *shape: pltpu.VMEM(shape, F32)
    short = lambda *shape: pltpu.VMEM(shape, BF)
    dma = pltpu.SemaphoreType.DMA
    scratch = dict(
        tokens=short(rows, D), cotangent=short(rows, D), qkv_own=short(each, 3 * D), mixed=short(rows, D), grad_tokens=plain(rows, D),
        g_encoded=plain(ENC // 4, D), g_qkv=plain(each, 3 * D), g_o=plain(each, D), g_cq=plain(each, D), g_ckv=plain(each, 2 * D),
        g_co=plain(each, D), g_in=plain(each, FF), g_out=plain(FF // count, D), g_table=plain(STEPS, wide),
        in_sem=dma((11,)), out_sem=dma((11,)),
        held=short(levels * each, 3 * D), w_pair=short(D, 384), transit=short(D // 2, 384), pack=short(D, CROSS + FF), w_out=short(FF, D),
        aux=short(count * 64, 128), tokens_all=short(tree, D), source_all=short(ENC, D),
        mod=plain(8, 6 * D), mod_served=plain(8, 6 * D), mod_grad=plain(8, 6 * D), bias=plain(blocks, tree), corner=plain(SPAN, SPAN),
        h1=short(tree, D), q_masked=short(2, tree, 128), key=short(tree, 128), value=short(tree, 128),
        key_t=short(128, tree), value_t=short(2, HEAD + 16, tree),
        weights=short(tiles * (tiles + 1) // 2, 2, SPAN, SPAN), inverse=plain(2, 8, tree),
        attended_t=plain(128, tree), attended=short(tree, 128), gathered=short(rows, D),
        cross_k=short(4, 2 * ENC, 128), cross_v=short(4, 2 * ENC, 128), cross_q=short(rows, D), cross_p=short(4, rows, 128),
        cross_out=short(rows, D), y1=plain(rows, D), db1=short(rows, D), h2=short(rows, D), h3=short(rows, D),
        act=short(rows, FF), d_hidden=short(rows, FF),
        d_cross=plain(ENC, 2 * D), dcq=short(rows, D), d_att_all=short(tree, 128),
        dk=plain(tree, 128), dv=plain(tree, 128),
        d_pair=short(tree, 384), from_core=short(4, SPAN, D), dh1_box=short(2, 2, SPAN, D),
        grad_pack=short(D, CROSS + FF), grad_w_out=short(FF, D), grad_pair=short(D, 384), source_part=plain(ENC, D),
        payload=plain(count * 8, 128), table_box=plain(count * 8, 128), table_rows=plain(levels * 16, 128), settle_box=plain(ENC, D),
        a_send=dma((tiles,)), a_recv=dma((tiles,)), d_send=dma((8,)), d_recv=dma((8,)),
        h_send=dma((tiles,)), h_core=dma((4,)), h_recv=dma((4,)),
        send=dma((7, Gather.sends(levels))), recv=dma((7, count)),
        pair_send=dma((GatherPair.sends(levels),)), pair_recv=dma((GatherPair.receives(levels),)),
        share_send=dma((Share.sends,)), share_recv=dma((8,)), spread_send=dma((3,)), spread_recv=dma((4,)),
        r_send=dma((6, Reduce.slots(levels))), r_recv=dma((6, Reduce.slots(levels))), line=plain(64, 128),
        rp_send=dma((ReducePair.slots(levels),)), rp_recv=dma((ReducePair.slots(levels),)),
        settle_send=dma((4,)), settle_recv=dma((4,)), t_send=dma((4 + 2 * levels,)), t_recv=dma((4 + 2 * levels,)),
    )
    for piece, (height, width, line_last) in enumerate(
        [(FF // count, end - start, False) for start, end in LAST]
        + [(each, end - start, True) for start, end in PACKED[2:] + PACKED[:2]]
    ):
        for n, box in enumerate(Reduce.boxes(levels, height, width, BF, line_last)):
            scratch[f"box{piece}_{n}"] = box
    for n, box in enumerate(ReducePair.boxes(levels, each, 384, BF)):
        scratch[f"box_pair{n}"] = box
    return scratch


def layer_kernel(levels, wide, names, refs):
    place = Place(levels)
    refs = dict(zip(names, refs))
    refs["y2"] = refs["dy"] = refs["grad_tokens"]
    refs["db2"] = refs["db"] = refs["h3"]
    refs["d_attn"] = refs["cross_q"]
    refs["dh1_part"] = refs["tokens_all"]
    w = Weights(place, refs)
    blk, leaf = place.blk, place.leaf
    rows = w.tokens.shape[0]
    tree = w.tokens_all.shape[0]
    tiles = tree // SPAN
    halves = rows // SPAN
    blocks = tree // BLOCK
    count = levels * 8
    each = D // count
    index = leaf * 4 + blk
    own_lanes = pl.ds(pl.multiple_of(place.pair * 128, 128), 128)

    mine = rows_of(index, each)
    moves = [
        (w.i_tokens, w.tokens), (w.i_qkv, w.qkv_own),
        (w.i_encoded, w.source_all.at[rows_of(blk, w.i_encoded.shape[0]), :]),
        (w.i_out, w.w_out.at[rows_of(index, w.i_out.shape[0]), :]),
    ]
    start = 0
    for name in ("i_o", "i_cq", "i_ckv", "i_co", "i_in"):
        width = refs[name].shape[1]
        moves.append((refs[name], w.pack.at[mine, start:start + width]))
        start += width
    copies = [pltpu.make_async_copy(src, dst, w.in_sem.at[n]) for n, (src, dst) in enumerate(moves)]
    for copy in copies:
        copy.start()
    lane = iota((1, 128), 1)
    parents = jnp.zeros((1, 128), F32)
    for block in range(blocks):
        parents = jnp.where(lane == block, w.parents[0, block].astype(F32), parents)
    w.line[...] = jnp.zeros_like(w.line)
    w.line[:STEPS, :wide] = w.i_table[...].astype(F32)
    w.line[STEPS:STEPS + 1, :] = jnp.full((1, 128), w.timestep[0].astype(F32))
    w.line[STEPS + 1:STEPS + 2, :] = parents
    w.aux[rows_of(index, 64), :] = w.line[...].astype(BF)
    place.greet()
    for copy in copies:
        copy.wait()
    late = pltpu.make_async_copy(w.i_cotangent, w.cotangent, w.in_sem.at[10])
    late.start()

    def keep_tokens():
        w.tokens_all[rows_of(blk, rows), :] = w.tokens[...]

    pl.when(place.main)(keep_tokens)
    for pair in range(4):
        for third in range(3):
            w.held[rows_of(place.z, each), 384 * pair + 128 * third:384 * pair + 128 * third + 128] = (
                w.qkv_own[:, D * third + 128 * pair:D * third + 128 * pair + 128])
    given = []

    def give(*outs):
        for name in outs:
            copy = pltpu.make_async_copy(refs[name], refs["o_" + name], w.out_sem.at[OUTS.index(name)])
            copy.start()
            given.append(copy)

    weave = GatherPair(place, w.held, w.w_pair, w.transit, w.pair_send, w.pair_recv)
    table = GatherLine(place, w.aux, 64, slice(None), w.send.at[6], w.recv.at[6])
    share = Share(place, w.tokens, w.tokens_all, w.share_send, w.share_recv)
    spread = Spread(place, w.source_all, w.i_encoded.shape[0], w.spread_send, w.spread_recv)
    loads = [
        (GatherLine if n < 2 else Gather)(place, w.pack, each, slice(*cut), w.send.at[n], w.recv.at[n]) for n, cut in enumerate(PACKED)
    ] + [
        Gather(place, w.w_out, FF // count, slice(*cut), w.send.at[4 + n], w.recv.at[4 + n], FIXED and n == 0) for n, cut in enumerate(LAST)
    ]
    weave_steps, table_steps, share_steps = weave.steps(), table.steps(), share.steps()
    load_steps = [load.steps() for load in loads]

    def ticks(steps, number=1):
        for turn in range(number):
            for step in steps:
                next(step, None)

    first, fore, rest = load_steps[:2], load_steps[2:4], load_steps[4:]
    beats = iter([first, first + fore + rest, first + fore, first + rest, fore + rest, fore + rest])

    def load_tick():
        ticks(next(beats, []))

    ticks([weave_steps, table_steps, share_steps])
    spread.start()
    w.mod_grad[...] = jnp.zeros_like(w.mod_grad)
    w.d_cross[...] = jnp.zeros_like(w.d_cross)
    w.dk[...] = jnp.zeros_like(w.dk)
    w.dv[...] = jnp.zeros_like(w.dv)
    row, column = iota((SPAN, SPAN), 0), iota((SPAN, SPAN), 1)
    w.corner[...] = jnp.where(((row < BLOCK) == (column < BLOCK)) & (row > column), -1e30, 0.0)
    ticks([weave_steps, table_steps])
    ticks(load_steps)
    ticks([table_steps, share_steps, weave_steps])
    ticks(load_steps[2:])
    ticks([table_steps, weave_steps], 6)
    load_tick()
    block_bias(aux_row(w.aux, place.served, STEPS + 1), w.bias, blocks)
    read_modulation(w.aux, w.timestep[0].astype(F32), w.mod, wide)
    read_modulation(w.aux, aux_row(w.aux, place.served, STEPS)[0:1, 0:1], w.mod_served, wide)

    def project(block):
        share.arrive(block)
        for half in range(halves):
            w.project(block * halves + half)

    project(blk)
    project(place.far)
    ticks([share_steps])
    project(place.near)
    ticks([share_steps])
    load_tick()
    project(place.opposite)

    def attended_copy(tile, pair, here):
        there = w.gathered.at[span(tile % halves), pl.ds(pl.multiple_of(pair * 128, 128), 128)]
        to_leaf, to_blk = (leaf, place.near) if here else (place.served, tile // halves)
        return remote(w.attended.at[span(tile), :], there, w.a_send.at[tile], w.a_recv.at[pair * halves + tile % halves], to_leaf, to_blk)

    def mine_too(tile):
        return (place.served == leaf) & (blk == tile // halves)

    for tile in range(tiles):
        w.attend(tile)
        away = jnp.logical_not(mine_too(tile))
        pl.when(away)(lambda tile=tile: attended_copy(tile, place.pair, False).start())

        def keep(tile=tile):
            w.gathered[span(tile % halves), own_lanes] = w.attended[span(tile), :]

        pl.when(jnp.logical_not(away))(keep)
        if tile in (tiles - 3, tiles - 1):
            load_tick()
    spread.arrive()
    w.cross_keys()
    for pair in range(4):
        for half in range(halves):
            other = jnp.logical_not(place.main & (place.pair == pair))
            pl.when(other)(lambda pair=pair, half=half: attended_copy(half, pair, True).wait_recv())
    for half in range(halves):
        w.middle(half)
        load_tick()
    late.wait()

    def writer(*outs):
        def store(there, value):
            start = 0
            for out, at, width in outs:
                out[there, at:at + width] = value[:, start:start + width]
                start += width

        return store

    writers = [
        writer((w.g_out, 0, D // 2)), writer((w.g_out, D // 2, D // 2)),
        writer((w.g_in, 0, FF // 2)), writer((w.g_in, FF // 2, FF // 2)),
        writer((w.g_o, 0, D), (w.g_cq, 0, D)), writer((w.g_ckv, 0, 2 * D), (w.g_co, 0, D)),
    ]
    sums = []
    for n, (total, height, cut) in enumerate(
        [(w.grad_w_out, FF // count, cut) for cut in LAST] + [(w.grad_pack, each, cut) for cut in PACKED[2:] + PACKED[:2]]
    ):
        sums.append(Reduce(place, total, height, slice(*cut), writers[n], [refs[f"box{n}_{k}"] for k in range(4)],
                           w.r_send.at[n], w.r_recv.at[n], n >= 2))
    out0, out1, in0, in1, cross0, cross1 = sum_steps = [job.steps() for job in sums]
    outs, units, cross = [out0, out1], [in0, in1], [cross0, cross1]
    half_way = FF // SPAN // 2
    loop(half_way, w.hidden)
    ticks([in0])
    loop(half_way // 2, lambda step: w.hidden(half_way + step))
    ticks([in0])
    loop(half_way // 2, lambda step: w.hidden(half_way + half_way // 2 + step))
    ticks(outs + [in1])
    for job in loads + [weave, table, share, spread]:
        job.finish()
    loop(halves, w.finish_forward)
    give("mixed")
    loop(halves, w.back_three)
    ticks(outs)

    def da_copy(src, pair, half):
        return remote(w.d_attn.at[span(half), pair * 128:pair * 128 + 128], w.d_att_all.at[span(src * halves + half), :],
                      w.d_send.at[pair * 2 + half], w.d_recv.at[src * 2 + half], 2 * place.z + pair % 2, 2 * place.core + pair // 2)

    def stays(pair):
        return place.main & (place.pair == pair)

    for half in range(halves):
        w.back_cross(half)
        for pair in range(4):
            pl.when(jnp.logical_not(stays(pair)))(lambda pair=pair, half=half: da_copy(blk, pair, half).start())

    def keep_da():
        w.d_att_all[rows_of(blk, rows), :] = w.d_attn[:, own_lanes]

    pl.when(place.main)(keep_da)
    ticks(outs + [in1])
    w.grad_into(4 * D, w.cross_out, w.db2)
    w.grad_into(0, w.gathered, w.db1)
    w.grad_into(D, w.h2, w.dcq)
    low_cross = w.d_cross[...].astype(BF)
    for step in range(2 * D // SPAN):
        columns = slice(2 * D + step * SPAN, 2 * D + (step + 1) * SPAN)
        w.grad_pack[:, columns] = dot_tn(w.source_all[...], low_cross[:, step * SPAN:(step + 1) * SPAN]).astype(BF)
    w.source_part[...] = dot_nt(low_cross, w.w_ckv)
    settle = Settle(place, w.source_part, w.g_encoded, w.settle_box, w.settle_send, w.settle_recv)
    settle_steps = settle.steps()
    ticks(cross + [settle_steps])
    for src in range(4):
        for half in range(halves):
            pl.when(jnp.logical_not(place.main & (blk == src)))(lambda src=src, half=half: da_copy(src, 0, half).wait_recv())

    tree_sum = TreeReduce(place, w.dh1_part, w.from_core, w.dh1_box, w.h_send, w.h_core, w.h_recv)
    plan = [
        (tiles - 1, cross + [settle_steps]), (tiles - 2, units), (tiles - 3, outs), (tiles - 4, cross),
        (tiles - 5, units), (tiles - 6, outs), (tiles - 7, cross),
    ]
    for tile in range(tiles - 1, -1, -1):
        w.attend_back(tile)
        tree_sum.offer(tile)
        if tile + 1 < tiles:
            tree_sum.collect(tile + 1)
        for when, steps in plan:
            if when == tile:
                ticks(steps)

    def pair_grad(step):
        w.grad_pair[span(step), :] = dot_tn(w.h1[:, span(step)], w.d_pair[...]).astype(BF)

    loop(D // SPAN, pair_grad)
    pair_sum = ReducePair(place, w.grad_pair, w.g_qkv, [refs[f"box_pair{n}"] for n in range(3)], w.rp_send, w.rp_recv)
    pair_steps = pair_sum.steps()
    ticks([pair_steps])
    tree_sum.collect(0)
    ticks([pair_steps])

    def last(half):
        tree_sum.arrive(half)
        here = span(half)
        dh1 = w.dh1_box[half, 0].astype(F32) + w.dh1_box[half, 1].astype(F32)
        unit, root = unit_rows(w.tokens[here, :].astype(F32))
        w.sums(0, dh1, dh1 * unit)
        w.grad_tokens[here, :] = w.dy[here, :] + norm_back(dh1, unit, root, w.mod[0:1, D:2 * D])

    for half in range(halves):
        last(half)
    give("grad_tokens")
    w.payload[...] = table_payload(w.mod_grad[0:1, :], wide, count)
    table_sum = TableSum(place, w.payload, w.table_box, w.table_rows, w.t_send, w.t_recv)
    table_steps = table_sum.steps()
    ticks([table_steps])
    ticks(sum_steps, 10)
    give("g_encoded", "g_o", "g_cq", "g_ckv", "g_co", "g_in", "g_out")
    ticks([pair_steps, table_steps], 10)
    give("g_qkv")

    leaves = levels * 2
    chosen = (iota((leaves, count * 64), 1) == iota((leaves, count * 64), 0) * 256 + STEPS).astype(BF)
    steps_all = dot(chosen, w.aux[...])
    line = iota((64, 128), 0).astype(F32)
    grad_table = jnp.zeros((64, 128), F32)
    for tree_at in range(leaves):
        grad_table = grad_table + jnp.where(line == steps_all[tree_at:tree_at + 1, :], w.table_rows[8 * tree_at:8 * tree_at + 1, :], 0.0)
    w.g_table[...] = grad_table[:STEPS, :wide]
    give("g_table")

    for tile in range(tiles):
        pl.when(jnp.logical_not(mine_too(tile)))(lambda tile=tile: attended_copy(tile, place.pair, False).wait_send())
        tree_sum.finish(tile)
    for pair in range(4):
        for half in range(halves):
            pl.when(jnp.logical_not(stays(pair)))(lambda pair=pair, half=half: da_copy(blk, pair, half).wait_send())
    for job in sums + [settle, pair_sum, table_sum]:
        job.finish()
    for copy in given:
        copy.wait()


def copy_kernel(count, refs):
    ins, outs, held, sems = refs[:count], refs[count:2 * count], refs[2 * count:3 * count], refs[3 * count]
    inward = [pltpu.make_async_copy(ins[n], held[n], sems.at[0, n]) for n in range(count)]
    outward = [pltpu.make_async_copy(held[n], outs[n], sems.at[1, n]) for n in range(count)]
    for copy in inward:
        copy.start()
    for copy, then in zip(inward, outward):
        copy.wait()
        then.start()
    for copy in outward:
        copy.wait()


def copy_all(arrays):
    return pl.pallas_call(
        lambda *refs: copy_kernel(len(arrays), refs),
        out_shape=[jax.ShapeDtypeStruct(array.shape, array.dtype) for array in arrays],
        in_specs=[ANY] * len(arrays),
        out_specs=[ANY] * len(arrays),
        scratch_shapes=[pltpu.VMEM(array.shape, array.dtype) for array in arrays] + [pltpu.SemaphoreType.DMA((2, len(arrays)))],
    )(*arrays)


def per_device(tokens, cotangent, encoded, parents, timestep, w_qkv, w_o, w_cq, w_ckv, w_co, w_in, w_out, mod_table):
    levels = lax.axis_size("leaf") // 2
    rows, wide = tokens.shape[0], mod_table.shape[1]
    blocks = parents.shape[1]
    tree = blocks * BLOCK
    ins = (tokens, cotangent, encoded, parents, timestep, w_qkv, w_o, w_cq, w_ckv, w_co, w_in, w_out, mod_table)
    scratch = layer_scratch(rows, tree, blocks, levels, wide)
    out = lambda like: jax.ShapeDtypeStruct(like.shape, F32)
    names = INS + tuple("o_" + name for name in OUTS) + tuple(scratch)
    return copy_all(pl.pallas_call(
        lambda *refs: layer_kernel(levels, wide, names, refs),
        out_shape=[jax.ShapeDtypeStruct((rows, D), BF), out(tokens), out(encoded)]
        + [out(weight) for weight in (w_qkv, w_o, w_cq, w_ckv, w_co, w_in, w_out, mod_table)],
        in_specs=[SMEM if name in ("parents", "timestep") else VMEM if name == "i_table" else ANY for name in INS],
        out_specs=[ANY] * len(OUTS),
        scratch_shapes=list(scratch.values()),
        compiler_params=pltpu.CompilerParams(collective_id=0, has_side_effects=True, vmem_limit_bytes=(64 << 20) - (64 << 10)),
    )(*ins))


def solution(mesh):
    fits = mesh.shape["blk"] == 4 and mesh.shape["leaf"] == 8
    return jax.shard_map(
        per_device if fits else generic_device,
        mesh=mesh,
        in_specs=(
            P(("leaf", "blk"), None),
            P(("leaf", "blk"), None),
            P(("leaf", "blk"), None),
            P("leaf", None),
            P("leaf"),
            P(("leaf", "blk"), None),
            P(("leaf", "blk"), None),
            P(("leaf", "blk"), None),
            P(("leaf", "blk"), None),
            P(("leaf", "blk"), None),
            P(("leaf", "blk"), None),
            P(("leaf", "blk"), None),
            P(None, ("leaf", "blk")),
        ),
        out_specs=(
            P(("leaf", "blk"), None),
            P(("leaf", "blk"), None),
            P(("leaf", "blk"), None),
            P(("leaf", "blk"), None),
            P(("leaf", "blk"), None),
            P(("leaf", "blk"), None),
            P(("leaf", "blk"), None),
            P(("leaf", "blk"), None),
            P(("leaf", "blk"), None),
            P(("leaf", "blk"), None),
            P(None, ("leaf", "blk")),
        ),
        check_vma=False,
    )
```

```python
import functools

import jax
import jax.numpy as jnp
from jax import lax
from jax.experimental import pallas as pl
from jax.experimental.pallas import tpu as pltpu
from jax.sharding import PartitionSpec as P

D = 512
HEADS = 8
HEAD = 64
BLOCK = 128
FF = 2048
ENC = 64
STEPS = 50


PRECISE = lax.Precision.HIGHEST
MASKED = -1e30


def ancestors(parent_row):
    count = parent_row.shape[0]
    indices = jnp.arange(count, dtype=jnp.int32)
    reach_map = (indices[:, None] == indices[None, :]).astype(jnp.float32)
    reach_map = jnp.minimum(
        reach_map + (parent_row[:, None] == indices[None, :]).astype(jnp.float32), 1.0
    )
    for rounds in range(max(1, (count - 1).bit_length())):
        reach_map = jnp.minimum(jnp.dot(reach_map, reach_map, precision=PRECISE), 1.0)
    return reach_map


def normalize(values, shift, scaling):
    centred = values - jnp.mean(values, axis=-1, keepdims=True)
    spread = jnp.mean(centred * centred, axis=-1, keepdims=True)
    return centred * lax.rsqrt(spread + 1e-05) * (1.0 + scaling) + shift


def span_link(reach_rows, span):
    return lax.dynamic_slice_in_dim(reach_rows, span * 4, 4, 1)


def span_reached(reach_rows, span):
    return jnp.max(span_link(reach_rows, span)) > 0.5


def span_mask(reach_rows, first_block, span, row_count, width):
    query_index = jnp.arange(row_count, dtype=jnp.int32)
    key_index = jnp.arange(width, dtype=jnp.int32)
    query_block = first_block + query_index // BLOCK
    key_block = span * 4 + key_index // BLOCK
    link = span_link(reach_rows, span)
    link = jnp.repeat(jnp.repeat(link, BLOCK, axis=0), BLOCK, axis=1)
    same = query_block[:, None] == key_block[None, :]
    return (link > 0.5) & (
        jnp.logical_not(same) | (key_index[None, :] % BLOCK <= query_index[:, None] % BLOCK)
    )


def scores_of(queries, key_rows, allowed):
    raw = jnp.einsum(
        "qhd,khd->hqk", queries, key_rows, preferred_element_type=jnp.float32
    ) * HEAD ** (-0.5)
    return jnp.where(allowed[None], raw, MASKED)


def split_spans(keys, values):
    width = 4 * BLOCK
    count = keys.shape[0] // width
    return (
        jnp.arange(count, dtype=jnp.int32),
        keys.reshape(count, width, HEADS, HEAD),
        values.reshape(count, width, HEADS, HEAD),
    )


def tree_forward_attention(queries, keys, values, reach_rows, first_block):
    row_count = queries.shape[0]
    width = 4 * BLOCK
    spans, key_spans, value_spans = split_spans(keys, values)

    def stats(carry, item):
        span, key_rows = item

        def stats_visit(state):
            top, total = state
            allowed = span_mask(reach_rows, first_block, span, row_count, width)
            score = scores_of(queries, key_rows, allowed)
            new_top = jnp.maximum(top, jnp.max(score, axis=-1))
            weight = jnp.where(allowed[None], jnp.exp(score - new_top[..., None]), 0.0)
            return (new_top, total * jnp.exp(top - new_top) + jnp.sum(weight, axis=-1))

        return (
            lax.cond(span_reached(reach_rows, span), stats_visit, lambda state: state, carry),
            None,
        )

    start = (
        jnp.full((HEADS, row_count), MASKED, jnp.float32),
        jnp.zeros((HEADS, row_count), jnp.float32),
    )
    (top, total), unused = lax.scan(stats, start, (spans, key_spans))
    log_total = top + jnp.log(total)

    def collect(accum, item):
        span, key_rows, value_rows = item

        def collect_visit(current):
            allowed = span_mask(reach_rows, first_block, span, row_count, width)
            weight = jnp.where(
                allowed[None],
                jnp.exp(scores_of(queries, key_rows, allowed) - log_total[..., None]),
                0.0,
            )
            return current + jnp.einsum(
                "hqk,khd->qhd",
                weight.astype(jnp.bfloat16),
                value_rows,
                preferred_element_type=jnp.float32,
            )

        return (
            lax.cond(span_reached(reach_rows, span), collect_visit, lambda current: current, accum),
            None,
        )

    attended, unused = lax.scan(
        collect, jnp.zeros((row_count, HEADS, HEAD), jnp.float32), (spans, key_spans, value_spans)
    )
    return (attended, log_total)


def tree_backward_attention(queries, keys, values, reach_rows, first_block, log_total, grad_attn):
    row_count = queries.shape[0]
    width = 4 * BLOCK
    spans, key_spans, value_spans = split_spans(keys, values)

    def probs_of(span, key_rows):
        allowed = span_mask(reach_rows, first_block, span, row_count, width)
        return jnp.where(
            allowed[None],
            jnp.exp(scores_of(queries, key_rows, allowed) - log_total[..., None]),
            0.0,
        )

    def inner_pass(total, item):
        span, key_rows, value_rows = item

        def inner_visit(current):
            weight = probs_of(span, key_rows)
            d_weight = jnp.einsum(
                "qhd,khd->hqk", grad_attn, value_rows, preferred_element_type=jnp.float32
            )
            return current + jnp.sum(weight * d_weight, axis=-1)

        return (
            lax.cond(span_reached(reach_rows, span), inner_visit, lambda current: current, total),
            None,
        )

    delta, unused = lax.scan(
        inner_pass, jnp.zeros((HEADS, row_count), jnp.float32), (spans, key_spans, value_spans)
    )

    def grad_pass(d_queries, item):
        span, key_rows, value_rows = item

        def grad_visit(current):
            weight = probs_of(span, key_rows)
            d_weight = jnp.einsum(
                "qhd,khd->hqk", grad_attn, value_rows, preferred_element_type=jnp.float32
            )
            d_score = (weight * (d_weight - delta[..., None])).astype(jnp.bfloat16)
            current = current + jnp.einsum(
                "hqk,khd->qhd", d_score, key_rows, preferred_element_type=jnp.float32
            )
            d_keys = jnp.einsum(
                "hqk,qhd->khd", d_score, queries, preferred_element_type=jnp.float32
            ) * HEAD ** (-0.5)
            d_values = jnp.einsum(
                "hqk,qhd->khd",
                weight.astype(jnp.bfloat16),
                grad_attn,
                preferred_element_type=jnp.float32,
            )
            return (
                current,
                jnp.concatenate((d_keys.reshape(width, D), d_values.reshape(width, D)), axis=1),
            )

        def skip(current):
            return (current, jnp.zeros((width, 2 * D), jnp.float32))

        return lax.cond(span_reached(reach_rows, span), grad_visit, skip, d_queries)

    d_queries, terms = lax.scan(
        grad_pass, jnp.zeros((row_count, HEADS, HEAD), jnp.float32), (spans, key_spans, value_spans)
    )
    return (d_queries * HEAD ** (-0.5), terms.reshape(-1, 2 * D))


def generic_device(
    tokens,
    cotangent,
    encoded,
    parents,
    timestep,
    w_qkv,
    w_o,
    w_cq,
    w_ckv,
    w_co,
    w_in,
    w_out,
    mod_table,
):
    gathered = (
        lax.all_gather(w_qkv, ("leaf", "blk"), axis=0, tiled=True),
        lax.all_gather(w_o, ("leaf", "blk"), axis=0, tiled=True),
        lax.all_gather(w_cq, ("leaf", "blk"), axis=0, tiled=True),
        lax.all_gather(w_ckv, ("leaf", "blk"), axis=0, tiled=True),
        lax.all_gather(w_co, ("leaf", "blk"), axis=0, tiled=True),
        lax.all_gather(w_in, ("leaf", "blk"), axis=0, tiled=True),
        lax.all_gather(w_out, ("leaf", "blk"), axis=0, tiled=True),
        lax.all_gather(mod_table, ("leaf", "blk"), axis=1, tiled=True),
    )
    g_qkv, g_o, g_cq, g_ckv, g_co, g_in, g_out, g_table = gathered
    select = (jnp.arange(STEPS, dtype=jnp.int32) == timestep[0]).astype(jnp.float32)
    modulate = jnp.dot(
        select.astype(jnp.bfloat16)[None, :], g_table, preferred_element_type=jnp.float32
    )[0]
    pieces = [modulate[i * D : (i + 1) * D] for i in range(6)]
    inputs = tokens.astype(jnp.float32)
    row_count = tokens.shape[0]
    local_blocks = row_count // BLOCK
    first_block = lax.axis_index("blk") * local_blocks
    reach_map = ancestors(parents[0])
    reach_rows = lax.dynamic_slice_in_dim(reach_map, first_block, local_blocks, 0)
    scaling = HEAD ** (-0.5)
    normed_one, pull_one = jax.vjp(normalize, inputs, pieces[0], pieces[1])
    h_first = normed_one.astype(jnp.bfloat16)
    projected = jnp.dot(h_first, g_qkv, preferred_element_type=jnp.float32).astype(jnp.bfloat16)
    queries = projected[:, :D].reshape(row_count, HEADS, HEAD)
    keys, values = (
        lax.all_gather(projected[:, D : 2 * D], "blk", axis=0, tiled=True),
        lax.all_gather(projected[:, 2 * D :], "blk", axis=0, tiled=True),
    )
    attended, log_total = tree_forward_attention(queries, keys, values, reach_rows, first_block)
    attn_low = attended.reshape(row_count, D).astype(jnp.bfloat16)
    middle_one = inputs + jnp.dot(attn_low, g_o, preferred_element_type=jnp.float32)
    normed_two, pull_two = jax.vjp(normalize, middle_one, pieces[2], pieces[3])
    h_second = normed_two.astype(jnp.bfloat16)
    cross_q = (
        jnp.dot(h_second, g_cq, preferred_element_type=jnp.float32)
        .astype(jnp.bfloat16)
        .reshape(row_count, HEADS, HEAD)
    )
    source_local = jnp.dot(encoded, g_ckv, preferred_element_type=jnp.float32).astype(jnp.bfloat16)
    source_all = lax.all_gather(source_local, "blk", axis=0, tiled=True)
    cross_k = source_all[:, :D].reshape(-1, HEADS, HEAD)
    cross_v = source_all[:, D:].reshape(-1, HEADS, HEAD)
    cross_raw = (
        jnp.einsum("qhd,khd->hqk", cross_q, cross_k, preferred_element_type=jnp.float32) * scaling
    )
    cross_prob = jax.nn.softmax(cross_raw, axis=-1)
    cross_low = cross_prob.astype(jnp.bfloat16)
    cross_out = (
        jnp.einsum("hqk,khd->qhd", cross_low, cross_v, preferred_element_type=jnp.float32)
        .reshape(row_count, D)
        .astype(jnp.bfloat16)
    )
    middle_two = middle_one + jnp.dot(cross_out, g_co, preferred_element_type=jnp.float32)
    normed_three, pull_three = jax.vjp(normalize, middle_two, pieces[4], pieces[5])
    h_third = normed_three.astype(jnp.bfloat16)
    hidden_pre = jnp.dot(h_third, g_in, preferred_element_type=jnp.float32)
    activated, pull_gelu = jax.vjp(
        lambda values_in: jax.nn.gelu(values_in, approximate=True), hidden_pre
    )
    act_low = activated.astype(jnp.bfloat16)
    result = middle_two + jnp.dot(act_low, g_out, preferred_element_type=jnp.float32)
    mixed_out = result.astype(jnp.bfloat16)
    back_weights = (
        lax.all_gather(w_qkv, ("leaf", "blk"), axis=0, tiled=True),
        lax.all_gather(w_o, ("leaf", "blk"), axis=0, tiled=True),
        lax.all_gather(w_cq, ("leaf", "blk"), axis=0, tiled=True),
        lax.all_gather(w_ckv, ("leaf", "blk"), axis=0, tiled=True),
        lax.all_gather(w_co, ("leaf", "blk"), axis=0, tiled=True),
        lax.all_gather(w_in, ("leaf", "blk"), axis=0, tiled=True),
        lax.all_gather(w_out, ("leaf", "blk"), axis=0, tiled=True),
        lax.all_gather(mod_table, ("leaf", "blk"), axis=1, tiled=True),
    )
    b_qkv, b_o, b_cq, b_ckv, b_co, b_in, b_out = back_weights[:7]
    d_act = jnp.dot(cotangent, b_out.T, preferred_element_type=jnp.float32)
    d_hidden = pull_gelu(d_act)[0].astype(jnp.bfloat16)
    grad_out_w = jnp.dot(act_low.T, cotangent, preferred_element_type=jnp.float32)
    grad_in_w = jnp.dot(h_third.T, d_hidden, preferred_element_type=jnp.float32)
    d_h_third = jnp.dot(d_hidden, b_in.T, preferred_element_type=jnp.float32)
    d_middle_part, d_shift_three, d_scale_three = pull_three(d_h_third)
    d_middle_two = cotangent.astype(jnp.float32) + d_middle_part
    d_branch_two = d_middle_two.astype(jnp.bfloat16)
    grad_co_w = jnp.dot(cross_out.T, d_branch_two, preferred_element_type=jnp.float32)
    d_cross_out = (
        jnp.dot(d_branch_two, b_co.T, preferred_element_type=jnp.float32)
        .astype(jnp.bfloat16)
        .reshape(row_count, HEADS, HEAD)
    )
    d_cross_prob = jnp.einsum(
        "qhd,khd->hqk", d_cross_out, cross_v, preferred_element_type=jnp.float32
    )
    d_cross_raw = (
        cross_prob * (d_cross_prob - jnp.sum(cross_prob * d_cross_prob, axis=-1, keepdims=True))
    ).astype(jnp.bfloat16)
    d_cross_q = (
        (
            jnp.einsum("hqk,khd->qhd", d_cross_raw, cross_k, preferred_element_type=jnp.float32)
            * scaling
        )
        .reshape(row_count, D)
        .astype(jnp.bfloat16)
    )
    d_cross_k = (
        jnp.einsum("hqk,qhd->khd", d_cross_raw, cross_q, preferred_element_type=jnp.float32)
        * scaling
    )
    d_cross_v = jnp.einsum(
        "hqk,qhd->khd", cross_low, d_cross_out, preferred_element_type=jnp.float32
    )
    source_terms = jnp.concatenate((d_cross_k.reshape(-1, D), d_cross_v.reshape(-1, D)), axis=1)
    d_source = lax.psum_scatter(
        source_terms.astype(jnp.bfloat16), "blk", scatter_dimension=0, tiled=True
    )
    grad_ckv_w = jnp.dot(encoded.T, d_source, preferred_element_type=jnp.float32)
    d_encoded = jnp.dot(d_source, b_ckv.T, preferred_element_type=jnp.float32)
    grad_cq_w = jnp.dot(h_second.T, d_cross_q, preferred_element_type=jnp.float32)
    d_h_second = jnp.dot(d_cross_q, b_cq.T, preferred_element_type=jnp.float32)
    d_middle_part, d_shift_two, d_scale_two = pull_two(d_h_second)
    d_middle_one = d_middle_two + d_middle_part
    d_branch_one = d_middle_one.astype(jnp.bfloat16)
    grad_o_w = jnp.dot(attn_low.T, d_branch_one, preferred_element_type=jnp.float32)
    d_attn = (
        jnp.dot(d_branch_one, b_o.T, preferred_element_type=jnp.float32)
        .astype(jnp.bfloat16)
        .reshape(row_count, HEADS, HEAD)
    )
    keys_back, values_back = (
        lax.all_gather(projected[:, D : 2 * D], "blk", axis=0, tiled=True),
        lax.all_gather(projected[:, 2 * D :], "blk", axis=0, tiled=True),
    )
    d_queries, key_terms = tree_backward_attention(
        queries, keys_back, values_back, reach_rows, first_block, log_total, d_attn
    )
    d_key_value = lax.psum_scatter(
        key_terms.astype(jnp.bfloat16), "blk", scatter_dimension=0, tiled=True
    ).astype(jnp.float32)
    d_projected = jnp.concatenate((d_queries.reshape(row_count, D), d_key_value), axis=1).astype(
        jnp.bfloat16
    )
    grad_qkv_w = jnp.dot(h_first.T, d_projected, preferred_element_type=jnp.float32)
    d_h_first = jnp.dot(d_projected, b_qkv.T, preferred_element_type=jnp.float32)
    d_input_part, d_shift_one, d_scale_one = pull_one(d_h_first)
    d_tokens = d_middle_one + d_input_part
    d_modulate = jnp.concatenate(
        (d_shift_one, d_scale_one, d_shift_two, d_scale_two, d_shift_three, d_scale_three)
    )
    grad_table_w = select[:, None] * d_modulate[None, :]
    gradients = (
        lax.psum_scatter(grad_qkv_w, ("leaf", "blk"), scatter_dimension=0, tiled=True),
        lax.psum_scatter(grad_o_w, ("leaf", "blk"), scatter_dimension=0, tiled=True),
        lax.psum_scatter(grad_cq_w, ("leaf", "blk"), scatter_dimension=0, tiled=True),
        lax.psum_scatter(grad_ckv_w, ("leaf", "blk"), scatter_dimension=0, tiled=True),
        lax.psum_scatter(grad_co_w, ("leaf", "blk"), scatter_dimension=0, tiled=True),
        lax.psum_scatter(grad_in_w, ("leaf", "blk"), scatter_dimension=0, tiled=True),
        lax.psum_scatter(grad_out_w, ("leaf", "blk"), scatter_dimension=0, tiled=True),
        lax.psum_scatter(grad_table_w, ("leaf", "blk"), scatter_dimension=1, tiled=True),
    )
    return (
        mixed_out,
        d_tokens,
        d_encoded,
        gradients[0],
        gradients[1],
        gradients[2],
        gradients[3],
        gradients[4],
        gradients[5],
        gradients[6],
        gradients[7],
    )


MESH = pl.DeviceIdType.MESH
BF = jnp.bfloat16
F32 = jnp.float32


class Place:
    def __init__(self, levels):
        leaf = lax.axis_index("leaf")
        blk = lax.axis_index("blk")
        self.levels = levels
        self.leaf = leaf
        self.blk = blk
        self.z = leaf // 2
        self.core = leaf % 2
        self.near = blk + 1 - 2 * (blk % 2)
        self.far = (blk + 2) % 4
        self.first = self.core * self.near + (1 - self.core) * self.far
        self.second = self.core * self.far + (1 - self.core) * self.near
        self.opposite = 3 - blk
        self.sibling = self.z * 2 + 1 - self.core
        self.side = blk // 2
        self.served = self.z * 2 + self.side
        self.pair = blk % 2 * 2 + self.core
        self.main = self.side == self.core
        self.line = [(leaf + 2 * step) % (2 * levels) for step in range(1, levels)]

    def greet(self):
        barrier = pltpu.get_barrier_semaphore()

        count = self.levels * 2

        def hello(leaf, blk):
            pl.semaphore_signal(barrier, inc=1, device_id=(leaf, blk), device_id_type=MESH)

        for blk in (self.near, self.far, self.opposite):
            hello(self.leaf, blk)
            hello(self.sibling, blk)
        for step in range(1, count):
            hello((self.leaf + step) % count, self.blk)
        pl.semaphore_wait(barrier, count + 5)


def remote(src, dst, send, recv, leaf, blk):
    return pltpu.make_async_remote_copy(
        src_ref=src, dst_ref=dst, send_sem=send, recv_sem=recv,
        device_id=(leaf, blk), device_id_type=MESH,
    )


def rows_of(start, count):
    return pl.ds(pl.multiple_of(start * count, count), count)


class Gather:
    def __init__(self, place, full, rows, columns, send_sem, recv_sem, fixed=False):
        self.place, self.full, self.rows, self.columns = place, full, rows, columns
        self.send_sem, self.recv_sem = send_sem, recv_sem
        self.sent = []
        self.first = place.near if fixed else place.first
        self.second = place.far if fixed else place.second

    def build(self, leaf, blk, to_leaf, to_blk, number):
        there = self.full.at[rows_of(leaf * 4 + blk, self.rows), self.columns]
        return remote(there, there, self.send_sem.at[number], self.recv_sem.at[leaf * 4 + blk], to_leaf, to_blk)

    def push(self, leaf, blk, *targets):
        for to_leaf, to_blk in targets:
            copy = self.build(leaf, blk, to_leaf, to_blk, len(self.sent))
            copy.start()
            self.sent.append(copy)

    def arrive(self, leaf, blk):
        p = self.place
        self.build(leaf, blk, p.leaf, self.second, 0).wait_recv()

    def steps(self):
        p = self.place
        sibling, second = (p.sibling, p.blk), (p.leaf, self.second)
        line = [(leaf, p.blk) for leaf in p.line]
        self.push(p.leaf, p.blk, (p.leaf, self.first), *line, sibling)
        yield
        self.arrive(p.leaf, self.first)
        self.push(p.leaf, self.first, *line, sibling)
        yield
        self.push(p.leaf, p.blk, second)
        self.push(p.leaf, self.first, second)
        for leaf in p.line:
            self.arrive(leaf, p.blk)
            self.push(leaf, p.blk, second, sibling)
        yield
        for leaf in p.line:
            self.arrive(leaf, self.first)
            self.push(leaf, self.first, second, sibling)
        yield
        for leaf in (p.leaf, *p.line):
            for blk in (self.second, p.opposite):
                self.arrive(leaf, blk)
                self.push(leaf, blk, sibling)
        yield
        for level in range(p.levels):
            for blk in range(4):
                self.arrive(2 * level + 1 - p.core, blk)
        yield

    def finish(self):
        for copy in self.sent:
            copy.wait_send()

    @staticmethod
    def sends(levels):
        return 8 * levels


class Spread:
    def __init__(self, place, full, rows, send_sem, recv_sem):
        self.place, self.full, self.rows = place, full, rows
        self.send_sem, self.recv_sem = send_sem, recv_sem

    def build(self, blk, to_blk, number):
        there = self.full.at[rows_of(blk, self.rows), :]
        return remote(there, there, self.send_sem.at[number], self.recv_sem.at[blk], self.place.leaf, to_blk)

    def start(self):
        p = self.place
        self.copies = [self.build(p.blk, to, n) for n, to in enumerate((p.near, p.far, p.opposite))]
        for copy in self.copies:
            copy.start()

    def arrive(self):
        p = self.place
        for blk in (p.near, p.far, p.opposite):
            self.build(blk, p.near, 0).wait_recv()

    def finish(self):
        for copy in self.copies:
            copy.wait_send()


class Reduce:
    def __init__(self, place, total, rows, columns, store, boxes, send_sem, recv_sem, line_last):
        self.place, self.total, self.rows, self.columns, self.store = place, total, rows, columns, store
        self.from_sibling, self.from_second, self.from_line, self.from_first = boxes
        self.send_sem, self.recv_sem = send_sem, recv_sem
        self.line_last = line_last
        self.sent = []

    @staticmethod
    def slots(levels):
        return 6 * levels

    @staticmethod
    def boxes(levels, rows, width, kind, line_last):
        line, first = (levels, levels) if line_last else (2 * levels, 1)
        return [pltpu.VMEM((slots * rows, width), kind) for slots in (4 * levels, 2 * levels, line, first)]

    def here(self, leaf, blk):
        return (leaf * 4 + blk) * self.rows

    def part(self, leaf, blk, count=1):
        return self.total.at[pl.ds(pl.multiple_of(self.here(leaf, blk), self.rows), self.rows * count), self.columns]

    def copy(self, src, box, position, count, number, leaf, blk, sender=None):
        there = box.at[pl.ds(pl.multiple_of(position * self.rows, self.rows), self.rows * count), :]
        sender = number if sender is None else sender
        return remote(there if src is None else src, there, self.send_sem.at[sender], self.recv_sem.at[number], leaf, blk)

    def send(self, *parts):
        copy = self.copy(*parts)
        copy.start()
        self.sent.append(copy)

    def arrived(self, box, position, count, number):
        self.copy(None, box, position, count, number, self.place.leaf, self.place.first).wait_recv()

    def value(self, start, *sources):
        unit = pl.ds(pl.multiple_of(start, 16), 16)
        value = self.total[unit, self.columns].astype(F32)
        for box, position in sources:
            value = value + box[pl.ds(pl.multiple_of(position, 16), 16), :].astype(F32)
        return unit, value

    def add(self, leaf, blk, *sources, count=1):
        def one(step):
            if len(sources) == 1:
                box, slot = sources[0]
                unit = pl.ds(pl.multiple_of(self.here(leaf, blk) + 16 * step, 16), 16)
                there = pl.ds(pl.multiple_of(slot * self.rows + 16 * step, 16), 16)
                self.total[unit, self.columns] = self.total[unit, self.columns] + box[there, :]
                return
            unit, value = self.value(self.here(leaf, blk) + 16 * step, *[(box, slot * self.rows + 16 * step) for box, slot in sources])
            self.total[unit, self.columns] = value.astype(self.total.dtype)

        loop(count * self.rows // 16, one)

    def give(self, *sources):
        for step in range(self.rows // 16):
            unit, value = self.value(self.here(self.place.leaf, self.place.blk) + 16 * step,
                                     *[(box, slot * self.rows + 16 * step) for box, slot in sources])
            self.store(pl.ds(16 * step, 16), value)

    def steps(self):
        p = self.place
        levels = p.levels
        for level in range(levels):
            self.send(self.part(2 * level + 1 - p.core, 0, 4), self.from_sibling, 4 * level, 4, level, p.sibling, p.blk)
        yield
        for level in range(levels):
            self.arrived(self.from_sibling, 4 * level, 4, level)
            leaf = 2 * level + p.core
            self.add(leaf, 0, (self.from_sibling, 4 * level), count=4)
            for which, blk in enumerate((p.second, p.opposite)):
                slot = 2 * level + which
                self.send(self.part(leaf, blk), self.from_second, slot, 1, levels + slot, p.leaf, p.second)
        yield
        for level in range(levels):
            leaf = 2 * level + p.core
            for which, blk in enumerate((p.blk, p.first)):
                slot = 2 * level + which
                self.arrived(self.from_second, slot, 1, levels + slot)
                self.add(leaf, blk, (self.from_second, slot))
                if self.line_last and which == 1:
                    self.send(self.part(leaf, p.first), self.from_first, level, 1, 5 * levels + level, p.leaf, p.first)
        if self.line_last:
            yield
            for level in range(levels):
                self.arrived(self.from_first, level, 1, 5 * levels + level)
                self.add(2 * level + p.core, p.blk, (self.from_first, level))
        shards = (p.blk,) if self.line_last else (p.blk, p.first)
        slots = len(shards)
        for leaf in p.line:
            for which, blk in enumerate(shards):
                self.send(self.part(leaf, blk), self.from_line, slots * p.z + which, 1, 3 * levels + slots * p.z + which,
                          leaf, p.blk, 3 * levels + slots * (leaf // 2) + which)
        yield
        came = []
        for which, blk in enumerate(shards):
            slots_of = [slots * (leaf // 2) + which for leaf in p.line]
            for slot in slots_of:
                self.arrived(self.from_line, slot, 1, 3 * levels + slot)
            came.append([(self.from_line, slot) for slot in slots_of])
        if self.line_last:
            self.give(*came[0])
            yield
            return
        self.add(p.leaf, p.first, *came[1])
        self.send(self.part(p.leaf, p.first), self.from_first, 0, 1, 5 * levels, p.leaf, p.first)
        yield
        self.arrived(self.from_first, 0, 1, 5 * levels)
        self.give(*came[0], (self.from_first, 0))
        yield

    def finish(self):
        for copy in self.sent:
            copy.wait_send()


class GatherLine(Gather):
    def steps(self):
        p = self.place
        sibling, first, second = (p.sibling, p.blk), (p.leaf, self.first), (p.leaf, self.second)
        self.push(p.leaf, p.blk, *[(leaf, p.blk) for leaf in p.line], sibling)
        yield
        self.push(p.leaf, p.blk, first, second)
        for leaf in p.line:
            self.arrive(leaf, p.blk)
            self.push(leaf, p.blk, first, second, sibling)
        yield
        for leaf in (p.leaf, *p.line):
            self.arrive(leaf, self.first)
            self.push(leaf, self.first, second, sibling)
        yield
        for leaf in (p.leaf, *p.line):
            for blk in (self.second, p.opposite):
                self.arrive(leaf, blk)
                self.push(leaf, blk, sibling)
        yield
        for level in range(p.levels):
            for blk in range(4):
                self.arrive(2 * level + 1 - p.core, blk)
        yield


class Share:
    def __init__(self, place, own, full, send_sem, recv_sem):
        self.place, self.own, self.full = place, own, full
        self.rows = own.shape[0]
        self.half = self.rows // 2
        self.send_sem, self.recv_sem = send_sem, recv_sem
        self.sent = []

    def build(self, blk, half, to_leaf, to_blk, number, own=False):
        there = self.full.at[pl.ds(pl.multiple_of(blk * self.rows + half * self.half, self.half), self.half), :]
        src = self.own.at[pl.ds(half * self.half, self.half), :] if own else there
        return remote(src, there, self.send_sem.at[number], self.recv_sem.at[blk * 2 + half], to_leaf, to_blk)

    def wait(self, blk, half):
        self.build(blk, half, self.place.sibling, self.place.blk, 0).wait_recv()

    def push(self, cond, *parts):
        number = len(self.sent)
        pl.when(cond)(lambda: self.build(*parts[:4], number, *parts[4:]).start())
        self.sent.append((cond, parts, number))

    def steps(self):
        p = self.place
        helps = jnp.logical_not(p.main)
        sibling = (p.sibling, p.blk)
        for half in range(2):
            self.push(helps, p.blk, half, p.leaf, p.far, True)
            self.push(p.main, p.blk, half, p.leaf, p.near, True)
        for half in range(2):
            self.push(p.main, p.blk, half, *sibling, True)
        yield
        for half in range(2):
            pl.when(p.main)(lambda half=half: self.wait(p.far, half))
            self.push(p.main, p.far, half, p.leaf, p.near)
            self.push(p.main, p.far, half, *sibling)
        yield
        for blk in (p.near, p.opposite):
            for half in range(2):
                pl.when(p.main)(lambda blk=blk, half=half: self.wait(blk, half))
                self.push(p.main, blk, half, *sibling)
            yield

    def arrive(self, blk):
        for half in range(2):
            pl.when(jnp.logical_not(self.place.main))(lambda half=half: self.wait(blk, half))

    def finish(self):
        for cond, parts, number in self.sent:
            pl.when(cond)(lambda parts=parts, number=number: self.build(*parts[:4], number, *parts[4:]).wait_send())

    sends = 14


class GatherPair:
    def __init__(self, place, held, full, transit, send_sem, recv_sem):
        self.place, self.held, self.full, self.transit = place, held, full, transit
        self.rows, self.width = held.shape[0] // place.levels, full.shape[1]
        self.send_sem, self.recv_sem = send_sem, recv_sem
        self.sent = []

    def start(self, copy):
        copy.start()
        self.sent.append(copy)

    def send_of(self):
        return self.send_sem.at[len(self.sent)]

    def columns(self, level, pair):
        return self.held.at[rows_of(level, self.rows), pl.ds(pl.multiple_of(pair * self.width, 128), self.width)]

    def along(self, level, to_leaf):
        there = self.held.at[rows_of(level, self.rows), :]
        return remote(there, there, self.send_of(), self.recv_sem.at[level], to_leaf, self.place.blk)

    def target(self, level, blk, other):
        p = self.place
        if other:
            return self.transit.at[rows_of(level * 4 + blk, self.rows), :]
        return self.full.at[rows_of((2 * level + p.core) * 4 + blk, self.rows), :]

    def piece(self, level, src_blk, to_blk, other):
        p = self.place
        src = self.columns(level, 2 * (to_blk % 2) + (1 - p.core if other else p.core))
        number = p.levels + (level * 4 + src_blk) * 2 + other
        return remote(src, self.target(level, src_blk, other), self.send_of(), self.recv_sem.at[number], p.leaf, to_blk)

    def hand(self, level, core):
        p = self.place
        there = self.full.at[rows_of(2 * level + core, 4 * self.rows), :]
        return remote(self.transit.at[rows_of(level, 4 * self.rows), :], there, self.send_of(),
                      self.recv_sem.at[9 * p.levels + level], p.sibling, p.blk)

    def offer(self, level):
        p = self.place
        for to_blk in (p.near, p.far, p.opposite):
            for other in range(2):
                self.start(self.piece(level, p.blk, to_blk, other))
        for other in range(2):
            pair = 2 * (p.blk % 2) + (1 - p.core if other else p.core)
            self.target(level, p.blk, other)[...] = self.columns(level, pair)[...]

    def steps(self):
        p = self.place
        for to_leaf in p.line:
            self.start(self.along(p.z, to_leaf))
        self.offer(p.z)
        yield
        for leaf in p.line:
            self.along(leaf // 2, p.sibling).wait_recv()
            self.offer(leaf // 2)
        yield
        for level in (p.z, *[leaf // 2 for leaf in p.line]):
            for blk in (p.near, p.far, p.opposite):
                for other in range(2):
                    self.piece(level, blk, p.near, other).wait_recv()
            self.start(self.hand(level, p.core))
        yield
        for level in range(p.levels):
            self.hand(level, 1 - p.core).wait_recv()
        yield

    def finish(self):
        for copy in self.sent:
            copy.wait_send()

    @staticmethod
    def sends(levels):
        return levels - 1 + 7 * levels

    @staticmethod
    def receives(levels):
        return 10 * levels


class ReducePair:
    def __init__(self, place, total, out, boxes, send_sem, recv_sem):
        self.place, self.total, self.out = place, total, out
        self.rows = total.shape[0] // (place.levels * 8)
        self.from_far, self.from_line, self.from_pair = boxes
        self.send_sem, self.recv_sem = send_sem, recv_sem
        self.sent = []

    @staticmethod
    def slots(levels):
        return 4 * levels + 4

    @staticmethod
    def boxes(levels, rows, width, kind):
        return [pltpu.VMEM((levels * 4 * rows, width), kind) for n in range(2)] + [pltpu.VMEM((4 * rows, width), kind)]

    def build(self, src, box, slot, rows, number, leaf, blk):
        there = box.at[rows_of(slot, rows), :]
        return remote(there if src is None else src, there, self.send_sem.at[len(self.sent)], self.recv_sem.at[number], leaf, blk)

    def send(self, *parts):
        copy = self.build(*parts)
        copy.start()
        self.sent.append(copy)

    def arrived(self, box, slot, rows, number):
        self.build(None, box, slot, rows, number, self.place.sibling, self.place.blk).wait_recv()

    def twin(self, leaf, side):
        return rows_of(leaf * 2 + side, 2 * self.rows)

    def add(self, leaf, *sources):
        here = self.twin(leaf, self.place.side)
        value = self.total[here, :].astype(F32)
        for box, slot in sources:
            value = value + box[rows_of(slot, 2 * self.rows), :].astype(F32)
        self.total[here, :] = value.astype(self.total.dtype)

    def steps(self):
        p = self.place
        levels, rows = p.levels, 2 * self.rows
        for leaf in range(2 * levels):
            self.send(self.total.at[self.twin(leaf, 1 - p.side), :], self.from_far, leaf, rows, leaf, p.leaf, p.far)
        yield
        for leaf in range(2 * levels):
            self.arrived(self.from_far, leaf, rows, leaf)
            self.add(leaf, (self.from_far, leaf))
        for to_leaf in p.line:
            for core in range(2):
                slot = 2 * p.z + core
                self.send(self.total.at[self.twin(to_leaf // 2 * 2 + core, p.side), :], self.from_line, slot, rows,
                          2 * levels + slot, to_leaf, p.blk)
        yield
        for core in range(2):
            slots = [leaf // 2 * 2 + core for leaf in p.line]
            for slot in slots:
                self.arrived(self.from_line, slot, rows, 2 * levels + slot)
            self.add(2 * p.z + core, *[(self.from_line, slot) for slot in slots])
        for leaf, blk in ((p.sibling, p.blk), (p.leaf, p.near), (p.sibling, p.near)):
            src = self.total.at[rows_of(leaf * 4 + blk, self.rows), :]
            self.send(src, self.from_pair, p.pair, self.rows, 4 * levels + p.pair, leaf, blk)
        self.store(p.pair, self.total[rows_of(p.leaf * 4 + p.blk, self.rows), :])
        yield
        column = p.blk % 2
        for pair in (2 * column + 1 - p.core, 2 * (1 - column) + p.core, 2 * (1 - column) + 1 - p.core):
            self.arrived(self.from_pair, pair, self.rows, 4 * levels + pair)
            self.store(pair, self.from_pair[rows_of(pair, self.rows), :])
        yield

    def store(self, pair, value):
        for third in range(3):
            lanes = pl.ds(pl.multiple_of(third * D + pair * 128, 128), 128)
            self.out[:, lanes] = value[:, third * 128:third * 128 + 128].astype(F32)

    def finish(self):
        for copy in self.sent:
            copy.wait_send()


class TreeReduce:
    def __init__(self, place, part, from_core, box, send_sem, core_sem, recv_sem):
        self.place, self.part, self.from_core, self.box = place, part, from_core, box
        self.send_sem, self.core_sem, self.recv_sem = send_sem, core_sem, recv_sem

    def to_core(self, tile):
        p = self.place
        return remote(self.part.at[span(tile), :], self.from_core.at[tile // 2], self.send_sem.at[tile],
                      self.core_sem.at[tile // 2], p.sibling, p.blk)

    def to_owner(self, tile, which):
        p = self.place
        return remote(self.part.at[span(tile), :], self.box.at[tile % 2, which], self.send_sem.at[tile],
                      self.recv_sem.at[tile % 2 * 2 + which], p.served, tile // 2)

    def roles(self, tile):
        p = self.place
        collects = p.core == tile % 2
        gate = p.blk % 2 == tile // 2 % 2
        owner = (p.leaf == p.served) & (p.blk == tile // 2)
        return collects, gate, owner

    def offer(self, tile):
        collects, gate, owner = self.roles(tile)
        pl.when(jnp.logical_not(collects))(lambda: self.to_core(tile).start())

    def collect(self, tile):
        collects, gate, owner = self.roles(tile)

        def go():
            self.to_core(tile).wait_recv()
            self.part[span(tile), :] = self.part[span(tile), :] + self.from_core[tile // 2]
            pl.when(gate & jnp.logical_not(owner))(lambda: self.to_owner(tile, 0).start())
            pl.when(jnp.logical_not(gate))(lambda: self.to_owner(tile, 1).start())

            def keep():
                self.box[tile % 2, 0] = self.part[span(tile), :]

            pl.when(owner)(keep)

        pl.when(collects)(go)

    def arrive(self, half):
        p = self.place
        kept = p.main & (p.core == half)
        pl.when(jnp.logical_not(kept))(lambda: self.to_owner(half, 0).wait_recv())
        self.to_owner(half, 1).wait_recv()

    def finish(self, tile):
        collects, gate, owner = self.roles(tile)
        pl.when(jnp.logical_not(collects))(lambda: self.to_core(tile).wait_send())
        pl.when(collects & gate & jnp.logical_not(owner))(lambda: self.to_owner(tile, 0).wait_send())
        pl.when(collects & jnp.logical_not(gate))(lambda: self.to_owner(tile, 1).wait_send())


class Settle:
    def __init__(self, place, part, out, box, send_sem, recv_sem):
        self.place, self.part, self.out, self.box = place, part, out, box
        self.send_sem, self.recv_sem = send_sem, recv_sem
        self.rows = out.shape[0]

    def build(self, src_blk, to_blk):
        p = self.place
        return remote(self.part.at[rows_of(to_blk, self.rows), :], self.box.at[rows_of(src_blk, self.rows), :],
                      self.send_sem.at[to_blk], self.recv_sem.at[src_blk], p.leaf, to_blk)

    def steps(self):
        p = self.place
        self.copies = [self.build(p.blk, to) for to in (p.near, p.far, p.opposite)]
        for copy in self.copies:
            copy.start()
        yield
        total = self.part[rows_of(p.blk, self.rows), :]
        for blk in (p.near, p.far, p.opposite):
            self.build(blk, p.near).wait_recv()
            total = total + self.box[rows_of(blk, self.rows), :]
        self.out[...] = total
        yield

    def finish(self):
        for copy in self.copies:
            copy.wait_send()


class TableSum:
    def __init__(self, place, payload, box, rows_box, send_sem, recv_sem):
        self.place, self.payload, self.box, self.rows_box = place, payload, box, rows_box
        self.send_sem, self.recv_sem = send_sem, recv_sem
        self.leaves = place.levels * 2
        self.rows = self.leaves * 8

    def first(self, src_blk, to_blk):
        return remote(self.payload.at[rows_of(to_blk, self.rows), :], self.box.at[rows_of(src_blk, self.rows), :],
                      self.send_sem.at[to_blk], self.recv_sem.at[src_blk], self.place.leaf, to_blk)

    def second(self, src_leaf, to_leaf):
        p = self.place
        start = p.blk * self.leaves + to_leaf
        return remote(self.payload.at[rows_of(start, 8), :], self.rows_box.at[rows_of(src_leaf, 8), :],
                      self.send_sem.at[4 + to_leaf], self.recv_sem.at[4 + src_leaf], to_leaf, p.blk)

    def steps(self):
        p = self.place
        peers = (p.near, p.far, p.opposite)
        others = [(p.leaf + step) % self.leaves for step in range(1, self.leaves)]
        for to in peers:
            self.first(p.blk, to).start()
        yield
        here = rows_of(p.blk, self.rows)
        total = self.payload[here, :]
        for src in peers:
            self.first(src, p.near).wait_recv()
            total = total + self.box[rows_of(src, self.rows), :]
        self.payload[here, :] = total
        for to in others:
            self.second(p.leaf, to).start()
        self.rows_box[rows_of(p.leaf, 8), :] = self.payload[rows_of(p.blk * self.leaves + p.leaf, 8), :]
        yield
        for src in others:
            self.second(src, others[0]).wait_recv()
        yield

    def finish(self):
        p = self.place
        for to in (p.near, p.far, p.opposite):
            self.first(p.blk, to).wait_send()
        for step in range(1, self.leaves):
            self.second(p.leaf, (p.leaf + step) % self.leaves).wait_send()


SPAN = 256
TINY = 1e-05


def dot(left, right):
    return lax.dot_general(left, right, (((1,), (0,)), ((), ())), preferred_element_type=F32)


def dot_nt(left, right):
    return lax.dot_general(left, right, (((1,), (1,)), ((), ())), preferred_element_type=F32)


def dot_tn(left, right):
    return lax.dot_general(left, right, (((0,), (0,)), ((), ())), preferred_element_type=F32)


def iota(shape, axis):
    return lax.broadcasted_iota(jnp.int32, shape, axis)


def span(start, count=SPAN):
    return pl.ds(pl.multiple_of(start * count, count), count)


def loop(count, body):
    def step(index, carry):
        body(index)
        return carry

    lax.fori_loop(0, count, step, 0)


def unit_rows(values):
    centred = values - jnp.mean(values, axis=-1, keepdims=True)
    root = lax.rsqrt(jnp.mean(centred * centred, axis=-1, keepdims=True) + TINY)
    return centred * root, root


def norm_back(grad, unit, root, scale):
    inner = grad * (1.0 + scale)
    return (
        inner
        - jnp.mean(inner, axis=-1, keepdims=True)
        - unit * jnp.mean(inner * unit, axis=-1, keepdims=True)
    ) * root


def spread_pattern(wide, group):
    column = iota((128, group), 1)
    turn = jnp.zeros((128, group), jnp.int32)
    for step in range(1, group // wide):
        turn = turn + (column >= step * wide).astype(jnp.int32)
    return (column - turn * wide == iota((128, group), 0)).astype(F32)


def shard_of_column(count, wide, group):
    column = iota((count, group), 1)
    turn = jnp.zeros((count, group), jnp.int32)
    for step in range(1, group // wide):
        turn = turn + (column >= step * wide).astype(jnp.int32)
    return turn


def aux_row(aux, leaf, row):
    chosen = (iota((8, aux.shape[0]), 1) == leaf * 256 + row).astype(BF)
    return dot(chosen, aux[...])[0:1, :]


def read_modulation(aux, timestep, mod, wide):
    count = aux.shape[0] // 64
    row = iota((count, aux.shape[0]), 0)
    column = iota((count, aux.shape[0]), 1)
    chosen = ((column - row * 64).astype(F32) == timestep).astype(BF)
    picked = dot(chosen, aux[...])
    group = wide * 4
    laid = dot(picked.astype(BF), spread_pattern(wide, group).astype(BF))
    offset = iota((count, group), 0) - shard_of_column(count, wide, group)
    for part in range(count // 4):
        mod[0:1, part * group:(part + 1) * group] = jnp.sum(
            jnp.where(offset == 4 * part, laid, 0.0), axis=0, keepdims=True
        )


def table_payload(sums, wide, count):
    group = wide * 4
    offset = iota((count, group), 0) - shard_of_column(count, wide, group)
    held = jnp.zeros((count, group), F32)
    for part in range(count // 4):
        held = held + jnp.where(offset == 4 * part, sums[0:1, part * group:(part + 1) * group], 0.0)
    cut = lax.dot_general(held, spread_pattern(wide, group), (((1,), (1,)), ((), ())),
                          preferred_element_type=F32, precision=lax.Precision.HIGHEST)
    leaves = count // 4
    row = iota((count * 8, count), 0)
    tile = sum((row >= 8 * step).astype(jnp.int32) for step in range(1, count))
    block = sum((row >= 8 * leaves * step).astype(jnp.int32) for step in range(1, 4))
    chosen = (iota((count * 8, count), 1) == (tile - block * leaves) * 4 + block).astype(F32)
    return lax.dot_general(chosen, cut, (((1,), (0,)), ((), ())),
                           preferred_element_type=F32, precision=lax.Precision.HIGHEST)


def block_bias(parents, bias, blocks):
    row, column = iota((128, 128), 0), iota((128, 128), 1)
    reach = (row == column).astype(F32)
    reach = jnp.maximum(reach, (row.astype(F32) == parents).astype(F32))
    for step in range((blocks - 1).bit_length()):
        low_reach = reach.astype(BF)
        reach = jnp.minimum(dot(low_reach, low_reach), 1.0)
    held = (reach[:blocks, :] - 1.0) * 1e30
    for block in range(blocks):
        bias[:, block * BLOCK:(block + 1) * BLOCK] = jnp.broadcast_to(held[:, block:block + 1], (blocks, BLOCK))


class Layer:
    def __init__(self, place, refs):
        self.place = place
        self.__dict__.update(refs)

    def project(self, chunk):
        rows = span(chunk)
        unit, root = unit_rows(self.tokens_all[rows, :].astype(F32))
        first = (unit * (1.0 + self.mod_served[0:1, D:2 * D]) + self.mod_served[0:1, 0:D]).astype(BF)
        self.h1[rows, :] = first
        made = dot(first, self.w_pair[...])
        lane = iota((SPAN, 128), 1)
        query = made[:, 0:128].astype(BF).astype(F32) * HEAD ** (-0.5)
        self.q_masked[0, rows, :] = jnp.where(lane < HEAD, query, 0.0).astype(BF)
        self.q_masked[1, rows, :] = jnp.where(lane >= HEAD, query, 0.0).astype(BF)
        key = made[:, 128:256]
        value = made[:, 256:384]
        self.key[rows, :] = key.astype(BF)
        self.value[rows, :] = value.astype(BF)
        self.key_t[:, rows] = key.T.astype(BF)
        value_t = value.T.astype(BF)
        ones = jnp.ones((16, SPAN), BF)
        self.value_t[0, 0:HEAD, rows] = value_t[:HEAD]
        self.value_t[1, 0:HEAD, rows] = value_t[HEAD:]
        self.value_t[0, HEAD:HEAD + 16, rows] = ones
        self.value_t[1, HEAD:HEAD + 16, rows] = ones

    def attend(self, tile):
        queries = slice(tile * SPAN, (tile + 1) * SPAN)
        base = tile * (tile + 1) // 2

        def score(j, head):
            raw = dot_nt(self.key[j * SPAN:(j + 1) * SPAN, :], self.q_masked[head, queries, :])
            upper = raw[:BLOCK] + self.bias[2 * j:2 * j + 1, queries]
            lower = raw[BLOCK:] + self.bias[2 * j + 1:2 * j + 2, queries]
            kept = jnp.concatenate((upper, lower), axis=0)
            return kept + self.corner[...] if j == tile else kept

        top = [jnp.full((8, SPAN), -3e30, F32) for head in range(2)]
        for j in range(tile + 1):
            for head in range(2):
                top[head] = jnp.maximum(top[head], jnp.max(score(j, head).reshape(SPAN // 8, 8, SPAN), axis=0))
        top = [jnp.max(each, axis=0, keepdims=True) for each in top]
        mix = [0.0, 0.0]
        for j in range(tile + 1):
            for head in range(2):
                weight = jnp.exp(score(j, head) - top[head]).astype(BF)
                self.weights[base + j, head] = weight
                mix[head] = mix[head] + dot(self.value_t[head, :, j * SPAN:(j + 1) * SPAN], weight)
        halves = []
        for head in range(2):
            inverse = 1.0 / mix[head][HEAD:HEAD + 8, :]
            self.inverse[head, :, queries] = inverse
            halves.append(mix[head][:HEAD, :] * inverse[0:1])
        attended_t = jnp.concatenate(halves, axis=0)
        self.attended_t[:, queries] = attended_t
        self.attended[queries, :] = attended_t.T.astype(BF)

    def cross_keys(self):
        made = dot(self.source_all[...], self.w_ckv).astype(BF)
        lane = iota((2 * ENC, 128), 1)
        row = iota((2 * ENC, 128), 0)
        own = (lane < HEAD) == (row < ENC)
        for pair in range(4):
            for box, start in ((self.cross_k, 0), (self.cross_v, D)):
                part = made[:, start + 128 * pair:start + 128 * pair + 128].astype(F32)
                box[pair] = jnp.where(own, jnp.concatenate((part, part), axis=0), 0.0).astype(BF)

    def middle(self, chunk):
        rows = span(chunk)
        y1 = self.tokens[rows, :].astype(F32) + dot(self.gathered[rows, :], self.w_o)
        self.y1[rows, :] = y1
        unit, root = unit_rows(y1)
        h2 = (unit * (1.0 + self.mod[0:1, 3 * D:4 * D]) + self.mod[0:1, 2 * D:3 * D]).astype(BF)
        self.h2[rows, :] = h2
        query = (dot(h2, self.w_cq).astype(BF).astype(F32) * HEAD ** (-0.5)).astype(BF)
        self.cross_q[rows, :] = query
        lane = iota((SPAN, 128), 1)
        same = ((iota((128, 128), 0) < ENC) == (iota((128, 128), 1) < ENC)).astype(BF)
        out = []
        for pair in range(4):
            raw = dot_nt(query[:, 128 * pair:128 * pair + 128], self.cross_k[pair])
            left = jnp.max(jnp.where(lane < ENC, raw, -3e38), axis=-1, keepdims=True)
            right = jnp.max(jnp.where(lane >= ENC, raw, -3e38), axis=-1, keepdims=True)
            weight = jnp.exp(raw - jnp.where(lane < ENC, left, right))
            weight = weight / dot(weight.astype(BF), same)
            self.cross_p[pair, rows, :] = weight.astype(BF)
            out.append(dot(weight.astype(BF), self.cross_v[pair]))
        cross = jnp.concatenate(out, axis=1).astype(BF)
        self.cross_out[rows, :] = cross
        y2 = y1 + dot(cross, self.w_co)
        self.y2[rows, :] = y2
        unit, root = unit_rows(y2)
        self.h3[rows, :] = (unit * (1.0 + self.mod[0:1, 5 * D:6 * D]) + self.mod[0:1, 4 * D:5 * D]).astype(BF)

    def hidden(self, chunk):
        units = span(chunk)
        u = dot(self.h3[...], self.w_in(units))
        dg = dot_nt(self.cotangent[...], self.w_out[units, :])
        square = u * u
        slope = 0.7978845608028654
        bend = jnp.tanh(u * (slope + slope * 0.044715 * square))
        half = 0.5 + 0.5 * bend
        self.act[:, units] = (u * half).astype(BF)
        turn = half + 0.5 * u * (1.0 - bend * bend) * (slope + 3.0 * slope * 0.044715 * square)
        self.d_hidden[:, units] = (dg * turn).astype(BF)
        self.grad_out(units, dot_tn(self.act[:, units], self.cotangent[...]).astype(BF))
        self.grad_in(units, dot_tn(self.h3[...], self.d_hidden[:, units]).astype(BF))

    def finish_forward(self, chunk):
        rows = span(chunk)
        self.mixed[rows, :] = (self.y2[rows, :] + dot(self.act[rows, :], self.w_out[...])).astype(BF)

    def sums(self, piece, shift, scale):
        self.mod_grad[0:1, 2 * piece * D:(2 * piece + 1) * D] += jnp.sum(shift, axis=0, keepdims=True)
        self.mod_grad[0:1, (2 * piece + 1) * D:(2 * piece + 2) * D] += jnp.sum(scale, axis=0, keepdims=True)

    def back_three(self, chunk):
        rows = span(chunk)
        dh3 = dot_nt(self.d_hidden[rows, :], self.w_in(slice(None)))
        unit, root = unit_rows(self.y2[rows, :])
        self.sums(2, dh3, dh3 * unit)
        dy2 = self.cotangent[rows, :].astype(F32) + norm_back(dh3, unit, root, self.mod[0:1, 5 * D:6 * D])
        self.dy[rows, :] = dy2
        self.db[rows, :] = dy2.astype(BF)

    def back_cross(self, chunk):
        rows = span(chunk)
        dca = dot_nt(self.db[rows, :], self.w_co).astype(BF)
        lane = iota((SPAN, 128), 1)
        row = iota((128, 128), 0)
        own = (row < ENC) == (iota((128, 128), 1) < HEAD)
        parts = []
        for pair in range(4):
            lanes = slice(128 * pair, 128 * pair + 128)
            low_weight = self.cross_p[pair, rows, :]
            weight = low_weight.astype(F32)
            dc = dot_nt(dca[:, lanes], self.cross_v[pair])
            both_ = weight * dc
            left = jnp.sum(jnp.where(lane < ENC, both_, 0.0), axis=-1, keepdims=True)
            right = jnp.sum(jnp.where(lane >= ENC, both_, 0.0), axis=-1, keepdims=True)
            ds = (weight * (dc - jnp.where(lane < ENC, left, right))).astype(BF)
            parts.append((dot(ds, self.cross_k[pair]) * HEAD ** (-0.5)).astype(BF))
            dk = jnp.where(own, dot_tn(ds, self.cross_q[rows, lanes]), 0.0)
            dv = jnp.where(own, dot_tn(low_weight, dca[:, lanes]), 0.0)
            self.d_cross[:, lanes] += dk[:ENC] + dk[ENC:]
            self.d_cross[:, 128 * pair + D:128 * pair + D + 128] += dv[:ENC] + dv[ENC:]
        dcq = jnp.concatenate(parts, axis=1)
        self.dcq[rows, :] = dcq
        dh2 = dot_nt(dcq, self.w_cq)
        unit, root = unit_rows(self.y1[rows, :])
        self.sums(1, dh2, dh2 * unit)
        dy1 = self.dy[rows, :] + norm_back(dh2, unit, root, self.mod[0:1, 3 * D:4 * D])
        self.dy[rows, :] = dy1
        low_dy1 = dy1.astype(BF)
        self.db1[rows, :] = low_dy1
        self.d_attn[rows, :] = dot_nt(low_dy1, self.w_o).astype(BF)

    def attend_back(self, tile):
        queries = slice(tile * SPAN, (tile + 1) * SPAN)
        base = tile * (tile + 1) // 2
        d_att_t = self.d_att_all[queries, :].astype(F32).T
        scaled = [d_att_t[HEAD * h:HEAD * h + HEAD] * self.inverse[h, 0:1, queries] for h in range(2)]
        delta = [
            jnp.sum(scaled[h] * self.attended_t[HEAD * h:HEAD * h + HEAD, queries], axis=0, keepdims=True)
            for h in range(2)
        ]
        flat = jnp.concatenate(scaled, axis=0).T
        lane = iota((SPAN, 128), 1)
        masked = [jnp.where((lane < HEAD) == (h == 0), flat, 0.0).astype(BF) for h in range(2)]
        dq_t = [0.0, 0.0]
        for j in range(tile + 1):
            keys = slice(j * SPAN, (j + 1) * SPAN)
            dk = dv = 0.0
            for head in range(2):
                dp = dot_nt(self.value[keys, :], masked[head])
                weight = self.weights[base + j, head]
                ds = (weight.astype(F32) * (dp - delta[head])).astype(BF)
                dk = dk + dot(ds, self.q_masked[head, queries, :])
                dv = dv + dot(weight, masked[head])
                dq_t[head] = dq_t[head] + dot(self.key_t[HEAD * head:HEAD * head + HEAD, keys], ds)
            self.dk[keys, :] += dk
            self.dv[keys, :] += dv
        self.d_pair[queries, 0:128] = (jnp.concatenate(dq_t, axis=0) * HEAD ** (-0.5)).T.astype(BF)
        self.d_pair[queries, 128:256] = self.dk[queries, :].astype(BF)
        self.d_pair[queries, 256:384] = self.dv[queries, :].astype(BF)
        self.dh1_part[queries, :] = dot_nt(self.d_pair[queries, :], self.w_pair[...]).astype(BF)


VMEM = pl.BlockSpec(memory_space=pltpu.VMEM)
SMEM = pl.BlockSpec(memory_space=pltpu.SMEM)
CROSS = 5 * D
PACKED = ((0, 2 * D), (2 * D, CROSS), (CROSS, CROSS + FF // 2), (CROSS + FF // 2, CROSS + FF))
FIXED = True
LAST = ((0, D // 2), (D // 2, D))


class Weights(Layer):
    w_o = property(lambda self: self.pack[:, 0:D])
    w_cq = property(lambda self: self.pack[:, D:2 * D])
    w_ckv = property(lambda self: self.pack[:, 2 * D:4 * D])
    w_co = property(lambda self: self.pack[:, 4 * D:CROSS])

    def w_in(self, units):
        return self.pack.at[:, CROSS:CROSS + FF][:, units]

    def grad_in(self, units, value):
        self.grad_pack.at[:, CROSS:CROSS + FF][:, units] = value

    def grad_out(self, units, value):
        self.grad_w_out[units, :] = value

    def grad_into(self, start, left, right):
        for step in range(right.shape[1] // SPAN):
            columns = slice(start + step * SPAN, start + (step + 1) * SPAN)
            self.grad_pack[:, columns] = dot_tn(left[...], right[:, step * SPAN:(step + 1) * SPAN]).astype(BF)


ANY = pl.BlockSpec(memory_space=pl.ANY)
INS = ("i_tokens", "i_cotangent", "i_encoded", "parents", "timestep", "i_qkv", "i_o", "i_cq", "i_ckv", "i_co", "i_in", "i_out", "i_table")
OUTS = ("mixed", "grad_tokens", "g_encoded", "g_qkv", "g_o", "g_cq", "g_ckv", "g_co", "g_in", "g_out", "g_table")


def layer_scratch(rows, tree, blocks, levels, wide):
    tiles = tree // SPAN
    count = levels * 8
    each = D // count
    plain = lambda *shape: pltpu.VMEM(shape, F32)
    short = lambda *shape: pltpu.VMEM(shape, BF)
    dma = pltpu.SemaphoreType.DMA
    scratch = dict(
        tokens=short(rows, D), cotangent=short(rows, D), qkv_own=short(each, 3 * D), mixed=short(rows, D), grad_tokens=plain(rows, D),
        g_encoded=plain(ENC // 4, D), g_qkv=plain(each, 3 * D), g_o=plain(each, D), g_cq=plain(each, D), g_ckv=plain(each, 2 * D),
        g_co=plain(each, D), g_in=plain(each, FF), g_out=plain(FF // count, D), g_table=plain(64, 128),
        in_sem=dma((11,)), out_sem=dma((11,)),
        held=short(levels * each, 3 * D), w_pair=short(D, 384), transit=short(D // 2, 384), pack=short(D, CROSS + FF), w_out=short(FF, D),
        aux=short(count * 64, 128), tokens_all=short(tree, D), source_all=short(ENC, D),
        mod=plain(8, 6 * D), mod_served=plain(8, 6 * D), mod_grad=plain(8, 6 * D), bias=plain(blocks, tree), corner=plain(SPAN, SPAN),
        h1=short(tree, D), q_masked=short(2, tree, 128), key=short(tree, 128), value=short(tree, 128),
        key_t=short(128, tree), value_t=short(2, HEAD + 16, tree),
        weights=short(tiles * (tiles + 1) // 2, 2, SPAN, SPAN), inverse=plain(2, 8, tree),
        attended_t=plain(128, tree), attended=short(tree, 128), gathered=short(rows, D),
        cross_k=short(4, 2 * ENC, 128), cross_v=short(4, 2 * ENC, 128), cross_q=short(rows, D), cross_p=short(4, rows, 128),
        cross_out=short(rows, D), y1=plain(rows, D), db1=short(rows, D), h2=short(rows, D), h3=short(rows, D),
        act=short(rows, FF), d_hidden=short(rows, FF),
        d_cross=plain(ENC, 2 * D), dcq=short(rows, D), d_att_all=short(tree, 128),
        dk=plain(tree, 128), dv=plain(tree, 128),
        d_pair=short(tree, 384), from_core=short(4, SPAN, D), dh1_box=short(2, 2, SPAN, D),
        grad_pack=short(D, CROSS + FF), grad_w_out=short(FF, D), grad_pair=short(D, 384), source_part=plain(ENC, D),
        payload=plain(count * 8, 128), table_box=plain(count * 8, 128), table_rows=plain(levels * 16, 128), settle_box=plain(ENC, D),
        a_send=dma((tiles,)), a_recv=dma((tiles,)), d_send=dma((8,)), d_recv=dma((8,)),
        h_send=dma((tiles,)), h_core=dma((4,)), h_recv=dma((4,)),
        send=dma((7, Gather.sends(levels))), recv=dma((7, count)),
        pair_send=dma((GatherPair.sends(levels),)), pair_recv=dma((GatherPair.receives(levels),)),
        share_send=dma((Share.sends,)), share_recv=dma((8,)), spread_send=dma((3,)), spread_recv=dma((4,)),
        r_send=dma((6, Reduce.slots(levels))), r_recv=dma((6, Reduce.slots(levels))), line=plain(64, 128),
        rp_send=dma((ReducePair.slots(levels),)), rp_recv=dma((ReducePair.slots(levels),)),
        settle_send=dma((4,)), settle_recv=dma((4,)), t_send=dma((4 + 2 * levels,)), t_recv=dma((4 + 2 * levels,)),
    )
    for piece, (height, width, line_last) in enumerate(
        [(FF // count, end - start, False) for start, end in LAST]
        + [(each, end - start, True) for start, end in PACKED[2:] + PACKED[:2]]
    ):
        for n, box in enumerate(Reduce.boxes(levels, height, width, BF, line_last)):
            scratch[f"box{piece}_{n}"] = box
    for n, box in enumerate(ReducePair.boxes(levels, each, 384, BF)):
        scratch[f"box_pair{n}"] = box
    return scratch


def layer_kernel(levels, wide, names, refs):
    place = Place(levels)
    refs = dict(zip(names, refs))
    refs["y2"] = refs["dy"] = refs["grad_tokens"]
    refs["db2"] = refs["db"] = refs["h3"]
    refs["d_attn"] = refs["cross_q"]
    refs["dh1_part"] = refs["tokens_all"]
    w = Weights(place, refs)
    blk, leaf = place.blk, place.leaf
    rows = w.tokens.shape[0]
    tree = w.tokens_all.shape[0]
    tiles = tree // SPAN
    halves = rows // SPAN
    blocks = tree // BLOCK
    count = levels * 8
    each = D // count
    index = leaf * 4 + blk
    own_lanes = pl.ds(pl.multiple_of(place.pair * 128, 128), 128)

    mine = rows_of(index, each)
    moves = [
        (w.i_tokens, w.tokens), (w.i_qkv, w.qkv_own),
        (w.i_encoded, w.source_all.at[rows_of(blk, w.i_encoded.shape[0]), :]),
        (w.i_out, w.w_out.at[rows_of(index, w.i_out.shape[0]), :]),
    ]
    start = 0
    for name in ("i_o", "i_cq", "i_ckv", "i_co", "i_in"):
        width = refs[name].shape[1]
        moves.append((refs[name], w.pack.at[mine, start:start + width]))
        start += width
    copies = [pltpu.make_async_copy(src, dst, w.in_sem.at[n]) for n, (src, dst) in enumerate(moves)]
    for copy in copies:
        copy.start()
    lane = iota((1, 128), 1)
    parents = jnp.zeros((1, 128), F32)
    for block in range(blocks):
        parents = jnp.where(lane == block, w.parents[0, block].astype(F32), parents)
    w.line[...] = jnp.zeros_like(w.line)
    w.line[:STEPS, :wide] = w.i_table[...].astype(F32)
    w.line[STEPS:STEPS + 1, :] = jnp.full((1, 128), w.timestep[0].astype(F32))
    w.line[STEPS + 1:STEPS + 2, :] = parents
    w.aux[rows_of(index, 64), :] = w.line[...].astype(BF)
    place.greet()
    for copy in copies:
        copy.wait()
    late = pltpu.make_async_copy(w.i_cotangent, w.cotangent, w.in_sem.at[10])
    late.start()

    def keep_tokens():
        w.tokens_all[rows_of(blk, rows), :] = w.tokens[...]

    pl.when(place.main)(keep_tokens)
    for pair in range(4):
        for third in range(3):
            w.held[rows_of(place.z, each), 384 * pair + 128 * third:384 * pair + 128 * third + 128] = (
                w.qkv_own[:, D * third + 128 * pair:D * third + 128 * pair + 128])
    given = []

    def give(*outs):
        for name in outs:
            copy = pltpu.make_async_copy(refs[name], refs["o_" + name], w.out_sem.at[OUTS.index(name)])
            copy.start()
            given.append(copy)

    weave = GatherPair(place, w.held, w.w_pair, w.transit, w.pair_send, w.pair_recv)
    table = GatherLine(place, w.aux, 64, slice(None), w.send.at[6], w.recv.at[6])
    share = Share(place, w.tokens, w.tokens_all, w.share_send, w.share_recv)
    spread = Spread(place, w.source_all, w.i_encoded.shape[0], w.spread_send, w.spread_recv)
    loads = [
        (GatherLine if n < 2 else Gather)(place, w.pack, each, slice(*cut), w.send.at[n], w.recv.at[n]) for n, cut in enumerate(PACKED)
    ] + [
        Gather(place, w.w_out, FF // count, slice(*cut), w.send.at[4 + n], w.recv.at[4 + n], FIXED and n == 0) for n, cut in enumerate(LAST)
    ]
    weave_steps, table_steps, share_steps = weave.steps(), table.steps(), share.steps()
    load_steps = [load.steps() for load in loads]

    def ticks(steps, number=1):
        for turn in range(number):
            for step in steps:
                next(step, None)

    first, fore, rest = load_steps[:2], load_steps[2:4], load_steps[4:]
    beats = iter([first, first + fore + rest, first + fore, first + rest, fore + rest, fore + rest])

    def load_tick():
        ticks(next(beats, []))

    ticks([weave_steps, table_steps, share_steps])
    spread.start()
    w.mod_grad[...] = jnp.zeros_like(w.mod_grad)
    w.d_cross[...] = jnp.zeros_like(w.d_cross)
    w.dk[...] = jnp.zeros_like(w.dk)
    w.dv[...] = jnp.zeros_like(w.dv)
    row, column = iota((SPAN, SPAN), 0), iota((SPAN, SPAN), 1)
    w.corner[...] = jnp.where(((row < BLOCK) == (column < BLOCK)) & (row > column), -1e30, 0.0)
    ticks([weave_steps, table_steps])
    ticks(load_steps)
    ticks([table_steps, share_steps, weave_steps])
    ticks(load_steps[2:])
    ticks([table_steps, weave_steps], 6)
    load_tick()
    block_bias(aux_row(w.aux, place.served, STEPS + 1), w.bias, blocks)
    read_modulation(w.aux, w.timestep[0].astype(F32), w.mod, wide)
    read_modulation(w.aux, aux_row(w.aux, place.served, STEPS)[0:1, 0:1], w.mod_served, wide)

    def project(block):
        share.arrive(block)
        for half in range(halves):
            w.project(block * halves + half)

    project(blk)
    project(place.far)
    ticks([share_steps])
    project(place.near)
    ticks([share_steps])
    load_tick()
    project(place.opposite)

    def attended_copy(tile, pair, here):
        there = w.gathered.at[span(tile % halves), pl.ds(pl.multiple_of(pair * 128, 128), 128)]
        to_leaf, to_blk = (leaf, place.near) if here else (place.served, tile // halves)
        return remote(w.attended.at[span(tile), :], there, w.a_send.at[tile], w.a_recv.at[pair * halves + tile % halves], to_leaf, to_blk)

    def mine_too(tile):
        return (place.served == leaf) & (blk == tile // halves)

    for tile in range(tiles):
        w.attend(tile)
        away = jnp.logical_not(mine_too(tile))
        pl.when(away)(lambda tile=tile: attended_copy(tile, place.pair, False).start())

        def keep(tile=tile):
            w.gathered[span(tile % halves), own_lanes] = w.attended[span(tile), :]

        pl.when(jnp.logical_not(away))(keep)
        if tile in (tiles - 3, tiles - 1):
            load_tick()
    spread.arrive()
    w.cross_keys()
    for pair in range(4):
        for half in range(halves):
            other = jnp.logical_not(place.main & (place.pair == pair))
            pl.when(other)(lambda pair=pair, half=half: attended_copy(half, pair, True).wait_recv())
    for half in range(halves):
        w.middle(half)
        load_tick()
    late.wait()

    def writer(*outs):
        def store(there, value):
            start = 0
            for out, at, width in outs:
                out[there, at:at + width] = value[:, start:start + width]
                start += width

        return store

    writers = [
        writer((w.g_out, 0, D // 2)), writer((w.g_out, D // 2, D // 2)),
        writer((w.g_in, 0, FF // 2)), writer((w.g_in, FF // 2, FF // 2)),
        writer((w.g_o, 0, D), (w.g_cq, 0, D)), writer((w.g_ckv, 0, 2 * D), (w.g_co, 0, D)),
    ]
    sums = []
    for n, (total, height, cut) in enumerate(
        [(w.grad_w_out, FF // count, cut) for cut in LAST] + [(w.grad_pack, each, cut) for cut in PACKED[2:] + PACKED[:2]]
    ):
        sums.append(Reduce(place, total, height, slice(*cut), writers[n], [refs[f"box{n}_{k}"] for k in range(4)],
                           w.r_send.at[n], w.r_recv.at[n], n >= 2))
    out0, out1, in0, in1, cross0, cross1 = sum_steps = [job.steps() for job in sums]
    outs, units, cross = [out0, out1], [in0, in1], [cross0, cross1]
    half_way = FF // SPAN // 2
    loop(half_way, w.hidden)
    ticks([in0])
    loop(half_way // 2, lambda step: w.hidden(half_way + step))
    ticks([in0])
    loop(half_way // 2, lambda step: w.hidden(half_way + half_way // 2 + step))
    ticks(outs + [in1])
    loop(halves, w.finish_forward)
    give("mixed")
    loop(halves, w.back_three)
    ticks(outs)

    def da_copy(src, pair, half):
        return remote(w.d_attn.at[span(half), pair * 128:pair * 128 + 128], w.d_att_all.at[span(src * halves + half), :],
                      w.d_send.at[pair * 2 + half], w.d_recv.at[src * 2 + half], 2 * place.z + pair % 2, 2 * place.core + pair // 2)

    def stays(pair):
        return place.main & (place.pair == pair)

    for half in range(halves):
        w.back_cross(half)
        for pair in range(4):
            pl.when(jnp.logical_not(stays(pair)))(lambda pair=pair, half=half: da_copy(blk, pair, half).start())

    def keep_da():
        w.d_att_all[rows_of(blk, rows), :] = w.d_attn[:, own_lanes]

    pl.when(place.main)(keep_da)
    ticks(outs + [in1])
    w.grad_into(4 * D, w.cross_out, w.db2)
    w.grad_into(0, w.gathered, w.db1)
    w.grad_into(D, w.h2, w.dcq)
    low_cross = w.d_cross[...].astype(BF)
    for step in range(2 * D // SPAN):
        columns = slice(2 * D + step * SPAN, 2 * D + (step + 1) * SPAN)
        w.grad_pack[:, columns] = dot_tn(w.source_all[...], low_cross[:, step * SPAN:(step + 1) * SPAN]).astype(BF)
    w.source_part[...] = dot_nt(low_cross, w.w_ckv)
    settle = Settle(place, w.source_part, w.g_encoded, w.settle_box, w.settle_send, w.settle_recv)
    settle_steps = settle.steps()
    ticks(cross + [settle_steps])
    for job in loads + [weave, table, share, spread]:
        job.finish()
    for src in range(4):
        for half in range(halves):
            pl.when(jnp.logical_not(place.main & (blk == src)))(lambda src=src, half=half: da_copy(src, 0, half).wait_recv())

    tree_sum = TreeReduce(place, w.dh1_part, w.from_core, w.dh1_box, w.h_send, w.h_core, w.h_recv)
    plan = [
        (tiles - 1, cross + [settle_steps]), (tiles - 2, units), (tiles - 3, outs), (tiles - 4, cross),
        (tiles - 5, units), (tiles - 6, outs), (tiles - 7, cross),
    ]
    for tile in range(tiles - 1, -1, -1):
        w.attend_back(tile)
        tree_sum.offer(tile)
        if tile + 1 < tiles:
            tree_sum.collect(tile + 1)
        for when, steps in plan:
            if when == tile:
                ticks(steps)

    def pair_grad(step):
        w.grad_pair[span(step), :] = dot_tn(w.h1[:, span(step)], w.d_pair[...]).astype(BF)

    loop(D // SPAN, pair_grad)
    pair_sum = ReducePair(place, w.grad_pair, w.g_qkv, [refs[f"box_pair{n}"] for n in range(3)], w.rp_send, w.rp_recv)
    pair_steps = pair_sum.steps()
    ticks([pair_steps])
    tree_sum.collect(0)
    ticks([pair_steps])

    def last(half):
        tree_sum.arrive(half)
        here = span(half)
        dh1 = w.dh1_box[half, 0].astype(F32) + w.dh1_box[half, 1].astype(F32)
        unit, root = unit_rows(w.tokens[here, :].astype(F32))
        w.sums(0, dh1, dh1 * unit)
        w.grad_tokens[here, :] = w.dy[here, :] + norm_back(dh1, unit, root, w.mod[0:1, D:2 * D])

    for half in range(halves):
        last(half)
    give("grad_tokens")
    w.payload[...] = table_payload(w.mod_grad[0:1, :], wide, count)
    table_sum = TableSum(place, w.payload, w.table_box, w.table_rows, w.t_send, w.t_recv)
    table_steps = table_sum.steps()
    ticks([table_steps])
    ticks(sum_steps, 10)
    give("g_encoded", "g_o", "g_cq", "g_ckv", "g_co", "g_in", "g_out")
    for tile in range(tiles):
        pl.when(jnp.logical_not(mine_too(tile)))(lambda tile=tile: attended_copy(tile, place.pair, False).wait_send())
        tree_sum.finish(tile)
    for pair in range(4):
        for half in range(halves):
            pl.when(jnp.logical_not(stays(pair)))(lambda pair=pair, half=half: da_copy(blk, pair, half).wait_send())
    for job in sums + [settle]:
        job.finish()
    ticks([pair_steps, table_steps], 10)
    give("g_qkv")

    leaves = levels * 2
    chosen = (iota((leaves, count * 64), 1) == iota((leaves, count * 64), 0) * 256 + STEPS).astype(BF)
    steps_all = dot(chosen, w.aux[...])
    line = iota((64, 128), 0).astype(F32)
    grad_table = jnp.zeros((64, 128), F32)
    for tree_at in range(leaves):
        grad_table = grad_table + jnp.where(line == steps_all[tree_at:tree_at + 1, :], w.table_rows[8 * tree_at:8 * tree_at + 1, :], 0.0)
    w.g_table[...] = grad_table
    give("g_table")

    for job in (pair_sum, table_sum):
        job.finish()
    for copy in given:
        copy.wait()


def copy_kernel(count, refs):
    ins, outs, held, sems = refs[:count], refs[count:2 * count], refs[2 * count:3 * count], refs[3 * count]
    inward = [pltpu.make_async_copy(ins[n], held[n], sems.at[0, n]) for n in range(count)]
    outward = [pltpu.make_async_copy(held[n], outs[n], sems.at[1, n]) for n in range(count)]
    for copy in inward:
        copy.start()
    for copy, then in zip(inward, outward):
        copy.wait()
        then.start()
    for copy in outward:
        copy.wait()


def copy_all(arrays):
    return pl.pallas_call(
        lambda *refs: copy_kernel(len(arrays), refs),
        out_shape=[jax.ShapeDtypeStruct(array.shape, array.dtype) for array in arrays],
        in_specs=[ANY] * len(arrays),
        out_specs=[ANY] * len(arrays),
        scratch_shapes=[pltpu.VMEM(array.shape, array.dtype) for array in arrays] + [pltpu.SemaphoreType.DMA((2, len(arrays)))],
    )(*arrays)


def per_device(tokens, cotangent, encoded, parents, timestep, w_qkv, w_o, w_cq, w_ckv, w_co, w_in, w_out, mod_table):
    levels = lax.axis_size("leaf") // 2
    rows, wide = tokens.shape[0], mod_table.shape[1]
    blocks = parents.shape[1]
    tree = blocks * BLOCK
    ins = (tokens, cotangent, encoded, parents, timestep, w_qkv, w_o, w_cq, w_ckv, w_co, w_in, w_out, mod_table)
    scratch = layer_scratch(rows, tree, blocks, levels, wide)
    out = lambda like: jax.ShapeDtypeStruct(like.shape, F32)
    names = INS + tuple("o_" + name for name in OUTS) + tuple(scratch)
    *outs, table_grad = copy_all(pl.pallas_call(
        lambda *refs: layer_kernel(levels, wide, names, refs),
        out_shape=[jax.ShapeDtypeStruct((rows, D), BF), out(tokens), out(encoded)]
        + [out(weight) for weight in (w_qkv, w_o, w_cq, w_ckv, w_co, w_in, w_out)] + [jax.ShapeDtypeStruct((64, 128), F32)],
        in_specs=[SMEM if name in ("parents", "timestep") else VMEM if name == "i_table" else ANY for name in INS],
        out_specs=[ANY] * len(OUTS),
        scratch_shapes=list(scratch.values()),
        compiler_params=pltpu.CompilerParams(collective_id=0, has_side_effects=True, vmem_limit_bytes=(64 << 20) - (64 << 10)),
    )(*ins))
    return (*outs, table_grad[:STEPS, :wide])


def solution(mesh):
    fits = mesh.shape["blk"] == 4 and mesh.shape["leaf"] == 8
    return jax.shard_map(
        per_device if fits else generic_device,
        mesh=mesh,
        in_specs=(
            P(("leaf", "blk"), None),
            P(("leaf", "blk"), None),
            P(("leaf", "blk"), None),
            P("leaf", None),
            P("leaf"),
            P(("leaf", "blk"), None),
            P(("leaf", "blk"), None),
            P(("leaf", "blk"), None),
            P(("leaf", "blk"), None),
            P(("leaf", "blk"), None),
            P(("leaf", "blk"), None),
            P(("leaf", "blk"), None),
            P(None, ("leaf", "blk")),
        ),
        out_specs=(
            P(("leaf", "blk"), None),
            P(("leaf", "blk"), None),
            P(("leaf", "blk"), None),
            P(("leaf", "blk"), None),
            P(("leaf", "blk"), None),
            P(("leaf", "blk"), None),
            P(("leaf", "blk"), None),
            P(("leaf", "blk"), None),
            P(("leaf", "blk"), None),
            P(("leaf", "blk"), None),
            P(None, ("leaf", "blk")),
        ),
        check_vma=False,
    )
```

```python
import functools

import jax
import jax.numpy as jnp
from jax import lax
from jax.experimental import pallas as pl
from jax.experimental.pallas import tpu as pltpu
from jax.sharding import PartitionSpec as P

D = 512
HEADS = 8
HEAD = 64
BLOCK = 128
FF = 2048
ENC = 64
STEPS = 50


PRECISE = lax.Precision.HIGHEST
MASKED = -1e30


def ancestors(parent_row):
    count = parent_row.shape[0]
    indices = jnp.arange(count, dtype=jnp.int32)
    reach_map = (indices[:, None] == indices[None, :]).astype(jnp.float32)
    reach_map = jnp.minimum(
        reach_map + (parent_row[:, None] == indices[None, :]).astype(jnp.float32), 1.0
    )
    for rounds in range(max(1, (count - 1).bit_length())):
        reach_map = jnp.minimum(jnp.dot(reach_map, reach_map, precision=PRECISE), 1.0)
    return reach_map


def normalize(values, shift, scaling):
    centred = values - jnp.mean(values, axis=-1, keepdims=True)
    spread = jnp.mean(centred * centred, axis=-1, keepdims=True)
    return centred * lax.rsqrt(spread + 1e-05) * (1.0 + scaling) + shift


def span_link(reach_rows, span):
    return lax.dynamic_slice_in_dim(reach_rows, span * 4, 4, 1)


def span_reached(reach_rows, span):
    return jnp.max(span_link(reach_rows, span)) > 0.5


def span_mask(reach_rows, first_block, span, row_count, width):
    query_index = jnp.arange(row_count, dtype=jnp.int32)
    key_index = jnp.arange(width, dtype=jnp.int32)
    query_block = first_block + query_index // BLOCK
    key_block = span * 4 + key_index // BLOCK
    link = span_link(reach_rows, span)
    link = jnp.repeat(jnp.repeat(link, BLOCK, axis=0), BLOCK, axis=1)
    same = query_block[:, None] == key_block[None, :]
    return (link > 0.5) & (
        jnp.logical_not(same) | (key_index[None, :] % BLOCK <= query_index[:, None] % BLOCK)
    )


def scores_of(queries, key_rows, allowed):
    raw = jnp.einsum(
        "qhd,khd->hqk", queries, key_rows, preferred_element_type=jnp.float32
    ) * HEAD ** (-0.5)
    return jnp.where(allowed[None], raw, MASKED)


def split_spans(keys, values):
    width = 4 * BLOCK
    count = keys.shape[0] // width
    return (
        jnp.arange(count, dtype=jnp.int32),
        keys.reshape(count, width, HEADS, HEAD),
        values.reshape(count, width, HEADS, HEAD),
    )


def tree_forward_attention(queries, keys, values, reach_rows, first_block):
    row_count = queries.shape[0]
    width = 4 * BLOCK
    spans, key_spans, value_spans = split_spans(keys, values)

    def stats(carry, item):
        span, key_rows = item

        def stats_visit(state):
            top, total = state
            allowed = span_mask(reach_rows, first_block, span, row_count, width)
            score = scores_of(queries, key_rows, allowed)
            new_top = jnp.maximum(top, jnp.max(score, axis=-1))
            weight = jnp.where(allowed[None], jnp.exp(score - new_top[..., None]), 0.0)
            return (new_top, total * jnp.exp(top - new_top) + jnp.sum(weight, axis=-1))

        return (
            lax.cond(span_reached(reach_rows, span), stats_visit, lambda state: state, carry),
            None,
        )

    start = (
        jnp.full((HEADS, row_count), MASKED, jnp.float32),
        jnp.zeros((HEADS, row_count), jnp.float32),
    )
    (top, total), unused = lax.scan(stats, start, (spans, key_spans))
    log_total = top + jnp.log(total)

    def collect(accum, item):
        span, key_rows, value_rows = item

        def collect_visit(current):
            allowed = span_mask(reach_rows, first_block, span, row_count, width)
            weight = jnp.where(
                allowed[None],
                jnp.exp(scores_of(queries, key_rows, allowed) - log_total[..., None]),
                0.0,
            )
            return current + jnp.einsum(
                "hqk,khd->qhd",
                weight.astype(jnp.bfloat16),
                value_rows,
                preferred_element_type=jnp.float32,
            )

        return (
            lax.cond(span_reached(reach_rows, span), collect_visit, lambda current: current, accum),
            None,
        )

    attended, unused = lax.scan(
        collect, jnp.zeros((row_count, HEADS, HEAD), jnp.float32), (spans, key_spans, value_spans)
    )
    return (attended, log_total)


def tree_backward_attention(queries, keys, values, reach_rows, first_block, log_total, grad_attn):
    row_count = queries.shape[0]
    width = 4 * BLOCK
    spans, key_spans, value_spans = split_spans(keys, values)

    def probs_of(span, key_rows):
        allowed = span_mask(reach_rows, first_block, span, row_count, width)
        return jnp.where(
            allowed[None],
            jnp.exp(scores_of(queries, key_rows, allowed) - log_total[..., None]),
            0.0,
        )

    def inner_pass(total, item):
        span, key_rows, value_rows = item

        def inner_visit(current):
            weight = probs_of(span, key_rows)
            d_weight = jnp.einsum(
                "qhd,khd->hqk", grad_attn, value_rows, preferred_element_type=jnp.float32
            )
            return current + jnp.sum(weight * d_weight, axis=-1)

        return (
            lax.cond(span_reached(reach_rows, span), inner_visit, lambda current: current, total),
            None,
        )

    delta, unused = lax.scan(
        inner_pass, jnp.zeros((HEADS, row_count), jnp.float32), (spans, key_spans, value_spans)
    )

    def grad_pass(d_queries, item):
        span, key_rows, value_rows = item

        def grad_visit(current):
            weight = probs_of(span, key_rows)
            d_weight = jnp.einsum(
                "qhd,khd->hqk", grad_attn, value_rows, preferred_element_type=jnp.float32
            )
            d_score = (weight * (d_weight - delta[..., None])).astype(jnp.bfloat16)
            current = current + jnp.einsum(
                "hqk,khd->qhd", d_score, key_rows, preferred_element_type=jnp.float32
            )
            d_keys = jnp.einsum(
                "hqk,qhd->khd", d_score, queries, preferred_element_type=jnp.float32
            ) * HEAD ** (-0.5)
            d_values = jnp.einsum(
                "hqk,qhd->khd",
                weight.astype(jnp.bfloat16),
                grad_attn,
                preferred_element_type=jnp.float32,
            )
            return (
                current,
                jnp.concatenate((d_keys.reshape(width, D), d_values.reshape(width, D)), axis=1),
            )

        def skip(current):
            return (current, jnp.zeros((width, 2 * D), jnp.float32))

        return lax.cond(span_reached(reach_rows, span), grad_visit, skip, d_queries)

    d_queries, terms = lax.scan(
        grad_pass, jnp.zeros((row_count, HEADS, HEAD), jnp.float32), (spans, key_spans, value_spans)
    )
    return (d_queries * HEAD ** (-0.5), terms.reshape(-1, 2 * D))


def generic_device(
    tokens,
    cotangent,
    encoded,
    parents,
    timestep,
    w_qkv,
    w_o,
    w_cq,
    w_ckv,
    w_co,
    w_in,
    w_out,
    mod_table,
):
    gathered = (
        lax.all_gather(w_qkv, ("leaf", "blk"), axis=0, tiled=True),
        lax.all_gather(w_o, ("leaf", "blk"), axis=0, tiled=True),
        lax.all_gather(w_cq, ("leaf", "blk"), axis=0, tiled=True),
        lax.all_gather(w_ckv, ("leaf", "blk"), axis=0, tiled=True),
        lax.all_gather(w_co, ("leaf", "blk"), axis=0, tiled=True),
        lax.all_gather(w_in, ("leaf", "blk"), axis=0, tiled=True),
        lax.all_gather(w_out, ("leaf", "blk"), axis=0, tiled=True),
        lax.all_gather(mod_table, ("leaf", "blk"), axis=1, tiled=True),
    )
    g_qkv, g_o, g_cq, g_ckv, g_co, g_in, g_out, g_table = gathered
    select = (jnp.arange(STEPS, dtype=jnp.int32) == timestep[0]).astype(jnp.float32)
    modulate = jnp.dot(
        select.astype(jnp.bfloat16)[None, :], g_table, preferred_element_type=jnp.float32
    )[0]
    pieces = [modulate[i * D : (i + 1) * D] for i in range(6)]
    inputs = tokens.astype(jnp.float32)
    row_count = tokens.shape[0]
    local_blocks = row_count // BLOCK
    first_block = lax.axis_index("blk") * local_blocks
    reach_map = ancestors(parents[0])
    reach_rows = lax.dynamic_slice_in_dim(reach_map, first_block, local_blocks, 0)
    scaling = HEAD ** (-0.5)
    normed_one, pull_one = jax.vjp(normalize, inputs, pieces[0], pieces[1])
    h_first = normed_one.astype(jnp.bfloat16)
    projected = jnp.dot(h_first, g_qkv, preferred_element_type=jnp.float32).astype(jnp.bfloat16)
    queries = projected[:, :D].reshape(row_count, HEADS, HEAD)
    keys, values = (
        lax.all_gather(projected[:, D : 2 * D], "blk", axis=0, tiled=True),
        lax.all_gather(projected[:, 2 * D :], "blk", axis=0, tiled=True),
    )
    attended, log_total = tree_forward_attention(queries, keys, values, reach_rows, first_block)
    attn_low = attended.reshape(row_count, D).astype(jnp.bfloat16)
    middle_one = inputs + jnp.dot(attn_low, g_o, preferred_element_type=jnp.float32)
    normed_two, pull_two = jax.vjp(normalize, middle_one, pieces[2], pieces[3])
    h_second = normed_two.astype(jnp.bfloat16)
    cross_q = (
        jnp.dot(h_second, g_cq, preferred_element_type=jnp.float32)
        .astype(jnp.bfloat16)
        .reshape(row_count, HEADS, HEAD)
    )
    source_local = jnp.dot(encoded, g_ckv, preferred_element_type=jnp.float32).astype(jnp.bfloat16)
    source_all = lax.all_gather(source_local, "blk", axis=0, tiled=True)
    cross_k = source_all[:, :D].reshape(-1, HEADS, HEAD)
    cross_v = source_all[:, D:].reshape(-1, HEADS, HEAD)
    cross_raw = (
        jnp.einsum("qhd,khd->hqk", cross_q, cross_k, preferred_element_type=jnp.float32) * scaling
    )
    cross_prob = jax.nn.softmax(cross_raw, axis=-1)
    cross_low = cross_prob.astype(jnp.bfloat16)
    cross_out = (
        jnp.einsum("hqk,khd->qhd", cross_low, cross_v, preferred_element_type=jnp.float32)
        .reshape(row_count, D)
        .astype(jnp.bfloat16)
    )
    middle_two = middle_one + jnp.dot(cross_out, g_co, preferred_element_type=jnp.float32)
    normed_three, pull_three = jax.vjp(normalize, middle_two, pieces[4], pieces[5])
    h_third = normed_three.astype(jnp.bfloat16)
    hidden_pre = jnp.dot(h_third, g_in, preferred_element_type=jnp.float32)
    activated, pull_gelu = jax.vjp(
        lambda values_in: jax.nn.gelu(values_in, approximate=True), hidden_pre
    )
    act_low = activated.astype(jnp.bfloat16)
    result = middle_two + jnp.dot(act_low, g_out, preferred_element_type=jnp.float32)
    mixed_out = result.astype(jnp.bfloat16)
    back_weights = (
        lax.all_gather(w_qkv, ("leaf", "blk"), axis=0, tiled=True),
        lax.all_gather(w_o, ("leaf", "blk"), axis=0, tiled=True),
        lax.all_gather(w_cq, ("leaf", "blk"), axis=0, tiled=True),
        lax.all_gather(w_ckv, ("leaf", "blk"), axis=0, tiled=True),
        lax.all_gather(w_co, ("leaf", "blk"), axis=0, tiled=True),
        lax.all_gather(w_in, ("leaf", "blk"), axis=0, tiled=True),
        lax.all_gather(w_out, ("leaf", "blk"), axis=0, tiled=True),
        lax.all_gather(mod_table, ("leaf", "blk"), axis=1, tiled=True),
    )
    b_qkv, b_o, b_cq, b_ckv, b_co, b_in, b_out = back_weights[:7]
    d_act = jnp.dot(cotangent, b_out.T, preferred_element_type=jnp.float32)
    d_hidden = pull_gelu(d_act)[0].astype(jnp.bfloat16)
    grad_out_w = jnp.dot(act_low.T, cotangent, preferred_element_type=jnp.float32)
    grad_in_w = jnp.dot(h_third.T, d_hidden, preferred_element_type=jnp.float32)
    d_h_third = jnp.dot(d_hidden, b_in.T, preferred_element_type=jnp.float32)
    d_middle_part, d_shift_three, d_scale_three = pull_three(d_h_third)
    d_middle_two = cotangent.astype(jnp.float32) + d_middle_part
    d_branch_two = d_middle_two.astype(jnp.bfloat16)
    grad_co_w = jnp.dot(cross_out.T, d_branch_two, preferred_element_type=jnp.float32)
    d_cross_out = (
        jnp.dot(d_branch_two, b_co.T, preferred_element_type=jnp.float32)
        .astype(jnp.bfloat16)
        .reshape(row_count, HEADS, HEAD)
    )
    d_cross_prob = jnp.einsum(
        "qhd,khd->hqk", d_cross_out, cross_v, preferred_element_type=jnp.float32
    )
    d_cross_raw = (
        cross_prob * (d_cross_prob - jnp.sum(cross_prob * d_cross_prob, axis=-1, keepdims=True))
    ).astype(jnp.bfloat16)
    d_cross_q = (
        (
            jnp.einsum("hqk,khd->qhd", d_cross_raw, cross_k, preferred_element_type=jnp.float32)
            * scaling
        )
        .reshape(row_count, D)
        .astype(jnp.bfloat16)
    )
    d_cross_k = (
        jnp.einsum("hqk,qhd->khd", d_cross_raw, cross_q, preferred_element_type=jnp.float32)
        * scaling
    )
    d_cross_v = jnp.einsum(
        "hqk,qhd->khd", cross_low, d_cross_out, preferred_element_type=jnp.float32
    )
    source_terms = jnp.concatenate((d_cross_k.reshape(-1, D), d_cross_v.reshape(-1, D)), axis=1)
    d_source = lax.psum_scatter(
        source_terms.astype(jnp.bfloat16), "blk", scatter_dimension=0, tiled=True
    )
    grad_ckv_w = jnp.dot(encoded.T, d_source, preferred_element_type=jnp.float32)
    d_encoded = jnp.dot(d_source, b_ckv.T, preferred_element_type=jnp.float32)
    grad_cq_w = jnp.dot(h_second.T, d_cross_q, preferred_element_type=jnp.float32)
    d_h_second = jnp.dot(d_cross_q, b_cq.T, preferred_element_type=jnp.float32)
    d_middle_part, d_shift_two, d_scale_two = pull_two(d_h_second)
    d_middle_one = d_middle_two + d_middle_part
    d_branch_one = d_middle_one.astype(jnp.bfloat16)
    grad_o_w = jnp.dot(attn_low.T, d_branch_one, preferred_element_type=jnp.float32)
    d_attn = (
        jnp.dot(d_branch_one, b_o.T, preferred_element_type=jnp.float32)
        .astype(jnp.bfloat16)
        .reshape(row_count, HEADS, HEAD)
    )
    keys_back, values_back = (
        lax.all_gather(projected[:, D : 2 * D], "blk", axis=0, tiled=True),
        lax.all_gather(projected[:, 2 * D :], "blk", axis=0, tiled=True),
    )
    d_queries, key_terms = tree_backward_attention(
        queries, keys_back, values_back, reach_rows, first_block, log_total, d_attn
    )
    d_key_value = lax.psum_scatter(
        key_terms.astype(jnp.bfloat16), "blk", scatter_dimension=0, tiled=True
    ).astype(jnp.float32)
    d_projected = jnp.concatenate((d_queries.reshape(row_count, D), d_key_value), axis=1).astype(
        jnp.bfloat16
    )
    grad_qkv_w = jnp.dot(h_first.T, d_projected, preferred_element_type=jnp.float32)
    d_h_first = jnp.dot(d_projected, b_qkv.T, preferred_element_type=jnp.float32)
    d_input_part, d_shift_one, d_scale_one = pull_one(d_h_first)
    d_tokens = d_middle_one + d_input_part
    d_modulate = jnp.concatenate(
        (d_shift_one, d_scale_one, d_shift_two, d_scale_two, d_shift_three, d_scale_three)
    )
    grad_table_w = select[:, None] * d_modulate[None, :]
    gradients = (
        lax.psum_scatter(grad_qkv_w, ("leaf", "blk"), scatter_dimension=0, tiled=True),
        lax.psum_scatter(grad_o_w, ("leaf", "blk"), scatter_dimension=0, tiled=True),
        lax.psum_scatter(grad_cq_w, ("leaf", "blk"), scatter_dimension=0, tiled=True),
        lax.psum_scatter(grad_ckv_w, ("leaf", "blk"), scatter_dimension=0, tiled=True),
        lax.psum_scatter(grad_co_w, ("leaf", "blk"), scatter_dimension=0, tiled=True),
        lax.psum_scatter(grad_in_w, ("leaf", "blk"), scatter_dimension=0, tiled=True),
        lax.psum_scatter(grad_out_w, ("leaf", "blk"), scatter_dimension=0, tiled=True),
        lax.psum_scatter(grad_table_w, ("leaf", "blk"), scatter_dimension=1, tiled=True),
    )
    return (
        mixed_out,
        d_tokens,
        d_encoded,
        gradients[0],
        gradients[1],
        gradients[2],
        gradients[3],
        gradients[4],
        gradients[5],
        gradients[6],
        gradients[7],
    )


MESH = pl.DeviceIdType.MESH
BF = jnp.bfloat16
F32 = jnp.float32


class Place:
    def __init__(self, levels):
        leaf = lax.axis_index("leaf")
        blk = lax.axis_index("blk")
        self.levels = levels
        self.leaf = leaf
        self.blk = blk
        self.z = leaf // 2
        self.core = leaf % 2
        self.near = blk + 1 - 2 * (blk % 2)
        self.far = (blk + 2) % 4
        self.first = self.core * self.near + (1 - self.core) * self.far
        self.second = self.core * self.far + (1 - self.core) * self.near
        self.opposite = 3 - blk
        self.sibling = self.z * 2 + 1 - self.core
        self.side = blk // 2
        self.served = self.z * 2 + self.side
        self.pair = blk % 2 * 2 + self.core
        self.main = self.side == self.core
        self.line = [(leaf + 2 * step) % (2 * levels) for step in range(1, levels)]

    def greet(self):
        barrier = pltpu.get_barrier_semaphore()

        count = self.levels * 2

        def hello(leaf, blk):
            pl.semaphore_signal(barrier, inc=1, device_id=(leaf, blk), device_id_type=MESH)

        for blk in (self.near, self.far, self.opposite):
            hello(self.leaf, blk)
            hello(self.sibling, blk)
        for step in range(1, count):
            hello((self.leaf + step) % count, self.blk)
        pl.semaphore_wait(barrier, count + 5)


def remote(src, dst, send, recv, leaf, blk):
    return pltpu.make_async_remote_copy(
        src_ref=src, dst_ref=dst, send_sem=send, recv_sem=recv,
        device_id=(leaf, blk), device_id_type=MESH,
    )


def rows_of(start, count):
    return pl.ds(pl.multiple_of(start * count, count), count)


class Gather:
    def __init__(self, place, full, rows, columns, send_sem, recv_sem, fixed=False):
        self.place, self.full, self.rows, self.columns = place, full, rows, columns
        self.send_sem, self.recv_sem = send_sem, recv_sem
        self.sent = []
        self.first = place.near if fixed else place.first
        self.second = place.far if fixed else place.second

    def build(self, leaf, blk, to_leaf, to_blk, number):
        there = self.full.at[rows_of(leaf * 4 + blk, self.rows), self.columns]
        return remote(there, there, self.send_sem.at[number], self.recv_sem.at[leaf * 4 + blk], to_leaf, to_blk)

    def push(self, leaf, blk, *targets):
        for to_leaf, to_blk in targets:
            copy = self.build(leaf, blk, to_leaf, to_blk, len(self.sent))
            copy.start()
            self.sent.append(copy)

    def arrive(self, leaf, blk):
        p = self.place
        self.build(leaf, blk, p.leaf, self.second, 0).wait_recv()

    def steps(self):
        p = self.place
        sibling, second = (p.sibling, p.blk), (p.leaf, self.second)
        line = [(leaf, p.blk) for leaf in p.line]
        self.push(p.leaf, p.blk, (p.leaf, self.first), *line, sibling)
        yield
        self.arrive(p.leaf, self.first)
        self.push(p.leaf, self.first, *line, sibling)
        yield
        self.push(p.leaf, p.blk, second)
        self.push(p.leaf, self.first, second)
        for leaf in p.line:
            self.arrive(leaf, p.blk)
            self.push(leaf, p.blk, second, sibling)
        yield
        for leaf in p.line:
            self.arrive(leaf, self.first)
            self.push(leaf, self.first, second, sibling)
        yield
        for leaf in (p.leaf, *p.line):
            for blk in (self.second, p.opposite):
                self.arrive(leaf, blk)
                self.push(leaf, blk, sibling)
        yield
        for level in range(p.levels):
            for blk in range(4):
                self.arrive(2 * level + 1 - p.core, blk)
        yield

    def finish(self):
        for copy in self.sent:
            copy.wait_send()

    @staticmethod
    def sends(levels):
        return 8 * levels


class Spread:
    def __init__(self, place, full, rows, send_sem, recv_sem):
        self.place, self.full, self.rows = place, full, rows
        self.send_sem, self.recv_sem = send_sem, recv_sem

    def build(self, blk, to_blk, number):
        there = self.full.at[rows_of(blk, self.rows), :]
        return remote(there, there, self.send_sem.at[number], self.recv_sem.at[blk], self.place.leaf, to_blk)

    def start(self):
        p = self.place
        self.copies = [self.build(p.blk, to, n) for n, to in enumerate((p.near, p.far, p.opposite))]
        for copy in self.copies:
            copy.start()

    def arrive(self):
        p = self.place
        for blk in (p.near, p.far, p.opposite):
            self.build(blk, p.near, 0).wait_recv()

    def finish(self):
        for copy in self.copies:
            copy.wait_send()


class Reduce:
    def __init__(self, place, total, rows, columns, store, boxes, send_sem, recv_sem, line_last):
        self.place, self.total, self.rows, self.columns, self.store = place, total, rows, columns, store
        self.from_sibling, self.from_second, self.from_line, self.from_first = boxes
        self.send_sem, self.recv_sem = send_sem, recv_sem
        self.line_last = line_last
        self.sent = []

    @staticmethod
    def slots(levels):
        return 6 * levels

    @staticmethod
    def boxes(levels, rows, width, kind, line_last):
        line, first = (levels, levels) if line_last else (2 * levels, 1)
        return [pltpu.VMEM((slots * rows, width), kind) for slots in (4 * levels, 2 * levels, line, first)]

    def here(self, leaf, blk):
        return (leaf * 4 + blk) * self.rows

    def part(self, leaf, blk, count=1):
        return self.total.at[pl.ds(pl.multiple_of(self.here(leaf, blk), self.rows), self.rows * count), self.columns]

    def copy(self, src, box, position, count, number, leaf, blk, sender=None):
        there = box.at[pl.ds(pl.multiple_of(position * self.rows, self.rows), self.rows * count), :]
        sender = number if sender is None else sender
        return remote(there if src is None else src, there, self.send_sem.at[sender], self.recv_sem.at[number], leaf, blk)

    def send(self, *parts):
        copy = self.copy(*parts)
        copy.start()
        self.sent.append(copy)

    def arrived(self, box, position, count, number):
        self.copy(None, box, position, count, number, self.place.leaf, self.place.first).wait_recv()

    def value(self, start, *sources):
        unit = pl.ds(pl.multiple_of(start, 16), 16)
        value = self.total[unit, self.columns].astype(F32)
        for box, position in sources:
            value = value + box[pl.ds(pl.multiple_of(position, 16), 16), :].astype(F32)
        return unit, value

    def add(self, leaf, blk, *sources, count=1):
        def one(step):
            unit, value = self.value(self.here(leaf, blk) + 16 * step, *[(box, slot * self.rows + 16 * step) for box, slot in sources])
            self.total[unit, self.columns] = value.astype(self.total.dtype)

        loop(count * self.rows // 16, one)

    def give(self, *sources):
        for step in range(self.rows // 16):
            unit, value = self.value(self.here(self.place.leaf, self.place.blk) + 16 * step,
                                     *[(box, slot * self.rows + 16 * step) for box, slot in sources])
            self.store(pl.ds(16 * step, 16), value)

    def steps(self):
        p = self.place
        levels = p.levels
        for level in range(levels):
            self.send(self.part(2 * level + 1 - p.core, 0, 4), self.from_sibling, 4 * level, 4, level, p.sibling, p.blk)
        yield
        for level in range(levels):
            self.arrived(self.from_sibling, 4 * level, 4, level)
            leaf = 2 * level + p.core
            self.add(leaf, 0, (self.from_sibling, 4 * level), count=4)
            for which, blk in enumerate((p.second, p.opposite)):
                slot = 2 * level + which
                self.send(self.part(leaf, blk), self.from_second, slot, 1, levels + slot, p.leaf, p.second)
        yield
        for level in range(levels):
            leaf = 2 * level + p.core
            for which, blk in enumerate((p.blk, p.first)):
                slot = 2 * level + which
                self.arrived(self.from_second, slot, 1, levels + slot)
                self.add(leaf, blk, (self.from_second, slot))
                if self.line_last and which == 1:
                    self.send(self.part(leaf, p.first), self.from_first, level, 1, 5 * levels + level, p.leaf, p.first)
        if self.line_last:
            yield
            for level in range(levels):
                self.arrived(self.from_first, level, 1, 5 * levels + level)
                self.add(2 * level + p.core, p.blk, (self.from_first, level))
        shards = (p.blk,) if self.line_last else (p.blk, p.first)
        slots = len(shards)
        for leaf in p.line:
            for which, blk in enumerate(shards):
                self.send(self.part(leaf, blk), self.from_line, slots * p.z + which, 1, 3 * levels + slots * p.z + which,
                          leaf, p.blk, 3 * levels + slots * (leaf // 2) + which)
        yield
        came = []
        for which, blk in enumerate(shards):
            slots_of = [slots * (leaf // 2) + which for leaf in p.line]
            for slot in slots_of:
                self.arrived(self.from_line, slot, 1, 3 * levels + slot)
            came.append([(self.from_line, slot) for slot in slots_of])
        if self.line_last:
            self.give(*came[0])
            yield
            return
        self.add(p.leaf, p.first, *came[1])
        self.send(self.part(p.leaf, p.first), self.from_first, 0, 1, 5 * levels, p.leaf, p.first)
        yield
        self.arrived(self.from_first, 0, 1, 5 * levels)
        self.give(*came[0], (self.from_first, 0))
        yield

    def finish(self):
        for copy in self.sent:
            copy.wait_send()


class GatherLine(Gather):
    def steps(self):
        p = self.place
        sibling, first, second = (p.sibling, p.blk), (p.leaf, self.first), (p.leaf, self.second)
        self.push(p.leaf, p.blk, *[(leaf, p.blk) for leaf in p.line], sibling)
        yield
        self.push(p.leaf, p.blk, first, second)
        for leaf in p.line:
            self.arrive(leaf, p.blk)
            self.push(leaf, p.blk, first, second, sibling)
        yield
        for leaf in (p.leaf, *p.line):
            self.arrive(leaf, self.first)
            self.push(leaf, self.first, second, sibling)
        yield
        for leaf in (p.leaf, *p.line):
            for blk in (self.second, p.opposite):
                self.arrive(leaf, blk)
                self.push(leaf, blk, sibling)
        yield
        for level in range(p.levels):
            for blk in range(4):
                self.arrive(2 * level + 1 - p.core, blk)
        yield


class Share:
    def __init__(self, place, own, full, send_sem, recv_sem):
        self.place, self.own, self.full = place, own, full
        self.rows = own.shape[0]
        self.half = self.rows // 2
        self.send_sem, self.recv_sem = send_sem, recv_sem
        self.sent = []

    def build(self, blk, half, to_leaf, to_blk, number, own=False):
        there = self.full.at[pl.ds(pl.multiple_of(blk * self.rows + half * self.half, self.half), self.half), :]
        src = self.own.at[pl.ds(half * self.half, self.half), :] if own else there
        return remote(src, there, self.send_sem.at[number], self.recv_sem.at[blk * 2 + half], to_leaf, to_blk)

    def wait(self, blk, half):
        self.build(blk, half, self.place.sibling, self.place.blk, 0).wait_recv()

    def push(self, cond, *parts):
        number = len(self.sent)
        pl.when(cond)(lambda: self.build(*parts[:4], number, *parts[4:]).start())
        self.sent.append((cond, parts, number))

    def steps(self):
        p = self.place
        helps = jnp.logical_not(p.main)
        sibling = (p.sibling, p.blk)
        for half in range(2):
            self.push(helps, p.blk, half, p.leaf, p.far, True)
            self.push(p.main, p.blk, half, p.leaf, p.near, True)
        for half in range(2):
            self.push(p.main, p.blk, half, *sibling, True)
        yield
        for half in range(2):
            pl.when(p.main)(lambda half=half: self.wait(p.far, half))
            self.push(p.main, p.far, half, p.leaf, p.near)
            self.push(p.main, p.far, half, *sibling)
        yield
        for blk in (p.near, p.opposite):
            for half in range(2):
                pl.when(p.main)(lambda blk=blk, half=half: self.wait(blk, half))
                self.push(p.main, blk, half, *sibling)
            yield

    def arrive(self, blk):
        for half in range(2):
            pl.when(jnp.logical_not(self.place.main))(lambda half=half: self.wait(blk, half))

    def finish(self):
        for cond, parts, number in self.sent:
            pl.when(cond)(lambda parts=parts, number=number: self.build(*parts[:4], number, *parts[4:]).wait_send())

    sends = 14


class GatherPair:
    def __init__(self, place, held, full, transit, send_sem, recv_sem):
        self.place, self.held, self.full, self.transit = place, held, full, transit
        self.rows, self.width = held.shape[0] // place.levels, full.shape[1]
        self.send_sem, self.recv_sem = send_sem, recv_sem
        self.sent = []

    def start(self, copy):
        copy.start()
        self.sent.append(copy)

    def send_of(self):
        return self.send_sem.at[len(self.sent)]

    def columns(self, level, pair):
        return self.held.at[rows_of(level, self.rows), pl.ds(pl.multiple_of(pair * self.width, 128), self.width)]

    def along(self, level, to_leaf):
        there = self.held.at[rows_of(level, self.rows), :]
        return remote(there, there, self.send_of(), self.recv_sem.at[level], to_leaf, self.place.blk)

    def target(self, level, blk, other):
        p = self.place
        if other:
            return self.transit.at[rows_of(level * 4 + blk, self.rows), :]
        return self.full.at[rows_of((2 * level + p.core) * 4 + blk, self.rows), :]

    def piece(self, level, src_blk, to_blk, other):
        p = self.place
        src = self.columns(level, 2 * (to_blk % 2) + (1 - p.core if other else p.core))
        number = p.levels + (level * 4 + src_blk) * 2 + other
        return remote(src, self.target(level, src_blk, other), self.send_of(), self.recv_sem.at[number], p.leaf, to_blk)

    def hand(self, level, core):
        p = self.place
        there = self.full.at[rows_of(2 * level + core, 4 * self.rows), :]
        return remote(self.transit.at[rows_of(level, 4 * self.rows), :], there, self.send_of(),
                      self.recv_sem.at[9 * p.levels + level], p.sibling, p.blk)

    def offer(self, level):
        p = self.place
        for to_blk in (p.near, p.far, p.opposite):
            for other in range(2):
                self.start(self.piece(level, p.blk, to_blk, other))
        for other in range(2):
            pair = 2 * (p.blk % 2) + (1 - p.core if other else p.core)
            self.target(level, p.blk, other)[...] = self.columns(level, pair)[...]

    def steps(self):
        p = self.place
        for to_leaf in p.line:
            self.start(self.along(p.z, to_leaf))
        self.offer(p.z)
        yield
        for leaf in p.line:
            self.along(leaf // 2, p.sibling).wait_recv()
            self.offer(leaf // 2)
        yield
        for level in (p.z, *[leaf // 2 for leaf in p.line]):
            for blk in (p.near, p.far, p.opposite):
                for other in range(2):
                    self.piece(level, blk, p.near, other).wait_recv()
            self.start(self.hand(level, p.core))
        yield
        for level in range(p.levels):
            self.hand(level, 1 - p.core).wait_recv()
        yield

    def finish(self):
        for copy in self.sent:
            copy.wait_send()

    @staticmethod
    def sends(levels):
        return levels - 1 + 7 * levels

    @staticmethod
    def receives(levels):
        return 10 * levels


class ReducePair:
    def __init__(self, place, total, out, boxes, send_sem, recv_sem):
        self.place, self.total, self.out = place, total, out
        self.rows = total.shape[0] // (place.levels * 8)
        self.from_far, self.from_line, self.from_pair = boxes
        self.send_sem, self.recv_sem = send_sem, recv_sem
        self.sent = []

    @staticmethod
    def slots(levels):
        return 4 * levels + 4

    @staticmethod
    def boxes(levels, rows, width, kind):
        return [pltpu.VMEM((levels * 4 * rows, width), kind) for n in range(2)] + [pltpu.VMEM((4 * rows, width), kind)]

    def build(self, src, box, slot, rows, number, leaf, blk):
        there = box.at[rows_of(slot, rows), :]
        return remote(there if src is None else src, there, self.send_sem.at[len(self.sent)], self.recv_sem.at[number], leaf, blk)

    def send(self, *parts):
        copy = self.build(*parts)
        copy.start()
        self.sent.append(copy)

    def arrived(self, box, slot, rows, number):
        self.build(None, box, slot, rows, number, self.place.sibling, self.place.blk).wait_recv()

    def twin(self, leaf, side):
        return rows_of(leaf * 2 + side, 2 * self.rows)

    def add(self, leaf, *sources):
        here = self.twin(leaf, self.place.side)
        value = self.total[here, :].astype(F32)
        for box, slot in sources:
            value = value + box[rows_of(slot, 2 * self.rows), :].astype(F32)
        self.total[here, :] = value.astype(self.total.dtype)

    def steps(self):
        p = self.place
        levels, rows = p.levels, 2 * self.rows
        for leaf in range(2 * levels):
            self.send(self.total.at[self.twin(leaf, 1 - p.side), :], self.from_far, leaf, rows, leaf, p.leaf, p.far)
        yield
        for leaf in range(2 * levels):
            self.arrived(self.from_far, leaf, rows, leaf)
            self.add(leaf, (self.from_far, leaf))
        for to_leaf in p.line:
            for core in range(2):
                slot = 2 * p.z + core
                self.send(self.total.at[self.twin(to_leaf // 2 * 2 + core, p.side), :], self.from_line, slot, rows,
                          2 * levels + slot, to_leaf, p.blk)
        yield
        for core in range(2):
            slots = [leaf // 2 * 2 + core for leaf in p.line]
            for slot in slots:
                self.arrived(self.from_line, slot, rows, 2 * levels + slot)
            self.add(2 * p.z + core, *[(self.from_line, slot) for slot in slots])
        for leaf, blk in ((p.sibling, p.blk), (p.leaf, p.near), (p.sibling, p.near)):
            src = self.total.at[rows_of(leaf * 4 + blk, self.rows), :]
            self.send(src, self.from_pair, p.pair, self.rows, 4 * levels + p.pair, leaf, blk)
        self.store(p.pair, self.total[rows_of(p.leaf * 4 + p.blk, self.rows), :])
        yield
        column = p.blk % 2
        for pair in (2 * column + 1 - p.core, 2 * (1 - column) + p.core, 2 * (1 - column) + 1 - p.core):
            self.arrived(self.from_pair, pair, self.rows, 4 * levels + pair)
            self.store(pair, self.from_pair[rows_of(pair, self.rows), :])
        yield

    def store(self, pair, value):
        for third in range(3):
            lanes = pl.ds(pl.multiple_of(third * D + pair * 128, 128), 128)
            self.out[:, lanes] = value[:, third * 128:third * 128 + 128].astype(F32)

    def finish(self):
        for copy in self.sent:
            copy.wait_send()


class TreeReduce:
    def __init__(self, place, part, from_core, box, send_sem, core_sem, recv_sem):
        self.place, self.part, self.from_core, self.box = place, part, from_core, box
        self.send_sem, self.core_sem, self.recv_sem = send_sem, core_sem, recv_sem

    def to_core(self, tile):
        p = self.place
        return remote(self.part.at[span(tile), :], self.from_core.at[tile // 2], self.send_sem.at[tile],
                      self.core_sem.at[tile // 2], p.sibling, p.blk)

    def to_owner(self, tile, which):
        p = self.place
        return remote(self.part.at[span(tile), :], self.box.at[tile % 2, which], self.send_sem.at[tile],
                      self.recv_sem.at[tile % 2 * 2 + which], p.served, tile // 2)

    def roles(self, tile):
        p = self.place
        collects = p.core == tile % 2
        gate = p.blk % 2 == tile // 2 % 2
        owner = (p.leaf == p.served) & (p.blk == tile // 2)
        return collects, gate, owner

    def offer(self, tile):
        collects, gate, owner = self.roles(tile)
        pl.when(jnp.logical_not(collects))(lambda: self.to_core(tile).start())

    def collect(self, tile):
        collects, gate, owner = self.roles(tile)

        def go():
            self.to_core(tile).wait_recv()
            total = self.part[span(tile), :].astype(F32) + self.from_core[tile // 2].astype(F32)
            self.part[span(tile), :] = total.astype(BF)
            pl.when(gate & jnp.logical_not(owner))(lambda: self.to_owner(tile, 0).start())
            pl.when(jnp.logical_not(gate))(lambda: self.to_owner(tile, 1).start())

            def keep():
                self.box[tile % 2, 0] = self.part[span(tile), :]

            pl.when(owner)(keep)

        pl.when(collects)(go)

    def arrive(self, half):
        p = self.place
        kept = p.main & (p.core == half)
        pl.when(jnp.logical_not(kept))(lambda: self.to_owner(half, 0).wait_recv())
        self.to_owner(half, 1).wait_recv()

    def finish(self, tile):
        collects, gate, owner = self.roles(tile)
        pl.when(jnp.logical_not(collects))(lambda: self.to_core(tile).wait_send())
        pl.when(collects & gate & jnp.logical_not(owner))(lambda: self.to_owner(tile, 0).wait_send())
        pl.when(collects & jnp.logical_not(gate))(lambda: self.to_owner(tile, 1).wait_send())


class Settle:
    def __init__(self, place, part, out, box, send_sem, recv_sem):
        self.place, self.part, self.out, self.box = place, part, out, box
        self.send_sem, self.recv_sem = send_sem, recv_sem
        self.rows = out.shape[0]

    def build(self, src_blk, to_blk):
        p = self.place
        return remote(self.part.at[rows_of(to_blk, self.rows), :], self.box.at[rows_of(src_blk, self.rows), :],
                      self.send_sem.at[to_blk], self.recv_sem.at[src_blk], p.leaf, to_blk)

    def steps(self):
        p = self.place
        self.copies = [self.build(p.blk, to) for to in (p.near, p.far, p.opposite)]
        for copy in self.copies:
            copy.start()
        yield
        total = self.part[rows_of(p.blk, self.rows), :]
        for blk in (p.near, p.far, p.opposite):
            self.build(blk, p.near).wait_recv()
            total = total + self.box[rows_of(blk, self.rows), :]
        self.out[...] = total
        yield

    def finish(self):
        for copy in self.copies:
            copy.wait_send()


class TableSum:
    def __init__(self, place, payload, box, rows_box, send_sem, recv_sem):
        self.place, self.payload, self.box, self.rows_box = place, payload, box, rows_box
        self.send_sem, self.recv_sem = send_sem, recv_sem
        self.leaves = place.levels * 2
        self.rows = self.leaves * 8

    def first(self, src_blk, to_blk):
        return remote(self.payload.at[rows_of(to_blk, self.rows), :], self.box.at[rows_of(src_blk, self.rows), :],
                      self.send_sem.at[to_blk], self.recv_sem.at[src_blk], self.place.leaf, to_blk)

    def second(self, src_leaf, to_leaf):
        p = self.place
        start = p.blk * self.leaves + to_leaf
        return remote(self.payload.at[rows_of(start, 8), :], self.rows_box.at[rows_of(src_leaf, 8), :],
                      self.send_sem.at[4 + to_leaf], self.recv_sem.at[4 + src_leaf], to_leaf, p.blk)

    def steps(self):
        p = self.place
        peers = (p.near, p.far, p.opposite)
        others = [(p.leaf + step) % self.leaves for step in range(1, self.leaves)]
        for to in peers:
            self.first(p.blk, to).start()
        yield
        here = rows_of(p.blk, self.rows)
        total = self.payload[here, :]
        for src in peers:
            self.first(src, p.near).wait_recv()
            total = total + self.box[rows_of(src, self.rows), :]
        self.payload[here, :] = total
        for to in others:
            self.second(p.leaf, to).start()
        self.rows_box[rows_of(p.leaf, 8), :] = self.payload[rows_of(p.blk * self.leaves + p.leaf, 8), :]
        yield
        for src in others:
            self.second(src, others[0]).wait_recv()
        yield

    def finish(self):
        p = self.place
        for to in (p.near, p.far, p.opposite):
            self.first(p.blk, to).wait_send()
        for step in range(1, self.leaves):
            self.second(p.leaf, (p.leaf + step) % self.leaves).wait_send()


SPAN = 256
TINY = 1e-05


def dot(left, right):
    return lax.dot_general(left, right, (((1,), (0,)), ((), ())), preferred_element_type=F32)


def dot_nt(left, right):
    return lax.dot_general(left, right, (((1,), (1,)), ((), ())), preferred_element_type=F32)


def dot_tn(left, right):
    return lax.dot_general(left, right, (((0,), (0,)), ((), ())), preferred_element_type=F32)


def iota(shape, axis):
    return lax.broadcasted_iota(jnp.int32, shape, axis)


def span(start, count=SPAN):
    if isinstance(start, int):
        return pl.ds(start * count, count)
    return pl.ds(pl.multiple_of(start * count, count), count)


def loop(count, body):
    def step(index, carry):
        body(index)
        return carry

    lax.fori_loop(0, count, step, 0)


def unit_rows(values):
    centred = values - jnp.mean(values, axis=-1, keepdims=True)
    root = lax.rsqrt(jnp.mean(centred * centred, axis=-1, keepdims=True) + TINY)
    return centred * root, root


def norm_back(grad, unit, root, scale):
    inner = grad * (1.0 + scale)
    return (
        inner
        - jnp.mean(inner, axis=-1, keepdims=True)
        - unit * jnp.mean(inner * unit, axis=-1, keepdims=True)
    ) * root


def spread_pattern(wide, group):
    column = iota((128, group), 1)
    turn = jnp.zeros((128, group), jnp.int32)
    for step in range(1, group // wide):
        turn = turn + (column >= step * wide).astype(jnp.int32)
    return (column - turn * wide == iota((128, group), 0)).astype(F32)


def shard_of_column(count, wide, group):
    column = iota((count, group), 1)
    turn = jnp.zeros((count, group), jnp.int32)
    for step in range(1, group // wide):
        turn = turn + (column >= step * wide).astype(jnp.int32)
    return turn


def aux_row(aux, leaf, row):
    chosen = (iota((8, aux.shape[0]), 1) == leaf * 256 + row).astype(BF)
    return dot(chosen, aux[...])[0:1, :]


def read_modulation(aux, timestep, mod, wide):
    count = aux.shape[0] // 64
    row = iota((count, aux.shape[0]), 0)
    column = iota((count, aux.shape[0]), 1)
    chosen = ((column - row * 64).astype(F32) == timestep).astype(BF)
    picked = dot(chosen, aux[...])
    group = wide * 4
    laid = dot(picked.astype(BF), spread_pattern(wide, group).astype(BF))
    offset = iota((count, group), 0) - shard_of_column(count, wide, group)
    for part in range(count // 4):
        mod[0:1, part * group:(part + 1) * group] = jnp.sum(
            jnp.where(offset == 4 * part, laid, 0.0), axis=0, keepdims=True
        )


def table_payload(sums, wide, count):
    group = wide * 4
    offset = iota((count, group), 0) - shard_of_column(count, wide, group)
    held = jnp.zeros((count, group), F32)
    for part in range(count // 4):
        held = held + jnp.where(offset == 4 * part, sums[0:1, part * group:(part + 1) * group], 0.0)
    cut = lax.dot_general(held, spread_pattern(wide, group), (((1,), (1,)), ((), ())),
                          preferred_element_type=F32, precision=lax.Precision.HIGHEST)
    leaves = count // 4
    row = iota((count * 8, count), 0)
    tile = sum((row >= 8 * step).astype(jnp.int32) for step in range(1, count))
    block = sum((row >= 8 * leaves * step).astype(jnp.int32) for step in range(1, 4))
    chosen = (iota((count * 8, count), 1) == (tile - block * leaves) * 4 + block).astype(F32)
    return lax.dot_general(chosen, cut, (((1,), (0,)), ((), ())),
                           preferred_element_type=F32, precision=lax.Precision.HIGHEST)


def block_bias(parents, bias, blocks):
    row, column = iota((128, 128), 0), iota((128, 128), 1)
    reach = (row == column).astype(F32)
    reach = jnp.maximum(reach, (row.astype(F32) == parents).astype(F32))
    for step in range((blocks - 1).bit_length()):
        low_reach = reach.astype(BF)
        reach = jnp.minimum(dot(low_reach, low_reach), 1.0)
    held = (reach[:blocks, :] - 1.0) * 1e30
    for block in range(blocks):
        bias[:, block * BLOCK:(block + 1) * BLOCK] = jnp.broadcast_to(held[:, block:block + 1], (blocks, BLOCK))


class Layer:
    def __init__(self, place, refs):
        self.place = place
        self.__dict__.update(refs)

    def project(self, chunk):
        rows = span(chunk)
        unit, root = unit_rows(self.tokens_all[rows, :].astype(F32))
        first = (unit * (1.0 + self.mod_served[0:1, D:2 * D]) + self.mod_served[0:1, 0:D]).astype(BF)
        self.h1[rows, :] = first
        made = dot(first, self.w_pair[...])
        lane = iota((SPAN, 128), 1)
        query = made[:, 0:128].astype(BF).astype(F32) * HEAD ** (-0.5)
        self.q_masked[0, rows, :] = jnp.where(lane < HEAD, query, 0.0).astype(BF)
        self.q_masked[1, rows, :] = jnp.where(lane >= HEAD, query, 0.0).astype(BF)
        key = made[:, 128:256]
        value = made[:, 256:384]
        self.key[rows, :] = key.astype(BF)
        self.value[rows, :] = value.astype(BF)
        self.key_t[:, rows] = key.T.astype(BF)
        value_t = value.T.astype(BF)
        ones = jnp.ones((16, SPAN), BF)
        self.value_t[0, 0:HEAD, rows] = value_t[:HEAD]
        self.value_t[1, 0:HEAD, rows] = value_t[HEAD:]
        self.value_t[0, HEAD:HEAD + 16, rows] = ones
        self.value_t[1, HEAD:HEAD + 16, rows] = ones

    def attend(self, tile):
        queries = slice(tile * SPAN, (tile + 1) * SPAN)
        base = tile * (tile + 1) // 2

        def score(j, head):
            raw = dot_nt(self.key[j * SPAN:(j + 1) * SPAN, :], self.q_masked[head, queries, :])
            upper = raw[:BLOCK] + self.bias[2 * j:2 * j + 1, queries]
            lower = raw[BLOCK:] + self.bias[2 * j + 1:2 * j + 2, queries]
            kept = jnp.concatenate((upper, lower), axis=0)
            return kept + self.corner[...] if j == tile else kept

        top = [jnp.full((8, SPAN), -3e30, F32) for head in range(2)]
        for j in range(tile + 1):
            for head in range(2):
                top[head] = jnp.maximum(top[head], jnp.max(score(j, head).reshape(SPAN // 8, 8, SPAN), axis=0))
        top = [jnp.max(each, axis=0, keepdims=True) for each in top]
        mix = [0.0, 0.0]
        for j in range(tile + 1):
            for head in range(2):
                weight = jnp.exp(score(j, head) - top[head]).astype(BF)
                self.weights[base + j, head] = weight
                mix[head] = mix[head] + dot(self.value_t[head, :, j * SPAN:(j + 1) * SPAN], weight)
        halves = []
        for head in range(2):
            inverse = 1.0 / mix[head][HEAD:HEAD + 8, :]
            self.inverse[head, :, queries] = inverse
            halves.append(mix[head][:HEAD, :] * inverse[0:1])
        attended_t = jnp.concatenate(halves, axis=0)
        self.attended_t[:, queries] = attended_t
        self.attended[queries, :] = attended_t.T.astype(BF)

    def cross_keys(self):
        made = dot(self.source_all[...], self.w_ckv).astype(BF)
        lane = iota((2 * ENC, 128), 1)
        row = iota((2 * ENC, 128), 0)
        own = (lane < HEAD) == (row < ENC)
        for pair in range(4):
            for box, start in ((self.cross_k, 0), (self.cross_v, D)):
                part = made[:, start + 128 * pair:start + 128 * pair + 128].astype(F32)
                box[pair] = jnp.where(own, jnp.concatenate((part, part), axis=0), 0.0).astype(BF)

    def middle(self, chunk):
        rows = span(chunk)
        y1 = self.tokens[rows, :].astype(F32) + dot(self.gathered[rows, :], self.w_o)
        self.y1[rows, :] = y1
        unit, root = unit_rows(y1)
        h2 = (unit * (1.0 + self.mod[0:1, 3 * D:4 * D]) + self.mod[0:1, 2 * D:3 * D]).astype(BF)
        self.h2[rows, :] = h2
        query = (dot(h2, self.w_cq).astype(BF).astype(F32) * HEAD ** (-0.5)).astype(BF)
        self.cross_q[rows, :] = query
        lane = iota((SPAN, 128), 1)
        same = ((iota((128, 128), 0) < ENC) == (iota((128, 128), 1) < ENC)).astype(BF)
        out = []
        for pair in range(4):
            raw = dot_nt(query[:, 128 * pair:128 * pair + 128], self.cross_k[pair])
            left = jnp.max(jnp.where(lane < ENC, raw, -3e38), axis=-1, keepdims=True)
            right = jnp.max(jnp.where(lane >= ENC, raw, -3e38), axis=-1, keepdims=True)
            weight = jnp.exp(raw - jnp.where(lane < ENC, left, right))
            weight = weight / dot(weight.astype(BF), same)
            self.cross_p[pair, rows, :] = weight.astype(BF)
            out.append(dot(weight.astype(BF), self.cross_v[pair]))
        cross = jnp.concatenate(out, axis=1).astype(BF)
        self.cross_out[rows, :] = cross
        y2 = y1 + dot(cross, self.w_co)
        self.y2[rows, :] = y2
        unit, root = unit_rows(y2)
        self.h3[rows, :] = (unit * (1.0 + self.mod[0:1, 5 * D:6 * D]) + self.mod[0:1, 4 * D:5 * D]).astype(BF)

    def hidden(self, chunk):
        units = span(chunk)
        u = dot(self.h3[...], self.w_in(units))
        dg = dot_nt(self.cotangent[...], self.w_out[units, :])
        square = u * u
        slope = 0.7978845608028654
        bend = jnp.tanh(u * (slope + slope * 0.044715 * square))
        half = 0.5 + 0.5 * bend
        self.act[:, units] = (u * half).astype(BF)
        turn = half + 0.5 * u * (1.0 - bend * bend) * (slope + 3.0 * slope * 0.044715 * square)
        self.d_hidden[:, units] = (dg * turn).astype(BF)
        self.grad_out(units, dot_tn(self.act[:, units], self.cotangent[...]).astype(BF))
        self.grad_in(units, dot_tn(self.h3[...], self.d_hidden[:, units]).astype(BF))

    def finish_forward(self, chunk):
        rows = span(chunk)
        self.mixed[rows, :] = (self.y2[rows, :] + dot(self.act[rows, :], self.w_out[...])).astype(BF)

    def sums(self, piece, shift, scale):
        self.mod_grad[0:1, 2 * piece * D:(2 * piece + 1) * D] += jnp.sum(shift, axis=0, keepdims=True)
        self.mod_grad[0:1, (2 * piece + 1) * D:(2 * piece + 2) * D] += jnp.sum(scale, axis=0, keepdims=True)

    def back_three(self, chunk):
        rows = span(chunk)
        dh3 = dot_nt(self.d_hidden[rows, :], self.w_in(slice(None)))
        unit, root = unit_rows(self.y2[rows, :])
        self.sums(2, dh3, dh3 * unit)
        dy2 = self.cotangent[rows, :].astype(F32) + norm_back(dh3, unit, root, self.mod[0:1, 5 * D:6 * D])
        self.dy[rows, :] = dy2
        self.db[rows, :] = dy2.astype(BF)

    def back_cross(self, chunk):
        rows = span(chunk)
        dca = dot_nt(self.db[rows, :], self.w_co).astype(BF)
        lane = iota((SPAN, 128), 1)
        row = iota((128, 128), 0)
        own = (row < ENC) == (iota((128, 128), 1) < HEAD)
        parts = []
        for pair in range(4):
            lanes = slice(128 * pair, 128 * pair + 128)
            low_weight = self.cross_p[pair, rows, :]
            weight = low_weight.astype(F32)
            dc = dot_nt(dca[:, lanes], self.cross_v[pair])
            both_ = weight * dc
            left = jnp.sum(jnp.where(lane < ENC, both_, 0.0), axis=-1, keepdims=True)
            right = jnp.sum(jnp.where(lane >= ENC, both_, 0.0), axis=-1, keepdims=True)
            ds = (weight * (dc - jnp.where(lane < ENC, left, right))).astype(BF)
            parts.append((dot(ds, self.cross_k[pair]) * HEAD ** (-0.5)).astype(BF))
            dk = jnp.where(own, dot_tn(ds, self.cross_q[rows, lanes]), 0.0)
            dv = jnp.where(own, dot_tn(low_weight, dca[:, lanes]), 0.0)
            self.d_cross[:, lanes] += dk[:ENC] + dk[ENC:]
            self.d_cross[:, 128 * pair + D:128 * pair + D + 128] += dv[:ENC] + dv[ENC:]
        dcq = jnp.concatenate(parts, axis=1)
        self.dcq[rows, :] = dcq
        dh2 = dot_nt(dcq, self.w_cq)
        unit, root = unit_rows(self.y1[rows, :])
        self.sums(1, dh2, dh2 * unit)
        dy1 = self.dy[rows, :] + norm_back(dh2, unit, root, self.mod[0:1, 3 * D:4 * D])
        self.dy[rows, :] = dy1
        low_dy1 = dy1.astype(BF)
        self.db1[rows, :] = low_dy1
        self.d_attn[rows, :] = dot_nt(low_dy1, self.w_o).astype(BF)

    def attend_back(self, tile):
        queries = slice(tile * SPAN, (tile + 1) * SPAN)
        base = tile * (tile + 1) // 2
        d_att_t = self.d_att_all[queries, :].astype(F32).T
        scaled = [d_att_t[HEAD * h:HEAD * h + HEAD] * self.inverse[h, 0:1, queries] for h in range(2)]
        delta = [
            jnp.sum(scaled[h] * self.attended_t[HEAD * h:HEAD * h + HEAD, queries], axis=0, keepdims=True)
            for h in range(2)
        ]
        flat = jnp.concatenate(scaled, axis=0).T
        lane = iota((SPAN, 128), 1)
        masked = [jnp.where((lane < HEAD) == (h == 0), flat, 0.0).astype(BF) for h in range(2)]
        dq_t = [0.0, 0.0]
        for j in range(tile + 1):
            keys = slice(j * SPAN, (j + 1) * SPAN)
            dk = dv = 0.0
            for head in range(2):
                dp = dot_nt(self.value[keys, :], masked[head])
                weight = self.weights[base + j, head]
                ds = (weight.astype(F32) * (dp - delta[head])).astype(BF)
                dk = dk + dot(ds, self.q_masked[head, queries, :])
                dv = dv + dot(weight, masked[head])
                dq_t[head] = dq_t[head] + dot(self.key_t[HEAD * head:HEAD * head + HEAD, keys], ds)
            self.dk[keys, :] += dk
            self.dv[keys, :] += dv
        self.d_pair[queries, 0:128] = (jnp.concatenate(dq_t, axis=0) * HEAD ** (-0.5)).T.astype(BF)
        self.d_pair[queries, 128:256] = self.dk[queries, :].astype(BF)
        self.d_pair[queries, 256:384] = self.dv[queries, :].astype(BF)
        self.dh1_part[queries, :] = dot_nt(self.d_pair[queries, :], self.w_pair[...]).astype(BF)


VMEM = pl.BlockSpec(memory_space=pltpu.VMEM)
SMEM = pl.BlockSpec(memory_space=pltpu.SMEM)
CROSS = 5 * D
PACKED = ((0, 2 * D), (2 * D, CROSS), (CROSS, CROSS + FF // 2), (CROSS + FF // 2, CROSS + FF))
FIXED = True
LAST = ((0, D // 2), (D // 2, D))


class Weights(Layer):
    w_o = property(lambda self: self.pack[:, 0:D])
    w_cq = property(lambda self: self.pack[:, D:2 * D])
    w_ckv = property(lambda self: self.pack[:, 2 * D:4 * D])
    w_co = property(lambda self: self.pack[:, 4 * D:CROSS])

    def w_in(self, units):
        return self.pack.at[:, CROSS:CROSS + FF][:, units]

    def grad_in(self, units, value):
        self.grad_pack.at[:, CROSS:CROSS + FF][:, units] = value

    def grad_out(self, units, value):
        self.grad_w_out[units, :] = value

    def grad_into(self, start, left, right):
        for step in range(right.shape[1] // SPAN):
            columns = slice(start + step * SPAN, start + (step + 1) * SPAN)
            self.grad_pack[:, columns] = dot_tn(left[...], right[:, step * SPAN:(step + 1) * SPAN]).astype(BF)


ANY = pl.BlockSpec(memory_space=pl.ANY)
INS = ("i_tokens", "i_cotangent", "i_encoded", "parents", "timestep", "i_qkv", "i_o", "i_cq", "i_ckv", "i_co", "i_in", "i_out", "i_table")
OUTS = ("mixed", "grad_tokens", "g_encoded", "g_qkv", "g_o", "g_cq", "g_ckv", "g_co", "g_in", "g_out", "g_table")


def layer_scratch(rows, tree, blocks, levels, wide):
    tiles = tree // SPAN
    count = levels * 8
    each = D // count
    plain = lambda *shape: pltpu.VMEM(shape, F32)
    short = lambda *shape: pltpu.VMEM(shape, BF)
    dma = pltpu.SemaphoreType.DMA
    scratch = dict(
        tokens=short(rows, D), cotangent=short(rows, D), qkv_own=short(each, 3 * D), mixed=short(rows, D), grad_tokens=plain(rows, D),
        g_encoded=plain(ENC // 4, D), g_qkv=plain(each, 3 * D), g_o=plain(each, D), g_cq=plain(each, D), g_ckv=plain(each, 2 * D),
        g_co=plain(each, D), g_in=plain(each, FF), g_out=plain(FF // count, D), g_table=plain(STEPS, wide),
        in_sem=dma((11,)), out_sem=dma((11,)),
        held=short(levels * each, 3 * D), w_pair=short(D, 384), transit=short(D // 2, 384), pack=short(D, CROSS + FF), w_out=short(FF, D),
        aux=short(count * 64, 128), tokens_all=short(tree, D), source_all=short(ENC, D),
        mod=plain(8, 6 * D), mod_served=plain(8, 6 * D), mod_grad=plain(8, 6 * D), bias=plain(blocks, tree), corner=plain(SPAN, SPAN),
        h1=short(tree, D), q_masked=short(2, tree, 128), key=short(tree, 128), value=short(tree, 128),
        key_t=short(128, tree), value_t=short(2, HEAD + 16, tree),
        weights=short(tiles * (tiles + 1) // 2, 2, SPAN, SPAN), inverse=plain(2, 8, tree),
        attended_t=plain(128, tree), attended=short(tree, 128), gathered=short(rows, D),
        cross_k=short(4, 2 * ENC, 128), cross_v=short(4, 2 * ENC, 128), cross_q=short(rows, D), cross_p=short(4, rows, 128),
        cross_out=short(rows, D), y1=plain(rows, D), db1=short(rows, D), h2=short(rows, D), h3=short(rows, D),
        act=short(rows, FF), d_hidden=short(rows, FF),
        d_cross=plain(ENC, 2 * D), dcq=short(rows, D), d_att_all=short(tree, 128),
        dk=plain(tree, 128), dv=plain(tree, 128),
        d_pair=short(tree, 384), from_core=short(4, SPAN, D), dh1_box=short(2, 2, SPAN, D),
        grad_pack=short(D, CROSS + FF), grad_w_out=short(FF, D), grad_pair=short(D, 384), source_part=plain(ENC, D),
        payload=plain(count * 8, 128), table_box=plain(count * 8, 128), table_rows=plain(levels * 16, 128), settle_box=plain(ENC, D),
        a_send=dma((tiles,)), a_recv=dma((tiles,)), d_send=dma((8,)), d_recv=dma((8,)),
        h_send=dma((tiles,)), h_core=dma((4,)), h_recv=dma((4,)),
        send=dma((7, Gather.sends(levels))), recv=dma((7, count)),
        pair_send=dma((GatherPair.sends(levels),)), pair_recv=dma((GatherPair.receives(levels),)),
        share_send=dma((Share.sends,)), share_recv=dma((8,)), spread_send=dma((3,)), spread_recv=dma((4,)),
        r_send=dma((6, Reduce.slots(levels))), r_recv=dma((6, Reduce.slots(levels))), line=plain(64, 128),
        rp_send=dma((ReducePair.slots(levels),)), rp_recv=dma((ReducePair.slots(levels),)),
        settle_send=dma((4,)), settle_recv=dma((4,)), t_send=dma((4 + 2 * levels,)), t_recv=dma((4 + 2 * levels,)),
    )
    for piece, (height, width, line_last) in enumerate(
        [(FF // count, end - start, False) for start, end in LAST]
        + [(each, end - start, True) for start, end in PACKED[2:] + PACKED[:2]]
    ):
        for n, box in enumerate(Reduce.boxes(levels, height, width, BF, line_last)):
            scratch[f"box{piece}_{n}"] = box
    for n, box in enumerate(ReducePair.boxes(levels, each, 384, BF)):
        scratch[f"box_pair{n}"] = box
    return scratch


def layer_kernel(levels, wide, names, refs):
    place = Place(levels)
    refs = dict(zip(names, refs))
    refs["y2"] = refs["dy"] = refs["grad_tokens"]
    refs["db2"] = refs["db"] = refs["h3"]
    refs["d_attn"] = refs["cross_q"]
    refs["dh1_part"] = refs["tokens_all"]
    w = Weights(place, refs)
    blk, leaf = place.blk, place.leaf
    rows = w.tokens.shape[0]
    tree = w.tokens_all.shape[0]
    tiles = tree // SPAN
    halves = rows // SPAN
    blocks = tree // BLOCK
    count = levels * 8
    each = D // count
    index = leaf * 4 + blk
    own_lanes = pl.ds(pl.multiple_of(place.pair * 128, 128), 128)

    mine = rows_of(index, each)
    moves = [
        (w.i_tokens, w.tokens), (w.i_qkv, w.qkv_own),
        (w.i_encoded, w.source_all.at[rows_of(blk, w.i_encoded.shape[0]), :]),
        (w.i_out, w.w_out.at[rows_of(index, w.i_out.shape[0]), :]),
    ]
    start = 0
    for name in ("i_o", "i_cq", "i_ckv", "i_co", "i_in"):
        width = refs[name].shape[1]
        moves.append((refs[name], w.pack.at[mine, start:start + width]))
        start += width
    copies = [pltpu.make_async_copy(src, dst, w.in_sem.at[n]) for n, (src, dst) in enumerate(moves)]
    for copy in copies:
        copy.start()
    lane = iota((1, 128), 1)
    parents = jnp.zeros((1, 128), F32)
    for block in range(blocks):
        parents = jnp.where(lane == block, w.parents[0, block].astype(F32), parents)
    w.line[...] = jnp.zeros_like(w.line)
    w.line[:STEPS, :wide] = w.i_table[...].astype(F32)
    w.line[STEPS:STEPS + 1, :] = jnp.full((1, 128), w.timestep[0].astype(F32))
    w.line[STEPS + 1:STEPS + 2, :] = parents
    w.aux[rows_of(index, 64), :] = w.line[...].astype(BF)
    place.greet()
    for copy in copies:
        copy.wait()
    late = pltpu.make_async_copy(w.i_cotangent, w.cotangent, w.in_sem.at[10])
    late.start()

    def keep_tokens():
        w.tokens_all[rows_of(blk, rows), :] = w.tokens[...]

    pl.when(place.main)(keep_tokens)
    for pair in range(4):
        for third in range(3):
            w.held[rows_of(place.z, each), 384 * pair + 128 * third:384 * pair + 128 * third + 128] = (
                w.qkv_own[:, D * third + 128 * pair:D * third + 128 * pair + 128])
    given = []

    def give(*outs):
        for name in outs:
            copy = pltpu.make_async_copy(refs[name], refs["o_" + name], w.out_sem.at[OUTS.index(name)])
            copy.start()
            given.append(copy)

    weave = GatherPair(place, w.held, w.w_pair, w.transit, w.pair_send, w.pair_recv)
    table = GatherLine(place, w.aux, 64, slice(None), w.send.at[6], w.recv.at[6])
    share = Share(place, w.tokens, w.tokens_all, w.share_send, w.share_recv)
    spread = Spread(place, w.source_all, w.i_encoded.shape[0], w.spread_send, w.spread_recv)
    loads = [
        (GatherLine if n < 2 else Gather)(place, w.pack, each, slice(*cut), w.send.at[n], w.recv.at[n]) for n, cut in enumerate(PACKED)
    ] + [
        Gather(place, w.w_out, FF // count, slice(*cut), w.send.at[4 + n], w.recv.at[4 + n], FIXED and n == 0) for n, cut in enumerate(LAST)
    ]
    weave_steps, table_steps, share_steps = weave.steps(), table.steps(), share.steps()
    load_steps = [load.steps() for load in loads]

    def ticks(steps, number=1):
        for turn in range(number):
            for step in steps:
                next(step, None)

    first, fore, rest = load_steps[:2], load_steps[2:4], load_steps[4:]
    beats = iter([first, first + fore + rest, first + fore, first + rest, fore + rest, fore + rest])

    def load_tick():
        ticks(next(beats, []))

    ticks([weave_steps, table_steps, share_steps])
    spread.start()
    w.mod_grad[...] = jnp.zeros_like(w.mod_grad)
    w.d_cross[...] = jnp.zeros_like(w.d_cross)
    w.dk[...] = jnp.zeros_like(w.dk)
    w.dv[...] = jnp.zeros_like(w.dv)
    row, column = iota((SPAN, SPAN), 0), iota((SPAN, SPAN), 1)
    w.corner[...] = jnp.where(((row < BLOCK) == (column < BLOCK)) & (row > column), -1e30, 0.0)
    ticks([weave_steps, table_steps])
    ticks(load_steps)
    ticks([table_steps, share_steps, weave_steps])
    ticks(load_steps[2:])
    ticks([table_steps, weave_steps], 6)
    load_tick()
    block_bias(aux_row(w.aux, place.served, STEPS + 1), w.bias, blocks)
    read_modulation(w.aux, w.timestep[0].astype(F32), w.mod, wide)
    read_modulation(w.aux, aux_row(w.aux, place.served, STEPS)[0:1, 0:1], w.mod_served, wide)

    def project(block):
        share.arrive(block)
        for half in range(halves):
            w.project(block * halves + half)

    project(blk)
    project(place.far)
    ticks([share_steps])
    project(place.near)
    ticks([share_steps])
    load_tick()
    project(place.opposite)

    def attended_copy(tile, pair, here):
        there = w.gathered.at[span(tile % halves), pl.ds(pl.multiple_of(pair * 128, 128), 128)]
        to_leaf, to_blk = (leaf, place.near) if here else (place.served, tile // halves)
        return remote(w.attended.at[span(tile), :], there, w.a_send.at[tile], w.a_recv.at[pair * halves + tile % halves], to_leaf, to_blk)

    def mine_too(tile):
        return (place.served == leaf) & (blk == tile // halves)

    for tile in range(tiles):
        w.attend(tile)
        away = jnp.logical_not(mine_too(tile))
        pl.when(away)(lambda tile=tile: attended_copy(tile, place.pair, False).start())

        def keep(tile=tile):
            w.gathered[span(tile % halves), own_lanes] = w.attended[span(tile), :]

        pl.when(jnp.logical_not(away))(keep)
        if tile in (tiles - 3, tiles - 1):
            load_tick()
    spread.arrive()
    w.cross_keys()
    for pair in range(4):
        for half in range(halves):
            other = jnp.logical_not(place.main & (place.pair == pair))
            pl.when(other)(lambda pair=pair, half=half: attended_copy(half, pair, True).wait_recv())
    for half in range(halves):
        w.middle(half)
        load_tick()
    late.wait()

    def writer(*outs):
        def store(there, value):
            start = 0
            for out, at, width in outs:
                out[there, at:at + width] = value[:, start:start + width]
                start += width

        return store

    writers = [
        writer((w.g_out, 0, D // 2)), writer((w.g_out, D // 2, D // 2)),
        writer((w.g_in, 0, FF // 2)), writer((w.g_in, FF // 2, FF // 2)),
        writer((w.g_o, 0, D), (w.g_cq, 0, D)), writer((w.g_ckv, 0, 2 * D), (w.g_co, 0, D)),
    ]
    sums = []
    for n, (total, height, cut) in enumerate(
        [(w.grad_w_out, FF // count, cut) for cut in LAST] + [(w.grad_pack, each, cut) for cut in PACKED[2:] + PACKED[:2]]
    ):
        sums.append(Reduce(place, total, height, slice(*cut), writers[n], [refs[f"box{n}_{k}"] for k in range(4)],
                           w.r_send.at[n], w.r_recv.at[n], n >= 2))
    out0, out1, in0, in1, cross0, cross1 = sum_steps = [job.steps() for job in sums]
    outs, units, cross = [out0, out1], [in0, in1], [cross0, cross1]
    half_way = FF // SPAN // 2
    for step in range(half_way):
        w.hidden(step)
    ticks([in0])
    for step in range(half_way, half_way + half_way // 2):
        w.hidden(step)
    ticks([in0])
    for step in range(half_way + half_way // 2, 2 * half_way):
        w.hidden(step)
    ticks(outs + [in1])
    for job in loads + [weave, table, share, spread]:
        job.finish()
    for half in range(halves):
        w.finish_forward(half)
    give("mixed")
    for half in range(halves):
        w.back_three(half)
    ticks(outs)

    def da_copy(src, pair, half):
        return remote(w.d_attn.at[span(half), pair * 128:pair * 128 + 128], w.d_att_all.at[span(src * halves + half), :],
                      w.d_send.at[pair * 2 + half], w.d_recv.at[src * 2 + half], 2 * place.z + pair % 2, 2 * place.core + pair // 2)

    def stays(pair):
        return place.main & (place.pair == pair)

    for half in range(halves):
        w.back_cross(half)
        for pair in range(4):
            pl.when(jnp.logical_not(stays(pair)))(lambda pair=pair, half=half: da_copy(blk, pair, half).start())

    def keep_da():
        w.d_att_all[rows_of(blk, rows), :] = w.d_attn[:, own_lanes]

    pl.when(place.main)(keep_da)
    ticks(outs + [in1])
    w.grad_into(4 * D, w.cross_out, w.db2)
    w.grad_into(0, w.gathered, w.db1)
    w.grad_into(D, w.h2, w.dcq)
    low_cross = w.d_cross[...].astype(BF)
    for step in range(2 * D // SPAN):
        columns = slice(2 * D + step * SPAN, 2 * D + (step + 1) * SPAN)
        w.grad_pack[:, columns] = dot_tn(w.source_all[...], low_cross[:, step * SPAN:(step + 1) * SPAN]).astype(BF)
    w.source_part[...] = dot_nt(low_cross, w.w_ckv)
    settle = Settle(place, w.source_part, w.g_encoded, w.settle_box, w.settle_send, w.settle_recv)
    settle_steps = settle.steps()
    ticks(cross + [settle_steps])
    for src in range(4):
        for half in range(halves):
            pl.when(jnp.logical_not(place.main & (blk == src)))(lambda src=src, half=half: da_copy(src, 0, half).wait_recv())

    tree_sum = TreeReduce(place, w.dh1_part, w.from_core, w.dh1_box, w.h_send, w.h_core, w.h_recv)
    plan = [
        (tiles - 1, cross + [settle_steps]), (tiles - 2, units), (tiles - 3, outs), (tiles - 4, cross),
        (tiles - 5, units), (tiles - 6, outs), (tiles - 7, cross),
    ]
    for tile in range(tiles - 1, -1, -1):
        w.attend_back(tile)
        tree_sum.offer(tile)
        if tile + 1 < tiles:
            tree_sum.collect(tile + 1)
        for when, steps in plan:
            if when == tile:
                ticks(steps)

    def pair_grad(step):
        w.grad_pair[span(step), :] = dot_tn(w.h1[:, span(step)], w.d_pair[...]).astype(BF)

    loop(D // SPAN, pair_grad)
    pair_sum = ReducePair(place, w.grad_pair, w.g_qkv, [refs[f"box_pair{n}"] for n in range(3)], w.rp_send, w.rp_recv)
    pair_steps = pair_sum.steps()
    ticks([pair_steps])
    tree_sum.collect(0)
    ticks([pair_steps])

    def last(half):
        tree_sum.arrive(half)
        here = span(half)
        dh1 = w.dh1_box[half, 0].astype(F32) + w.dh1_box[half, 1].astype(F32)
        unit, root = unit_rows(w.tokens[here, :].astype(F32))
        w.sums(0, dh1, dh1 * unit)
        w.grad_tokens[here, :] = w.dy[here, :] + norm_back(dh1, unit, root, w.mod[0:1, D:2 * D])

    for half in range(halves):
        last(half)
    give("grad_tokens")
    w.payload[...] = table_payload(w.mod_grad[0:1, :], wide, count)
    table_sum = TableSum(place, w.payload, w.table_box, w.table_rows, w.t_send, w.t_recv)
    table_steps = table_sum.steps()
    ticks([table_steps])
    ticks(sum_steps, 10)
    give("g_encoded", "g_o", "g_cq", "g_ckv", "g_co", "g_in", "g_out")
    ticks([pair_steps, table_steps], 10)
    give("g_qkv")

    leaves = levels * 2
    chosen = (iota((leaves, count * 64), 1) == iota((leaves, count * 64), 0) * 256 + STEPS).astype(BF)
    steps_all = dot(chosen, w.aux[...])
    line = iota((64, 128), 0).astype(F32)
    grad_table = jnp.zeros((64, 128), F32)
    for tree_at in range(leaves):
        grad_table = grad_table + jnp.where(line == steps_all[tree_at:tree_at + 1, :], w.table_rows[8 * tree_at:8 * tree_at + 1, :], 0.0)
    w.g_table[...] = grad_table[:STEPS, :wide]
    give("g_table")

    for tile in range(tiles):
        pl.when(jnp.logical_not(mine_too(tile)))(lambda tile=tile: attended_copy(tile, place.pair, False).wait_send())
        tree_sum.finish(tile)
    for pair in range(4):
        for half in range(halves):
            pl.when(jnp.logical_not(stays(pair)))(lambda pair=pair, half=half: da_copy(blk, pair, half).wait_send())
    for job in sums + [settle, pair_sum, table_sum]:
        job.finish()
    for copy in given:
        copy.wait()


def copy_kernel(count, refs):
    ins, outs, held, sems = refs[:count], refs[count:2 * count], refs[2 * count:3 * count], refs[3 * count]
    inward = [pltpu.make_async_copy(ins[n], held[n], sems.at[0, n]) for n in range(count)]
    outward = [pltpu.make_async_copy(held[n], outs[n], sems.at[1, n]) for n in range(count)]
    for copy in inward:
        copy.start()
    for copy, then in zip(inward, outward):
        copy.wait()
        then.start()
    for copy in outward:
        copy.wait()


def copy_all(arrays):
    return pl.pallas_call(
        lambda *refs: copy_kernel(len(arrays), refs),
        out_shape=[jax.ShapeDtypeStruct(array.shape, array.dtype) for array in arrays],
        in_specs=[ANY] * len(arrays),
        out_specs=[ANY] * len(arrays),
        scratch_shapes=[pltpu.VMEM(array.shape, array.dtype) for array in arrays] + [pltpu.SemaphoreType.DMA((2, len(arrays)))],
    )(*arrays)


def per_device(tokens, cotangent, encoded, parents, timestep, w_qkv, w_o, w_cq, w_ckv, w_co, w_in, w_out, mod_table):
    levels = lax.axis_size("leaf") // 2
    rows, wide = tokens.shape[0], mod_table.shape[1]
    blocks = parents.shape[1]
    tree = blocks * BLOCK
    ins = (tokens, cotangent, encoded, parents, timestep, w_qkv, w_o, w_cq, w_ckv, w_co, w_in, w_out, mod_table)
    scratch = layer_scratch(rows, tree, blocks, levels, wide)
    out = lambda like: jax.ShapeDtypeStruct(like.shape, F32)
    names = INS + tuple("o_" + name for name in OUTS) + tuple(scratch)
    return copy_all(pl.pallas_call(
        lambda *refs: layer_kernel(levels, wide, names, refs),
        out_shape=[jax.ShapeDtypeStruct((rows, D), BF), out(tokens), out(encoded)]
        + [out(weight) for weight in (w_qkv, w_o, w_cq, w_ckv, w_co, w_in, w_out, mod_table)],
        in_specs=[SMEM if name in ("parents", "timestep") else VMEM if name == "i_table" else ANY for name in INS],
        out_specs=[ANY] * len(OUTS),
        scratch_shapes=list(scratch.values()),
        compiler_params=pltpu.CompilerParams(collective_id=0, has_side_effects=True, vmem_limit_bytes=(64 << 20) - (64 << 10)),
    )(*ins))


def solution(mesh):
    fits = mesh.shape["blk"] == 4 and mesh.shape["leaf"] == 8
    return jax.shard_map(
        per_device if fits else generic_device,
        mesh=mesh,
        in_specs=(
            P(("leaf", "blk"), None),
            P(("leaf", "blk"), None),
            P(("leaf", "blk"), None),
            P("leaf", None),
            P("leaf"),
            P(("leaf", "blk"), None),
            P(("leaf", "blk"), None),
            P(("leaf", "blk"), None),
            P(("leaf", "blk"), None),
            P(("leaf", "blk"), None),
            P(("leaf", "blk"), None),
            P(("leaf", "blk"), None),
            P(None, ("leaf", "blk")),
        ),
        out_specs=(
            P(("leaf", "blk"), None),
            P(("leaf", "blk"), None),
            P(("leaf", "blk"), None),
            P(("leaf", "blk"), None),
            P(("leaf", "blk"), None),
            P(("leaf", "blk"), None),
            P(("leaf", "blk"), None),
            P(("leaf", "blk"), None),
            P(("leaf", "blk"), None),
            P(("leaf", "blk"), None),
            P(None, ("leaf", "blk")),
        ),
        check_vma=False,
    )
```
